32 devices in a mesh: dp: 4 (over y, x), tensor: 8 (over z, core).
Axes of the slice: x: 2, y: 2, z: 4, core: 2. Of those that a mesh axis runs over, the one named last changes fastest.
Arguments:
- tokens: bfloat16 [8, 1024, 2048], P('dp', 'tensor'), may hold values from -6 to 6
- cotangent: bfloat16 [8, 1024, 2048], P('dp', 'tensor'), may hold values from -6 to 6
- lengths: int32 [8], P('dp'), may hold values from 256 to 1024, as said below
- ln1_gain: float32 [2048], replicated, may hold values from 0.25 to 1.75
- ln1_shift: float32 [2048], replicated, may hold values from -1.5 to 1.5
- qkv_weight: bfloat16 [3, 2048, 2048], P(None, None, 'tensor'), may hold values from -0.125 to 0.125
- qkv_bias: float32 [2, 2048], P(None, 'tensor'), may hold values from -2.5 to 2.5
- out_weight: bfloat16 [2048, 2048], P('tensor'), may hold values from -1 to 1
- out_bias: float32 [2048], replicated, may hold values from -1.5 to 1.5
- ln2_gain: float32 [2048], replicated, may hold values from 0.25 to 1.75
- ln2_shift: float32 [2048], replicated, may hold values from -1.5 to 1.5
- up_weight: bfloat16 [2048, 8192], P(None, 'tensor'), may hold values from -0.125 to 0.125
- up_bias: float32 [8192], P('tensor'), may hold values from -2.5 to 2.5
- down_weight: bfloat16 [8192, 2048], P('tensor'), may hold values from -0.0625 to 0.0625
- down_bias: float32 [2048], replicated, may hold values from -1.5 to 1.5
Outputs:
- output: bfloat16 [8, 1024, 2048], P('dp', 'tensor')
- input_grad: float32 [8, 1024, 2048], P('dp', 'tensor')
- ln1_gain_grad: float32 [2048], replicated
- ln1_shift_grad: float32 [2048], replicated
- qkv_weight_grad: float32 [3, 2048, 2048], P(None, None, 'tensor')
- qkv_bias_grad: float32 [2, 2048], P(None, 'tensor')
- out_weight_grad: float32 [2048, 2048], P('tensor')
- out_bias_grad: float32 [2048], replicated
- ln2_gain_grad: float32 [2048], replicated
- ln2_shift_grad: float32 [2048], replicated
- up_weight_grad: float32 [2048, 8192], P(None, 'tensor')
- up_bias_grad: float32 [8192], P('tensor')
- down_weight_grad: float32 [8192, 2048], P('tensor')
- down_bias_grad: float32 [2048], replicated
The draws below stay inside these ranges and needn't reach their ends.
Inputs may be any that keep to these rules, and one draw needn't show every extreme that they name: A sequence's valid tokens are its first lengths[s] slots; some sequence has exactly 1024 and some exactly 256.
All inputs are finite; a program needn't handle non-finite values.
Results may differ from the reference program's by a relative error of at most 0.018.
Values may be sent and summed in bfloat16 or wider, within the bound.
A program may use at most 256 MiB of HBM per device.

```python
import jax
import jax.numpy as jnp
from jax import lax

D = 2048
HEADS = 16
HD = 128
FF = 8192
SLOT = 1024
SEQS = 8
LEN_MIN = 256
N_TENSOR = 8


def draw_lengths(key, part):
    drawn_lengths = jax.random.randint(jax.random.fold_in(key, 11), (SEQS,), LEN_MIN, SLOT + 1)
    shuffled = jax.random.permutation(jax.random.fold_in(key, 12), SEQS)
    drawn_lengths = drawn_lengths.at[shuffled[0]].set(SLOT)
    drawn_lengths = drawn_lengths.at[shuffled[1]].set(LEN_MIN)
    return drawn_lengths.astype(jnp.int32)


def block_scale(key, shape, cuts, smallest, top_value):
    factor_of, own = 1.0, jax.random.fold_in(key, 6)
    for axis_at, blocks in cuts:
        heights = jnp.exp(jax.random.uniform(jax.random.fold_in(own, axis_at), (blocks,), jnp.float32, smallest / len(cuts), top_value / len(cuts)))
        factor_of = factor_of * jnp.repeat(heights, shape[axis_at] // blocks).reshape([-1 if axis == axis_at else 1 for axis in range(len(shape))])
    return factor_of


def gaussian(stream_key, shape, deviation, limit, shards=(), held_as=jnp.bfloat16):
    values = jax.random.normal(stream_key, shape, jnp.float32) * deviation
    if len(shards) > 0:
        values = block_scale(stream_key, shape, shards, -0.22, 0.18) * values
    return jnp.clip(values, min=-limit, max=limit).astype(held_as)


def setup_inputs(seed: int = 0) -> dict:
    seeds = jax.random.split(jax.random.key(seed), 16)
    tokens = gaussian(seeds[0], (SEQS, SLOT, D), 1.0, 6.0, ((0, 4), (1, 8)))
    cotangent = gaussian(seeds[1], (SEQS, SLOT, D), 1.0, 6.0, ((0, 4), (1, 8)))
    lengths = draw_lengths(jax.random.fold_in(seeds[15], 71), 0)
    ln1_gain = jnp.clip(1.0 + 0.15 * jax.random.normal(seeds[3], (D,), jnp.float32), 0.25, 1.75)
    ln1_shift = gaussian(seeds[4], (D,), 0.3, 1.5, (), jnp.float32)
    qkv_weight = gaussian(seeds[5], (3, D, D), D ** -0.5, 0.125, ((2, 8),))
    qkv_bias = gaussian(seeds[6], (2, D), 0.5, 2.5, ((1, 8),), jnp.float32)
    out_weight = gaussian(seeds[7], (D, D), (D // 64) ** -0.5, 1.0, ((0, 8),))
    out_bias = gaussian(seeds[8], (D,), 0.3, 1.5, (), jnp.float32)
    ln2_gain = jnp.clip(1.0 + 0.15 * jax.random.normal(seeds[9], (D,), jnp.float32), 0.25, 1.75)
    ln2_shift = gaussian(seeds[10], (D,), 0.3, 1.5, (), jnp.float32)
    up_weight = gaussian(seeds[11], (D, FF), D ** -0.5, 0.125, ((1, 8),))
    up_bias = gaussian(seeds[12], (FF,), 0.5, 2.5, ((0, 8),), jnp.float32)
    down_weight = gaussian(seeds[13], (FF, D), FF ** -0.5, 0.0625, ((0, 8),))
    down_bias = gaussian(seeds[14], (D,), 0.3, 1.5, (), jnp.float32)
    return {"tokens": tokens, "cotangent": cotangent, "lengths": lengths, "ln1_gain": ln1_gain, "ln1_shift": ln1_shift, "qkv_weight": qkv_weight, "qkv_bias": qkv_bias, "out_weight": out_weight, "out_bias": out_bias, "ln2_gain": ln2_gain, "ln2_shift": ln2_shift, "up_weight": up_weight, "up_bias": up_bias, "down_weight": down_weight, "down_bias": down_bias}


@jax.custom_vjp
def low(v):
    return lax.optimization_barrier(v.astype(jnp.bfloat16)).astype(jnp.float32)

@jax.custom_vjp
def low_back(v):
    return v

def low_keep(v):
    return (low(v), None)

def low_pass(kept, grad):
    return (grad,)

def back_keep(v):
    return (v, None)

def back_low(kept, grad):
    return (low(grad),)
low.defvjp(low_keep, low_pass)
low_back.defvjp(back_keep, back_low)

def rounded(values):
    return low(low_back(values))

def matmul(left_rows, right_rows):
    flat = left_rows.reshape(-1, left_rows.shape[-1])
    result = jnp.dot(flat, right_rows, precision=lax.Precision.HIGHEST)
    return result.reshape(left_rows.shape[:-1] + (right_rows.shape[-1],))

def shard_products(left_rows, right_rows):
    shard_width = left_rows.shape[-1] // N_TENSOR
    total = jnp.zeros(left_rows.shape[:-1] + (right_rows.shape[-1],), jnp.float32)
    for shard_index in range(N_TENSOR):
        first = shard_index * shard_width
        piece = matmul(left_rows[..., first:first + shard_width], right_rows[first:first + shard_width])
        total = total + rounded(piece)
    return total

def layer_norm(values, norm_gain, norm_shift):
    centre = values - lax.optimization_barrier(jnp.mean(values, axis=-1, keepdims=True))
    spread = lax.optimization_barrier(jnp.mean(centre * centre, axis=-1, keepdims=True))
    return centre * lax.rsqrt(spread + 1e-05) * norm_gain + norm_shift

def attend(item):
    query, key_rows, value_rows, length = item
    slot_count = query.shape[0]
    scores = low_back(jnp.einsum('qhd,khd->hqk', query, key_rows, precision=lax.Precision.HIGHEST))
    row_ids = lax.broadcasted_iota(jnp.int32, (slot_count, slot_count), 0)
    col_ids = lax.broadcasted_iota(jnp.int32, (slot_count, slot_count), 1)
    allowed = (col_ids <= row_ids) & (col_ids < length)
    scores = jnp.where(allowed[None], scores, -1e+30)
    probs = low(jax.nn.softmax(scores, axis=-1))
    return jnp.einsum('hqk,khd->qhd', probs, value_rows, precision=lax.Precision.HIGHEST)

def forward(inputs, lengths, ln1_gain, ln1_shift, qkv_weight, qkv_bias, out_weight, out_bias, ln2_gain, ln2_shift, up_weight, up_bias, down_weight, down_bias):
    seq_count, slot_count, model_width = inputs.shape
    head_shape = (seq_count, slot_count, HEADS, HD)
    normed_one = low(layer_norm(inputs, ln1_gain, ln1_shift))
    query = rounded((matmul(normed_one, qkv_weight[0]) + qkv_bias[0]) * HD ** (-0.5))
    key_rows = rounded(matmul(normed_one, qkv_weight[1]))
    value_rows = rounded(matmul(normed_one, qkv_weight[2]) + qkv_bias[1])
    attended = lax.map(jax.checkpoint(attend), (query.reshape(head_shape), key_rows.reshape(head_shape), value_rows.reshape(head_shape), lengths))
    mixed_heads = rounded(attended.reshape(seq_count, slot_count, model_width))
    hidden_state = inputs + shard_products(mixed_heads, out_weight) + out_bias
    normed_two = low(layer_norm(hidden_state, ln2_gain, ln2_shift))
    pre_act = low_back(matmul(normed_two, up_weight) + up_bias)
    activated = low(jax.nn.gelu(pre_act, approximate=False))
    return hidden_state + shard_products(activated, down_weight) + down_bias

def reference(tokens, cotangent, lengths, ln1_gain, ln1_shift, qkv_weight, qkv_bias, out_weight, out_bias, ln2_gain, ln2_shift, up_weight, up_bias, down_weight, down_bias):
    inputs = tokens.astype(jnp.float32)
    slot_ids = lax.broadcasted_iota(jnp.int32, (tokens.shape[0], tokens.shape[1]), 1)
    valid_rows = (slot_ids < lengths[:, None]).astype(jnp.float32)

    def wrapped(inputs, ln1_gain, ln1_shift, qkv_weight, qkv_bias, out_weight, out_bias, ln2_gain, ln2_shift, up_weight, up_bias, down_weight, down_bias):
        return forward(inputs, lengths, ln1_gain, ln1_shift, qkv_weight, qkv_bias, out_weight, out_bias, ln2_gain, ln2_shift, up_weight, up_bias, down_weight, down_bias)
    block_out, backward = jax.vjp(wrapped, inputs, ln1_gain, ln1_shift, qkv_weight.astype(jnp.float32), qkv_bias, out_weight.astype(jnp.float32), out_bias, ln2_gain, ln2_shift, up_weight.astype(jnp.float32), up_bias, down_weight.astype(jnp.float32), down_bias)
    grads = backward(cotangent.astype(jnp.float32) * valid_rows[:, :, None])
    return (block_out.astype(jnp.bfloat16), grads[0], grads[1], grads[2], grads[3], grads[4], grads[5], grads[6], grads[7], grads[8], grads[9], grads[10], grads[11], grads[12])
```

```python
import jax
import jax.numpy as jnp
from jax import lax
from jax.sharding import PartitionSpec as P

HD = 128


norm_epsilon = 1e-05
block_rows = 512


def layer_norm(values, norm_gain, norm_shift):
    centre = values - jnp.mean(values, axis=-1, keepdims=True)
    spread = jnp.mean(centre * centre, axis=-1, keepdims=True)
    return centre * lax.rsqrt(spread + norm_epsilon) * norm_gain + norm_shift


def gelu_exact(values):
    return jax.nn.gelu(values, approximate=False)


def flat_product(left_rows, right_rows):
    flat = left_rows.reshape(-1, left_rows.shape[-1])
    result = jnp.dot(flat, right_rows, preferred_element_type=jnp.float32)
    return result.reshape(left_rows.shape[:-1] + (right_rows.shape[-1],))


def product_back(left_rows, right_rows):
    flat = left_rows.reshape(-1, left_rows.shape[-1])
    result = lax.dot_general(
        flat, right_rows, (((1,), (1,)), ((), ())), preferred_element_type=jnp.float32
    )
    return result.reshape(left_rows.shape[:-1] + (right_rows.shape[0],))


def rows_product(left_rows, right_rows):
    left_flat = left_rows.reshape(-1, left_rows.shape[-1])
    right_flat = right_rows.reshape(-1, right_rows.shape[-1])
    return lax.dot_general(
        left_flat, right_flat, (((0,), (0,)), ((), ())), preferred_element_type=jnp.float32
    )


def sum_groups(part):
    return lax.psum(part.astype(jnp.bfloat16), "dp").astype(jnp.float32)


def allowed_mask(first_row, row_count, slot_count, length):
    row_ids = first_row + lax.broadcasted_iota(jnp.int32, (row_count, slot_count), 0)
    col_ids = lax.broadcasted_iota(jnp.int32, (row_count, slot_count), 1)
    return (col_ids <= row_ids) & (col_ids < length)


def block_scores(query_block, key_rows, first_row, length):
    scores = jnp.einsum("qhd,khd->hqk", query_block, key_rows, preferred_element_type=jnp.float32)
    allowed = allowed_mask(first_row, query_block.shape[0], key_rows.shape[0], length)
    return jnp.where(allowed[None], scores, -1e30)


def attend_forward(query_rows, key_rows, value_rows, length):
    slot_count = query_rows.shape[0]
    step_rows = min(block_rows, slot_count)
    outputs = []
    totals = []
    for block_index in range(slot_count // step_rows):
        first_row = block_index * step_rows
        query_block = query_rows[first_row : first_row + step_rows]
        scores = block_scores(query_block, key_rows, first_row, length)
        row_peak = jnp.max(scores, axis=-1, keepdims=True)
        log_total = row_peak + jnp.log(jnp.sum(jnp.exp(scores - row_peak), axis=-1, keepdims=True))
        weights = jnp.exp(scores - log_total).astype(jnp.bfloat16)
        outputs.append(
            jnp.einsum("hqk,khd->qhd", weights, value_rows, preferred_element_type=jnp.float32)
        )
        totals.append(log_total)
    return (jnp.concatenate(outputs, axis=0), jnp.concatenate(totals, axis=1))


def attend_backward(query_rows, key_rows, value_rows, grad_rows, log_totals, length):
    slot_count = query_rows.shape[0]
    step_rows = min(block_rows, slot_count)
    grad_keys = jnp.zeros(key_rows.shape, jnp.float32)
    grad_values = jnp.zeros(value_rows.shape, jnp.float32)
    grad_queries = []
    for block_index in range(slot_count // step_rows):
        first_row = block_index * step_rows
        query_block = query_rows[first_row : first_row + step_rows]
        grad_block = grad_rows[first_row : first_row + step_rows]
        scores = block_scores(query_block, key_rows, first_row, length)
        probs = jnp.exp(scores - log_totals[:, first_row : first_row + step_rows])
        grad_probs = jnp.einsum(
            "qhd,khd->hqk", grad_block, value_rows, preferred_element_type=jnp.float32
        )
        centre = jnp.sum(probs * grad_probs, axis=-1, keepdims=True)
        grad_scores = (probs * (grad_probs - centre)).astype(jnp.bfloat16)
        grad_queries.append(
            jnp.einsum("hqk,khd->qhd", grad_scores, key_rows, preferred_element_type=jnp.float32)
        )
        grad_keys = grad_keys + jnp.einsum(
            "hqk,qhd->khd", grad_scores, query_block, preferred_element_type=jnp.float32
        )
        grad_values = grad_values + jnp.einsum(
            "hqk,qhd->khd",
            probs.astype(jnp.bfloat16),
            grad_block,
            preferred_element_type=jnp.float32,
        )
    return (jnp.concatenate(grad_queries, axis=0), grad_keys, grad_values)


def body(
    tokens,
    cotangent,
    lengths,
    ln1_gain,
    ln1_shift,
    qkv_weight,
    qkv_bias,
    out_weight,
    out_bias,
    ln2_gain,
    ln2_shift,
    up_weight,
    up_bias,
    down_weight,
    down_bias,
):
    seq_count, local_rows, model_width = tokens.shape
    part_width = qkv_weight.shape[2]
    head_count = part_width // HD
    score_scale = HD ** (-0.5)
    inputs = tokens.astype(jnp.float32)
    normed_one = layer_norm(inputs, ln1_gain, ln1_shift).astype(jnp.bfloat16)
    gathered_one = lax.all_gather(normed_one, "tensor", axis=1, tiled=True)
    slot_count = gathered_one.shape[1]
    head_shape = (seq_count, slot_count, head_count, HD)
    query_rows = (
        ((flat_product(gathered_one, qkv_weight[0]) + qkv_bias[0]) * score_scale)
        .astype(jnp.bfloat16)
        .reshape(head_shape)
    )
    key_rows = flat_product(gathered_one, qkv_weight[1]).astype(jnp.bfloat16).reshape(head_shape)
    value_rows = (
        (flat_product(gathered_one, qkv_weight[2]) + qkv_bias[1])
        .astype(jnp.bfloat16)
        .reshape(head_shape)
    )
    attended, log_totals = lax.map(
        lambda item: attend_forward(item[0], item[1], item[2], item[3]),
        (query_rows, key_rows, value_rows, lengths),
    )
    mixed_heads = attended.reshape(seq_count, slot_count, part_width).astype(jnp.bfloat16)
    attn_local = lax.psum_scatter(
        flat_product(mixed_heads, out_weight).astype(jnp.bfloat16),
        "tensor",
        scatter_dimension=1,
        tiled=True,
    ).astype(jnp.float32)
    hidden_state = inputs + attn_local + out_bias
    normed_two = layer_norm(hidden_state, ln2_gain, ln2_shift).astype(jnp.bfloat16)
    gathered_two = lax.all_gather(normed_two, "tensor", axis=1, tiled=True)
    pre_act = flat_product(gathered_two, up_weight) + up_bias
    activated = gelu_exact(pre_act).astype(jnp.bfloat16)
    mlp_local = lax.psum_scatter(
        flat_product(activated, down_weight).astype(jnp.bfloat16),
        "tensor",
        scatter_dimension=1,
        tiled=True,
    ).astype(jnp.float32)
    output = (hidden_state + mlp_local + down_bias).astype(jnp.bfloat16)
    slot_ids = lax.axis_index("tensor") * local_rows + lax.broadcasted_iota(
        jnp.int32, (seq_count, local_rows), 1
    )
    valid_rows = (slot_ids < lengths[:, None]).astype(jnp.float32)
    grad_out = cotangent.astype(jnp.float32) * valid_rows[:, :, None]
    down_bias_grad = jnp.sum(grad_out, axis=(0, 1))
    grad_mlp = lax.all_gather(grad_out.astype(jnp.bfloat16), "tensor", axis=1, tiled=True)
    down_weight_grad = sum_groups(rows_product(activated, grad_mlp))
    grad_act = product_back(grad_mlp, down_weight)
    unused_act, gelu_back = jax.vjp(gelu_exact, pre_act)
    grad_pre = gelu_back(grad_act)[0].astype(jnp.bfloat16)
    up_bias_grad = jnp.sum(grad_pre.astype(jnp.float32), axis=(0, 1))
    up_weight_grad = sum_groups(rows_product(gathered_two, grad_pre))
    norm_two_grad = lax.psum_scatter(
        product_back(grad_pre, up_weight).astype(jnp.bfloat16),
        "tensor",
        scatter_dimension=1,
        tiled=True,
    ).astype(jnp.float32)
    unused_two, norm_two_back = jax.vjp(layer_norm, hidden_state, ln2_gain, ln2_shift)
    hidden_ln_grad, ln2_gain_grad, ln2_shift_grad = norm_two_back(norm_two_grad)
    hidden_grad = grad_out + hidden_ln_grad
    out_bias_grad = jnp.sum(hidden_grad, axis=(0, 1))
    grad_attn = lax.all_gather(hidden_grad.astype(jnp.bfloat16), "tensor", axis=1, tiled=True)
    out_weight_grad = rows_product(mixed_heads, grad_attn)
    grad_heads = product_back(grad_attn, out_weight).astype(jnp.bfloat16).reshape(head_shape)
    grad_query, grad_key, grad_value = lax.map(
        lambda item: attend_backward(item[0], item[1], item[2], item[3], item[4], item[5]),
        (query_rows, key_rows, value_rows, grad_heads, log_totals, lengths),
    )
    flat_shape = (seq_count, slot_count, part_width)
    grad_query = grad_query.reshape(flat_shape).astype(jnp.bfloat16)
    grad_key = grad_key.reshape(flat_shape).astype(jnp.bfloat16)
    grad_value = grad_value.reshape(flat_shape).astype(jnp.bfloat16)
    qkv_weight_grad = jnp.stack(
        [
            score_scale * rows_product(gathered_one, grad_query),
            rows_product(gathered_one, grad_key),
            rows_product(gathered_one, grad_value),
        ]
    )
    qkv_weight_grad, out_weight_grad, up_weight_grad, down_weight_grad = lax.optimization_barrier(
        (qkv_weight_grad, out_weight_grad, up_weight_grad, down_weight_grad)
    )
    qkv_weight_grad = sum_groups(qkv_weight_grad)
    out_weight_grad = sum_groups(out_weight_grad)
    qkv_bias_grad = jnp.stack(
        [
            score_scale * jnp.sum(grad_query.astype(jnp.float32), axis=(0, 1)),
            jnp.sum(grad_value.astype(jnp.float32), axis=(0, 1)),
        ]
    )
    norm_one_part = (
        score_scale * product_back(grad_query, qkv_weight[0])
        + product_back(grad_key, qkv_weight[1])
        + product_back(grad_value, qkv_weight[2])
    )
    norm_one_grad = lax.psum_scatter(
        norm_one_part.astype(jnp.bfloat16), "tensor", scatter_dimension=1, tiled=True
    ).astype(jnp.float32)
    unused_one, norm_one_back = jax.vjp(layer_norm, inputs, ln1_gain, ln1_shift)
    input_ln_grad, ln1_gain_grad, ln1_shift_grad = norm_one_back(norm_one_grad)
    input_grad = hidden_grad + input_ln_grad
    qkv_bias_grad, up_bias_grad = lax.psum((qkv_bias_grad, up_bias_grad), "dp")
    ln1_gain_grad, ln1_shift_grad, out_bias_grad, ln2_gain_grad, ln2_shift_grad, down_bias_grad = (
        lax.psum(
            (
                ln1_gain_grad,
                ln1_shift_grad,
                out_bias_grad,
                ln2_gain_grad,
                ln2_shift_grad,
                down_bias_grad,
            ),
            ("dp", "tensor"),
        )
    )
    return (
        output,
        input_grad,
        ln1_gain_grad,
        ln1_shift_grad,
        qkv_weight_grad,
        qkv_bias_grad,
        out_weight_grad,
        out_bias_grad,
        ln2_gain_grad,
        ln2_shift_grad,
        up_weight_grad,
        up_bias_grad,
        down_weight_grad,
        down_bias_grad,
    )


def solution(mesh):
    in_specs = (
        P("dp", "tensor", None),
        P("dp", "tensor", None),
        P("dp"),
        P(),
        P(),
        P(None, None, "tensor"),
        P(None, "tensor"),
        P("tensor", None),
        P(),
        P(),
        P(),
        P(None, "tensor"),
        P("tensor"),
        P("tensor", None),
        P(),
    )
    out_specs = (
        P("dp", "tensor", None),
        P("dp", "tensor", None),
        P(),
        P(),
        P(None, None, "tensor"),
        P(None, "tensor"),
        P("tensor", None),
        P(),
        P(),
        P(),
        P(None, "tensor"),
        P("tensor"),
        P("tensor", None),
        P(),
    )
    return jax.shard_map(body, mesh=mesh, in_specs=in_specs, out_specs=out_specs, check_vma=False)
```

```python
import functools

import jax
import jax.numpy as jnp
from jax import lax
from jax.experimental import pallas as pl
from jax.experimental.pallas import tpu as pltpu
from jax.sharding import PartitionSpec as P

HD = 128


norm_epsilon = 1e-05
block_rows = 512


def layer_norm(values, norm_gain, norm_shift):
    centre = values - jnp.mean(values, axis=-1, keepdims=True)
    spread = jnp.mean(centre * centre, axis=-1, keepdims=True)
    return centre * lax.rsqrt(spread + norm_epsilon) * norm_gain + norm_shift


def gelu_exact(values):
    return jax.nn.gelu(values, approximate=False)


def flat_product(left_rows, right_rows):
    flat = left_rows.reshape(-1, left_rows.shape[-1])
    result = jnp.dot(flat, right_rows, preferred_element_type=jnp.float32)
    return result.reshape(left_rows.shape[:-1] + (right_rows.shape[-1],))


def product_back(left_rows, right_rows):
    flat = left_rows.reshape(-1, left_rows.shape[-1])
    result = lax.dot_general(
        flat, right_rows, (((1,), (1,)), ((), ())), preferred_element_type=jnp.float32
    )
    return result.reshape(left_rows.shape[:-1] + (right_rows.shape[0],))


def rows_product(left_rows, right_rows):
    left_flat = left_rows.reshape(-1, left_rows.shape[-1])
    right_flat = right_rows.reshape(-1, right_rows.shape[-1])
    return lax.dot_general(
        left_flat, right_flat, (((0,), (0,)), ((), ())), preferred_element_type=jnp.float32
    )


def sum_groups(part):
    return lax.psum(part.astype(jnp.bfloat16), "dp").astype(jnp.float32)


def allowed_mask(first_row, row_count, slot_count, length):
    row_ids = first_row + lax.broadcasted_iota(jnp.int32, (row_count, slot_count), 0)
    col_ids = lax.broadcasted_iota(jnp.int32, (row_count, slot_count), 1)
    return (col_ids <= row_ids) & (col_ids < length)


def block_scores(query_block, key_rows, first_row, length):
    scores = jnp.einsum("qhd,khd->hqk", query_block, key_rows, preferred_element_type=jnp.float32)
    allowed = allowed_mask(first_row, query_block.shape[0], key_rows.shape[0], length)
    return jnp.where(allowed[None], scores, -1e30)


def attend_forward(query_rows, key_rows, value_rows, length):
    slot_count = query_rows.shape[0]
    step_rows = min(block_rows, slot_count)
    outputs = []
    totals = []
    for block_index in range(slot_count // step_rows):
        first_row = block_index * step_rows
        query_block = query_rows[first_row : first_row + step_rows]
        scores = block_scores(query_block, key_rows, first_row, length)
        row_peak = jnp.max(scores, axis=-1, keepdims=True)
        log_total = row_peak + jnp.log(jnp.sum(jnp.exp(scores - row_peak), axis=-1, keepdims=True))
        weights = jnp.exp(scores - log_total).astype(jnp.bfloat16)
        outputs.append(
            jnp.einsum("hqk,khd->qhd", weights, value_rows, preferred_element_type=jnp.float32)
        )
        totals.append(log_total)
    return (jnp.concatenate(outputs, axis=0), jnp.concatenate(totals, axis=1))


def attend_backward(query_rows, key_rows, value_rows, grad_rows, log_totals, length):
    slot_count = query_rows.shape[0]
    step_rows = min(block_rows, slot_count)
    grad_keys = jnp.zeros(key_rows.shape, jnp.float32)
    grad_values = jnp.zeros(value_rows.shape, jnp.float32)
    grad_queries = []
    for block_index in range(slot_count // step_rows):
        first_row = block_index * step_rows
        query_block = query_rows[first_row : first_row + step_rows]
        grad_block = grad_rows[first_row : first_row + step_rows]
        scores = block_scores(query_block, key_rows, first_row, length)
        probs = jnp.exp(scores - log_totals[:, first_row : first_row + step_rows])
        grad_probs = jnp.einsum(
            "qhd,khd->hqk", grad_block, value_rows, preferred_element_type=jnp.float32
        )
        centre = jnp.sum(probs * grad_probs, axis=-1, keepdims=True)
        grad_scores = (probs * (grad_probs - centre)).astype(jnp.bfloat16)
        grad_queries.append(
            jnp.einsum("hqk,khd->qhd", grad_scores, key_rows, preferred_element_type=jnp.float32)
        )
        grad_keys = grad_keys + jnp.einsum(
            "hqk,qhd->khd", grad_scores, query_block, preferred_element_type=jnp.float32
        )
        grad_values = grad_values + jnp.einsum(
            "hqk,qhd->khd",
            probs.astype(jnp.bfloat16),
            grad_block,
            preferred_element_type=jnp.float32,
        )
    return (jnp.concatenate(grad_queries, axis=0), grad_keys, grad_values)


MESH = pl.DeviceIdType.MESH
UP, DOWN, SIDE = 0, 1, 2
VMEM = pltpu.VMEM
DMA = pltpu.SemaphoreType.DMA
f32 = jnp.float32
bf16 = jnp.bfloat16


class Place:
    def __init__(self, n):
        self.n, self.chips = n, n // 2
        self.me = lax.axis_index("tensor")
        self.chip, self.core = self.me // 2, lax.rem(self.me, 2)
        self.side = self.me + 1 - 2 * self.core
        self.below = self.chip > 0
        self.above = self.chip < self.chips - 1

    def greet(self):
        barrier = pltpu.get_barrier_semaphore()

        def tell(target):
            pl.semaphore_signal(
                barrier, inc=1, device_id={"tensor": target}, device_id_type=MESH
            )

        tell(self.side)
        pl.when(self.below)(lambda: tell(self.me - 2))
        pl.when(self.above)(lambda: tell(self.me + 2))
        peers = 1 + self.below.astype(jnp.int32) + self.above.astype(jnp.int32)
        pl.semaphore_wait(barrier, peers)


def rows_of(index, rows):
    return pl.ds(pl.multiple_of(index * rows, rows), rows)


class Gather:
    def __init__(self, at, rows, buf, send, recv):
        self.at, self.rows, self.buf, self.send, self.recv = at, rows, buf, send, recv
        self.seqs = buf.shape[0]

    @staticmethod
    def scratch(n, seqs):
        return [DMA((3, seqs, n // 2)), DMA((seqs, n))]

    def piece(self, s, o, k):
        return self.buf.at[s, rows_of(2 * o + k, self.rows)]

    def copy(self, s, o, kind):
        at = self.at
        target = (at.me + 2, at.me - 2, at.side)[kind]
        piece = self.piece(s, o, at.core)
        return pltpu.make_async_remote_copy(
            src_ref=piece,
            dst_ref=piece,
            send_sem=self.send.at[kind, s, o],
            recv_sem=self.recv.at[s, 2 * o + at.core],
            device_id={"tensor": target},
            device_id_type=MESH,
        )

    def arrived(self, s, o, k):
        at = self.at
        piece = self.piece(s, o, k)
        pltpu.make_async_remote_copy(
            src_ref=piece,
            dst_ref=piece,
            send_sem=self.send.at[SIDE, s, o],
            recv_sem=self.recv.at[s, 2 * o + k],
            device_id={"tensor": at.side},
            device_id_type=MESH,
        ).wait_recv()

    def start(self, s):
        at = self.at
        pl.when(at.above)(lambda: self.copy(s, at.chip, UP).start())
        pl.when(at.below)(lambda: self.copy(s, at.chip, DOWN).start())
        self.copy(s, at.chip, SIDE).start()

    def units(self):
        return self.seqs * (1 + 2 * (self.at.chips - 1))

    def unit(self, u):
        at = self.at
        per = 1 + 2 * (at.chips - 1)
        s, v = u // per, lax.rem(u, per)
        d = (v + 1) // 2
        o = at.chip + (2 * lax.rem(v, 2) - 1) * d
        return s, o, (o >= 0) & (o < at.chips) & (u >= 0) & (u < self.units()), v == 0

    def forward(self, u):
        at = self.at
        s, o, there, own = self.unit(u)

        @pl.when(there & jnp.logical_not(own))
        def _():
            self.arrived(s, o, at.core)
            pl.when((o < at.chip) & at.above)(lambda: self.copy(s, o, UP).start())
            pl.when((o > at.chip) & at.below)(lambda: self.copy(s, o, DOWN).start())
            self.copy(s, o, SIDE).start()

    def finish(self):
        at = self.at

        def one(i, carry):
            s, o = i // at.chips, lax.rem(i, at.chips)
            pl.when((o <= at.chip) & at.above)(lambda: self.copy(s, o, UP).wait_send())
            pl.when((o >= at.chip) & at.below)(lambda: self.copy(s, o, DOWN).wait_send())
            self.copy(s, o, SIDE).wait_send()
            return carry

        lax.fori_loop(0, self.seqs * at.chips, one, 0)


class Scatter:
    def __init__(self, at, rows, part, side, link, side_send, side_recv, send, recv):
        self.at, self.rows = at, rows
        self.part, self.side, self.link = part, side, link
        self.side_send, self.side_recv, self.send, self.recv = side_send, side_recv, send, recv
        self.seqs = part.shape[0]

    @staticmethod
    def scratch(n, seqs, rows, width):
        chips = n // 2
        return [
            VMEM((seqs, chips, 2 * rows, width), bf16),
            VMEM((seqs, chips, rows, width), bf16),
            VMEM((seqs, chips + 1, rows, width), bf16),
            DMA((seqs, chips)),
            DMA((seqs, chips)),
            DMA((seqs, chips)),
            DMA((seqs, chips + 1)),
        ]

    def units(self):
        return self.seqs * (2 * self.at.chips - 1)

    def unit(self, u):
        at = self.at
        per = 2 * at.chips - 1
        s, v = u // per, lax.rem(u, per)
        j = v // 2
        up = lax.rem(v, 2) == 0
        last = v == per - 1
        o = jnp.where(last, at.chip, jnp.where(up, at.chips - 1 - j, j))
        there = last | jnp.where(up, o > at.chip, o < at.chip)
        return s, o, there & (u >= 0) & (u < self.units())

    def side_copy(self, s, o):
        at = self.at
        return pltpu.make_async_remote_copy(
            src_ref=self.part.at[s, o, rows_of(1 - at.core, self.rows)],
            dst_ref=self.side.at[s, o],
            send_sem=self.side_send.at[s, o],
            recv_sem=self.side_recv.at[s, o],
            device_id={"tensor": at.side},
            device_id_type=MESH,
        )

    def link_copy(self, s, o, slot, target):
        return pltpu.make_async_remote_copy(
            src_ref=self.part.at[s, o, rows_of(self.at.core, self.rows)],
            dst_ref=self.link.at[s, slot],
            send_sem=self.send.at[s, o],
            recv_sem=self.recv.at[s, slot],
            device_id={"tensor": target},
            device_id_type=MESH,
        )

    def share(self, s, o):
        self.side_copy(s, o).start()

    def blocks(self, body):
        step = 16
        lax.fori_loop(0, self.rows // step, lambda i, c: (body(pl.multiple_of(i * step, step), step), c)[1], 0)

    def add_up(self, s, o, slots):
        base = self.at.core * self.rows

        def body(first, step):
            here = pl.ds(pl.multiple_of(base + first, step), step)
            there = pl.ds(first, step)
            total = self.part[s, o, here].astype(f32) + self.side[s, o, there].astype(f32)
            for slot in slots:
                total += self.link[s, slot, there].astype(f32)
            self.part[s, o, here] = total.astype(bf16)

        self.blocks(body)

    def pass_on(self, u, final):
        at = self.at
        s, o, there = self.unit(u)

        @pl.when(there)
        def _():
            self.side_copy(s, o).wait_recv()

            @pl.when(o > at.chip)
            def _():
                @pl.when(at.below)
                def _():
                    self.link_copy(s, o, o, at.me).wait_recv()
                    self.add_up(s, o, [o])

                pl.when(jnp.logical_not(at.below))(lambda: self.add_up(s, o, []))
                self.link_copy(s, o, o, at.me + 2).start()

            @pl.when(o < at.chip)
            def _():
                @pl.when(at.above)
                def _():
                    self.link_copy(s, o, o, at.me).wait_recv()
                    self.add_up(s, o, [o])

                pl.when(jnp.logical_not(at.above))(lambda: self.add_up(s, o, []))
                slot = jnp.where(o == at.chip - 1, at.chips, o)
                self.link_copy(s, o, slot, at.me - 2).start()

            @pl.when(o == at.chip)
            def _():
                pl.when(at.below)(lambda: self.link_copy(s, o, o, at.me).wait_recv())
                pl.when(at.above)(lambda: self.link_copy(s, o, at.chips, at.me).wait_recv())
                for slot, used in ((o, at.below), (at.chips, at.above)):
                    @pl.when(jnp.logical_not(used))
                    def _():
                        def clear(first, step):
                            self.link[s, slot, pl.ds(first, step)] = jnp.zeros(
                                (step, self.link.shape[-1]), bf16
                            )

                        self.blocks(clear)
                base = at.core * self.rows

                def body(first, step):
                    here = pl.ds(pl.multiple_of(base + first, step), step)
                    there = pl.ds(first, step)
                    total = self.part[s, o, here].astype(f32) + self.side[s, o, there].astype(f32)
                    total += self.link[s, o, there].astype(f32)
                    total += self.link[s, at.chips, there].astype(f32)
                    final(s, there, total)

                self.blocks(body)

    def finish(self):
        at = self.at

        def one(i, carry):
            s, o = i // at.chips, lax.rem(i, at.chips)
            self.side_copy(s, o).wait_send()
            pl.when(o != at.chip)(lambda: self.link_copy(s, o, o, at.side).wait_send())
            return carry

        lax.fori_loop(0, self.seqs * at.chips, one, 0)


def norm_rows(values, gain, shift):
    centre = values - jnp.mean(values, axis=-1, keepdims=True)
    spread = jnp.mean(centre * centre, axis=-1, keepdims=True)
    return centre * lax.rsqrt(spread + norm_epsilon) * gain + shift


def gather_project_kernel(
    n, tokens, gain, shift, weight, bias, gathered, heads, buf, send, recv, out_sem
):
    at = Place(n)
    seqs, rows, width = tokens.shape
    ring = Gather(at, rows, buf, send, recv)
    at.greet()
    for s in range(seqs):
        def block(i, carry):
            first = pl.multiple_of(i * 16, 16)
            values = norm_rows(tokens[s, pl.ds(first, 16)].astype(f32), gain[...], shift[...])
            buf[s, pl.ds(pl.multiple_of(at.me * rows + first, 16), 16)] = values.astype(bf16)
            return carry

        lax.fori_loop(0, rows // 16, block, 0)
        ring.start(s)

    def keep(s, o):
        here = rows_of(o, 2 * rows)
        return pltpu.make_async_copy(buf.at[s, here], gathered.at[s, here], out_sem.at[s, o])

    def step(u, carry):
        ring.forward(u)
        s, o, there, own = ring.unit(u - 2)

        @pl.when(there)
        def _():
            ring.arrived(s, o, 1 - at.core)
            keep(s, o).start()
            here = rows_of(o, 2 * rows)
            for j in range(3):
                total = jnp.dot(buf[s, here], weight[j], preferred_element_type=f32)
                if j == 0:
                    total = (total + bias[0:1]) * HD ** (-0.5)
                if j == 2:
                    total = total + bias[1:2]
                heads[j, s, here] = total.astype(bf16)

        return carry

    lax.fori_loop(0, ring.units() + 2, step, 0)
    ring.finish()

    def close(i, carry):
        keep(i // at.chips, lax.rem(i, at.chips)).wait()
        return carry

    lax.fori_loop(0, seqs * at.chips, close, 0)


def whole(count):
    return [pl.BlockSpec(memory_space=VMEM)] * count


def gather_project(n, tokens, gain, shift, weight, bias):
    seqs, rows, width = tokens.shape
    part = weight.shape[2]
    return pl.pallas_call(
        functools.partial(gather_project_kernel, n),
        out_shape=(
            jax.ShapeDtypeStruct((seqs, n * rows, width), bf16),
            jax.ShapeDtypeStruct((3, seqs, n * rows, part), bf16),
        ),
        in_specs=whole(5),
        out_specs=(pl.BlockSpec(memory_space=pl.ANY), pl.BlockSpec(memory_space=VMEM)),
        scratch_shapes=[VMEM((seqs, n * rows, width), bf16)]
        + Gather.scratch(n, seqs)
        + [DMA((seqs, n // 2))],
        compiler_params=pltpu.CompilerParams(
            collective_id=0, has_side_effects=True, vmem_limit_bytes=40 * 2**20
        ),
        name="gather_project",
    )(tokens, gain, shift, weight, bias)


def project_scatter_kernel(
    n, mixed, weight, tokens, bias, gain, shift, hidden, normed, *scratch
):
    at = Place(n)
    seqs, rows, width = tokens.shape
    line = Scatter(at, rows, *scratch)
    at.greet()

    def final(s, there, total):
        values = tokens[s, there].astype(f32) + total + bias[...]
        hidden[s, there] = values
        normed[s, there] = norm_rows(values, gain[...], shift[...]).astype(bf16)

    def step(u, carry):
        s, o, there = line.unit(u)

        @pl.when(there)
        def _():
            here = rows_of(o, 2 * rows)
            for j in range(width // 512):
                cols = pl.ds(j * 512, 512)
                total = jnp.dot(mixed[s, here], weight[:, cols], preferred_element_type=f32)
                line.part[s, o, :, cols] = total.astype(bf16)
            line.share(s, o)

        line.pass_on(u - 1, final)
        return carry

    lax.fori_loop(0, line.units() + 1, step, 0)
    line.finish()


def project_scatter(n, mixed, weight, tokens, bias, gain, shift):
    seqs, rows, width = tokens.shape
    return pl.pallas_call(
        functools.partial(project_scatter_kernel, n),
        out_shape=(
            jax.ShapeDtypeStruct((seqs, rows, width), f32),
            jax.ShapeDtypeStruct((seqs, rows, width), bf16),
        ),
        in_specs=whole(6),
        out_specs=tuple(whole(2)),
        scratch_shapes=Scatter.scratch(n, seqs, rows, width),
        compiler_params=pltpu.CompilerParams(
            collective_id=1, has_side_effects=True, vmem_limit_bytes=40 * 2**20
        ),
        name="project_scatter",
    )(mixed, weight, tokens, bias, gain, shift)


def heads_scatter_kernel(n, query, key, value, weight, grad, *scratch):
    at = Place(n)
    seqs, rows, width = grad.shape
    line = Scatter(at, rows, *scratch)
    at.greet()

    def final(s, there, total):
        grad[s, there] = total

    def step(u, carry):
        s, o, there = line.unit(u)

        @pl.when(there)
        def _():
            here = rows_of(o, 2 * rows)
            for j in range(width // 512):
                cols = pl.ds(j * 512, 512)
                total = 0.0
                for part, scale, i in ((query, HD ** (-0.5), 0), (key, 1.0, 1), (value, 1.0, 2)):
                    total += scale * lax.dot_general(
                        part[s, here],
                        weight[i, cols],
                        (((1,), (1,)), ((), ())),
                        preferred_element_type=f32,
                    )
                line.part[s, o, :, cols] = total.astype(bf16)
            line.share(s, o)

        line.pass_on(u - 1, final)
        return carry

    lax.fori_loop(0, line.units() + 1, step, 0)
    line.finish()


def heads_scatter(n, query, key, value, weight):
    seqs, slots, part = query.shape
    width = weight.shape[1]
    rows = slots // n
    return pl.pallas_call(
        functools.partial(heads_scatter_kernel, n),
        out_shape=jax.ShapeDtypeStruct((seqs, rows, width), f32),
        in_specs=whole(4),
        out_specs=whole(1)[0],
        scratch_shapes=Scatter.scratch(n, seqs, rows, width),
        compiler_params=pltpu.CompilerParams(
            collective_id=2, has_side_effects=True, vmem_limit_bytes=40 * 2**20
        ),
        name="heads_scatter",
    )(query, key, value, weight)


def body(
    tokens,
    cotangent,
    lengths,
    ln1_gain,
    ln1_shift,
    qkv_weight,
    qkv_bias,
    out_weight,
    out_bias,
    ln2_gain,
    ln2_shift,
    up_weight,
    up_bias,
    down_weight,
    down_bias,
):
    seq_count, local_rows, model_width = tokens.shape
    part_width = qkv_weight.shape[2]
    head_count = part_width // HD
    score_scale = HD ** (-0.5)
    inputs = tokens.astype(jnp.float32)
    n = lax.axis_size("tensor")
    gathered_one, heads = gather_project(
        n, tokens, ln1_gain[None], ln1_shift[None], qkv_weight, qkv_bias
    )
    slot_count = gathered_one.shape[1]
    head_shape = (seq_count, slot_count, head_count, HD)
    query_rows, key_rows, value_rows = [heads[j].reshape(head_shape) for j in range(3)]
    attended, log_totals = lax.map(
        lambda item: attend_forward(item[0], item[1], item[2], item[3]),
        (query_rows, key_rows, value_rows, lengths),
    )
    mixed_heads = attended.reshape(seq_count, slot_count, part_width).astype(jnp.bfloat16)
    hidden_state, normed_two = project_scatter(
        n, mixed_heads, out_weight, tokens, out_bias[None], ln2_gain[None], ln2_shift[None]
    )
    gathered_two = lax.all_gather(normed_two, "tensor", axis=1, tiled=True)
    pre_act = flat_product(gathered_two, up_weight) + up_bias
    activated = gelu_exact(pre_act).astype(jnp.bfloat16)
    mlp_local = lax.psum_scatter(
        flat_product(activated, down_weight).astype(jnp.bfloat16),
        "tensor",
        scatter_dimension=1,
        tiled=True,
    ).astype(jnp.float32)
    output = (hidden_state + mlp_local + down_bias).astype(jnp.bfloat16)
    slot_ids = lax.axis_index("tensor") * local_rows + lax.broadcasted_iota(
        jnp.int32, (seq_count, local_rows), 1
    )
    valid_rows = (slot_ids < lengths[:, None]).astype(jnp.float32)
    grad_out = cotangent.astype(jnp.float32) * valid_rows[:, :, None]
    down_bias_grad = jnp.sum(grad_out, axis=(0, 1))
    grad_mlp = lax.all_gather(grad_out.astype(jnp.bfloat16), "tensor", axis=1, tiled=True)
    down_weight_grad = sum_groups(rows_product(activated, grad_mlp))
    grad_act = product_back(grad_mlp, down_weight)
    unused_act, gelu_back = jax.vjp(gelu_exact, pre_act)
    grad_pre = gelu_back(grad_act)[0].astype(jnp.bfloat16)
    up_bias_grad = jnp.sum(grad_pre.astype(jnp.float32), axis=(0, 1))
    up_weight_grad = sum_groups(rows_product(gathered_two, grad_pre))
    norm_two_grad = lax.psum_scatter(
        product_back(grad_pre, up_weight).astype(jnp.bfloat16),
        "tensor",
        scatter_dimension=1,
        tiled=True,
    ).astype(jnp.float32)
    unused_two, norm_two_back = jax.vjp(layer_norm, hidden_state, ln2_gain, ln2_shift)
    hidden_ln_grad, ln2_gain_grad, ln2_shift_grad = norm_two_back(norm_two_grad)
    hidden_grad = grad_out + hidden_ln_grad
    out_bias_grad = jnp.sum(hidden_grad, axis=(0, 1))
    grad_attn = lax.all_gather(hidden_grad.astype(jnp.bfloat16), "tensor", axis=1, tiled=True)
    out_weight_grad = rows_product(mixed_heads, grad_attn)
    grad_heads = product_back(grad_attn, out_weight).astype(jnp.bfloat16).reshape(head_shape)
    grad_query, grad_key, grad_value = lax.map(
        lambda item: attend_backward(item[0], item[1], item[2], item[3], item[4], item[5]),
        (query_rows, key_rows, value_rows, grad_heads, log_totals, lengths),
    )
    flat_shape = (seq_count, slot_count, part_width)
    grad_query = grad_query.reshape(flat_shape).astype(jnp.bfloat16)
    grad_key = grad_key.reshape(flat_shape).astype(jnp.bfloat16)
    grad_value = grad_value.reshape(flat_shape).astype(jnp.bfloat16)
    qkv_weight_grad = jnp.stack(
        [
            score_scale * rows_product(gathered_one, grad_query),
            rows_product(gathered_one, grad_key),
            rows_product(gathered_one, grad_value),
        ]
    )
    qkv_weight_grad, out_weight_grad, up_weight_grad, down_weight_grad = lax.optimization_barrier(
        (qkv_weight_grad, out_weight_grad, up_weight_grad, down_weight_grad)
    )
    qkv_weight_grad = sum_groups(qkv_weight_grad)
    out_weight_grad = sum_groups(out_weight_grad)
    qkv_bias_grad = jnp.stack(
        [
            score_scale * jnp.sum(grad_query.astype(jnp.float32), axis=(0, 1)),
            jnp.sum(grad_value.astype(jnp.float32), axis=(0, 1)),
        ]
    )
    norm_one_grad = heads_scatter(n, grad_query, grad_key, grad_value, qkv_weight)
    unused_one, norm_one_back = jax.vjp(layer_norm, inputs, ln1_gain, ln1_shift)
    input_ln_grad, ln1_gain_grad, ln1_shift_grad = norm_one_back(norm_one_grad)
    input_grad = hidden_grad + input_ln_grad
    qkv_bias_grad, up_bias_grad = lax.psum((qkv_bias_grad, up_bias_grad), "dp")
    ln1_gain_grad, ln1_shift_grad, out_bias_grad, ln2_gain_grad, ln2_shift_grad, down_bias_grad = (
        lax.psum(
            (
                ln1_gain_grad,
                ln1_shift_grad,
                out_bias_grad,
                ln2_gain_grad,
                ln2_shift_grad,
                down_bias_grad,
            ),
            ("dp", "tensor"),
        )
    )
    return (
        output,
        input_grad,
        ln1_gain_grad,
        ln1_shift_grad,
        qkv_weight_grad,
        qkv_bias_grad,
        out_weight_grad,
        out_bias_grad,
        ln2_gain_grad,
        ln2_shift_grad,
        up_weight_grad,
        up_bias_grad,
        down_weight_grad,
        down_bias_grad,
    )


def solution(mesh):
    in_specs = (
        P("dp", "tensor", None),
        P("dp", "tensor", None),
        P("dp"),
        P(),
        P(),
        P(None, None, "tensor"),
        P(None, "tensor"),
        P("tensor", None),
        P(),
        P(),
        P(),
        P(None, "tensor"),
        P("tensor"),
        P("tensor", None),
        P(),
    )
    out_specs = (
        P("dp", "tensor", None),
        P("dp", "tensor", None),
        P(),
        P(),
        P(None, None, "tensor"),
        P(None, "tensor"),
        P("tensor", None),
        P(),
        P(),
        P(),
        P(None, "tensor"),
        P("tensor"),
        P("tensor", None),
        P(),
    )
    return jax.shard_map(body, mesh=mesh, in_specs=in_specs, out_specs=out_specs, check_vma=False)
```

```python
import functools

import jax
import jax.numpy as jnp
from jax import lax
from jax.experimental import pallas as pl
from jax.experimental.pallas import tpu as pltpu
from jax.sharding import PartitionSpec as P

HD = 128


norm_epsilon = 1e-05
block_rows = 512


def layer_norm(values, norm_gain, norm_shift):
    centre = values - jnp.mean(values, axis=-1, keepdims=True)
    spread = jnp.mean(centre * centre, axis=-1, keepdims=True)
    return centre * lax.rsqrt(spread + norm_epsilon) * norm_gain + norm_shift


def gelu_exact(values):
    return jax.nn.gelu(values, approximate=False)


def flat_product(left_rows, right_rows):
    flat = left_rows.reshape(-1, left_rows.shape[-1])
    result = jnp.dot(flat, right_rows, preferred_element_type=jnp.float32)
    return result.reshape(left_rows.shape[:-1] + (right_rows.shape[-1],))


def product_back(left_rows, right_rows):
    flat = left_rows.reshape(-1, left_rows.shape[-1])
    result = lax.dot_general(
        flat, right_rows, (((1,), (1,)), ((), ())), preferred_element_type=jnp.float32
    )
    return result.reshape(left_rows.shape[:-1] + (right_rows.shape[0],))


def rows_product(left_rows, right_rows):
    left_flat = left_rows.reshape(-1, left_rows.shape[-1])
    right_flat = right_rows.reshape(-1, right_rows.shape[-1])
    return lax.dot_general(
        left_flat, right_flat, (((0,), (0,)), ((), ())), preferred_element_type=jnp.float32
    )


def sum_groups(parts):
    parts = [part.astype(jnp.bfloat16) for part in parts]
    return [total.astype(jnp.float32) for total in lax.psum(parts, "dp")]


def allowed_mask(first_row, row_count, slot_count, length):
    row_ids = first_row + lax.broadcasted_iota(jnp.int32, (row_count, slot_count), 0)
    col_ids = lax.broadcasted_iota(jnp.int32, (row_count, slot_count), 1)
    return (col_ids <= row_ids) & (col_ids < length)


def block_scores(query_block, key_rows, first_row, length):
    scores = jnp.einsum("qhd,khd->hqk", query_block, key_rows, preferred_element_type=jnp.float32)
    allowed = allowed_mask(first_row, query_block.shape[0], key_rows.shape[0], length)
    return jnp.where(allowed[None], scores, -1e30)


def attend_forward(query_rows, key_rows, value_rows, length):
    slot_count = query_rows.shape[0]
    step_rows = min(block_rows, slot_count)
    outputs = []
    totals = []
    for block_index in range(slot_count // step_rows):
        first_row = block_index * step_rows
        query_block = query_rows[first_row : first_row + step_rows]
        scores = block_scores(query_block, key_rows, first_row, length)
        row_peak = jnp.max(scores, axis=-1, keepdims=True)
        log_total = row_peak + jnp.log(jnp.sum(jnp.exp(scores - row_peak), axis=-1, keepdims=True))
        weights = jnp.exp(scores - log_total).astype(jnp.bfloat16)
        outputs.append(
            jnp.einsum("hqk,khd->qhd", weights, value_rows, preferred_element_type=jnp.float32)
        )
        totals.append(log_total)
    return (jnp.concatenate(outputs, axis=0), jnp.concatenate(totals, axis=1))


def attend_backward(query_rows, key_rows, value_rows, grad_rows, log_totals, length):
    slot_count = query_rows.shape[0]
    step_rows = min(block_rows, slot_count)
    grad_keys = jnp.zeros(key_rows.shape, jnp.float32)
    grad_values = jnp.zeros(value_rows.shape, jnp.float32)
    grad_queries = []
    for block_index in range(slot_count // step_rows):
        first_row = block_index * step_rows
        query_block = query_rows[first_row : first_row + step_rows]
        grad_block = grad_rows[first_row : first_row + step_rows]
        scores = block_scores(query_block, key_rows, first_row, length)
        probs = jnp.exp(scores - log_totals[:, first_row : first_row + step_rows])
        grad_probs = jnp.einsum(
            "qhd,khd->hqk", grad_block, value_rows, preferred_element_type=jnp.float32
        )
        centre = jnp.sum(probs * grad_probs, axis=-1, keepdims=True)
        grad_scores = (probs * (grad_probs - centre)).astype(jnp.bfloat16)
        grad_queries.append(
            jnp.einsum("hqk,khd->qhd", grad_scores, key_rows, preferred_element_type=jnp.float32)
        )
        grad_keys = grad_keys + jnp.einsum(
            "hqk,qhd->khd", grad_scores, query_block, preferred_element_type=jnp.float32
        )
        grad_values = grad_values + jnp.einsum(
            "hqk,qhd->khd",
            probs.astype(jnp.bfloat16),
            grad_block,
            preferred_element_type=jnp.float32,
        )
    return (jnp.concatenate(grad_queries, axis=0), grad_keys, grad_values)


MESH = pl.DeviceIdType.MESH
UP, DOWN, SIDE = 0, 1, 2
VMEM = pltpu.VMEM
DMA = pltpu.SemaphoreType.DMA
f32 = jnp.float32
bf16 = jnp.bfloat16


class Place:
    def __init__(self, n):
        self.n, self.chips = n, n // 2
        self.me = lax.axis_index("tensor")
        self.chip, self.core = self.me // 2, lax.rem(self.me, 2)
        self.side = self.me + 1 - 2 * self.core
        self.below = self.chip > 0
        self.above = self.chip < self.chips - 1

    def greet(self):
        barrier = pltpu.get_barrier_semaphore()

        def tell(target):
            pl.semaphore_signal(
                barrier, inc=1, device_id={"tensor": target}, device_id_type=MESH
            )

        tell(self.side)
        pl.when(self.below)(lambda: tell(self.me - 2))
        pl.when(self.above)(lambda: tell(self.me + 2))
        peers = 1 + self.below.astype(jnp.int32) + self.above.astype(jnp.int32)
        pl.semaphore_wait(barrier, peers)


def rows_of(index, rows):
    return pl.ds(pl.multiple_of(index * rows, rows), rows)


class Gather:
    def __init__(self, at, rows, buf, send, recv):
        self.at, self.rows, self.buf, self.send, self.recv = at, rows, buf, send, recv
        self.seqs = buf.shape[0]

    @staticmethod
    def scratch(n, seqs):
        return [DMA((3, seqs, n // 2)), DMA((seqs, n))]

    def piece(self, s, o, k):
        return self.buf.at[s, rows_of(2 * o + k, self.rows)]

    def copy(self, s, o, kind):
        at = self.at
        target = (at.me + 2, at.me - 2, at.side)[kind]
        piece = self.piece(s, o, at.core)
        return pltpu.make_async_remote_copy(
            src_ref=piece,
            dst_ref=piece,
            send_sem=self.send.at[kind, s, o],
            recv_sem=self.recv.at[s, 2 * o + at.core],
            device_id={"tensor": target},
            device_id_type=MESH,
        )

    def arrived(self, s, o, k):
        at = self.at
        piece = self.piece(s, o, k)
        pltpu.make_async_remote_copy(
            src_ref=piece,
            dst_ref=piece,
            send_sem=self.send.at[SIDE, s, o],
            recv_sem=self.recv.at[s, 2 * o + k],
            device_id={"tensor": at.side},
            device_id_type=MESH,
        ).wait_recv()

    def start(self, s):
        at = self.at
        pl.when(at.above)(lambda: self.copy(s, at.chip, UP).start())
        pl.when(at.below)(lambda: self.copy(s, at.chip, DOWN).start())
        self.copy(s, at.chip, SIDE).start()

    def units(self):
        return self.seqs * (1 + 2 * (self.at.chips - 1))

    def unit(self, u):
        at = self.at
        per = 1 + 2 * (at.chips - 1)
        s, v = u // per, lax.rem(u, per)
        d = (v + 1) // 2
        o = at.chip + (2 * lax.rem(v, 2) - 1) * d
        return s, o, (o >= 0) & (o < at.chips) & (u >= 0) & (u < self.units()), v == 0

    def forward(self, u):
        at = self.at
        s, o, there, own = self.unit(u)

        @pl.when(there & jnp.logical_not(own))
        def _():
            self.arrived(s, o, at.core)
            pl.when((o < at.chip) & at.above)(lambda: self.copy(s, o, UP).start())
            pl.when((o > at.chip) & at.below)(lambda: self.copy(s, o, DOWN).start())
            self.copy(s, o, SIDE).start()

    def finish(self):
        at = self.at

        def one(i, carry):
            s, o = i // at.chips, lax.rem(i, at.chips)
            pl.when((o <= at.chip) & at.above)(lambda: self.copy(s, o, UP).wait_send())
            pl.when((o >= at.chip) & at.below)(lambda: self.copy(s, o, DOWN).wait_send())
            self.copy(s, o, SIDE).wait_send()
            return carry

        lax.fori_loop(0, self.seqs * at.chips, one, 0)


class Scatter:
    def __init__(self, at, rows, part, side, link, side_send, side_recv, send, recv):
        self.at, self.rows = at, rows
        self.part, self.side, self.link = part, side, link
        self.side_send, self.side_recv, self.send, self.recv = side_send, side_recv, send, recv
        self.seqs = part.shape[0]

    @staticmethod
    def scratch(n, seqs, rows, width):
        chips = n // 2
        return [
            VMEM((seqs, chips, 2 * rows, width), bf16),
            VMEM((seqs, chips, rows, width), bf16),
            VMEM((seqs, chips + 1, rows, width), bf16),
            DMA((seqs, chips)),
            DMA((seqs, chips)),
            DMA((seqs, chips)),
            DMA((seqs, chips + 1)),
        ]

    def units(self):
        return self.seqs * (2 * self.at.chips - 1)

    def unit(self, u):
        at = self.at
        per = 2 * (at.chips - 1)
        v = lax.rem(u, per)
        last = u >= self.seqs * per
        s = jnp.where(last, u - self.seqs * per, u // per)
        up = lax.rem(v, 2) == 0
        away = jnp.where(up, at.chips - 1 - v // 2, v // 2)
        o = jnp.where(last, at.chip, away)
        there = last | jnp.where(up, away > at.chip, away < at.chip)
        return s, o, there & (u >= 0) & (u < self.units())

    def side_copy(self, s, o):
        at = self.at
        return pltpu.make_async_remote_copy(
            src_ref=self.part.at[s, o, rows_of(1 - at.core, self.rows)],
            dst_ref=self.side.at[s, o],
            send_sem=self.side_send.at[s, o],
            recv_sem=self.side_recv.at[s, o],
            device_id={"tensor": at.side},
            device_id_type=MESH,
        )

    def link_copy(self, s, o, slot, target):
        return pltpu.make_async_remote_copy(
            src_ref=self.part.at[s, o, rows_of(self.at.core, self.rows)],
            dst_ref=self.link.at[s, slot],
            send_sem=self.send.at[s, o],
            recv_sem=self.recv.at[s, slot],
            device_id={"tensor": target},
            device_id_type=MESH,
        )

    def share(self, s, o):
        self.side_copy(s, o).start()

    def blocks(self, body):
        step = 16
        lax.fori_loop(0, self.rows // step, lambda i, c: (body(pl.multiple_of(i * step, step), step), c)[1], 0)

    def add_up(self, s, o, slots):
        base = self.at.core * self.rows

        def body(first, step):
            here = pl.ds(pl.multiple_of(base + first, step), step)
            there = pl.ds(first, step)
            total = self.part[s, o, here].astype(f32) + self.side[s, o, there].astype(f32)
            for slot in slots:
                total += self.link[s, slot, there].astype(f32)
            self.part[s, o, here] = total.astype(bf16)

        self.blocks(body)

    def pass_on(self, u, final):
        at = self.at
        s, o, there = self.unit(u)

        @pl.when(there)
        def _():
            self.side_copy(s, o).wait_recv()

            @pl.when(o > at.chip)
            def _():
                @pl.when(at.below)
                def _():
                    self.link_copy(s, o, o, at.me).wait_recv()
                    self.add_up(s, o, [o])

                pl.when(jnp.logical_not(at.below))(lambda: self.add_up(s, o, []))
                self.link_copy(s, o, o, at.me + 2).start()

            @pl.when(o < at.chip)
            def _():
                @pl.when(at.above)
                def _():
                    self.link_copy(s, o, o, at.me).wait_recv()
                    self.add_up(s, o, [o])

                pl.when(jnp.logical_not(at.above))(lambda: self.add_up(s, o, []))
                slot = jnp.where(o == at.chip - 1, at.chips, o)
                self.link_copy(s, o, slot, at.me - 2).start()

            @pl.when(o == at.chip)
            def _():
                pl.when(at.below)(lambda: self.link_copy(s, o, o, at.me).wait_recv())
                pl.when(at.above)(lambda: self.link_copy(s, o, at.chips, at.me).wait_recv())
                for slot, used in ((o, at.below), (at.chips, at.above)):
                    @pl.when(jnp.logical_not(used))
                    def _():
                        def clear(first, step):
                            self.link[s, slot, pl.ds(first, step)] = jnp.zeros(
                                (step, self.link.shape[-1]), bf16
                            )

                        self.blocks(clear)
                base = at.core * self.rows

                def body(first, step):
                    here = pl.ds(pl.multiple_of(base + first, step), step)
                    there = pl.ds(first, step)
                    total = self.part[s, o, here].astype(f32) + self.side[s, o, there].astype(f32)
                    total += self.link[s, o, there].astype(f32)
                    total += self.link[s, at.chips, there].astype(f32)
                    final(s, there, total)

                self.blocks(body)

    def finish(self):
        at = self.at

        def one(i, carry):
            s, o = i // at.chips, lax.rem(i, at.chips)
            self.side_copy(s, o).wait_send()
            pl.when(o != at.chip)(lambda: self.link_copy(s, o, o, at.side).wait_send())
            return carry

        lax.fori_loop(0, self.seqs * at.chips, one, 0)


def norm_rows(values, gain, shift):
    centre = values - jnp.mean(values, axis=-1, keepdims=True)
    spread = jnp.mean(centre * centre, axis=-1, keepdims=True)
    return centre * lax.rsqrt(spread + norm_epsilon) * gain + shift


def gather_project_kernel(
    n, tokens, gain, shift, weight, bias, gathered, heads, buf, send, recv, out_sem
):
    at = Place(n)
    seqs, rows, width = tokens.shape
    ring = Gather(at, rows, buf, send, recv)
    at.greet()
    for s in range(seqs):
        def block(i, carry):
            first = pl.multiple_of(i * 16, 16)
            values = norm_rows(tokens[s, pl.ds(first, 16)].astype(f32), gain[...], shift[...])
            buf[s, pl.ds(pl.multiple_of(at.me * rows + first, 16), 16)] = values.astype(bf16)
            return carry

        lax.fori_loop(0, rows // 16, block, 0)
        ring.start(s)

    def keep(s, o):
        here = rows_of(o, 2 * rows)
        return pltpu.make_async_copy(buf.at[s, here], gathered.at[s, here], out_sem.at[s, o])

    def step(u, carry):
        ring.forward(u)
        s, o, there, own = ring.unit(u - 2)

        @pl.when(there)
        def _():
            ring.arrived(s, o, 1 - at.core)
            keep(s, o).start()
            here = rows_of(o, 2 * rows)
            for j in range(3):
                total = jnp.dot(buf[s, here], weight[j], preferred_element_type=f32)
                if j == 0:
                    total = (total + bias[0:1]) * HD ** (-0.5)
                if j == 2:
                    total = total + bias[1:2]
                heads[j, s, here] = total.astype(bf16)

        return carry

    lax.fori_loop(0, ring.units() + 2, step, 0)
    ring.finish()

    def close(i, carry):
        keep(i // at.chips, lax.rem(i, at.chips)).wait()
        return carry

    lax.fori_loop(0, seqs * at.chips, close, 0)


def whole(count):
    return [pl.BlockSpec(memory_space=VMEM)] * count


def gather_project(n, tokens, gain, shift, weight, bias):
    seqs, rows, width = tokens.shape
    part = weight.shape[2]
    return pl.pallas_call(
        functools.partial(gather_project_kernel, n),
        out_shape=(
            jax.ShapeDtypeStruct((seqs, n * rows, width), bf16),
            jax.ShapeDtypeStruct((3, seqs, n * rows, part), bf16),
        ),
        in_specs=whole(5),
        out_specs=(pl.BlockSpec(memory_space=pl.ANY), pl.BlockSpec(memory_space=VMEM)),
        scratch_shapes=[VMEM((seqs, n * rows, width), bf16)]
        + Gather.scratch(n, seqs)
        + [DMA((seqs, n // 2))],
        compiler_params=pltpu.CompilerParams(
            collective_id=0, has_side_effects=True, vmem_limit_bytes=40 * 2**20
        ),
        name="gather_project",
    )(tokens, gain, shift, weight, bias)


def project_scatter_kernel(
    n, mixed, weight, tokens, bias, gain, shift, hidden, normed, *scratch
):
    at = Place(n)
    seqs, rows, width = tokens.shape
    line = Scatter(at, rows, *scratch)
    at.greet()

    def final(s, there, total):
        values = tokens[s, there].astype(f32) + total + bias[...]
        hidden[s, there] = values
        normed[s, there] = norm_rows(values, gain[...], shift[...]).astype(bf16)

    def step(u, carry):
        s, o, there = line.unit(u)

        @pl.when(there)
        def _():
            here = rows_of(o, 2 * rows)
            for j in range(width // 512):
                cols = pl.ds(j * 512, 512)
                total = jnp.dot(mixed[s, here], weight[:, cols], preferred_element_type=f32)
                line.part[s, o, :, cols] = total.astype(bf16)
            line.share(s, o)

        line.pass_on(u - 2, final)
        return carry

    lax.fori_loop(0, line.units() + 2, step, 0)
    line.finish()


def project_scatter(n, mixed, weight, tokens, bias, gain, shift):
    seqs, rows, width = tokens.shape
    return pl.pallas_call(
        functools.partial(project_scatter_kernel, n),
        out_shape=(
            jax.ShapeDtypeStruct((seqs, rows, width), f32),
            jax.ShapeDtypeStruct((seqs, rows, width), bf16),
        ),
        in_specs=whole(6),
        out_specs=tuple(whole(2)),
        scratch_shapes=Scatter.scratch(n, seqs, rows, width),
        compiler_params=pltpu.CompilerParams(
            collective_id=1, has_side_effects=True, vmem_limit_bytes=40 * 2**20
        ),
        name="project_scatter",
    )(mixed, weight, tokens, bias, gain, shift)


def heads_scatter_kernel(n, query, key, value, weight, grad, *scratch):
    at = Place(n)
    seqs, rows, width = grad.shape
    line = Scatter(at, rows, *scratch)
    at.greet()

    def final(s, there, total):
        grad[s, there] = total

    def step(u, carry):
        s, o, there = line.unit(u)

        @pl.when(there)
        def _():
            here = rows_of(o, 2 * rows)
            for j in range(width // 512):
                cols = pl.ds(j * 512, 512)
                total = 0.0
                for part, scale, i in ((query, HD ** (-0.5), 0), (key, 1.0, 1), (value, 1.0, 2)):
                    total += scale * lax.dot_general(
                        part[s, here],
                        weight[i, cols],
                        (((1,), (1,)), ((), ())),
                        preferred_element_type=f32,
                    )
                line.part[s, o, :, cols] = total.astype(bf16)
            line.share(s, o)

        line.pass_on(u - 2, final)
        return carry

    lax.fori_loop(0, line.units() + 2, step, 0)
    line.finish()


def heads_scatter(n, query, key, value, weight):
    seqs, slots, part = query.shape
    width = weight.shape[1]
    rows = slots // n
    return pl.pallas_call(
        functools.partial(heads_scatter_kernel, n),
        out_shape=jax.ShapeDtypeStruct((seqs, rows, width), f32),
        in_specs=whole(4),
        out_specs=whole(1)[0],
        scratch_shapes=Scatter.scratch(n, seqs, rows, width),
        compiler_params=pltpu.CompilerParams(
            collective_id=2, has_side_effects=True, vmem_limit_bytes=40 * 2**20
        ),
        name="heads_scatter",
    )(query, key, value, weight)


def normal_cdf(values):
    x = jnp.clip(values * 0.7071067811865476, -3.832506856900711, 3.832506856900711)
    x2 = x * x
    top = 0.00022905065861350646
    for c in (0.0034082910107109506, 0.050955695062380861, 0.18520832239976145, 1.128379143519084):
        top = top * x2 + c
    low = -1.1791602954361697e-7
    for c in (
        0.000023547966471313185,
        0.0010179625278914885,
        0.014070470171167667,
        0.11098505178285362,
        0.49746925110067538,
        1.0,
    ):
        low = low * x2 + c
    return 0.5 + 0.5 * (x * top / low)


NT = (((1,), (1,)), ((), ()))
TN = (((0,), (0,)), ((), ()))


def mlp_kernel(
    n,
    normed,
    grad_all,
    up_weight,
    up_bias,
    down_weight,
    mlp_part,
    norm_grad,
    up_grad,
    up_bias_grad,
    down_grad,
    buf,
    send,
    recv,
    *scratch,
):
    at = Place(n)
    seqs, rows, width = normed.shape
    units_wide = up_weight.shape[1]
    line = Scatter(at, rows, *scratch[:7])
    act, pre, out_stage, out_sem, up_stage, up_sem, down_stage, down_sem = scratch[7:]
    ring = Gather(at, rows, buf, send, recv)
    at.greet()
    for s in range(seqs):
        buf[s, rows_of(at.me, rows)] = normed[s]
        ring.start(s)
    up_bias_grad[...] = jnp.zeros_like(up_bias_grad)
    ft = min(512, units_wide)

    def out_copy(s, o):
        return pltpu.make_async_copy(
            out_stage, mlp_part.at[s, rows_of(o, 2 * rows)], out_sem.at[0]
        )

    def work(s, o, first):
        ring.arrived(s, o, 1 - at.core)
        here = rows_of(o, 2 * rows)
        for j in range(units_wide // ft):
            cols = pl.ds(j * ft, ft)
            value = jnp.dot(buf[s, here], up_weight[:, cols], preferred_element_type=f32)
            value = value + up_bias[:, cols]
            spread = normal_cdf(value)
            act[s, here, cols] = (value * spread).astype(bf16)
            slope = spread + value * (0.3989422804014327 * jnp.exp(-0.5 * value * value))
            grad = lax.dot_general(
                grad_all[s, here], down_weight[cols], NT, preferred_element_type=f32
            )
            grad = (grad * slope).astype(bf16)
            pre[s, here, cols] = grad
            up_bias_grad[:, cols] += jnp.sum(grad.astype(f32), axis=0, keepdims=True)
        for j in range(width // 512):
            cols = pl.ds(j * 512, 512)
            line.part[s, o, :, cols] = lax.dot_general(
                pre[s, here], up_weight[cols], NT, preferred_element_type=f32
            ).astype(bf16)
        line.share(s, o)
        pl.when(jnp.logical_not(first))(lambda: out_copy(s, o).wait())
        for j in range(width // 512):
            cols = pl.ds(j * 512, 512)
            out_stage[:, cols] = jnp.dot(
                act[s, here], down_weight[:, cols], preferred_element_type=f32
            ).astype(bf16)
        out_copy(s, o).start()

    def final(s, there, total):
        norm_grad[s, there] = total

    down_tiles = down_grad.shape[0] // down_stage.shape[1]
    up_tiles = up_grad.shape[0] // up_stage.shape[1]
    flat = seqs * rows * n

    def down_copy(t):
        size = down_stage.shape[1]
        return pltpu.make_async_copy(
            down_stage.at[t % 2], down_grad.at[pl.ds(t * size, size)], down_sem.at[t % 2]
        )

    def up_copy(t):
        size = up_stage.shape[1]
        return pltpu.make_async_copy(
            up_stage.at[t % 2], up_grad.at[pl.ds(t * size, size)], up_sem.at[t % 2]
        )

    def weight_tile(i):
        for t in range(down_tiles):
            @pl.when(i == t)
            def _():
                size = down_stage.shape[1]
                if t >= 2:
                    down_copy(t - 2).wait()
                total = 0.0
                for s in range(seqs):
                    total += lax.dot_general(
                        act[s, :, pl.ds(t * size, size)], grad_all[s], TN, preferred_element_type=f32
                    )
                down_stage[t % 2] = total.astype(bf16)
                down_copy(t).start()
        for t in range(up_tiles):
            @pl.when(i == t + down_tiles)
            def _():
                size = up_stage.shape[1]
                if t >= 2:
                    up_copy(t - 2).wait()
                total = 0.0
                for s in range(seqs):
                    total += lax.dot_general(
                        buf[s, :, pl.ds(t * size, size)], pre[s], TN, preferred_element_type=f32
                    )
                up_stage[t % 2] = total.astype(bf16)
                up_copy(t).start()

    lag = ring.units() // seqs + 2

    def step(u, carry):
        ring.forward(u)
        line.pass_on(u - lag, final)
        s, o, there, own = ring.unit(u - 1)
        pl.when(there)(lambda: work(s, o, u == 1))
        weight_tile(u - ring.units() - 1)
        return carry

    count = max(line.units() + lag, ring.units() + 1 + down_tiles + up_tiles)
    lax.fori_loop(0, count, step, 0)
    ring.finish()
    line.finish()
    for t in range(max(down_tiles - 2, 0), down_tiles):
        down_copy(t).wait()
    for t in range(max(up_tiles - 2, 0), up_tiles):
        up_copy(t).wait()
    out_copy(0, 0).wait()


def mlp_block(n, normed, grad_all, up_weight, up_bias, down_weight):
    seqs, rows, width = normed.shape
    slots = n * rows
    units = up_weight.shape[1]
    hbm = pl.BlockSpec(memory_space=pl.ANY)
    vmem = pl.BlockSpec(memory_space=VMEM)
    down_size, up_size = min(256, units), 512
    return pl.pallas_call(
        functools.partial(mlp_kernel, n),
        out_shape=(
            jax.ShapeDtypeStruct((seqs, slots, width), bf16),
            jax.ShapeDtypeStruct((seqs, rows, width), f32),
            jax.ShapeDtypeStruct((width, units), bf16),
            jax.ShapeDtypeStruct((1, units), f32),
            jax.ShapeDtypeStruct((units, width), bf16),
        ),
        in_specs=whole(5),
        out_specs=(hbm, vmem, hbm, vmem, hbm),
        scratch_shapes=[VMEM((seqs, slots, width), bf16)]
        + Gather.scratch(n, seqs)
        + Scatter.scratch(n, seqs, rows, width)
        + [
            VMEM((seqs, slots, units), bf16),
            VMEM((seqs, slots, units), bf16),
            VMEM((2 * rows, width), bf16),
            DMA((1,)),
            VMEM((2, up_size, units), bf16),
            DMA((2,)),
            VMEM((2, down_size, width), bf16),
            DMA((2,)),
        ],
        compiler_params=pltpu.CompilerParams(
            collective_id=3, has_side_effects=True, vmem_limit_bytes=60 * 2**20
        ),
        name="mlp_block",
    )(normed, grad_all, up_weight, up_bias, down_weight)


def attn_grad_kernel(
    n,
    grad,
    mlp_part,
    hidden,
    bias,
    weight,
    mixed,
    output,
    grad_heads,
    weight_grad,
    buf,
    send,
    recv,
    *scratch,
):
    at = Place(n)
    seqs, rows, width = grad.shape
    line = Scatter(at, rows, *scratch[:7])
    load_sem = scratch[7]
    ring = Gather(at, rows, buf, send, recv)

    def load(s, o):
        return pltpu.make_async_copy(
            mlp_part.at[s, rows_of(o, 2 * rows)], line.part.at[s, o], load_sem.at[s, o]
        )

    def load_unit(u, carry):
        s, o, there = line.unit(u)
        pl.when(there)(lambda: load(s, o).start())
        return carry

    lax.fori_loop(0, line.units(), load_unit, 0)
    at.greet()
    for s in range(seqs):
        buf[s, rows_of(at.me, rows)] = grad[s]
        ring.start(s)

    def final(s, there, total):
        output[s, there] = (hidden[s, there] + total + bias[...]).astype(bf16)

    def step(u, carry):
        ring.forward(u)
        s, o, there = line.unit(u)

        @pl.when(there)
        def _():
            load(s, o).wait()
            line.share(s, o)

        line.pass_on(u - 1, final)
        s, o, there, own = ring.unit(u - 1)

        @pl.when(there)
        def _():
            ring.arrived(s, o, 1 - at.core)
            here = rows_of(o, 2 * rows)
            grad_heads[s, here] = lax.dot_general(
                buf[s, here], weight[...], NT, preferred_element_type=f32
            ).astype(bf16)

        return carry

    lax.fori_loop(0, max(line.units(), ring.units()) + 1, step, 0)
    for j in range(width // 512):
        cols = pl.ds(j * 512, 512)
        total = 0.0
        for s in range(seqs):
            total += lax.dot_general(mixed[s], buf[s, :, cols], TN, preferred_element_type=f32)
        weight_grad[:, cols] = total.astype(bf16)
    ring.finish()
    line.finish()


def attn_grad(n, grad, mlp_part, hidden, bias, weight, mixed):
    seqs, rows, width = grad.shape
    slots = n * rows
    part = weight.shape[0]
    vmem = pl.BlockSpec(memory_space=VMEM)
    return pl.pallas_call(
        functools.partial(attn_grad_kernel, n),
        out_shape=(
            jax.ShapeDtypeStruct((seqs, rows, width), bf16),
            jax.ShapeDtypeStruct((seqs, slots, part), bf16),
            jax.ShapeDtypeStruct((part, width), bf16),
        ),
        in_specs=[vmem, pl.BlockSpec(memory_space=pl.ANY), vmem, vmem, vmem, vmem],
        out_specs=tuple(whole(3)),
        scratch_shapes=[VMEM((seqs, slots, width), bf16)]
        + Gather.scratch(n, seqs)
        + Scatter.scratch(n, seqs, rows, width)
        + [DMA((seqs, n // 2))],
        compiler_params=pltpu.CompilerParams(
            collective_id=4, has_side_effects=True, vmem_limit_bytes=48 * 2**20
        ),
        name="attn_grad",
    )(grad, mlp_part, hidden, bias, weight, mixed)


def body(
    tokens,
    cotangent,
    lengths,
    ln1_gain,
    ln1_shift,
    qkv_weight,
    qkv_bias,
    out_weight,
    out_bias,
    ln2_gain,
    ln2_shift,
    up_weight,
    up_bias,
    down_weight,
    down_bias,
):
    seq_count, local_rows, model_width = tokens.shape
    part_width = qkv_weight.shape[2]
    head_count = part_width // HD
    score_scale = HD ** (-0.5)
    inputs = tokens.astype(jnp.float32)
    n = lax.axis_size("tensor")
    gathered_one, heads = gather_project(
        n, tokens, ln1_gain[None], ln1_shift[None], qkv_weight, qkv_bias
    )
    slot_count = gathered_one.shape[1]
    head_shape = (seq_count, slot_count, head_count, HD)
    query_rows, key_rows, value_rows = [heads[j].reshape(head_shape) for j in range(3)]
    attended, log_totals = lax.map(
        lambda item: attend_forward(item[0], item[1], item[2], item[3]),
        (query_rows, key_rows, value_rows, lengths),
    )
    mixed_heads = attended.reshape(seq_count, slot_count, part_width).astype(jnp.bfloat16)
    hidden_state, normed_two = project_scatter(
        n, mixed_heads, out_weight, tokens, out_bias[None], ln2_gain[None], ln2_shift[None]
    )
    slot_ids = lax.axis_index("tensor") * local_rows + lax.broadcasted_iota(
        jnp.int32, (seq_count, local_rows), 1
    )
    valid_rows = (slot_ids < lengths[:, None]).astype(jnp.float32)
    grad_out = cotangent.astype(jnp.float32) * valid_rows[:, :, None]
    down_bias_grad = jnp.sum(grad_out, axis=(0, 1))
    grad_mlp = lax.all_gather(grad_out.astype(jnp.bfloat16), "tensor", axis=1, tiled=True)
    mlp_part, norm_two_grad, up_weight_grad, up_bias_grad, down_weight_grad = mlp_block(
        n, normed_two, grad_mlp, up_weight, up_bias[None], down_weight
    )
    up_bias_grad = up_bias_grad[0]
    up_weight_grad, down_weight_grad = sum_groups((up_weight_grad, down_weight_grad))
    unused_two, norm_two_back = jax.vjp(layer_norm, hidden_state, ln2_gain, ln2_shift)
    hidden_ln_grad, ln2_gain_grad, ln2_shift_grad = norm_two_back(norm_two_grad)
    hidden_grad = grad_out + hidden_ln_grad
    out_bias_grad = jnp.sum(hidden_grad, axis=(0, 1))
    output, grad_heads, out_weight_grad = attn_grad(
        n,
        hidden_grad.astype(jnp.bfloat16),
        mlp_part,
        hidden_state,
        down_bias[None],
        out_weight,
        mixed_heads,
    )
    grad_heads = grad_heads.reshape(head_shape)
    grad_query, grad_key, grad_value = lax.map(
        lambda item: attend_backward(item[0], item[1], item[2], item[3], item[4], item[5]),
        (query_rows, key_rows, value_rows, grad_heads, log_totals, lengths),
    )
    flat_shape = (seq_count, slot_count, part_width)
    grad_query = grad_query.reshape(flat_shape).astype(jnp.bfloat16)
    grad_key = grad_key.reshape(flat_shape).astype(jnp.bfloat16)
    grad_value = grad_value.reshape(flat_shape).astype(jnp.bfloat16)
    qkv_weight_grad = jnp.stack(
        [
            score_scale * rows_product(gathered_one, grad_query),
            rows_product(gathered_one, grad_key),
            rows_product(gathered_one, grad_value),
        ]
    )
    qkv_weight_grad, out_weight_grad, up_weight_grad, down_weight_grad = lax.optimization_barrier(
        (qkv_weight_grad, out_weight_grad, up_weight_grad, down_weight_grad)
    )
    qkv_weight_grad, out_weight_grad = sum_groups((qkv_weight_grad, out_weight_grad))
    qkv_bias_grad = jnp.stack(
        [
            score_scale * jnp.sum(grad_query.astype(jnp.float32), axis=(0, 1)),
            jnp.sum(grad_value.astype(jnp.float32), axis=(0, 1)),
        ]
    )
    norm_one_grad = heads_scatter(n, grad_query, grad_key, grad_value, qkv_weight)
    unused_one, norm_one_back = jax.vjp(layer_norm, inputs, ln1_gain, ln1_shift)
    input_ln_grad, ln1_gain_grad, ln1_shift_grad = norm_one_back(norm_one_grad)
    input_grad = hidden_grad + input_ln_grad
    qkv_bias_grad, up_bias_grad = lax.psum((qkv_bias_grad, up_bias_grad), "dp")
    ln1_gain_grad, ln1_shift_grad, out_bias_grad, ln2_gain_grad, ln2_shift_grad, down_bias_grad = (
        lax.psum(
            (
                ln1_gain_grad,
                ln1_shift_grad,
                out_bias_grad,
                ln2_gain_grad,
                ln2_shift_grad,
                down_bias_grad,
            ),
            ("dp", "tensor"),
        )
    )
    return (
        output,
        input_grad,
        ln1_gain_grad,
        ln1_shift_grad,
        qkv_weight_grad,
        qkv_bias_grad,
        out_weight_grad,
        out_bias_grad,
        ln2_gain_grad,
        ln2_shift_grad,
        up_weight_grad,
        up_bias_grad,
        down_weight_grad,
        down_bias_grad,
    )


def solution(mesh):
    in_specs = (
        P("dp", "tensor", None),
        P("dp", "tensor", None),
        P("dp"),
        P(),
        P(),
        P(None, None, "tensor"),
        P(None, "tensor"),
        P("tensor", None),
        P(),
        P(),
        P(),
        P(None, "tensor"),
        P("tensor"),
        P("tensor", None),
        P(),
    )
    out_specs = (
        P("dp", "tensor", None),
        P("dp", "tensor", None),
        P(),
        P(),
        P(None, None, "tensor"),
        P(None, "tensor"),
        P("tensor", None),
        P(),
        P(),
        P(),
        P(None, "tensor"),
        P("tensor"),
        P("tensor", None),
        P(),
    )
    return jax.shard_map(body, mesh=mesh, in_specs=in_specs, out_specs=out_specs, check_vma=False)
```

```python
import functools

import jax
import jax.numpy as jnp
from jax import lax
from jax.experimental import pallas as pl
from jax.experimental.pallas import tpu as pltpu
from jax.sharding import PartitionSpec as P

HD = 128


norm_epsilon = 1e-05
block_rows = 512


def layer_norm(values, norm_gain, norm_shift):
    centre = values - jnp.mean(values, axis=-1, keepdims=True)
    spread = jnp.mean(centre * centre, axis=-1, keepdims=True)
    return centre * lax.rsqrt(spread + norm_epsilon) * norm_gain + norm_shift


def gelu_exact(values):
    return jax.nn.gelu(values, approximate=False)


def flat_product(left_rows, right_rows):
    flat = left_rows.reshape(-1, left_rows.shape[-1])
    result = jnp.dot(flat, right_rows, preferred_element_type=jnp.float32)
    return result.reshape(left_rows.shape[:-1] + (right_rows.shape[-1],))


def product_back(left_rows, right_rows):
    flat = left_rows.reshape(-1, left_rows.shape[-1])
    result = lax.dot_general(
        flat, right_rows, (((1,), (1,)), ((), ())), preferred_element_type=jnp.float32
    )
    return result.reshape(left_rows.shape[:-1] + (right_rows.shape[0],))


def rows_product(left_rows, right_rows):
    left_flat = left_rows.reshape(-1, left_rows.shape[-1])
    right_flat = right_rows.reshape(-1, right_rows.shape[-1])
    return lax.dot_general(
        left_flat, right_flat, (((0,), (0,)), ((), ())), preferred_element_type=jnp.float32
    )


def sum_groups(parts):
    parts = [part.astype(jnp.bfloat16) for part in parts]
    return [total.astype(jnp.float32) for total in lax.psum(parts, "dp")]


def allowed_mask(first_row, row_count, slot_count, length):
    row_ids = first_row + lax.broadcasted_iota(jnp.int32, (row_count, slot_count), 0)
    col_ids = lax.broadcasted_iota(jnp.int32, (row_count, slot_count), 1)
    return (col_ids <= row_ids) & (col_ids < length)


def block_scores(query_block, key_rows, first_row, length):
    scores = jnp.einsum("qhd,khd->hqk", query_block, key_rows, preferred_element_type=jnp.float32)
    allowed = allowed_mask(first_row, query_block.shape[0], key_rows.shape[0], length)
    return jnp.where(allowed[None], scores, -1e30)


def attend_forward(query_rows, key_rows, value_rows, length):
    slot_count = query_rows.shape[0]
    step_rows = min(block_rows, slot_count)
    outputs = []
    totals = []
    for block_index in range(slot_count // step_rows):
        first_row = block_index * step_rows
        query_block = query_rows[first_row : first_row + step_rows]
        scores = block_scores(query_block, key_rows, first_row, length)
        row_peak = jnp.max(scores, axis=-1, keepdims=True)
        log_total = row_peak + jnp.log(jnp.sum(jnp.exp(scores - row_peak), axis=-1, keepdims=True))
        weights = jnp.exp(scores - log_total).astype(jnp.bfloat16)
        outputs.append(
            jnp.einsum("hqk,khd->qhd", weights, value_rows, preferred_element_type=jnp.float32)
        )
        totals.append(log_total)
    return (jnp.concatenate(outputs, axis=0), jnp.concatenate(totals, axis=1))


def attend_backward(query_rows, key_rows, value_rows, grad_rows, log_totals, length):
    slot_count = query_rows.shape[0]
    step_rows = min(block_rows, slot_count)
    grad_keys = jnp.zeros(key_rows.shape, jnp.float32)
    grad_values = jnp.zeros(value_rows.shape, jnp.float32)
    grad_queries = []
    for block_index in range(slot_count // step_rows):
        first_row = block_index * step_rows
        query_block = query_rows[first_row : first_row + step_rows]
        grad_block = grad_rows[first_row : first_row + step_rows]
        scores = block_scores(query_block, key_rows, first_row, length)
        probs = jnp.exp(scores - log_totals[:, first_row : first_row + step_rows])
        grad_probs = jnp.einsum(
            "qhd,khd->hqk", grad_block, value_rows, preferred_element_type=jnp.float32
        )
        centre = jnp.sum(probs * grad_probs, axis=-1, keepdims=True)
        grad_scores = (probs * (grad_probs - centre)).astype(jnp.bfloat16)
        grad_queries.append(
            jnp.einsum("hqk,khd->qhd", grad_scores, key_rows, preferred_element_type=jnp.float32)
        )
        grad_keys = grad_keys + jnp.einsum(
            "hqk,qhd->khd", grad_scores, query_block, preferred_element_type=jnp.float32
        )
        grad_values = grad_values + jnp.einsum(
            "hqk,qhd->khd",
            probs.astype(jnp.bfloat16),
            grad_block,
            preferred_element_type=jnp.float32,
        )
    return (jnp.concatenate(grad_queries, axis=0), grad_keys, grad_values)


MESH = pl.DeviceIdType.MESH
UP, DOWN, SIDE = 0, 1, 2
VMEM = pltpu.VMEM
DMA = pltpu.SemaphoreType.DMA
f32 = jnp.float32
bf16 = jnp.bfloat16
NT = (((1,), (1,)), ((), ()))
TN = (((0,), (0,)), ((), ()))


class Place:
    def __init__(self, n):
        self.n, self.chips = n, n // 2
        self.me = lax.axis_index("tensor")
        self.chip, self.core = self.me // 2, lax.rem(self.me, 2)
        self.side = self.me + 1 - 2 * self.core
        self.below = self.chip > 0
        self.above = self.chip < self.chips - 1
        self.group = lax.axis_index("dp")
        self.group_bits = lax.axis_size("dp").bit_length() - 1
        self.bits = n.bit_length() - 1

    def group_peer(self, q):
        mine = lax.rem(self.group // 2**q, 2)
        return self.group + (1 - 2 * mine) * 2**q, mine

    def peer(self, q):
        mine = lax.rem(self.me // 2**q, 2)
        return self.me + (1 - 2 * mine) * 2**q

    def greet(self, groups=False, cube=False):
        barrier = pltpu.get_barrier_semaphore()

        def tell(target):
            pl.semaphore_signal(
                barrier, inc=1, device_id={"tensor": target}, device_id_type=MESH
            )

        tell(self.side)
        pl.when(self.below)(lambda: tell(self.me - 2))
        pl.when(self.above)(lambda: tell(self.me + 2))
        peers = 1 + self.below.astype(jnp.int32) + self.above.astype(jnp.int32)
        if groups:
            for q in range(self.group_bits):
                pl.semaphore_signal(
                    barrier, inc=1, device_id={"dp": self.group_peer(q)[0]}, device_id_type=MESH
                )
            peers = peers + self.group_bits
        if cube:
            for q in range(self.bits):
                tell(self.peer(q))
            peers = peers + self.bits
        pl.semaphore_wait(barrier, peers)


def rows_of(index, rows):
    return pl.ds(pl.multiple_of(index * rows, rows), rows)


class Gather:
    def __init__(self, at, rows, buf, send, recv):
        self.at, self.rows, self.buf, self.send, self.recv = at, rows, buf, send, recv
        self.seqs = buf.shape[0]

    @staticmethod
    def scratch(n, seqs):
        return [DMA((3, seqs, n // 2)), DMA((seqs, n))]

    def piece(self, s, o, k):
        return self.buf.at[s, rows_of(2 * o + k, self.rows)]

    def copy(self, s, o, kind):
        at = self.at
        target = (at.me + 2, at.me - 2, at.side)[kind]
        piece = self.piece(s, o, at.core)
        return pltpu.make_async_remote_copy(
            src_ref=piece,
            dst_ref=piece,
            send_sem=self.send.at[kind, s, o],
            recv_sem=self.recv.at[s, 2 * o + at.core],
            device_id={"tensor": target},
            device_id_type=MESH,
        )

    def arrived(self, s, o, k):
        at = self.at
        piece = self.piece(s, o, k)
        pltpu.make_async_remote_copy(
            src_ref=piece,
            dst_ref=piece,
            send_sem=self.send.at[SIDE, s, o],
            recv_sem=self.recv.at[s, 2 * o + k],
            device_id={"tensor": at.side},
            device_id_type=MESH,
        ).wait_recv()

    def start(self, s):
        at = self.at
        pl.when(at.above)(lambda: self.copy(s, at.chip, UP).start())
        pl.when(at.below)(lambda: self.copy(s, at.chip, DOWN).start())
        self.copy(s, at.chip, SIDE).start()

    def units(self):
        return self.seqs * (1 + 2 * (self.at.chips - 1))

    def unit(self, u):
        at = self.at
        per = 1 + 2 * (at.chips - 1)
        s, v = u // per, lax.rem(u, per)
        d = (v + 1) // 2
        o = at.chip + (2 * lax.rem(v, 2) - 1) * d
        return s, o, (o >= 0) & (o < at.chips) & (u >= 0) & (u < self.units()), v == 0

    def forward(self, u):
        at = self.at
        s, o, there, own = self.unit(u)

        pl.when(there & own & (s > 0))(lambda: self.start(s))

        @pl.when(there & jnp.logical_not(own))
        def _():
            self.arrived(s, o, at.core)
            pl.when((o < at.chip) & at.above)(lambda: self.copy(s, o, UP).start())
            pl.when((o > at.chip) & at.below)(lambda: self.copy(s, o, DOWN).start())
            self.copy(s, o, SIDE).start()

    def finish(self):
        at = self.at

        def one(i, carry):
            s, o = i // at.chips, lax.rem(i, at.chips)
            pl.when((o <= at.chip) & at.above)(lambda: self.copy(s, o, UP).wait_send())
            pl.when((o >= at.chip) & at.below)(lambda: self.copy(s, o, DOWN).wait_send())
            self.copy(s, o, SIDE).wait_send()
            return carry

        lax.fori_loop(0, self.seqs * at.chips, one, 0)


class Scatter:
    def __init__(self, at, rows, part, side, link, side_send, side_recv, send, recv):
        self.at, self.rows = at, rows
        self.part, self.side, self.link = part, side, link
        self.side_send, self.side_recv, self.send, self.recv = side_send, side_recv, send, recv
        self.seqs = part.shape[0]

    @staticmethod
    def scratch(n, seqs, rows, width):
        chips = n // 2
        return [
            VMEM((seqs, chips, 2 * rows, width), bf16),
            VMEM((seqs, chips, rows, width), bf16),
            VMEM((seqs, chips + 1, rows, width), bf16),
            DMA((seqs, chips)),
            DMA((seqs, chips)),
            DMA((seqs, chips)),
            DMA((seqs, chips + 1)),
        ]

    def units(self):
        return self.seqs * (2 * self.at.chips - 1)

    def unit(self, u):
        at = self.at
        per = 2 * (at.chips - 1)
        v = lax.rem(u, per)
        last = u >= self.seqs * per
        s = jnp.where(last, u - self.seqs * per, u // per)
        up = lax.rem(v, 2) == 0
        away = jnp.where(up, at.chips - 1 - v // 2, v // 2)
        o = jnp.where(last, at.chip, away)
        there = last | jnp.where(up, away > at.chip, away < at.chip)
        return s, o, there & (u >= 0) & (u < self.units())

    def side_copy(self, s, o):
        at = self.at
        return pltpu.make_async_remote_copy(
            src_ref=self.part.at[s, o, rows_of(1 - at.core, self.rows)],
            dst_ref=self.side.at[s, o],
            send_sem=self.side_send.at[s, o],
            recv_sem=self.side_recv.at[s, o],
            device_id={"tensor": at.side},
            device_id_type=MESH,
        )

    def link_copy(self, s, o, slot, target):
        return pltpu.make_async_remote_copy(
            src_ref=self.part.at[s, o, rows_of(self.at.core, self.rows)],
            dst_ref=self.link.at[s, slot],
            send_sem=self.send.at[s, o],
            recv_sem=self.recv.at[s, slot],
            device_id={"tensor": target},
            device_id_type=MESH,
        )

    def share(self, s, o):
        self.side_copy(s, o).start()

    def blocks(self, body):
        step = 16
        lax.fori_loop(0, self.rows // step, lambda i, c: (body(pl.multiple_of(i * step, step), step), c)[1], 0)

    def add_up(self, s, o, slots):
        base = self.at.core * self.rows

        def body(first, step):
            here = pl.ds(pl.multiple_of(base + first, step), step)
            there = pl.ds(first, step)
            total = self.part[s, o, here].astype(f32) + self.side[s, o, there].astype(f32)
            for slot in slots:
                total += self.link[s, slot, there].astype(f32)
            self.part[s, o, here] = total.astype(bf16)

        self.blocks(body)

    def pass_on(self, u, final):
        at = self.at
        s, o, there = self.unit(u)

        @pl.when(there)
        def _():
            self.side_copy(s, o).wait_recv()

            @pl.when(o > at.chip)
            def _():
                @pl.when(at.below)
                def _():
                    self.link_copy(s, o, o, at.me).wait_recv()
                    self.add_up(s, o, [o])

                pl.when(jnp.logical_not(at.below))(lambda: self.add_up(s, o, []))
                self.link_copy(s, o, o, at.me + 2).start()

            @pl.when(o < at.chip)
            def _():
                @pl.when(at.above)
                def _():
                    self.link_copy(s, o, o, at.me).wait_recv()
                    self.add_up(s, o, [o])

                pl.when(jnp.logical_not(at.above))(lambda: self.add_up(s, o, []))
                slot = jnp.where(o == at.chip - 1, at.chips, o)
                self.link_copy(s, o, slot, at.me - 2).start()

            @pl.when(o == at.chip)
            def _():
                pl.when(at.below)(lambda: self.link_copy(s, o, o, at.me).wait_recv())
                pl.when(at.above)(lambda: self.link_copy(s, o, at.chips, at.me).wait_recv())
                for slot, used in ((o, at.below), (at.chips, at.above)):
                    @pl.when(jnp.logical_not(used))
                    def _():
                        def clear(first, step):
                            self.link[s, slot, pl.ds(first, step)] = jnp.zeros(
                                (step, self.link.shape[-1]), bf16
                            )

                        self.blocks(clear)
                base = at.core * self.rows

                def body(first, step):
                    here = pl.ds(pl.multiple_of(base + first, step), step)
                    there = pl.ds(first, step)
                    total = self.part[s, o, here].astype(f32) + self.side[s, o, there].astype(f32)
                    total += self.link[s, o, there].astype(f32)
                    total += self.link[s, at.chips, there].astype(f32)
                    final(s, there, total)

                self.blocks(body)

    def finish(self):
        at = self.at

        def one(i, carry):
            s, o = i // at.chips, lax.rem(i, at.chips)
            self.side_copy(s, o).wait_send()
            pl.when(o != at.chip)(lambda: self.link_copy(s, o, o, at.side).wait_send())
            return carry

        lax.fori_loop(0, self.seqs * at.chips, one, 0)


class GroupSum:
    def __init__(self, at, rows, tiles, inbox, send, recv, keep_sem, out, turn=0, skip=0):
        self.at, self.tiles, self.inbox, self.send, self.recv = at, tiles, inbox, send, recv
        self.keep_sem, self.out, self.skip, self.turn, self.rows = keep_sem, out, skip, turn, rows
        self.bits = at.group_bits
        self.count = send.shape[0]

    @staticmethod
    def scratch(dp, count, rows, width, skip=0):
        phases = 2 * (dp.bit_length() - 1)
        return [
            VMEM((count, rows >> skip, width), bf16),
            VMEM((count, rows - rows // dp, width), bf16),
            DMA((count, phases)),
            DMA((count, phases)),
            DMA((count,)),
        ]

    def peer(self, t, i):
        which = lax.rem(t + i + self.turn, self.bits)
        peer, mine = 0, 0
        for q in range(self.bits):
            other, bit = self.at.group_peer(q)
            peer = peer + jnp.where(which == q, other, 0)
            mine = mine + jnp.where(which == q, bit, 0)
        return peer, mine

    def base(self, t, i):
        first = 0
        for p in range(i):
            first = first + self.peer(t, p)[1] * (self.rows >> (p + 1))
        return first

    def span(self, first, size):
        return pl.ds(pl.multiple_of(first, 16), size)

    def tile(self, t, first, size):
        return self.tiles.at[t, self.span(first - self.base(t, self.skip), size)]

    def box(self, t, i):
        return self.inbox.at[t, pl.ds(self.rows - (self.rows >> i), self.rows >> (i + 1))]

    def remote(self, source, target, t, phase, peer):
        return pltpu.make_async_remote_copy(
            src_ref=source,
            dst_ref=target,
            send_sem=self.send.at[t, phase],
            recv_sem=self.recv.at[t, phase],
            device_id={"dp": peer},
            device_id_type=MESH,
        )

    def halve(self, t, i):
        peer, mine = self.peer(t, i)
        half = self.rows >> (i + 1)
        source = self.tile(t, self.base(t, i) + (1 - mine) * half, half)
        return self.remote(source, self.box(t, i), t, i, peer)

    def add(self, t, i):
        half = self.rows >> (i + 1)
        keep = self.base(t, i + 1) - self.base(t, self.skip)
        box = self.rows - (self.rows >> i)

        def body(j, carry):
            here = self.span(keep + j * 16, 16)
            there = self.span(box + j * 16, 16)
            total = self.tiles[t, here].astype(f32) + self.inbox[t, there].astype(f32)
            self.tiles[t, here] = total.astype(bf16)
            return carry

        lax.fori_loop(0, half // 16, body, 0)

    def keep(self, t):
        first, size = self.base(t, self.bits), self.rows >> self.bits
        return pltpu.make_async_copy(
            self.tile(t, first, size), self.out.at[t, self.span(first, size)], self.keep_sem.at[t]
        )

    def double(self, t, i, back=False):
        peer, mine = self.peer(t, i)
        half = self.rows >> (i + 1)
        first = self.base(t, i) + ((1 - mine) if back else mine) * half
        piece = self.out.at[t, self.span(first, half)]
        source = piece
        if i == self.bits - 1 and not back:
            source = self.tile(t, first, half)
        return self.remote(source, piece, t, 2 * self.bits - 1 - i, peer)

    def events(self):
        return self.count * (2 * self.bits + 1 - self.skip)

    def event(self, e, loaded=None):
        k, t = e // self.count + self.skip, lax.rem(e, self.count)
        bits = self.bits

        def at_stage(stage):
            if stage == 0:
                self.halve(t, 0).start()
            elif stage <= bits:
                if stage > self.skip:
                    self.halve(t, stage - 1).wait_recv()
                else:
                    loaded(t)
                self.add(t, stage - 1)
                if stage < bits:
                    self.halve(t, stage).start()
                else:
                    self.keep(t).start()
                    self.double(t, bits - 1).start()
            else:
                i = 2 * bits - stage
                self.double(t, i, back=True).wait_recv()
                if i == bits - 1:
                    self.keep(t).wait()
                if i > 0:
                    self.double(t, i - 1).start()

        for stage in range(self.skip, 2 * bits + 1):
            pl.when((k == stage) & (e >= 0))(functools.partial(at_stage, stage))

    def finish(self):
        def one(t, carry):
            for i in range(self.bits):
                if i >= self.skip:
                    self.halve(t, i).wait_send()
                self.double(t, i).wait_send()
            return carry

        lax.fori_loop(0, self.count, one, 0)


class SmallSum:
    def __init__(self, at, rows, inbox, send, recv, everywhere):
        self.at, self.rows, self.inbox, self.send, self.recv = at, rows, inbox, send, recv
        self.phases = at.group_bits + (at.bits if everywhere else 0)

    @staticmethod
    def scratch(dp, n, count, width, everywhere):
        phases = (dp.bit_length() - 1) + (n.bit_length() - 1 if everywhere else 0)
        return [
            VMEM((phases + 1, count, width), f32),
            VMEM((phases, count, width), f32),
            DMA((phases,)),
            DMA((phases,)),
        ]

    def copy(self, i):
        at = self.at
        if i < at.group_bits:
            target = {"dp": at.group_peer(i)[0]}
        else:
            target = {"tensor": at.peer(i - at.group_bits)}
        return pltpu.make_async_remote_copy(
            src_ref=self.rows.at[i],
            dst_ref=self.inbox.at[i],
            send_sem=self.send.at[i],
            recv_sem=self.recv.at[i],
            device_id=target,
            device_id_type=MESH,
        )

    def event(self, e):
        def run(i):
            if i > 0:
                self.copy(i - 1).wait_recv()
                self.rows[i] = self.rows[i - 1] + self.inbox[i - 1]
            if i < self.phases:
                self.copy(i).start()

        for i in range(self.phases + 1):
            if isinstance(e, int):
                if e == i:
                    run(i)
            else:
                pl.when(e == i)(functools.partial(run, i))

    def finish(self):
        for i in range(self.phases):
            self.copy(i).wait_send()


def norm_rows(values, gain, shift):
    centre = values - jnp.mean(values, axis=-1, keepdims=True)
    spread = jnp.mean(centre * centre, axis=-1, keepdims=True)
    return centre * lax.rsqrt(spread + norm_epsilon) * gain + shift


def norm_rows_back(values, grad, gain):
    centre = values - jnp.mean(values, axis=-1, keepdims=True)
    scale = lax.rsqrt(jnp.mean(centre * centre, axis=-1, keepdims=True) + norm_epsilon)
    unit = centre * scale
    w = grad * gain
    back = w - jnp.mean(w, axis=-1, keepdims=True)
    back = scale * (back - unit * jnp.mean(w * unit, axis=-1, keepdims=True))
    return back, grad * unit


def add_row(ref, row, values):
    ref[row : row + 1] += jnp.sum(values, axis=0, keepdims=True)


def gather_project_kernel(
    n, tokens, gain, shift, weight, bias, gathered, heads, buf, send, recv, out_sem
):
    at = Place(n)
    seqs, rows, width = tokens.shape
    ring = Gather(at, rows, buf, send, recv)
    at.greet()
    for s in range(seqs):
        def block(i, carry):
            first = pl.multiple_of(i * 16, 16)
            values = norm_rows(tokens[s, pl.ds(first, 16)].astype(f32), gain[...], shift[...])
            buf[s, pl.ds(pl.multiple_of(at.me * rows + first, 16), 16)] = values.astype(bf16)
            return carry

        lax.fori_loop(0, rows // 16, block, 0)
        if s == 0:
            ring.start(s)

    def keep(s, o):
        here = rows_of(o, 2 * rows)
        return pltpu.make_async_copy(buf.at[s, here], gathered.at[s, here], out_sem.at[s, o])

    def step(u, carry):
        ring.forward(u)
        s, o, there, own = ring.unit(u - 2)

        @pl.when(there)
        def _():
            ring.arrived(s, o, 1 - at.core)
            keep(s, o).start()
            here = rows_of(o, 2 * rows)
            for j in range(3):
                total = jnp.dot(buf[s, here], weight[j], preferred_element_type=f32)
                if j == 0:
                    total = (total + bias[0:1]) * HD ** (-0.5)
                if j == 2:
                    total = total + bias[1:2]
                heads[j, s, here] = total.astype(bf16)

        return carry

    lax.fori_loop(0, ring.units() + 2, step, 0)
    ring.finish()

    def close(i, carry):
        keep(i // at.chips, lax.rem(i, at.chips)).wait()
        return carry

    lax.fori_loop(0, seqs * at.chips, close, 0)


def whole(count):
    return [pl.BlockSpec(memory_space=VMEM)] * count


def gather_project(n, tokens, gain, shift, weight, bias):
    seqs, rows, width = tokens.shape
    part = weight.shape[2]
    return pl.pallas_call(
        functools.partial(gather_project_kernel, n),
        out_shape=(
            jax.ShapeDtypeStruct((seqs, n * rows, width), bf16),
            jax.ShapeDtypeStruct((3, seqs, n * rows, part), bf16),
        ),
        in_specs=whole(5),
        out_specs=(pl.BlockSpec(memory_space=pl.ANY), pl.BlockSpec(memory_space=VMEM)),
        scratch_shapes=[VMEM((seqs, n * rows, width), bf16)]
        + Gather.scratch(n, seqs)
        + [DMA((seqs, n // 2))],
        compiler_params=pltpu.CompilerParams(
            collective_id=0, has_side_effects=True, vmem_limit_bytes=40 * 2**20
        ),
        name="gather_project",
    )(tokens, gain, shift, weight, bias)


def project_scatter_kernel(
    n, mixed, weight, tokens, bias, gain, shift, hidden, normed, *scratch
):
    at = Place(n)
    seqs, rows, width = tokens.shape
    line = Scatter(at, rows, *scratch)
    at.greet()

    def final(s, there, total):
        values = tokens[s, there].astype(f32) + total + bias[...]
        hidden[s, there] = values
        normed[s, there] = norm_rows(values, gain[...], shift[...]).astype(bf16)

    def step(u, carry):
        s, o, there = line.unit(u)

        @pl.when(there)
        def _():
            here = rows_of(o, 2 * rows)
            for j in range(width // 512):
                cols = pl.ds(j * 512, 512)
                total = jnp.dot(mixed[s, here], weight[:, cols], preferred_element_type=f32)
                line.part[s, o, :, cols] = total.astype(bf16)
            line.share(s, o)

        line.pass_on(u - 2, final)
        return carry

    lax.fori_loop(0, line.units() + 2, step, 0)
    line.finish()


def project_scatter(n, mixed, weight, tokens, bias, gain, shift):
    seqs, rows, width = tokens.shape
    return pl.pallas_call(
        functools.partial(project_scatter_kernel, n),
        out_shape=(
            jax.ShapeDtypeStruct((seqs, rows, width), f32),
            jax.ShapeDtypeStruct((seqs, rows, width), bf16),
        ),
        in_specs=whole(6),
        out_specs=tuple(whole(2)),
        scratch_shapes=Scatter.scratch(n, seqs, rows, width),
        compiler_params=pltpu.CompilerParams(
            collective_id=1, has_side_effects=True, vmem_limit_bytes=40 * 2**20
        ),
        name="project_scatter",
    )(mixed, weight, tokens, bias, gain, shift)


def heads_scatter_kernel(
    n,
    query,
    key,
    value,
    weight,
    gathered,
    out_part,
    tokens,
    gain,
    hidden_grad,
    bias_part,
    grad,
    sums_all,
    weight_grad,
    out_grad,
    bias_grad,
    *scratch,
):
    at = Place(n)
    seqs, rows, width = hidden_grad.shape
    line = Scatter(at, rows, *scratch[:7])
    weight_sum = GroupSum(at, width, *scratch[7:12], weight_grad)
    out_sum = GroupSum(at, out_part.shape[0], *scratch[12:17], out_grad, turn=1)
    small = SmallSum(at, *scratch[17:21], True)
    small_bias = SmallSum(at, *scratch[21:25], False)
    out_sum.tiles[0] = out_part[...]
    small.rows[0] = jnp.zeros(small.rows.shape[1:], f32)
    small_bias.rows[0] = bias_part[...]
    at.greet(groups=True, cube=True)

    def final(s, there, total):
        back, terms = norm_rows_back(tokens[s, there].astype(f32), total, gain[...])
        grad[s, there] = hidden_grad[s, there] + back
        small.rows[0, 0:1] += jnp.sum(terms, axis=0, keepdims=True)
        small.rows[0, 1:2] += jnp.sum(total, axis=0, keepdims=True)

    parts = ((query, HD ** (-0.5)), (key, 1.0), (value, 1.0))

    def weight_tile(j):
        for first in range(0, width, 512):
            total = 0.0
            for s in range(seqs):
                total += lax.dot_general(
                    gathered[s, :, pl.ds(first, 512)],
                    parts[j][0][s],
                    TN,
                    preferred_element_type=f32,
                )
            weight_sum.tiles[j, pl.ds(first, 512)] = (parts[j][1] * total).astype(bf16)

    def step(u, carry):
        s, o, there = line.unit(u)

        @pl.when(there)
        def _():
            here = rows_of(o, 2 * rows)
            for j in range(width // 512):
                cols = pl.ds(j * 512, 512)
                total = 0.0
                for i in range(3):
                    total += parts[i][1] * lax.dot_general(
                        parts[i][0][s, here], weight[i, cols], NT, preferred_element_type=f32
                    )
                line.part[s, o, :, cols] = total.astype(bf16)
            line.share(s, o)

        line.pass_on(u - 2, final)
        for j in range(3):
            pl.when(u == j)(functools.partial(weight_tile, j))
        pl.when(u < weight_sum.events())(lambda: weight_sum.event(u))
        pl.when(lax.rem(u, 3) == 0)(lambda: out_sum.event(u // 3))
        small_bias.event(u)
        return carry

    count = max(line.units() + 2, weight_sum.events(), 3 * out_sum.events())
    lax.fori_loop(0, count, step, 0)
    for e in range(small.phases + 1):
        small.event(e)
    sums_all[...] = small.rows[small.phases]
    bias_grad[...] = small_bias.rows[small_bias.phases]
    line.finish()
    weight_sum.finish()
    out_sum.finish()
    small.finish()
    small_bias.finish()


def heads_scatter(
    n, query, key, value, weight, gathered, out_part, tokens, gain, hidden_grad, bias_part
):
    seqs, slots, part = query.shape
    width = weight.shape[1]
    rows = slots // n
    dp = lax.axis_size("dp")
    vmem = pl.BlockSpec(memory_space=VMEM)
    hbm = pl.BlockSpec(memory_space=pl.ANY)
    return pl.pallas_call(
        functools.partial(heads_scatter_kernel, n),
        out_shape=(
            jax.ShapeDtypeStruct((seqs, rows, width), f32),
            jax.ShapeDtypeStruct((2, width), f32),
            jax.ShapeDtypeStruct((3, width, part), bf16),
            jax.ShapeDtypeStruct((1, part, width), bf16),
            jax.ShapeDtypeStruct((2, part), f32),
        ),
        in_specs=whole(10),
        out_specs=(vmem, vmem, hbm, hbm, vmem),
        scratch_shapes=Scatter.scratch(n, seqs, rows, width)
        + GroupSum.scratch(dp, 3, width, part)
        + GroupSum.scratch(dp, 1, part, width)
        + SmallSum.scratch(dp, n, 2, width, True)
        + SmallSum.scratch(dp, n, 2, part, False),
        compiler_params=pltpu.CompilerParams(
            collective_id=2, has_side_effects=True, vmem_limit_bytes=62 * 2**20
        ),
        name="heads_scatter",
    )(query, key, value, weight, gathered, out_part, tokens, gain, hidden_grad, bias_part)


def normal_cdf(values):
    x = jnp.clip(values * 0.7071067811865476, -3.832506856900711, 3.832506856900711)
    x2 = x * x
    top = 0.00022905065861350646
    for c in (0.0034082910107109506, 0.050955695062380861, 0.18520832239976145, 1.128379143519084):
        top = top * x2 + c
    low = -1.1791602954361697e-7
    for c in (
        0.000023547966471313185,
        0.0010179625278914885,
        0.014070470171167667,
        0.11098505178285362,
        0.49746925110067538,
        1.0,
    ):
        low = low * x2 + c
    return 0.5 + 0.5 * (x * top / low)


def mlp_kernel(
    n,
    normed,
    grad_all,
    up_weight,
    up_bias,
    down_weight,
    hidden,
    gain,
    mlp_part,
    hidden_grad,
    grad_low,
    sums,
    up_grad,
    up_bias_grad,
    down_grad,
    up_box,
    down_box,
    buf,
    send,
    recv,
    *scratch,
):
    at = Place(n)
    seqs, rows, width = normed.shape
    units_wide = up_weight.shape[1]
    line = Scatter(at, rows, *scratch[:7])
    act, pre, out_stage, out_sem, up_stage, down_stage, tile_sem, half_send, half_recv = scratch[7:]
    ring = Gather(at, rows, buf, send, recv)
    at.greet(groups=True)
    for s in range(seqs):
        buf[s, rows_of(at.me, rows)] = normed[s]
    ring.start(0)
    up_bias_grad[...] = jnp.zeros_like(up_bias_grad)
    sums[...] = jnp.zeros_like(sums)
    ft = min(512, units_wide)

    def out_copy(s, o):
        return pltpu.make_async_copy(
            out_stage, mlp_part.at[s, rows_of(o, 2 * rows)], out_sem.at[0]
        )

    def work(s, o, first):
        ring.arrived(s, o, 1 - at.core)
        here = rows_of(o, 2 * rows)
        for j in range(units_wide // ft):
            cols = pl.ds(j * ft, ft)
            value = jnp.dot(buf[s, here], up_weight[:, cols], preferred_element_type=f32)
            value = value + up_bias[:, cols]
            spread = normal_cdf(value)
            act[s, here, cols] = (value * spread).astype(bf16)
            slope = spread + value * (0.3989422804014327 * jnp.exp(-0.5 * value * value))
            grad = lax.dot_general(
                grad_all[s, here], down_weight[cols], NT, preferred_element_type=f32
            )
            grad = (grad * slope).astype(bf16)
            pre[s, here, cols] = grad
            up_bias_grad[:, cols] += jnp.sum(grad.astype(f32), axis=0, keepdims=True)
        for j in range(width // 512):
            cols = pl.ds(j * 512, 512)
            line.part[s, o, :, cols] = lax.dot_general(
                pre[s, here], up_weight[cols], NT, preferred_element_type=f32
            ).astype(bf16)
        line.share(s, o)
        pl.when(jnp.logical_not(first))(lambda: out_copy(s, o).wait())
        for j in range(width // 512):
            cols = pl.ds(j * 512, 512)
            out_stage[:, cols] = jnp.dot(
                act[s, here], down_weight[:, cols], preferred_element_type=f32
            ).astype(bf16)
        out_copy(s, o).start()

    def final(s, there, total):
        back, terms = norm_rows_back(hidden[s, there], total, gain[...])
        first = pl.multiple_of(at.me * rows + there.start, 16)
        grad_out = grad_all[s, pl.ds(first, there.size)].astype(f32)
        grad = grad_out + back
        hidden_grad[s, there] = grad
        grad_low[s, there] = grad.astype(bf16)
        add_row(sums, 0, terms)
        add_row(sums, 1, total)
        add_row(sums, 2, grad)
        add_row(sums, 3, grad_out)

    kinds = ((down_stage, down_grad, down_box, 0), (up_stage, up_grad, up_box, 1))

    def tile_copy(kind, t):
        stage, grad, box, turn = kinds[kind]
        return pltpu.make_async_copy(stage, grad.at[t], tile_sem.at[kind])

    def tile_half(kind, t):
        stage, grad, box, turn = kinds[kind]
        half = box.shape[1]
        which = (t + turn) % at.group_bits
        peer, mine = at.group_peer(which)
        return pltpu.make_async_remote_copy(
            src_ref=grad.at[t, rows_of(1 - mine, half)],
            dst_ref=box.at[t],
            send_sem=half_send.at[kind, t],
            recv_sem=half_recv.at[kind, t],
            device_id={"dp": peer},
            device_id_type=MESH,
        )

    def tile_sent(kind, t):
        tile_copy(kind, t).wait()
        tile_half(kind, t).start()

    order = [(i % 2, i // 2) for i in range(8)]

    def weight_tile(i):
        for j, (kind, t) in enumerate(order):
            @pl.when(i == j)
            def _():
                stage = kinds[kind][0]
                cols = pl.ds(t * stage.shape[0], stage.shape[0])
                total = 0.0
                for s in range(seqs):
                    if kind == 0:
                        left, right = act[s, :, cols], grad_all[s]
                    else:
                        left, right = buf[s, :, cols], pre[s]
                    total += lax.dot_general(left, right, TN, preferred_element_type=f32)
                if j >= 1:
                    tile_sent(*order[j - 1])
                stage[...] = total.astype(bf16)
                tile_copy(kind, t).start()

        pl.when(i == 8)(lambda: tile_sent(*order[7]))

    lag = ring.units() // seqs + 2

    def step(u, carry):
        ring.forward(u)
        line.pass_on(u - lag, final)
        s, o, there, own = ring.unit(u - 1)
        pl.when(there)(lambda: work(s, o, u == 1))
        weight_tile(u - ring.units() - 1)
        return carry

    count = max(line.units() + lag, ring.units() + 2 + len(order))
    lax.fori_loop(0, count, step, 0)
    ring.finish()
    line.finish()
    for kind, t in order:
        tile_half(kind, t).wait()
    out_copy(0, 0).wait()


def mlp_block(n, normed, grad_all, up_weight, up_bias, down_weight, hidden, gain):
    seqs, rows, width = normed.shape
    slots = n * rows
    units = up_weight.shape[1]
    hbm = pl.BlockSpec(memory_space=pl.ANY)
    vmem = pl.BlockSpec(memory_space=VMEM)
    down_size, up_size = units // 4, width // 4
    return pl.pallas_call(
        functools.partial(mlp_kernel, n),
        out_shape=(
            jax.ShapeDtypeStruct((seqs, slots, width), bf16),
            jax.ShapeDtypeStruct((seqs, rows, width), f32),
            jax.ShapeDtypeStruct((seqs, rows, width), bf16),
            jax.ShapeDtypeStruct((4, width), f32),
            jax.ShapeDtypeStruct((4, up_size, units), bf16),
            jax.ShapeDtypeStruct((1, units), f32),
            jax.ShapeDtypeStruct((4, down_size, width), bf16),
            jax.ShapeDtypeStruct((4, up_size // 2, units), bf16),
            jax.ShapeDtypeStruct((4, down_size // 2, width), bf16),
        ),
        in_specs=whole(7),
        out_specs=(hbm, vmem, vmem, vmem, hbm, vmem, hbm, hbm, hbm),
        scratch_shapes=[VMEM((seqs, slots, width), bf16)]
        + Gather.scratch(n, seqs)
        + Scatter.scratch(n, seqs, rows, width)
        + [
            VMEM((seqs, slots, units), bf16),
            VMEM((seqs, slots, units), bf16),
            VMEM((2 * rows, width), bf16),
            DMA((1,)),
            VMEM((up_size, units), bf16),
            VMEM((down_size, width), bf16),
            DMA((2,)),
            DMA((2, 4)),
            DMA((2, 4)),
        ],
        compiler_params=pltpu.CompilerParams(
            collective_id=3, has_side_effects=True, vmem_limit_bytes=62 * 2**20
        ),
        name="mlp_block",
    )(normed, grad_all, up_weight, up_bias, down_weight, hidden, gain)


def attn_grad_kernel(
    n,
    grad,
    mlp_part,
    hidden,
    bias,
    weight,
    mixed,
    sums,
    up_bias_part,
    up_part,
    down_part,
    up_box,
    down_box,
    output,
    grad_heads,
    weight_grad,
    sums_all,
    up_bias_grad,
    up_grad,
    down_grad,
    buf,
    send,
    recv,
    *scratch,
):
    at = Place(n)
    seqs, rows, width = grad.shape
    line = Scatter(at, rows, *scratch[:7])
    load_sem, tile_sem, box_sem = scratch[7:10]
    ring = Gather(at, rows, buf, send, recv)
    up_sum = GroupSum(at, up_part.shape[1], *scratch[10:15], up_grad, turn=1, skip=1)
    down_sum = GroupSum(at, down_part.shape[1], *scratch[15:20], down_grad, skip=1)
    small = SmallSum(at, *scratch[20:24], True)
    small_bias = SmallSum(at, *scratch[24:28], False)
    pairs = ((up_sum, up_part, up_box), (down_sum, down_part, down_box))

    def tile_load(i, t):
        group, part, box = pairs[i]
        half = box.shape[1]
        return (
            pltpu.make_async_copy(
                part.at[t, group.span(group.base(t, 1), half)], group.tiles.at[t], tile_sem.at[i, t]
            ),
            pltpu.make_async_copy(box.at[t], group.box(t, 0), box_sem.at[i, t]),
        )

    def tile_loaded(i, t):
        for copy in tile_load(i, t):
            copy.wait()

    for t in range(4):
        for i in range(2):
            for copy in tile_load(i, t):
                copy.start()
    small.rows[0] = sums[...]
    small_bias.rows[0] = up_bias_part[...]

    def load(s, o):
        return pltpu.make_async_copy(
            mlp_part.at[s, rows_of(o, 2 * rows)], line.part.at[s, o], load_sem.at[s, o]
        )

    def load_unit(u, carry):
        s, o, there = line.unit(u)
        pl.when(there)(lambda: load(s, o).start())
        return carry

    lax.fori_loop(0, line.units(), load_unit, 0)
    at.greet(groups=True, cube=True)
    for s in range(seqs):
        buf[s, rows_of(at.me, rows)] = grad[s]
    ring.start(0)

    def final(s, there, total):
        output[s, there] = (hidden[s, there] + total + bias[...]).astype(bf16)

    def step(u, carry):
        ring.forward(u)
        s, o, there = line.unit(u)

        @pl.when(there)
        def _():
            load(s, o).wait()
            line.share(s, o)

        line.pass_on(u - 1, final)
        s, o, there, own = ring.unit(u - 1)

        @pl.when(there)
        def _():
            ring.arrived(s, o, 1 - at.core)
            here = rows_of(o, 2 * rows)
            grad_heads[s, here] = lax.dot_general(
                buf[s, here], weight[...], NT, preferred_element_type=f32
            ).astype(bf16)

        for i in range(2):
            group = pairs[i][0]
            pl.when(u < group.events())(
                functools.partial(group.event, u, functools.partial(tile_loaded, i))
            )
        small.event(u)
        small_bias.event(u)
        return carry

    count = max(line.units() + 1, ring.units() + 1, up_sum.events(), down_sum.events())
    lax.fori_loop(0, count, step, 0)
    sums_all[...] = small.rows[small.phases]
    up_bias_grad[...] = small_bias.rows[small_bias.phases]
    for j in range(width // 512):
        cols = pl.ds(j * 512, 512)
        total = 0.0
        for s in range(seqs):
            total += lax.dot_general(mixed[s], buf[s, :, cols], TN, preferred_element_type=f32)
        weight_grad[:, cols] = total.astype(bf16)
    ring.finish()
    line.finish()
    small.finish()
    small_bias.finish()
    up_sum.finish()
    down_sum.finish()


def attn_grad(
    n,
    grad,
    mlp_part,
    hidden,
    bias,
    weight,
    mixed,
    sums,
    up_bias_part,
    up_part,
    down_part,
    up_box,
    down_box,
):
    seqs, rows, width = grad.shape
    slots = n * rows
    part = weight.shape[0]
    units = up_part.shape[2]
    dp = lax.axis_size("dp")
    vmem = pl.BlockSpec(memory_space=VMEM)
    hbm = pl.BlockSpec(memory_space=pl.ANY)
    return pl.pallas_call(
        functools.partial(attn_grad_kernel, n),
        out_shape=(
            jax.ShapeDtypeStruct((seqs, rows, width), bf16),
            jax.ShapeDtypeStruct((seqs, slots, part), bf16),
            jax.ShapeDtypeStruct((part, width), bf16),
            jax.ShapeDtypeStruct(sums.shape, f32),
            jax.ShapeDtypeStruct((1, units), f32),
            jax.ShapeDtypeStruct(up_part.shape, bf16),
            jax.ShapeDtypeStruct(down_part.shape, bf16),
        ),
        in_specs=[vmem, hbm] + [vmem] * 6 + [hbm] * 4,
        out_specs=(vmem,) * 5 + (hbm, hbm),
        scratch_shapes=[VMEM((seqs, slots, width), bf16)]
        + Gather.scratch(n, seqs)
        + Scatter.scratch(n, seqs, rows, width)
        + [DMA((seqs, n // 2)), DMA((2, 4)), DMA((2, 4))]
        + GroupSum.scratch(dp, 4, width // 4, units, 1)
        + GroupSum.scratch(dp, 4, units // 4, width, 1)
        + SmallSum.scratch(dp, n, sums.shape[0], width, True)
        + SmallSum.scratch(dp, n, 1, units, False),
        compiler_params=pltpu.CompilerParams(
            collective_id=4, has_side_effects=True, vmem_limit_bytes=62 * 2**20
        ),
        name="attn_grad",
    )(
        grad,
        mlp_part,
        hidden,
        bias,
        weight,
        mixed,
        sums,
        up_bias_part,
        up_part,
        down_part,
        up_box,
        down_box,
    )


def body(
    tokens,
    cotangent,
    lengths,
    ln1_gain,
    ln1_shift,
    qkv_weight,
    qkv_bias,
    out_weight,
    out_bias,
    ln2_gain,
    ln2_shift,
    up_weight,
    up_bias,
    down_weight,
    down_bias,
):
    seq_count, local_rows, model_width = tokens.shape
    part_width = qkv_weight.shape[2]
    head_count = part_width // HD
    score_scale = HD ** (-0.5)
    n = lax.axis_size("tensor")
    gathered_one, heads = gather_project(
        n, tokens, ln1_gain[None], ln1_shift[None], qkv_weight, qkv_bias
    )
    slot_count = gathered_one.shape[1]
    head_shape = (seq_count, slot_count, head_count, HD)
    query_rows, key_rows, value_rows = [heads[j].reshape(head_shape) for j in range(3)]
    attended, log_totals = lax.map(
        lambda item: attend_forward(item[0], item[1], item[2], item[3]),
        (query_rows, key_rows, value_rows, lengths),
    )
    mixed_heads = attended.reshape(seq_count, slot_count, part_width).astype(jnp.bfloat16)
    hidden_state, normed_two = project_scatter(
        n, mixed_heads, out_weight, tokens, out_bias[None], ln2_gain[None], ln2_shift[None]
    )
    slot_ids = lax.axis_index("tensor") * local_rows + lax.broadcasted_iota(
        jnp.int32, (seq_count, local_rows), 1
    )
    valid_rows = (slot_ids < lengths[:, None]).astype(jnp.float32)
    grad_out = cotangent.astype(jnp.float32) * valid_rows[:, :, None]
    grad_low, heads = lax.optimization_barrier((grad_out.astype(jnp.bfloat16), heads))
    grad_mlp = lax.all_gather(grad_low, "tensor", axis=1, tiled=True)
    (
        mlp_part,
        hidden_grad,
        grad_attn,
        sums,
        up_part,
        up_bias_part,
        down_part,
        up_box,
        down_box,
    ) = mlp_block(
        n, normed_two, grad_mlp, up_weight, up_bias[None], down_weight, hidden_state, ln2_gain[None]
    )
    output, grad_heads, out_part, sums, up_bias_grad, up_weight_grad, down_weight_grad = attn_grad(
        n,
        grad_attn,
        mlp_part,
        hidden_state,
        down_bias[None],
        out_weight,
        mixed_heads,
        sums,
        up_bias_part,
        up_part,
        down_part,
        up_box,
        down_box,
    )
    ln2_gain_grad, ln2_shift_grad, out_bias_grad, down_bias_grad = [sums[i] for i in range(4)]
    up_bias_grad = up_bias_grad[0]
    up_weight_grad = up_weight_grad.astype(jnp.float32).reshape(up_weight.shape)
    down_weight_grad = down_weight_grad.astype(jnp.float32).reshape(down_weight.shape)
    grad_heads = grad_heads.reshape(head_shape)
    grad_query, grad_key, grad_value = lax.map(
        lambda item: attend_backward(item[0], item[1], item[2], item[3], item[4], item[5]),
        (query_rows, key_rows, value_rows, grad_heads, log_totals, lengths),
    )
    flat_shape = (seq_count, slot_count, part_width)
    grad_query = grad_query.reshape(flat_shape).astype(jnp.bfloat16)
    grad_key = grad_key.reshape(flat_shape).astype(jnp.bfloat16)
    grad_value = grad_value.reshape(flat_shape).astype(jnp.bfloat16)
    qkv_bias_grad = jnp.stack(
        [
            score_scale * jnp.sum(grad_query.astype(jnp.float32), axis=(0, 1)),
            jnp.sum(grad_value.astype(jnp.float32), axis=(0, 1)),
        ]
    )
    input_grad, sums_one, qkv_weight_grad, out_weight_grad, qkv_bias_grad = heads_scatter(
        n,
        grad_query,
        grad_key,
        grad_value,
        qkv_weight,
        gathered_one,
        out_part,
        tokens,
        ln1_gain[None],
        hidden_grad,
        qkv_bias_grad,
    )
    ln1_gain_grad, ln1_shift_grad = sums_one[0], sums_one[1]
    qkv_weight_grad = qkv_weight_grad.astype(jnp.float32)
    out_weight_grad = out_weight_grad[0].astype(jnp.float32)
    return (
        output,
        input_grad,
        ln1_gain_grad,
        ln1_shift_grad,
        qkv_weight_grad,
        qkv_bias_grad,
        out_weight_grad,
        out_bias_grad,
        ln2_gain_grad,
        ln2_shift_grad,
        up_weight_grad,
        up_bias_grad,
        down_weight_grad,
        down_bias_grad,
    )


def solution(mesh):
    in_specs = (
        P("dp", "tensor", None),
        P("dp", "tensor", None),
        P("dp"),
        P(),
        P(),
        P(None, None, "tensor"),
        P(None, "tensor"),
        P("tensor", None),
        P(),
        P(),
        P(),
        P(None, "tensor"),
        P("tensor"),
        P("tensor", None),
        P(),
    )
    out_specs = (
        P("dp", "tensor", None),
        P("dp", "tensor", None),
        P(),
        P(),
        P(None, None, "tensor"),
        P(None, "tensor"),
        P("tensor", None),
        P(),
        P(),
        P(),
        P(None, "tensor"),
        P("tensor"),
        P("tensor", None),
        P(),
    )
    return jax.shard_map(body, mesh=mesh, in_specs=in_specs, out_specs=out_specs, check_vma=False)
```

```python
import functools
import heapq

import jax
import jax.numpy as jnp
from jax import lax
from jax.experimental import pallas as pl
from jax.experimental.pallas import tpu as pltpu
from jax.sharding import PartitionSpec as P

HD = 128


norm_epsilon = 1e-05
block_rows = 512


def layer_norm(values, norm_gain, norm_shift):
    centre = values - jnp.mean(values, axis=-1, keepdims=True)
    spread = jnp.mean(centre * centre, axis=-1, keepdims=True)
    return centre * lax.rsqrt(spread + norm_epsilon) * norm_gain + norm_shift


def gelu_exact(values):
    return jax.nn.gelu(values, approximate=False)


def flat_product(left_rows, right_rows):
    flat = left_rows.reshape(-1, left_rows.shape[-1])
    result = jnp.dot(flat, right_rows, preferred_element_type=jnp.float32)
    return result.reshape(left_rows.shape[:-1] + (right_rows.shape[-1],))


def product_back(left_rows, right_rows):
    flat = left_rows.reshape(-1, left_rows.shape[-1])
    result = lax.dot_general(
        flat, right_rows, (((1,), (1,)), ((), ())), preferred_element_type=jnp.float32
    )
    return result.reshape(left_rows.shape[:-1] + (right_rows.shape[0],))


def rows_product(left_rows, right_rows):
    left_flat = left_rows.reshape(-1, left_rows.shape[-1])
    right_flat = right_rows.reshape(-1, right_rows.shape[-1])
    return lax.dot_general(
        left_flat, right_flat, (((0,), (0,)), ((), ())), preferred_element_type=jnp.float32
    )


def sum_groups(parts):
    parts = [part.astype(jnp.bfloat16) for part in parts]
    return [total.astype(jnp.float32) for total in lax.psum(parts, "dp")]


def allowed_mask(first_row, row_count, slot_count, length):
    row_ids = first_row + lax.broadcasted_iota(jnp.int32, (row_count, slot_count), 0)
    col_ids = lax.broadcasted_iota(jnp.int32, (row_count, slot_count), 1)
    return (col_ids <= row_ids) & (col_ids < length)


def block_scores(query_block, key_rows, first_row, length):
    scores = jnp.einsum("qhd,khd->hqk", query_block, key_rows, preferred_element_type=jnp.float32)
    allowed = allowed_mask(first_row, query_block.shape[0], key_rows.shape[0], length)
    return jnp.where(allowed[None], scores, -1e30)


def attend_forward(query_rows, key_rows, value_rows, length):
    slot_count = query_rows.shape[0]
    step_rows = min(block_rows, slot_count)
    outputs = []
    totals = []
    for block_index in range(slot_count // step_rows):
        first_row = block_index * step_rows
        query_block = query_rows[first_row : first_row + step_rows]
        scores = block_scores(query_block, key_rows, first_row, length)
        row_peak = jnp.max(scores, axis=-1, keepdims=True)
        log_total = row_peak + jnp.log(jnp.sum(jnp.exp(scores - row_peak), axis=-1, keepdims=True))
        weights = jnp.exp(scores - log_total).astype(jnp.bfloat16)
        outputs.append(
            jnp.einsum("hqk,khd->qhd", weights, value_rows, preferred_element_type=jnp.float32)
        )
        totals.append(log_total)
    return (jnp.concatenate(outputs, axis=0), jnp.concatenate(totals, axis=1))


def attend_backward(query_rows, key_rows, value_rows, grad_rows, log_totals, length):
    slot_count = query_rows.shape[0]
    step_rows = min(block_rows, slot_count)
    grad_keys = jnp.zeros(key_rows.shape, jnp.float32)
    grad_values = jnp.zeros(value_rows.shape, jnp.float32)
    grad_queries = []
    for block_index in range(slot_count // step_rows):
        first_row = block_index * step_rows
        query_block = query_rows[first_row : first_row + step_rows]
        grad_block = grad_rows[first_row : first_row + step_rows]
        scores = block_scores(query_block, key_rows, first_row, length)
        probs = jnp.exp(scores - log_totals[:, first_row : first_row + step_rows])
        grad_probs = jnp.einsum(
            "qhd,khd->hqk", grad_block, value_rows, preferred_element_type=jnp.float32
        )
        centre = jnp.sum(probs * grad_probs, axis=-1, keepdims=True)
        grad_scores = (probs * (grad_probs - centre)).astype(jnp.bfloat16)
        grad_queries.append(
            jnp.einsum("hqk,khd->qhd", grad_scores, key_rows, preferred_element_type=jnp.float32)
        )
        grad_keys = grad_keys + jnp.einsum(
            "hqk,qhd->khd", grad_scores, query_block, preferred_element_type=jnp.float32
        )
        grad_values = grad_values + jnp.einsum(
            "hqk,qhd->khd",
            probs.astype(jnp.bfloat16),
            grad_block,
            preferred_element_type=jnp.float32,
        )
    return (jnp.concatenate(grad_queries, axis=0), grad_keys, grad_values)


MESH = pl.DeviceIdType.MESH
UP, DOWN, SIDE = 0, 1, 2
VMEM = pltpu.VMEM
DMA = pltpu.SemaphoreType.DMA
f32 = jnp.float32
bf16 = jnp.bfloat16
NT = (((1,), (1,)), ((), ()))
TN = (((0,), (0,)), ((), ()))


def order_of(chips, ops_of, backlog=8.0, hop=1.5):
    todo = [sorted(ops_of(c)) for c in range(chips)]
    order = [[] for _ in range(chips)]
    free, busy, have, queue = {}, [False] * chips, set(), []

    def push(time, what):
        heapq.heappush(queue, (time, len(pushed), what))
        pushed.append(0)

    pushed = []
    for c in range(chips):
        push(0.0, (c, None, ()))
    now = 0.0
    while queue:
        now, _, (c, signal, after) = heapq.heappop(queue)
        if signal is not None:
            have.add(signal)
        for part in after:
            if part[0] == "free":
                busy[c] = False
            elif part[0] == "send":
                _, link, to, sig, span = part
                start = max(now, free.get((c, link), 0.0))
                free[c, link] = start + span
                push(start + span + hop, (to, sig, ()))
            else:
                push(now + part[1], (c, part[2], ()))
        if busy[c]:
            continue
        for op in todo[c]:
            rank, code, needs, time, sends, gives = op
            if any(need not in have for need in needs):
                continue
            late = max([free.get((c, send[0]), 0.0) - now for send in sends], default=0.0)
            if late > backlog:
                push(now + late - backlog, (c, None, ()))
                continue
            todo[c].remove(op)
            order[c].append(code)
            busy[c] = True
            ends = [("free",)] + [("send",) + send for send in sends]
            push(now + time, (c, None, ends + [("give",) + give for give in gives]))
            break
    assert not any(todo)
    return order, now


PIECE = 12.0


def gather_ops(c, chips, seqs, kind, name, rank=0, time=0.5):
    ops = []
    for s in range(seqs):
        for o in range(chips):
            sends = []
            if o <= c < chips - 1:
                sends.append((c + 1, c + 1, (name, c + 1, s, o), PIECE))
            if o >= c > 0:
                sends.append((c - 1, c - 1, (name, c - 1, s, o), PIECE))
            needs = [] if o == c else [(name, c, s, o)]
            both = [(3.0, (name, c, s, o, "both"))]
            ops.append(((rank, s, abs(o - c)), (kind, s, o), needs, time, sends, both))
    return ops


def scatter_ops(c, chips, seqs, kind, name, part, rank=1, time=1.3, last=2.0):
    ops = []
    for s in range(seqs):
        for o in range(chips):
            needs = [(part, c, s, o)]
            if o >= c > 0:
                needs.append((name, c, s, o, "below"))
            if o <= c < chips - 1:
                needs.append((name, c, s, o, "above"))
            sends = []
            if o > c:
                sends = [(c + 1, c + 1, (name, c + 1, s, o, "below"), PIECE)]
            if o < c:
                sends = [(c - 1, c - 1, (name, c - 1, s, o, "above"), PIECE)]
            order = (rank, s, -abs(o - c)) if o != c else (8, s, 0)
            ops.append((order, (kind, s, o), needs, last if o == c else time, sends, []))
    return ops


def work_ops(c, chips, seqs, kind, needs_of, gives, time, rank=2, far=False):
    return [
        (
            (rank, s, -abs(o - c) if far else abs(o - c)),
            (kind, s, o),
            needs_of(s, o),
            time,
            [],
            [(3.0, (gives, c, s, o))],
        )
        for s in range(seqs)
        for o in range(chips)
    ]


def group_ops(c, bits, count, span, code_of, skip, turn, first_time, rank=3, name="group"):
    ops = []
    for t in range(count):
        for stage in range(skip, 2 * bits + 1):
            needs = []
            if stage > skip:
                needs = [(name, c, t, stage)]
            sends = []
            if stage < 2 * bits:
                i = stage if stage < bits else 2 * bits - 1 - stage
                axis = "axis%d" % ((t + turn + i) % bits)
                sends = [(axis, c, (name, c, t, stage + 1), span / 2**i)]
            time = first_time if stage == 0 else 0.7
            code = code_of((stage - skip) * count + t)
            ops.append(((rank, stage, t), code, needs, time, sends, []))
    return ops


class Plan:
    def __init__(self, at, seqs, ops_of):
        chips = at.chips
        order, self.length = order_of(chips, ops_of)
        self.per, self.chips, self.seqs = 128, chips, seqs
        self.count = max(len(codes) for codes in order)
        assert 8 * seqs * chips <= self.per
        rows = []
        for codes in order:
            flat = [(kind * seqs + s) * chips + o for kind, s, o in codes]
            flat += [7 * seqs * chips] * (self.count - len(flat) + 4)
            rows.append(
                [sum(flat[i + j] * self.per**j for j in range(4)) for i in range(0, self.count, 4)]
            )
        self.words = []
        for w in range(len(rows[0])):
            word = jnp.int32(rows[0][w])
            for c in range(1, chips):
                word = jnp.where(at.chip == c, jnp.int32(rows[c][w]), word)
            self.words.append(word)

    def step(self, k):
        which, slot = k // 4, lax.rem(k, 4)
        word = jnp.int32(0)
        for w, value in enumerate(self.words):
            word = jnp.where(which == w, value, word)
        code = word
        for j in range(1, 4):
            code = jnp.where(slot == j, word // self.per**j, code)
        code = lax.rem(code, self.per)
        each = self.seqs * self.chips
        return code // each, lax.rem(code, each) // self.chips, lax.rem(code, self.chips)

    def run(self, actions, beside=None):
        def step(k, carry):
            kind, s, o = self.step(k)
            for which, action in actions.items():
                pl.when(kind == which)(functools.partial(action, s, o))
            if beside is not None:
                beside(k)
            return carry

        lax.fori_loop(0, self.count, step, 0)


class Place:
    def __init__(self, n):
        self.n, self.chips = n, n // 2
        self.me = lax.axis_index("tensor")
        self.chip, self.core = self.me // 2, lax.rem(self.me, 2)
        self.side = self.me + 1 - 2 * self.core
        self.below = self.chip > 0
        self.above = self.chip < self.chips - 1
        self.group = lax.axis_index("dp")
        self.group_bits = lax.axis_size("dp").bit_length() - 1
        self.bits = n.bit_length() - 1

    def group_peer(self, q):
        mine = lax.rem(self.group // 2**q, 2)
        return self.group + (1 - 2 * mine) * 2**q, mine

    def peer(self, q):
        mine = lax.rem(self.me // 2**q, 2)
        return self.me + (1 - 2 * mine) * 2**q

    def greet(self, groups=False, cube=False):
        barrier = pltpu.get_barrier_semaphore()

        def tell(target):
            pl.semaphore_signal(
                barrier, inc=1, device_id={"tensor": target}, device_id_type=MESH
            )

        tell(self.side)
        pl.when(self.below)(lambda: tell(self.me - 2))
        pl.when(self.above)(lambda: tell(self.me + 2))
        peers = 1 + self.below.astype(jnp.int32) + self.above.astype(jnp.int32)
        if groups:
            for q in range(self.group_bits):
                pl.semaphore_signal(
                    barrier, inc=1, device_id={"dp": self.group_peer(q)[0]}, device_id_type=MESH
                )
            peers = peers + self.group_bits
        if cube:
            for q in range(self.bits):
                tell(self.peer(q))
            peers = peers + self.bits
        pl.semaphore_wait(barrier, peers)


def rows_of(index, rows):
    return pl.ds(pl.multiple_of(index * rows, rows), rows)


class Gather:
    def __init__(self, at, rows, buf, send, recv):
        self.at, self.rows, self.buf, self.send, self.recv = at, rows, buf, send, recv
        self.seqs = buf.shape[0]

    @staticmethod
    def scratch(n, seqs):
        return [DMA((3, seqs, n // 2)), DMA((seqs, n))]

    def piece(self, s, o, k):
        return self.buf.at[s, rows_of(2 * o + k, self.rows)]

    def copy(self, s, o, kind):
        at = self.at
        target = (at.me + 2, at.me - 2, at.side)[kind]
        piece = self.piece(s, o, at.core)
        return pltpu.make_async_remote_copy(
            src_ref=piece,
            dst_ref=piece,
            send_sem=self.send.at[kind, s, o],
            recv_sem=self.recv.at[s, 2 * o + at.core],
            device_id={"tensor": target},
            device_id_type=MESH,
        )

    def arrived(self, s, o, k):
        at = self.at
        piece = self.piece(s, o, k)
        pltpu.make_async_remote_copy(
            src_ref=piece,
            dst_ref=piece,
            send_sem=self.send.at[SIDE, s, o],
            recv_sem=self.recv.at[s, 2 * o + k],
            device_id={"tensor": at.side},
            device_id_type=MESH,
        ).wait_recv()

    def relay(self, s, o):
        at = self.at
        pl.when(o != at.chip)(lambda: self.arrived(s, o, at.core))
        pl.when((o <= at.chip) & at.above)(lambda: self.copy(s, o, UP).start())
        pl.when((o >= at.chip) & at.below)(lambda: self.copy(s, o, DOWN).start())
        self.copy(s, o, SIDE).start()

    def finish(self):
        at = self.at

        def one(i, carry):
            s, o = i // at.chips, lax.rem(i, at.chips)
            pl.when((o <= at.chip) & at.above)(lambda: self.copy(s, o, UP).wait_send())
            pl.when((o >= at.chip) & at.below)(lambda: self.copy(s, o, DOWN).wait_send())
            self.copy(s, o, SIDE).wait_send()
            return carry

        lax.fori_loop(0, self.seqs * at.chips, one, 0)


class Scatter:
    def __init__(self, at, rows, part, side, link, side_send, side_recv, send, recv):
        self.at, self.rows = at, rows
        self.part, self.side, self.link = part, side, link
        self.side_send, self.side_recv, self.send, self.recv = side_send, side_recv, send, recv
        self.seqs = part.shape[0]

    @staticmethod
    def scratch(n, seqs, rows, width):
        chips = n // 2
        return [
            VMEM((seqs, chips, 2 * rows, width), bf16),
            VMEM((seqs, chips, rows, width), bf16),
            VMEM((seqs, chips + 1, rows, width), bf16),
            DMA((seqs, chips)),
            DMA((seqs, chips)),
            DMA((seqs, chips)),
            DMA((seqs, chips + 1)),
        ]

    def side_copy(self, s, o):
        at = self.at
        return pltpu.make_async_remote_copy(
            src_ref=self.part.at[s, o, rows_of(1 - at.core, self.rows)],
            dst_ref=self.side.at[s, o],
            send_sem=self.side_send.at[s, o],
            recv_sem=self.side_recv.at[s, o],
            device_id={"tensor": at.side},
            device_id_type=MESH,
        )

    def link_copy(self, s, o, slot, target):
        return pltpu.make_async_remote_copy(
            src_ref=self.part.at[s, o, rows_of(self.at.core, self.rows)],
            dst_ref=self.link.at[s, slot],
            send_sem=self.send.at[s, o],
            recv_sem=self.recv.at[s, slot],
            device_id={"tensor": target},
            device_id_type=MESH,
        )

    def share(self, s, o):
        self.side_copy(s, o).start()

    def blocks(self, body):
        step = 16
        lax.fori_loop(0, self.rows // step, lambda i, c: (body(pl.multiple_of(i * step, step), step), c)[1], 0)

    def add_up(self, s, o, slots):
        base = self.at.core * self.rows

        def body(first, step):
            here = pl.ds(pl.multiple_of(base + first, step), step)
            there = pl.ds(first, step)
            total = self.part[s, o, here].astype(f32) + self.side[s, o, there].astype(f32)
            for slot in slots:
                total += self.link[s, slot, there].astype(f32)
            self.part[s, o, here] = total.astype(bf16)

        self.blocks(body)

    def pass_on(self, final, s, o):
        at = self.at
        self.side_copy(s, o).wait_recv()

        @pl.when(o > at.chip)
        def _():
            @pl.when(at.below)
            def _():
                self.link_copy(s, o, o, at.me).wait_recv()
                self.add_up(s, o, [o])

            pl.when(jnp.logical_not(at.below))(lambda: self.add_up(s, o, []))
            self.link_copy(s, o, o, at.me + 2).start()

        @pl.when(o < at.chip)
        def _():
            @pl.when(at.above)
            def _():
                self.link_copy(s, o, o, at.me).wait_recv()
                self.add_up(s, o, [o])

            pl.when(jnp.logical_not(at.above))(lambda: self.add_up(s, o, []))
            slot = jnp.where(o == at.chip - 1, at.chips, o)
            self.link_copy(s, o, slot, at.me - 2).start()

        @pl.when(o == at.chip)
        def _():
            pl.when(at.below)(lambda: self.link_copy(s, o, o, at.me).wait_recv())
            pl.when(at.above)(lambda: self.link_copy(s, o, at.chips, at.me).wait_recv())
            for slot, used in ((o, at.below), (at.chips, at.above)):
                @pl.when(jnp.logical_not(used))
                def _():
                    def clear(first, step):
                        self.link[s, slot, pl.ds(first, step)] = jnp.zeros(
                            (step, self.link.shape[-1]), bf16
                        )

                    self.blocks(clear)
            base = at.core * self.rows

            def body(first, step):
                here = pl.ds(pl.multiple_of(base + first, step), step)
                there = pl.ds(first, step)
                total = self.part[s, o, here].astype(f32) + self.side[s, o, there].astype(f32)
                total += self.link[s, o, there].astype(f32)
                total += self.link[s, at.chips, there].astype(f32)
                final(s, there, total)

            self.blocks(body)

    def finish(self):
        at = self.at

        def one(i, carry):
            s, o = i // at.chips, lax.rem(i, at.chips)
            self.side_copy(s, o).wait_send()
            pl.when(o != at.chip)(lambda: self.link_copy(s, o, o, at.side).wait_send())
            return carry

        lax.fori_loop(0, self.seqs * at.chips, one, 0)


class GroupSum:
    def __init__(self, at, rows, tiles, inbox, send, recv, keep_sem, out, turn=0, skip=0):
        self.at, self.tiles, self.inbox, self.send, self.recv = at, tiles, inbox, send, recv
        self.keep_sem, self.out, self.skip, self.turn, self.rows = keep_sem, out, skip, turn, rows
        self.bits = at.group_bits
        self.count = send.shape[0]

    @staticmethod
    def scratch(dp, count, rows, width, skip=0):
        phases = 2 * (dp.bit_length() - 1)
        return [
            VMEM((count, rows >> skip, width), bf16),
            VMEM((count, rows - rows // dp, width), bf16),
            DMA((count, phases)),
            DMA((count, phases)),
            DMA((count,)),
        ]

    def peer(self, t, i):
        which = lax.rem(t + i + self.turn, self.bits)
        peer, mine = 0, 0
        for q in range(self.bits):
            other, bit = self.at.group_peer(q)
            peer = peer + jnp.where(which == q, other, 0)
            mine = mine + jnp.where(which == q, bit, 0)
        return peer, mine

    def base(self, t, i):
        first = 0
        for p in range(i):
            first = first + self.peer(t, p)[1] * (self.rows >> (p + 1))
        return first

    def span(self, first, size):
        return pl.ds(pl.multiple_of(first, 16), size)

    def tile(self, t, first, size):
        return self.tiles.at[t, self.span(first - self.base(t, self.skip), size)]

    def box(self, t, i):
        return self.inbox.at[t, pl.ds(self.rows - (self.rows >> i), self.rows >> (i + 1))]

    def remote(self, source, target, t, phase, peer):
        return pltpu.make_async_remote_copy(
            src_ref=source,
            dst_ref=target,
            send_sem=self.send.at[t, phase],
            recv_sem=self.recv.at[t, phase],
            device_id={"dp": peer},
            device_id_type=MESH,
        )

    def halve(self, t, i):
        peer, mine = self.peer(t, i)
        half = self.rows >> (i + 1)
        source = self.tile(t, self.base(t, i) + (1 - mine) * half, half)
        return self.remote(source, self.box(t, i), t, i, peer)

    def add(self, t, i):
        half = self.rows >> (i + 1)
        keep = self.base(t, i + 1) - self.base(t, self.skip)
        box = self.rows - (self.rows >> i)

        def body(j, carry):
            here = self.span(keep + j * 16, 16)
            there = self.span(box + j * 16, 16)
            total = self.tiles[t, here].astype(f32) + self.inbox[t, there].astype(f32)
            self.tiles[t, here] = total.astype(bf16)
            return carry

        lax.fori_loop(0, half // 16, body, 0)

    def keep(self, t):
        first, size = self.base(t, self.bits), self.rows >> self.bits
        return pltpu.make_async_copy(
            self.tile(t, first, size), self.out.at[t, self.span(first, size)], self.keep_sem.at[t]
        )

    def double(self, t, i, back=False):
        peer, mine = self.peer(t, i)
        half = self.rows >> (i + 1)
        first = self.base(t, i) + ((1 - mine) if back else mine) * half
        piece = self.out.at[t, self.span(first, half)]
        source = piece
        if i == self.bits - 1 and not back:
            source = self.tile(t, first, half)
        return self.remote(source, piece, t, 2 * self.bits - 1 - i, peer)

    def events(self):
        return self.count * (2 * self.bits + 1 - self.skip)

    def event(self, e, loaded=None):
        k, t = e // self.count + self.skip, lax.rem(e, self.count)
        bits = self.bits

        def at_stage(stage):
            if stage == 0:
                self.halve(t, 0).start()
            elif stage <= bits:
                if stage > self.skip:
                    self.halve(t, stage - 1).wait_recv()
                else:
                    loaded(t)
                self.add(t, stage - 1)
                if stage < bits:
                    self.halve(t, stage).start()
                else:
                    self.keep(t).start()
                    self.double(t, bits - 1).start()
            else:
                i = 2 * bits - stage
                self.double(t, i, back=True).wait_recv()
                if i == bits - 1:
                    self.keep(t).wait()
                if i > 0:
                    self.double(t, i - 1).start()

        for stage in range(self.skip, 2 * bits + 1):
            pl.when((k == stage) & (e >= 0))(functools.partial(at_stage, stage))

    def finish(self):
        def one(t, carry):
            for i in range(self.bits):
                if i >= self.skip:
                    self.halve(t, i).wait_send()
                self.double(t, i).wait_send()
            return carry

        lax.fori_loop(0, self.count, one, 0)


class SmallSum:
    def __init__(self, at, rows, inbox, send, recv, everywhere):
        self.at, self.rows, self.inbox, self.send, self.recv = at, rows, inbox, send, recv
        self.phases = at.group_bits + (at.bits if everywhere else 0)

    @staticmethod
    def scratch(dp, n, count, width, everywhere):
        phases = (dp.bit_length() - 1) + (n.bit_length() - 1 if everywhere else 0)
        return [
            VMEM((phases + 1, count, width), f32),
            VMEM((phases, count, width), f32),
            DMA((phases,)),
            DMA((phases,)),
        ]

    def copy(self, i):
        at = self.at
        if i < at.group_bits:
            target = {"dp": at.group_peer(i)[0]}
        else:
            target = {"tensor": at.peer(i - at.group_bits)}
        return pltpu.make_async_remote_copy(
            src_ref=self.rows.at[i],
            dst_ref=self.inbox.at[i],
            send_sem=self.send.at[i],
            recv_sem=self.recv.at[i],
            device_id=target,
            device_id_type=MESH,
        )

    def event(self, e):
        def run(i):
            if i > 0:
                self.copy(i - 1).wait_recv()
                self.rows[i] = self.rows[i - 1] + self.inbox[i - 1]
            if i < self.phases:
                self.copy(i).start()

        for i in range(self.phases + 1):
            if isinstance(e, int):
                if e == i:
                    run(i)
            else:
                pl.when(e == i)(functools.partial(run, i))

    def finish(self):
        for i in range(self.phases):
            self.copy(i).wait_send()


def norm_rows(values, gain, shift):
    centre = values - jnp.mean(values, axis=-1, keepdims=True)
    spread = jnp.mean(centre * centre, axis=-1, keepdims=True)
    return centre * lax.rsqrt(spread + norm_epsilon) * gain + shift


def norm_rows_back(values, grad, gain):
    centre = values - jnp.mean(values, axis=-1, keepdims=True)
    scale = lax.rsqrt(jnp.mean(centre * centre, axis=-1, keepdims=True) + norm_epsilon)
    unit = centre * scale
    w = grad * gain
    back = w - jnp.mean(w, axis=-1, keepdims=True)
    back = scale * (back - unit * jnp.mean(w * unit, axis=-1, keepdims=True))
    return back, grad * unit


def add_row(ref, row, values):
    ref[row : row + 1] += jnp.sum(values, axis=0, keepdims=True)


def gather_project_kernel(
    n, tokens, gain, shift, weight, bias, gathered, heads, buf, send, recv, out_sem
):
    at = Place(n)
    seqs, rows, width = tokens.shape
    ring = Gather(at, rows, buf, send, recv)
    at.greet()
    for s in range(seqs):
        def block(i, carry):
            first = pl.multiple_of(i * 16, 16)
            values = norm_rows(tokens[s, pl.ds(first, 16)].astype(f32), gain[...], shift[...])
            buf[s, pl.ds(pl.multiple_of(at.me * rows + first, 16), 16)] = values.astype(bf16)
            return carry

        lax.fori_loop(0, rows // 16, block, 0)

    def keep(s, o):
        here = rows_of(o, 2 * rows)
        return pltpu.make_async_copy(buf.at[s, here], gathered.at[s, here], out_sem.at[s, o])

    def work(s, o):
        ring.arrived(s, o, 1 - at.core)
        keep(s, o).start()
        here = rows_of(o, 2 * rows)
        for j in range(3):
            total = jnp.dot(buf[s, here], weight[j], preferred_element_type=f32)
            if j == 0:
                total = (total + bias[0:1]) * HD ** (-0.5)
            if j == 2:
                total = total + bias[1:2]
            heads[j, s, here] = total.astype(bf16)

    def ops_of(c):
        return gather_ops(c, at.chips, seqs, 0, "in") + work_ops(
            c, at.chips, seqs, 1, lambda s, o: [("in", c, s, o, "both")], "done", 1.0
        )

    Plan(at, seqs, ops_of).run({0: ring.relay, 1: work})
    ring.finish()

    def close(i, carry):
        keep(i // at.chips, lax.rem(i, at.chips)).wait()
        return carry

    lax.fori_loop(0, seqs * at.chips, close, 0)


def whole(count):
    return [pl.BlockSpec(memory_space=VMEM)] * count


def gather_project(n, tokens, gain, shift, weight, bias):
    seqs, rows, width = tokens.shape
    part = weight.shape[2]
    return pl.pallas_call(
        functools.partial(gather_project_kernel, n),
        out_shape=(
            jax.ShapeDtypeStruct((seqs, n * rows, width), bf16),
            jax.ShapeDtypeStruct((3, seqs, n * rows, part), bf16),
        ),
        in_specs=whole(5),
        out_specs=(pl.BlockSpec(memory_space=pl.ANY), pl.BlockSpec(memory_space=VMEM)),
        scratch_shapes=[VMEM((seqs, n * rows, width), bf16)]
        + Gather.scratch(n, seqs)
        + [DMA((seqs, n // 2))],
        compiler_params=pltpu.CompilerParams(
            collective_id=0, has_side_effects=True, vmem_limit_bytes=40 * 2**20
        ),
        name="gather_project",
    )(tokens, gain, shift, weight, bias)


def project_scatter_kernel(
    n, mixed, weight, tokens, bias, gain, shift, hidden, normed, *scratch
):
    at = Place(n)
    seqs, rows, width = tokens.shape
    line = Scatter(at, rows, *scratch)
    at.greet()

    def final(s, there, total):
        values = tokens[s, there].astype(f32) + total + bias[...]
        hidden[s, there] = values
        normed[s, there] = norm_rows(values, gain[...], shift[...]).astype(bf16)

    def work(s, o):
        here = rows_of(o, 2 * rows)
        for j in range(width // 512):
            cols = pl.ds(j * 512, 512)
            total = jnp.dot(mixed[s, here], weight[:, cols], preferred_element_type=f32)
            line.part[s, o, :, cols] = total.astype(bf16)
        line.share(s, o)

    def ops_of(c):
        return work_ops(
            c, at.chips, seqs, 0, lambda s, o: [], "part", 1.0, rank=0, far=True
        ) + scatter_ops(c, at.chips, seqs, 1, "out", "part", last=4.0)

    Plan(at, seqs, ops_of).run({0: work, 1: functools.partial(line.pass_on, final)})
    line.finish()


def project_scatter(n, mixed, weight, tokens, bias, gain, shift):
    seqs, rows, width = tokens.shape
    return pl.pallas_call(
        functools.partial(project_scatter_kernel, n),
        out_shape=(
            jax.ShapeDtypeStruct((seqs, rows, width), f32),
            jax.ShapeDtypeStruct((seqs, rows, width), bf16),
        ),
        in_specs=whole(6),
        out_specs=tuple(whole(2)),
        scratch_shapes=Scatter.scratch(n, seqs, rows, width),
        compiler_params=pltpu.CompilerParams(
            collective_id=1, has_side_effects=True, vmem_limit_bytes=40 * 2**20
        ),
        name="project_scatter",
    )(mixed, weight, tokens, bias, gain, shift)


def heads_scatter_kernel(
    n,
    query,
    key,
    value,
    weight,
    gathered,
    out_part,
    tokens,
    gain,
    hidden_grad,
    bias_part,
    grad,
    sums_all,
    weight_grad,
    out_grad,
    bias_grad,
    *scratch,
):
    at = Place(n)
    seqs, rows, width = hidden_grad.shape
    line = Scatter(at, rows, *scratch[:7])
    weight_sum = GroupSum(at, width, *scratch[7:12], weight_grad)
    out_sum = GroupSum(at, out_part.shape[0], *scratch[12:17], out_grad, turn=1)
    small = SmallSum(at, *scratch[17:21], True)
    small_bias = SmallSum(at, *scratch[21:25], False)
    out_sum.tiles[0] = out_part[...]
    small.rows[0] = jnp.zeros(small.rows.shape[1:], f32)
    small_bias.rows[0] = bias_part[...]
    at.greet(groups=True, cube=True)

    def final(s, there, total):
        back, terms = norm_rows_back(tokens[s, there].astype(f32), total, gain[...])
        grad[s, there] = hidden_grad[s, there] + back
        small.rows[0, 0:1] += jnp.sum(terms, axis=0, keepdims=True)
        small.rows[0, 1:2] += jnp.sum(total, axis=0, keepdims=True)

    parts = ((query, HD ** (-0.5)), (key, 1.0), (value, 1.0))

    def weight_tile(j):
        for first in range(0, width, 512):
            total = 0.0
            for s in range(seqs):
                total += lax.dot_general(
                    gathered[s, :, pl.ds(first, 512)],
                    parts[j][0][s],
                    TN,
                    preferred_element_type=f32,
                )
            weight_sum.tiles[j, pl.ds(first, 512)] = (parts[j][1] * total).astype(bf16)

    def work(s, o):
        here = rows_of(o, 2 * rows)
        for j in range(width // 512):
            cols = pl.ds(j * 512, 512)
            total = 0.0
            for i in range(3):
                total += parts[i][1] * lax.dot_general(
                    parts[i][0][s, here], weight[i, cols], NT, preferred_element_type=f32
                )
            line.part[s, o, :, cols] = total.astype(bf16)
        line.share(s, o)

    each = seqs * at.chips

    def weight_event(first, s, o):
        e = first + s * at.chips + o
        for j in range(3):
            pl.when(e == j)(functools.partial(weight_tile, j))
        weight_sum.event(e)

    def out_event(s, o):
        out_sum.event(s * at.chips + o)

    def code_of(kind, e):
        return (kind + e // each, e % each // at.chips, e % at.chips)

    def ops_of(c):
        chips = at.chips
        return (
            work_ops(c, chips, seqs, 0, lambda s, o: [], "part", 1.5, rank=0, far=True)
            + scatter_ops(c, chips, seqs, 1, "out", "part", last=4.0)
            + group_ops(
                c, at.group_bits, 3, PIECE, lambda e: code_of(2, e), 0, 0, 2.7, name="qkv"
            )
            + group_ops(
                c, at.group_bits, 1, PIECE, lambda e: code_of(5, e), 0, 1, 0.7, name="out_sum"
            )
        )

    actions = {0: work, 1: functools.partial(line.pass_on, final), 5: out_event}
    for i in range(3):
        actions[2 + i] = functools.partial(weight_event, i * each)
    Plan(at, seqs, ops_of).run(actions, small_bias.event)
    for e in range(small.phases + 1):
        small.event(e)
    sums_all[...] = small.rows[small.phases]
    bias_grad[...] = small_bias.rows[small_bias.phases]
    line.finish()
    weight_sum.finish()
    out_sum.finish()
    small.finish()
    small_bias.finish()


def heads_scatter(
    n, query, key, value, weight, gathered, out_part, tokens, gain, hidden_grad, bias_part
):
    seqs, slots, part = query.shape
    width = weight.shape[1]
    rows = slots // n
    dp = lax.axis_size("dp")
    vmem = pl.BlockSpec(memory_space=VMEM)
    hbm = pl.BlockSpec(memory_space=pl.ANY)
    return pl.pallas_call(
        functools.partial(heads_scatter_kernel, n),
        out_shape=(
            jax.ShapeDtypeStruct((seqs, rows, width), f32),
            jax.ShapeDtypeStruct((2, width), f32),
            jax.ShapeDtypeStruct((3, width, part), bf16),
            jax.ShapeDtypeStruct((1, part, width), bf16),
            jax.ShapeDtypeStruct((2, part), f32),
        ),
        in_specs=whole(10),
        out_specs=(vmem, vmem, hbm, hbm, vmem),
        scratch_shapes=Scatter.scratch(n, seqs, rows, width)
        + GroupSum.scratch(dp, 3, width, part)
        + GroupSum.scratch(dp, 1, part, width)
        + SmallSum.scratch(dp, n, 2, width, True)
        + SmallSum.scratch(dp, n, 2, part, False),
        compiler_params=pltpu.CompilerParams(
            collective_id=2, has_side_effects=True, vmem_limit_bytes=62 * 2**20
        ),
        name="heads_scatter",
    )(query, key, value, weight, gathered, out_part, tokens, gain, hidden_grad, bias_part)


def normal_cdf(values):
    x = jnp.clip(values * 0.7071067811865476, -3.832506856900711, 3.832506856900711)
    x2 = x * x
    top = 0.00022905065861350646
    for c in (0.0034082910107109506, 0.050955695062380861, 0.18520832239976145, 1.128379143519084):
        top = top * x2 + c
    low = -1.1791602954361697e-7
    for c in (
        0.000023547966471313185,
        0.0010179625278914885,
        0.014070470171167667,
        0.11098505178285362,
        0.49746925110067538,
        1.0,
    ):
        low = low * x2 + c
    return 0.5 + 0.5 * (x * top / low)


def mlp_kernel(
    n,
    normed,
    grad_all,
    up_weight,
    up_bias,
    down_weight,
    hidden,
    gain,
    mlp_part,
    hidden_grad,
    grad_low,
    sums,
    up_grad,
    up_bias_grad,
    down_grad,
    up_box,
    down_box,
    buf,
    send,
    recv,
    *scratch,
):
    at = Place(n)
    seqs, rows, width = normed.shape
    units_wide = up_weight.shape[1]
    line = Scatter(at, rows, *scratch[:7])
    act, pre, out_stage, out_sem, up_stage, down_stage, tile_sem, half_send, half_recv = scratch[7:]
    ring = Gather(at, rows, buf, send, recv)
    at.greet(groups=True)
    for s in range(seqs):
        buf[s, rows_of(at.me, rows)] = normed[s]
    up_bias_grad[...] = jnp.zeros_like(up_bias_grad)
    sums[...] = jnp.zeros_like(sums)
    ft = min(512, units_wide)

    def out_copy(s, o):
        return pltpu.make_async_copy(
            out_stage, mlp_part.at[s, rows_of(o, 2 * rows)], out_sem.at[0]
        )

    def work(s, o):
        ring.arrived(s, o, 1 - at.core)
        here = rows_of(o, 2 * rows)
        for j in range(units_wide // ft):
            cols = pl.ds(j * ft, ft)
            value = jnp.dot(buf[s, here], up_weight[:, cols], preferred_element_type=f32)
            value = value + up_bias[:, cols]
            spread = normal_cdf(value)
            act[s, here, cols] = (value * spread).astype(bf16)
            slope = spread + value * (0.3989422804014327 * jnp.exp(-0.5 * value * value))
            grad = lax.dot_general(
                grad_all[s, here], down_weight[cols], NT, preferred_element_type=f32
            )
            grad = (grad * slope).astype(bf16)
            pre[s, here, cols] = grad
            up_bias_grad[:, cols] += jnp.sum(grad.astype(f32), axis=0, keepdims=True)
        for j in range(width // 512):
            cols = pl.ds(j * 512, 512)
            line.part[s, o, :, cols] = lax.dot_general(
                pre[s, here], up_weight[cols], NT, preferred_element_type=f32
            ).astype(bf16)
        line.share(s, o)
        pl.when((s > 0) | (o != at.chip))(lambda: out_copy(s, o).wait())
        for j in range(width // 512):
            cols = pl.ds(j * 512, 512)
            out_stage[:, cols] = jnp.dot(
                act[s, here], down_weight[:, cols], preferred_element_type=f32
            ).astype(bf16)
        out_copy(s, o).start()

    def final(s, there, total):
        back, terms = norm_rows_back(hidden[s, there], total, gain[...])
        first = pl.multiple_of(at.me * rows + there.start, 16)
        grad_out = grad_all[s, pl.ds(first, there.size)].astype(f32)
        grad = grad_out + back
        hidden_grad[s, there] = grad
        grad_low[s, there] = grad.astype(bf16)
        add_row(sums, 0, terms)
        add_row(sums, 1, total)
        add_row(sums, 2, grad)
        add_row(sums, 3, grad_out)

    kinds = ((down_stage, down_grad, down_box, 0), (up_stage, up_grad, up_box, 1))

    def tile_copy(kind, t):
        stage, grad, box, turn = kinds[kind]
        return pltpu.make_async_copy(stage, grad.at[t], tile_sem.at[kind])

    def tile_half(kind, t):
        stage, grad, box, turn = kinds[kind]
        half = box.shape[1]
        which = (t + turn) % at.group_bits
        peer, mine = at.group_peer(which)
        return pltpu.make_async_remote_copy(
            src_ref=grad.at[t, rows_of(1 - mine, half)],
            dst_ref=box.at[t],
            send_sem=half_send.at[kind, t],
            recv_sem=half_recv.at[kind, t],
            device_id={"dp": peer},
            device_id_type=MESH,
        )

    def tile_sent(kind, t):
        tile_copy(kind, t).wait()
        tile_half(kind, t).start()

    order = [(i % 2, i // 2) for i in range(8)]

    def weight_tile(i):
        for j, (kind, t) in enumerate(order):
            @pl.when(i == j)
            def _():
                stage = kinds[kind][0]
                cols = pl.ds(t * stage.shape[0], stage.shape[0])
                total = 0.0
                for s in range(seqs):
                    if kind == 0:
                        left, right = act[s, :, cols], grad_all[s]
                    else:
                        left, right = buf[s, :, cols], pre[s]
                    total += lax.dot_general(left, right, TN, preferred_element_type=f32)
                if j >= 1:
                    tile_sent(*order[j - 1])
                stage[...] = total.astype(bf16)
                tile_copy(kind, t).start()

    def tile_work(s, o):
        weight_tile(s * at.chips + o)

    def ops_of(c):
        chips = at.chips
        units = [(s, o) for s in range(seqs) for o in range(chips)]
        ops = (
            gather_ops(c, chips, seqs, 0, "in")
            + scatter_ops(c, chips, seqs, 1, "back", "part", last=4.0)
            + work_ops(
                c, chips, seqs, 2, lambda s, o: [("in", c, s, o, "both")], "part", 5.7
            )
        )
        for i in range(len(ops)):
            rank, code, needs, time, sends, gives = ops[i]
            if code[0] == 2 and code[1:] != (0, c):
                ops[i] = (rank, code, needs + [("first", c)], time, sends, gives)
            if code == (2, 0, c):
                ops[i] = (rank, code, needs, time, sends, gives + [(0.0, ("first", c))])
        for e in range(len(order)):
            needs = [("part", c, s, o) for s, o in units]
            needs += [("tile", c, e - 1)] if e else []
            sends = [("axis%d" % (e % 2), c, ("half", c, e), PIECE)]
            code = (3, e // chips, e % chips)
            ops.append(((4, e, 0), code, needs, 2.7, sends, [(0.0, ("tile", c, e))]))
        return ops

    Plan(at, seqs, ops_of).run(
        {0: ring.relay, 1: functools.partial(line.pass_on, final), 2: work, 3: tile_work}
    )
    tile_sent(*order[7])
    ring.finish()
    line.finish()
    for kind, t in order:
        tile_half(kind, t).wait()
    out_copy(0, 0).wait()


def mlp_block(n, normed, grad_all, up_weight, up_bias, down_weight, hidden, gain):
    seqs, rows, width = normed.shape
    slots = n * rows
    units = up_weight.shape[1]
    hbm = pl.BlockSpec(memory_space=pl.ANY)
    vmem = pl.BlockSpec(memory_space=VMEM)
    down_size, up_size = units // 4, width // 4
    return pl.pallas_call(
        functools.partial(mlp_kernel, n),
        out_shape=(
            jax.ShapeDtypeStruct((seqs, slots, width), bf16),
            jax.ShapeDtypeStruct((seqs, rows, width), f32),
            jax.ShapeDtypeStruct((seqs, rows, width), bf16),
            jax.ShapeDtypeStruct((4, width), f32),
            jax.ShapeDtypeStruct((4, up_size, units), bf16),
            jax.ShapeDtypeStruct((1, units), f32),
            jax.ShapeDtypeStruct((4, down_size, width), bf16),
            jax.ShapeDtypeStruct((4, up_size // 2, units), bf16),
            jax.ShapeDtypeStruct((4, down_size // 2, width), bf16),
        ),
        in_specs=whole(7),
        out_specs=(hbm, vmem, vmem, vmem, hbm, vmem, hbm, hbm, hbm),
        scratch_shapes=[VMEM((seqs, slots, width), bf16)]
        + Gather.scratch(n, seqs)
        + Scatter.scratch(n, seqs, rows, width)
        + [
            VMEM((seqs, slots, units), bf16),
            VMEM((seqs, slots, units), bf16),
            VMEM((2 * rows, width), bf16),
            DMA((1,)),
            VMEM((up_size, units), bf16),
            VMEM((down_size, width), bf16),
            DMA((2,)),
            DMA((2, 4)),
            DMA((2, 4)),
        ],
        compiler_params=pltpu.CompilerParams(
            collective_id=3, has_side_effects=True, vmem_limit_bytes=62 * 2**20
        ),
        name="mlp_block",
    )(normed, grad_all, up_weight, up_bias, down_weight, hidden, gain)


def attn_grad_kernel(
    n,
    grad,
    mlp_part,
    hidden,
    bias,
    weight,
    mixed,
    sums,
    up_bias_part,
    up_part,
    down_part,
    up_box,
    down_box,
    output,
    grad_heads,
    weight_grad,
    sums_all,
    up_bias_grad,
    up_grad,
    down_grad,
    buf,
    send,
    recv,
    *scratch,
):
    at = Place(n)
    seqs, rows, width = grad.shape
    line = Scatter(at, rows, *scratch[:7])
    load_sem, tile_sem, box_sem = scratch[7:10]
    ring = Gather(at, rows, buf, send, recv)
    up_sum = GroupSum(at, up_part.shape[1], *scratch[10:15], up_grad, turn=1, skip=1)
    down_sum = GroupSum(at, down_part.shape[1], *scratch[15:20], down_grad, skip=1)
    small = SmallSum(at, *scratch[20:24], True)
    small_bias = SmallSum(at, *scratch[24:28], False)
    pairs = ((up_sum, up_part, up_box), (down_sum, down_part, down_box))

    def tile_load(i, t):
        group, part, box = pairs[i]
        half = box.shape[1]
        return (
            pltpu.make_async_copy(
                part.at[t, group.span(group.base(t, 1), half)], group.tiles.at[t], tile_sem.at[i, t]
            ),
            pltpu.make_async_copy(box.at[t], group.box(t, 0), box_sem.at[i, t]),
        )

    def tile_loaded(i, t):
        for copy in tile_load(i, t):
            copy.wait()

    for t in range(4):
        for i in range(2):
            for copy in tile_load(i, t):
                copy.start()
    small.rows[0] = sums[...]
    small_bias.rows[0] = up_bias_part[...]

    def load(s, o):
        return pltpu.make_async_copy(
            mlp_part.at[s, rows_of(o, 2 * rows)], line.part.at[s, o], load_sem.at[s, o]
        )

    def load_one(i, carry):
        load(i // at.chips, lax.rem(i, at.chips)).start()
        return carry

    each = seqs * at.chips
    lax.fori_loop(0, each, load_one, 0)
    for s in range(seqs):
        buf[s, rows_of(at.me, rows)] = grad[s]
    at.greet(groups=True, cube=True)

    def final(s, there, total):
        output[s, there] = (hidden[s, there] + total + bias[...]).astype(bf16)

    def share(s, o):
        load(s, o).wait()
        line.share(s, o)

    def work(s, o):
        ring.arrived(s, o, 1 - at.core)
        here = rows_of(o, 2 * rows)
        grad_heads[s, here] = lax.dot_general(
            buf[s, here], weight[...], NT, preferred_element_type=f32
        ).astype(bf16)

    def event(i, s, o):
        e = s * at.chips + o
        for j in range(2):
            group = pairs[j][0]
            group.event(e + i * each, functools.partial(tile_loaded, j))

    def ops_of(c):
        chips = at.chips
        code_of = lambda e: (4 + e // each, e % each // chips, e % chips)
        return (
            gather_ops(c, chips, seqs, 0, "in")
            + scatter_ops(c, chips, seqs, 1, "out", "part", last=4.0)
            + work_ops(c, chips, seqs, 2, lambda s, o: [("in", c, s, o, "both")], "done", 1.0)
            + work_ops(c, chips, seqs, 3, lambda s, o: [], "part", 0.3, rank=0, far=True)
            + group_ops(c, at.group_bits, 4, PIECE, code_of, 1, 0, 0.7)
        )

    actions = {0: ring.relay, 1: functools.partial(line.pass_on, final), 2: work, 3: share}
    for i in range(3):
        actions[4 + i] = functools.partial(event, i)

    def beside(k):
        pl.when(lax.rem(k, 3) == 0)(lambda: small.event(k // 3))
        small_bias.event(k)

    Plan(at, seqs, ops_of).run(actions, beside)
    sums_all[...] = small.rows[small.phases]
    up_bias_grad[...] = small_bias.rows[small_bias.phases]
    for j in range(width // 512):
        cols = pl.ds(j * 512, 512)
        total = 0.0
        for s in range(seqs):
            total += lax.dot_general(mixed[s], buf[s, :, cols], TN, preferred_element_type=f32)
        weight_grad[:, cols] = total.astype(bf16)
    ring.finish()
    line.finish()
    small.finish()
    small_bias.finish()
    up_sum.finish()
    down_sum.finish()


def attn_grad(
    n,
    grad,
    mlp_part,
    hidden,
    bias,
    weight,
    mixed,
    sums,
    up_bias_part,
    up_part,
    down_part,
    up_box,
    down_box,
):
    seqs, rows, width = grad.shape
    slots = n * rows
    part = weight.shape[0]
    units = up_part.shape[2]
    dp = lax.axis_size("dp")
    vmem = pl.BlockSpec(memory_space=VMEM)
    hbm = pl.BlockSpec(memory_space=pl.ANY)
    return pl.pallas_call(
        functools.partial(attn_grad_kernel, n),
        out_shape=(
            jax.ShapeDtypeStruct((seqs, rows, width), bf16),
            jax.ShapeDtypeStruct((seqs, slots, part), bf16),
            jax.ShapeDtypeStruct((part, width), bf16),
            jax.ShapeDtypeStruct(sums.shape, f32),
            jax.ShapeDtypeStruct((1, units), f32),
            jax.ShapeDtypeStruct(up_part.shape, bf16),
            jax.ShapeDtypeStruct(down_part.shape, bf16),
        ),
        in_specs=[vmem, hbm] + [vmem] * 6 + [hbm] * 4,
        out_specs=(vmem,) * 5 + (hbm, hbm),
        scratch_shapes=[VMEM((seqs, slots, width), bf16)]
        + Gather.scratch(n, seqs)
        + Scatter.scratch(n, seqs, rows, width)
        + [DMA((seqs, n // 2)), DMA((2, 4)), DMA((2, 4))]
        + GroupSum.scratch(dp, 4, width // 4, units, 1)
        + GroupSum.scratch(dp, 4, units // 4, width, 1)
        + SmallSum.scratch(dp, n, sums.shape[0], width, True)
        + SmallSum.scratch(dp, n, 1, units, False),
        compiler_params=pltpu.CompilerParams(
            collective_id=4, has_side_effects=True, vmem_limit_bytes=62 * 2**20
        ),
        name="attn_grad",
    )(
        grad,
        mlp_part,
        hidden,
        bias,
        weight,
        mixed,
        sums,
        up_bias_part,
        up_part,
        down_part,
        up_box,
        down_box,
    )


def body(
    tokens,
    cotangent,
    lengths,
    ln1_gain,
    ln1_shift,
    qkv_weight,
    qkv_bias,
    out_weight,
    out_bias,
    ln2_gain,
    ln2_shift,
    up_weight,
    up_bias,
    down_weight,
    down_bias,
):
    seq_count, local_rows, model_width = tokens.shape
    part_width = qkv_weight.shape[2]
    head_count = part_width // HD
    score_scale = HD ** (-0.5)
    n = lax.axis_size("tensor")
    gathered_one, heads = gather_project(
        n, tokens, ln1_gain[None], ln1_shift[None], qkv_weight, qkv_bias
    )
    slot_count = gathered_one.shape[1]
    head_shape = (seq_count, slot_count, head_count, HD)
    query_rows, key_rows, value_rows = [heads[j].reshape(head_shape) for j in range(3)]
    attended, log_totals = lax.map(
        lambda item: attend_forward(item[0], item[1], item[2], item[3]),
        (query_rows, key_rows, value_rows, lengths),
    )
    mixed_heads = attended.reshape(seq_count, slot_count, part_width).astype(jnp.bfloat16)
    hidden_state, normed_two = project_scatter(
        n, mixed_heads, out_weight, tokens, out_bias[None], ln2_gain[None], ln2_shift[None]
    )
    slot_ids = lax.axis_index("tensor") * local_rows + lax.broadcasted_iota(
        jnp.int32, (seq_count, local_rows), 1
    )
    valid_rows = (slot_ids < lengths[:, None]).astype(jnp.float32)
    grad_out = cotangent.astype(jnp.float32) * valid_rows[:, :, None]
    grad_low, heads = lax.optimization_barrier((grad_out.astype(jnp.bfloat16), heads))
    grad_mlp = lax.all_gather(grad_low, "tensor", axis=1, tiled=True)
    (
        mlp_part,
        hidden_grad,
        grad_attn,
        sums,
        up_part,
        up_bias_part,
        down_part,
        up_box,
        down_box,
    ) = mlp_block(
        n, normed_two, grad_mlp, up_weight, up_bias[None], down_weight, hidden_state, ln2_gain[None]
    )
    output, grad_heads, out_part, sums, up_bias_grad, up_weight_grad, down_weight_grad = attn_grad(
        n,
        grad_attn,
        mlp_part,
        hidden_state,
        down_bias[None],
        out_weight,
        mixed_heads,
        sums,
        up_bias_part,
        up_part,
        down_part,
        up_box,
        down_box,
    )
    ln2_gain_grad, ln2_shift_grad, out_bias_grad, down_bias_grad = [sums[i] for i in range(4)]
    up_bias_grad = up_bias_grad[0]
    up_weight_grad = up_weight_grad.astype(jnp.float32).reshape(up_weight.shape)
    down_weight_grad = down_weight_grad.astype(jnp.float32).reshape(down_weight.shape)
    grad_heads = grad_heads.reshape(head_shape)
    grad_query, grad_key, grad_value = lax.map(
        lambda item: attend_backward(item[0], item[1], item[2], item[3], item[4], item[5]),
        (query_rows, key_rows, value_rows, grad_heads, log_totals, lengths),
    )
    flat_shape = (seq_count, slot_count, part_width)
    grad_query = grad_query.reshape(flat_shape).astype(jnp.bfloat16)
    grad_key = grad_key.reshape(flat_shape).astype(jnp.bfloat16)
    grad_value = grad_value.reshape(flat_shape).astype(jnp.bfloat16)
    qkv_bias_grad = jnp.stack(
        [
            score_scale * jnp.sum(grad_query.astype(jnp.float32), axis=(0, 1)),
            jnp.sum(grad_value.astype(jnp.float32), axis=(0, 1)),
        ]
    )
    input_grad, sums_one, qkv_weight_grad, out_weight_grad, qkv_bias_grad = heads_scatter(
        n,
        grad_query,
        grad_key,
        grad_value,
        qkv_weight,
        gathered_one,
        out_part,
        tokens,
        ln1_gain[None],
        hidden_grad,
        qkv_bias_grad,
    )
    ln1_gain_grad, ln1_shift_grad = sums_one[0], sums_one[1]
    qkv_weight_grad = qkv_weight_grad.astype(jnp.float32)
    out_weight_grad = out_weight_grad[0].astype(jnp.float32)
    return (
        output,
        input_grad,
        ln1_gain_grad,
        ln1_shift_grad,
        qkv_weight_grad,
        qkv_bias_grad,
        out_weight_grad,
        out_bias_grad,
        ln2_gain_grad,
        ln2_shift_grad,
        up_weight_grad,
        up_bias_grad,
        down_weight_grad,
        down_bias_grad,
    )


def solution(mesh):
    in_specs = (
        P("dp", "tensor", None),
        P("dp", "tensor", None),
        P("dp"),
        P(),
        P(),
        P(None, None, "tensor"),
        P(None, "tensor"),
        P("tensor", None),
        P(),
        P(),
        P(),
        P(None, "tensor"),
        P("tensor"),
        P("tensor", None),
        P(),
    )
    out_specs = (
        P("dp", "tensor", None),
        P("dp", "tensor", None),
        P(),
        P(),
        P(None, None, "tensor"),
        P(None, "tensor"),
        P("tensor", None),
        P(),
        P(),
        P(),
        P(None, "tensor"),
        P("tensor"),
        P("tensor", None),
        P(),
    )
    return jax.shard_map(body, mesh=mesh, in_specs=in_specs, out_specs=out_specs, check_vma=False)
```

```python
import functools
import heapq

import jax
import jax.numpy as jnp
from jax import lax
from jax.experimental import pallas as pl
from jax.experimental.pallas import tpu as pltpu
from jax.sharding import PartitionSpec as P

HD = 128


norm_epsilon = 1e-05

MESH = pl.DeviceIdType.MESH
UP, DOWN, SIDE = 0, 1, 2
VMEM = pltpu.VMEM
DMA = pltpu.SemaphoreType.DMA
f32 = jnp.float32
bf16 = jnp.bfloat16
NT = (((1,), (1,)), ((), ()))
TN = (((0,), (0,)), ((), ()))


def order_of(chips, ops_of, backlog=8.0, hop=1.5):
    todo = [sorted(ops_of(c)) for c in range(chips)]
    order = [[] for _ in range(chips)]
    free, busy, have, queue = {}, [False] * chips, set(), []

    def push(time, what):
        heapq.heappush(queue, (time, len(pushed), what))
        pushed.append(0)

    pushed = []
    for c in range(chips):
        push(0.0, (c, None, ()))
    now = 0.0
    while queue:
        now, _, (c, signal, after) = heapq.heappop(queue)
        if signal is not None:
            have.add(signal)
        for part in after:
            if part[0] == "free":
                busy[c] = False
            elif part[0] == "send":
                _, link, to, sig, span = part
                start = max(now, free.get((c, link), 0.0))
                free[c, link] = start + span
                push(start + span + hop, (to, sig, ()))
            else:
                push(now + part[1], (c, part[2], ()))
        if busy[c]:
            continue
        for op in todo[c]:
            rank, code, needs, time, sends, gives = op
            if any(need not in have for need in needs):
                continue
            late = max([free.get((c, send[0]), 0.0) - now for send in sends], default=0.0)
            if late > backlog:
                push(now + late - backlog, (c, None, ()))
                continue
            todo[c].remove(op)
            order[c].append(code)
            busy[c] = True
            ends = [("free",)] + [("send",) + send for send in sends]
            push(now + time, (c, None, ends + [("give",) + give for give in gives]))
            break
    assert not any(todo)
    return order, now


PIECE = 12.0


def gather_ops(c, chips, seqs, kind, name, rank=0, time=0.5, gate=False):
    ops = []
    for s in range(seqs):
        for o in range(chips):
            sends = []
            if o <= c < chips - 1:
                sends.append((c + 1, c + 1, (name, c + 1, s, o), PIECE))
            if o >= c > 0:
                sends.append((c - 1, c - 1, (name, c - 1, s, o), PIECE))
            needs = [] if o == c else [(name, c, s, o)]
            if gate and o == c and s > 0:
                for other in range(chips):
                    if other < c < chips - 1 or other > c > 0:
                        needs.append((name, c, s - 1, other))
            both = [(3.0, (name, c, s, o, "both"))]
            ops.append(((rank, s, abs(o - c)), (kind, s, o), needs, time, sends, both))
    return ops


def scatter_ops(c, chips, seqs, kind, name, part, rank=1, time=1.3, last=2.0):
    ops = []
    for s in range(seqs):
        for o in range(chips):
            needs = [(part, c, s, o)]
            if o >= c > 0:
                needs.append((name, c, s, o, "below"))
            if o <= c < chips - 1:
                needs.append((name, c, s, o, "above"))
            sends = []
            if o > c:
                sends = [(c + 1, c + 1, (name, c + 1, s, o, "below"), PIECE)]
            if o < c:
                sends = [(c - 1, c - 1, (name, c - 1, s, o, "above"), PIECE)]
            order = (rank, s, -abs(o - c)) if o != c else (8, s, 0)
            ops.append((order, (kind, s, o), needs, last if o == c else time, sends, []))
    return ops


def work_ops(c, chips, seqs, kind, needs_of, gives, time, rank=2, far=False):
    return [
        (
            (rank, s, -abs(o - c) if far else abs(o - c)),
            (kind, s, o),
            needs_of(s, o),
            time,
            [],
            [(3.0, (gives, c, s, o))],
        )
        for s in range(seqs)
        for o in range(chips)
    ]


def group_ops(c, bits, count, span, code_of, skip, turn, first_time, rank=3, name="group"):
    ops = []
    for t in range(count):
        for stage in range(skip, 2 * bits + 1):
            needs = []
            if stage > skip:
                needs = [(name, c, t, stage)]
            sends = []
            if stage < 2 * bits:
                i = stage if stage < bits else 2 * bits - 1 - stage
                axis = "axis%d" % ((t + turn + i) % bits)
                sends = [(axis, c, (name, c, t, stage + 1), span / 2**i)]
            time = first_time if stage == 0 else 0.7
            code = code_of((stage - skip) * count + t)
            ops.append(((rank, stage, t), code, needs, time, sends, []))
    return ops


class Plan:
    def __init__(self, at, seqs, ops_of):
        chips = at.chips
        order, self.length = order_of(chips, ops_of)
        self.per, self.chips, self.seqs = 128, chips, seqs
        self.count = max(len(codes) for codes in order)
        assert 8 * seqs * chips <= self.per
        rows = []
        for codes in order:
            flat = [(kind * seqs + s) * chips + o for kind, s, o in codes]
            flat += [7 * seqs * chips] * (self.count - len(flat) + 4)
            rows.append(
                [sum(flat[i + j] * self.per**j for j in range(4)) for i in range(0, self.count, 4)]
            )
        self.words = []
        for w in range(len(rows[0])):
            word = jnp.int32(rows[0][w])
            for c in range(1, chips):
                word = jnp.where(at.chip == c, jnp.int32(rows[c][w]), word)
            self.words.append(word)

    def step(self, k):
        which, slot = k // 4, lax.rem(k, 4)
        word = jnp.int32(0)
        for w, value in enumerate(self.words):
            word = jnp.where(which == w, value, word)
        code = word
        for j in range(1, 4):
            code = jnp.where(slot == j, word // self.per**j, code)
        code = lax.rem(code, self.per)
        each = self.seqs * self.chips
        return code // each, lax.rem(code, each) // self.chips, lax.rem(code, self.chips)

    def run(self, actions, beside=None):
        def step(k, carry):
            kind, s, o = self.step(k)
            for which, action in actions.items():
                pl.when(kind == which)(functools.partial(action, s, o))
            if beside is not None:
                beside(k)
            return carry

        lax.fori_loop(0, self.count, step, 0)


class Place:
    def __init__(self, n):
        self.n, self.chips = n, n // 2
        self.me = lax.axis_index("tensor")
        self.chip, self.core = self.me // 2, lax.rem(self.me, 2)
        self.side = self.me + 1 - 2 * self.core
        self.below = self.chip > 0
        self.above = self.chip < self.chips - 1
        self.group = lax.axis_index("dp")
        self.group_bits = lax.axis_size("dp").bit_length() - 1
        self.bits = n.bit_length() - 1

    def group_peer(self, q):
        mine = lax.rem(self.group // 2**q, 2)
        return self.group + (1 - 2 * mine) * 2**q, mine

    def peer(self, q):
        mine = lax.rem(self.me // 2**q, 2)
        return self.me + (1 - 2 * mine) * 2**q

    def greet(self, groups=False, cube=False):
        barrier = pltpu.get_barrier_semaphore()

        def tell(target):
            pl.semaphore_signal(
                barrier, inc=1, device_id={"tensor": target}, device_id_type=MESH
            )

        tell(self.side)
        pl.when(self.below)(lambda: tell(self.me - 2))
        pl.when(self.above)(lambda: tell(self.me + 2))
        peers = 1 + self.below.astype(jnp.int32) + self.above.astype(jnp.int32)
        if groups:
            for q in range(self.group_bits):
                pl.semaphore_signal(
                    barrier, inc=1, device_id={"dp": self.group_peer(q)[0]}, device_id_type=MESH
                )
            peers = peers + self.group_bits
        if cube:
            for q in range(self.bits):
                tell(self.peer(q))
            peers = peers + self.bits
        pl.semaphore_wait(barrier, peers)


def rows_of(index, rows):
    return pl.ds(pl.multiple_of(index * rows, rows), rows)


class Gather:
    def __init__(self, at, rows, buf, send, recv):
        self.at, self.rows, self.buf, self.send, self.recv = at, rows, buf, send, recv
        self.seqs = buf.shape[0]

    @staticmethod
    def scratch(n, seqs):
        return [DMA((3, seqs, n // 2)), DMA((seqs, n))]

    def piece(self, s, o, k):
        return self.buf.at[s, rows_of(2 * o + k, self.rows)]

    def copy(self, s, o, kind):
        at = self.at
        target = (at.me + 2, at.me - 2, at.side)[kind]
        piece = self.piece(s, o, at.core)
        return pltpu.make_async_remote_copy(
            src_ref=piece,
            dst_ref=piece,
            send_sem=self.send.at[kind, s, o],
            recv_sem=self.recv.at[s, 2 * o + at.core],
            device_id={"tensor": target},
            device_id_type=MESH,
        )

    def arrived(self, s, o, k):
        at = self.at
        piece = self.piece(s, o, k)
        pltpu.make_async_remote_copy(
            src_ref=piece,
            dst_ref=piece,
            send_sem=self.send.at[SIDE, s, o],
            recv_sem=self.recv.at[s, 2 * o + k],
            device_id={"tensor": at.side},
            device_id_type=MESH,
        ).wait_recv()

    def relay(self, s, o):
        at = self.at
        pl.when(o != at.chip)(lambda: self.arrived(s, o, at.core))
        pl.when((o <= at.chip) & at.above)(lambda: self.copy(s, o, UP).start())
        pl.when((o >= at.chip) & at.below)(lambda: self.copy(s, o, DOWN).start())
        self.copy(s, o, SIDE).start()

    def finish(self):
        at = self.at

        def one(i, carry):
            s, o = i // at.chips, lax.rem(i, at.chips)
            pl.when((o <= at.chip) & at.above)(lambda: self.copy(s, o, UP).wait_send())
            pl.when((o >= at.chip) & at.below)(lambda: self.copy(s, o, DOWN).wait_send())
            self.copy(s, o, SIDE).wait_send()
            return carry

        lax.fori_loop(0, self.seqs * at.chips, one, 0)


class Scatter:
    def __init__(self, at, rows, part, side, link, side_send, side_recv, send, recv):
        self.at, self.rows = at, rows
        self.part, self.side, self.link = part, side, link
        self.side_send, self.side_recv, self.send, self.recv = side_send, side_recv, send, recv
        self.seqs = part.shape[0]

    @staticmethod
    def scratch(n, seqs, rows, width):
        chips = n // 2
        return [
            VMEM((seqs, chips, 2 * rows, width), bf16),
            VMEM((seqs, chips, rows, width), bf16),
            VMEM((seqs, chips + 1, rows, width), bf16),
            DMA((seqs, chips)),
            DMA((seqs, chips)),
            DMA((seqs, chips)),
            DMA((seqs, chips + 1)),
        ]

    def side_copy(self, s, o):
        at = self.at
        return pltpu.make_async_remote_copy(
            src_ref=self.part.at[s, o, rows_of(1 - at.core, self.rows)],
            dst_ref=self.side.at[s, o],
            send_sem=self.side_send.at[s, o],
            recv_sem=self.side_recv.at[s, o],
            device_id={"tensor": at.side},
            device_id_type=MESH,
        )

    def link_copy(self, s, o, slot, target):
        return pltpu.make_async_remote_copy(
            src_ref=self.part.at[s, o, rows_of(self.at.core, self.rows)],
            dst_ref=self.link.at[s, slot],
            send_sem=self.send.at[s, o],
            recv_sem=self.recv.at[s, slot],
            device_id={"tensor": target},
            device_id_type=MESH,
        )

    def share(self, s, o):
        self.side_copy(s, o).start()

    def blocks(self, body):
        step = 16
        lax.fori_loop(0, self.rows // step, lambda i, c: (body(pl.multiple_of(i * step, step), step), c)[1], 0)

    def add_up(self, s, o, slots):
        base = self.at.core * self.rows

        def body(first, step):
            here = pl.ds(pl.multiple_of(base + first, step), step)
            there = pl.ds(first, step)
            total = self.part[s, o, here].astype(f32) + self.side[s, o, there].astype(f32)
            for slot in slots:
                total += self.link[s, slot, there].astype(f32)
            self.part[s, o, here] = total.astype(bf16)

        self.blocks(body)

    def pass_on(self, final, s, o):
        at = self.at
        self.side_copy(s, o).wait_recv()

        @pl.when(o > at.chip)
        def _():
            @pl.when(at.below)
            def _():
                self.link_copy(s, o, o, at.me).wait_recv()
                self.add_up(s, o, [o])

            pl.when(jnp.logical_not(at.below))(lambda: self.add_up(s, o, []))
            self.link_copy(s, o, o, at.me + 2).start()

        @pl.when(o < at.chip)
        def _():
            @pl.when(at.above)
            def _():
                self.link_copy(s, o, o, at.me).wait_recv()
                self.add_up(s, o, [o])

            pl.when(jnp.logical_not(at.above))(lambda: self.add_up(s, o, []))
            slot = jnp.where(o == at.chip - 1, at.chips, o)
            self.link_copy(s, o, slot, at.me - 2).start()

        @pl.when(o == at.chip)
        def _():
            pl.when(at.below)(lambda: self.link_copy(s, o, o, at.me).wait_recv())
            pl.when(at.above)(lambda: self.link_copy(s, o, at.chips, at.me).wait_recv())
            for slot, used in ((o, at.below), (at.chips, at.above)):
                @pl.when(jnp.logical_not(used))
                def _():
                    def clear(first, step):
                        self.link[s, slot, pl.ds(first, step)] = jnp.zeros(
                            (step, self.link.shape[-1]), bf16
                        )

                    self.blocks(clear)
            base = at.core * self.rows

            def body(first, step):
                here = pl.ds(pl.multiple_of(base + first, step), step)
                there = pl.ds(first, step)
                total = self.part[s, o, here].astype(f32) + self.side[s, o, there].astype(f32)
                total += self.link[s, o, there].astype(f32)
                total += self.link[s, at.chips, there].astype(f32)
                final(s, there, total)

            self.blocks(body)

    def finish(self):
        at = self.at

        def one(i, carry):
            s, o = i // at.chips, lax.rem(i, at.chips)
            self.side_copy(s, o).wait_send()
            pl.when(o != at.chip)(lambda: self.link_copy(s, o, o, at.side).wait_send())
            return carry

        lax.fori_loop(0, self.seqs * at.chips, one, 0)


class GroupSum:
    def __init__(self, at, rows, tiles, inbox, send, recv, keep_sem, out, turn=0, skip=0):
        self.at, self.tiles, self.inbox, self.send, self.recv = at, tiles, inbox, send, recv
        self.keep_sem, self.out, self.skip, self.turn, self.rows = keep_sem, out, skip, turn, rows
        self.bits = at.group_bits
        self.count = send.shape[0]

    @staticmethod
    def scratch(dp, count, rows, width, skip=0):
        phases = 2 * (dp.bit_length() - 1)
        return [
            VMEM((count, rows >> skip, width), bf16),
            VMEM((count, rows - rows // dp, width), bf16),
            DMA((count, phases)),
            DMA((count, phases)),
            DMA((count,)),
        ]

    def peer(self, t, i):
        which = lax.rem(t + i + self.turn, self.bits)
        peer, mine = 0, 0
        for q in range(self.bits):
            other, bit = self.at.group_peer(q)
            peer = peer + jnp.where(which == q, other, 0)
            mine = mine + jnp.where(which == q, bit, 0)
        return peer, mine

    def base(self, t, i):
        first = 0
        for p in range(i):
            first = first + self.peer(t, p)[1] * (self.rows >> (p + 1))
        return first

    def span(self, first, size):
        return pl.ds(pl.multiple_of(first, 16), size)

    def tile(self, t, first, size):
        return self.tiles.at[t, self.span(first - self.base(t, self.skip), size)]

    def box(self, t, i):
        return self.inbox.at[t, pl.ds(self.rows - (self.rows >> i), self.rows >> (i + 1))]

    def remote(self, source, target, t, phase, peer):
        return pltpu.make_async_remote_copy(
            src_ref=source,
            dst_ref=target,
            send_sem=self.send.at[t, phase],
            recv_sem=self.recv.at[t, phase],
            device_id={"dp": peer},
            device_id_type=MESH,
        )

    def halve(self, t, i):
        peer, mine = self.peer(t, i)
        half = self.rows >> (i + 1)
        source = self.tile(t, self.base(t, i) + (1 - mine) * half, half)
        return self.remote(source, self.box(t, i), t, i, peer)

    def add(self, t, i):
        half = self.rows >> (i + 1)
        keep = self.base(t, i + 1) - self.base(t, self.skip)
        box = self.rows - (self.rows >> i)

        def body(j, carry):
            here = self.span(keep + j * 16, 16)
            there = self.span(box + j * 16, 16)
            total = self.tiles[t, here].astype(f32) + self.inbox[t, there].astype(f32)
            self.tiles[t, here] = total.astype(bf16)
            return carry

        lax.fori_loop(0, half // 16, body, 0)

    def keep(self, t):
        first, size = self.base(t, self.bits), self.rows >> self.bits
        return pltpu.make_async_copy(
            self.tile(t, first, size), self.out.at[t, self.span(first, size)], self.keep_sem.at[t]
        )

    def double(self, t, i, back=False):
        peer, mine = self.peer(t, i)
        half = self.rows >> (i + 1)
        first = self.base(t, i) + ((1 - mine) if back else mine) * half
        piece = self.out.at[t, self.span(first, half)]
        source = piece
        if i == self.bits - 1 and not back:
            source = self.tile(t, first, half)
        return self.remote(source, piece, t, 2 * self.bits - 1 - i, peer)

    def events(self):
        return self.count * (2 * self.bits + 1 - self.skip)

    def event(self, e, loaded=None):
        k, t = e // self.count + self.skip, lax.rem(e, self.count)
        bits = self.bits

        def at_stage(stage):
            if stage == 0:
                self.halve(t, 0).start()
            elif stage <= bits:
                if stage > self.skip:
                    self.halve(t, stage - 1).wait_recv()
                else:
                    loaded(t)
                self.add(t, stage - 1)
                if stage < bits:
                    self.halve(t, stage).start()
                else:
                    self.keep(t).start()
                    self.double(t, bits - 1).start()
            else:
                i = 2 * bits - stage
                self.double(t, i, back=True).wait_recv()
                if i == bits - 1:
                    self.keep(t).wait()
                if i > 0:
                    self.double(t, i - 1).start()

        for stage in range(self.skip, 2 * bits + 1):
            pl.when((k == stage) & (e >= 0))(functools.partial(at_stage, stage))

    def finish(self):
        def one(t, carry):
            for i in range(self.bits):
                if i >= self.skip:
                    self.halve(t, i).wait_send()
                self.double(t, i).wait_send()
            return carry

        lax.fori_loop(0, self.count, one, 0)


class SmallSum:
    def __init__(self, at, rows, inbox, send, recv, everywhere):
        self.at, self.rows, self.inbox, self.send, self.recv = at, rows, inbox, send, recv
        self.phases = at.group_bits + (at.bits if everywhere else 0)

    @staticmethod
    def scratch(dp, n, count, width, everywhere):
        phases = (dp.bit_length() - 1) + (n.bit_length() - 1 if everywhere else 0)
        return [
            VMEM((phases + 1, count, width), f32),
            VMEM((phases, count, width), f32),
            DMA((phases,)),
            DMA((phases,)),
        ]

    def copy(self, i):
        at = self.at
        if i < at.group_bits:
            target = {"dp": at.group_peer(i)[0]}
        else:
            target = {"tensor": at.peer(i - at.group_bits)}
        return pltpu.make_async_remote_copy(
            src_ref=self.rows.at[i],
            dst_ref=self.inbox.at[i],
            send_sem=self.send.at[i],
            recv_sem=self.recv.at[i],
            device_id=target,
            device_id_type=MESH,
        )

    def event(self, e):
        def run(i):
            if i > 0:
                self.copy(i - 1).wait_recv()
                self.rows[i] = self.rows[i - 1] + self.inbox[i - 1]
            if i < self.phases:
                self.copy(i).start()

        for i in range(self.phases + 1):
            if isinstance(e, int):
                if e == i:
                    run(i)
            else:
                pl.when(e == i)(functools.partial(run, i))

    def finish(self):
        for i in range(self.phases):
            self.copy(i).wait_send()


def norm_rows(values, gain, shift):
    centre = values - jnp.mean(values, axis=-1, keepdims=True)
    spread = jnp.mean(centre * centre, axis=-1, keepdims=True)
    return centre * lax.rsqrt(spread + norm_epsilon) * gain + shift


def norm_rows_back(values, grad, gain):
    centre = values - jnp.mean(values, axis=-1, keepdims=True)
    scale = lax.rsqrt(jnp.mean(centre * centre, axis=-1, keepdims=True) + norm_epsilon)
    unit = centre * scale
    w = grad * gain
    back = w - jnp.mean(w, axis=-1, keepdims=True)
    back = scale * (back - unit * jnp.mean(w * unit, axis=-1, keepdims=True))
    return back, grad * unit


def add_row(ref, row, values):
    ref[row : row + 1] += jnp.sum(values, axis=0, keepdims=True)


def head_probs(query, keys, first, length):
    rows, cols = query.shape[0], keys.shape[0]
    scores = lax.dot_general(query, keys, NT, preferred_element_type=f32)
    row_ids = first + lax.broadcasted_iota(jnp.int32, (rows, cols), 0)
    col_ids = lax.broadcasted_iota(jnp.int32, (rows, cols), 1)
    scores = jnp.where((col_ids <= row_ids) & (col_ids < length), scores, -1e30)
    probs = jnp.exp(scores - jnp.max(scores, axis=-1, keepdims=True))
    return probs * (1.0 / jnp.sum(probs, axis=-1, keepdims=True))


def attend(heads, lengths, mixed, block, s):
    slots, part = mixed.shape[1:]

    def one(h, carry):
        cols = pl.ds(pl.multiple_of(h * HD, HD), HD)
        for first in range(0, slots, block):
            rows, seen = pl.ds(first, block), pl.ds(0, first + block)
            probs = head_probs(heads[0, s, rows, cols], heads[1, s, seen, cols], first, lengths[s])
            mixed[s, rows, cols] = jnp.dot(
                probs.astype(bf16), heads[2, s, seen, cols], preferred_element_type=f32
            ).astype(bf16)
        return carry

    lax.fori_loop(0, part // HD, one, 0)


def attend_back(heads, grad_heads, lengths, grads, grad_key, grad_value, block, s):
    slots, part = grad_heads.shape[1:]

    def one(h, carry):
        cols = pl.ds(pl.multiple_of(h * HD, HD), HD)
        grad_key[...] = jnp.zeros_like(grad_key)
        grad_value[...] = jnp.zeros_like(grad_value)
        for first in range(0, slots, block):
            rows, seen = pl.ds(first, block), pl.ds(0, first + block)
            query, grad = heads[0, s, rows, cols], grad_heads[s, rows, cols]
            keys = heads[1, s, seen, cols]
            probs = head_probs(query, keys, first, lengths[s])
            grad_value[seen] += lax.dot_general(
                probs.astype(bf16), grad, TN, preferred_element_type=f32
            )
            back = lax.dot_general(
                grad, heads[2, s, seen, cols], NT, preferred_element_type=f32
            )
            centre = jnp.sum(probs * back, axis=-1, keepdims=True)
            scores = (probs * (back - centre)).astype(bf16)
            grads[0, s, rows, cols] = jnp.dot(
                scores, keys, preferred_element_type=f32
            ).astype(bf16)
            grad_key[seen] += lax.dot_general(scores, query, TN, preferred_element_type=f32)
        grads[1, s, :, cols] = grad_key[...].astype(bf16)
        grads[2, s, :, cols] = grad_value[...].astype(bf16)
        return carry

    lax.fori_loop(0, part // HD, one, 0)


def attention_block_kernel(
    n,
    tokens,
    cotangent,
    lengths,
    gain,
    shift,
    weight,
    bias,
    out_weight,
    out_bias,
    gain_two,
    shift_two,
    gathered,
    heads,
    mixed,
    hidden,
    normed,
    grad_all,
    buf,
    send,
    recv,
    keep_sem,
    grad_send,
    grad_recv,
    masked,
    mask_sem,
    *scratch,
):
    at = Place(n)
    seqs, rows, width = tokens.shape
    ring = Gather(at, rows, buf, send, recv)
    grad_ring = Gather(at, rows, grad_all, grad_send, grad_recv)
    line = Scatter(at, rows, *scratch)

    def mask_copy(s):
        return pltpu.make_async_copy(
            masked.at[s], grad_all.at[s, rows_of(at.me, rows)], mask_sem.at[s]
        )

    for s in range(seqs):
        def block(i, carry):
            first = pl.multiple_of(i * 16, 16)
            here = pl.ds(first, 16)
            values = norm_rows(tokens[s, here].astype(f32), gain[...], shift[...])
            buf[s, pl.ds(pl.multiple_of(at.me * rows + first, 16), 16)] = values.astype(bf16)
            slot = at.me * rows + first + lax.broadcasted_iota(jnp.int32, (16, width), 0)
            grad = jnp.where(slot < lengths[s], cotangent[s, here].astype(f32), 0.0)
            masked[s, here] = grad.astype(bf16)
            return carry

        lax.fori_loop(0, rows // 16, block, 0)
        mask_copy(s).start()
    at.greet()
    for s in range(seqs):
        mask_copy(s).wait()

    def keep(s, o):
        here = rows_of(o, 2 * rows)
        return pltpu.make_async_copy(buf.at[s, here], gathered.at[s, here], keep_sem.at[s, o])

    def project(s, o):
        ring.arrived(s, o, 1 - at.core)
        keep(s, o).start()
        here = rows_of(o, 2 * rows)
        for j in range(3):
            total = jnp.dot(buf[s, here], weight[j], preferred_element_type=f32)
            if j == 0:
                total = (total + bias[0:1]) * HD ** (-0.5)
            if j == 2:
                total = total + bias[1:2]
            heads[j, s, here] = total.astype(bf16)

    def final(s, there, total):
        values = tokens[s, there].astype(f32) + total + out_bias[...]
        hidden[s, there] = values
        normed[s, there] = norm_rows(values, gain_two[...], shift_two[...]).astype(bf16)

    def mix(s, o):
        attend(heads, lengths, mixed, min(512, n * rows), s)

    def project_out(s, o):
        here = rows_of(o, 2 * rows)
        for j in range(width // 512):
            cols = pl.ds(j * 512, 512)
            total = jnp.dot(mixed[s, here], out_weight[:, cols], preferred_element_type=f32)
            line.part[s, o, :, cols] = total.astype(bf16)
        line.share(s, o)

    def ops_of(c):
        chips = at.chips
        mixing = []
        for s in range(seqs):
            needs = [("heads", c, s, o) for o in range(chips)]
            mixing.append(((2, s, 0), (2, s, 0), needs, 6.0, [], [(0.0, ("mixed", c, s))]))
        return (
            gather_ops(c, chips, seqs, 0, "in", gate=True)
            + work_ops(
                c, chips, seqs, 1, lambda s, o: [("in", c, s, o, "both")], "heads", 1.0
            )
            + mixing
            + work_ops(
                c, chips, seqs, 3, lambda s, o: [("mixed", c, s)], "part", 1.0, far=True
            )
            + scatter_ops(c, chips, seqs, 4, "out", "part", last=4.0)
            + gather_ops(c, chips, seqs, 5, "grad", rank=6)
        )

    Plan(at, seqs, ops_of).run(
        {
            0: ring.relay,
            1: project,
            2: mix,
            3: project_out,
            4: functools.partial(line.pass_on, final),
            5: grad_ring.relay,
        }
    )
    ring.finish()
    line.finish()
    grad_ring.finish()

    def close(i, carry):
        s, o = i // at.chips, lax.rem(i, at.chips)
        grad_ring.arrived(s, o, 1 - at.core)
        keep(s, o).wait()
        return carry

    lax.fori_loop(0, seqs * at.chips, close, 0)


def whole(count):
    return [pl.BlockSpec(memory_space=VMEM)] * count


def attention_block(
    n,
    tokens,
    cotangent,
    lengths,
    gain,
    shift,
    weight,
    bias,
    out_weight,
    out_bias,
    gain_two,
    shift_two,
):
    seqs, rows, width = tokens.shape
    part = weight.shape[2]
    vmem = pl.BlockSpec(memory_space=VMEM)
    hbm = pl.BlockSpec(memory_space=pl.ANY)
    smem = pl.BlockSpec(memory_space=pltpu.SMEM)
    return pl.pallas_call(
        functools.partial(attention_block_kernel, n),
        out_shape=(
            jax.ShapeDtypeStruct((seqs, n * rows, width), bf16),
            jax.ShapeDtypeStruct((3, seqs, n * rows, part), bf16),
            jax.ShapeDtypeStruct((seqs, n * rows, part), bf16),
            jax.ShapeDtypeStruct((seqs, rows, width), f32),
            jax.ShapeDtypeStruct((seqs, rows, width), bf16),
            jax.ShapeDtypeStruct((seqs, n * rows, width), bf16),
        ),
        in_specs=[vmem, vmem, smem] + [vmem] * 8,
        out_specs=(hbm, vmem, vmem, vmem, vmem, hbm),
        scratch_shapes=[VMEM((seqs, n * rows, width), bf16)]
        + Gather.scratch(n, seqs)
        + [DMA((seqs, n // 2))]
        + Gather.scratch(n, seqs)
        + [VMEM((seqs, rows, width), bf16), DMA((seqs,))]
        + Scatter.scratch(n, seqs, rows, width),
        compiler_params=pltpu.CompilerParams(
            collective_id=0, has_side_effects=True, vmem_limit_bytes=60 * 2**20
        ),
        name="attention_block",
    )(
        tokens,
        cotangent,
        lengths,
        gain,
        shift,
        weight,
        bias,
        out_weight,
        out_bias,
        gain_two,
        shift_two,
    )


def heads_scatter_kernel(
    n,
    grads,
    weight,
    gathered,
    out_part,
    tokens,
    gain,
    hidden_grad,
    grad,
    sums_all,
    weight_grad,
    out_grad,
    bias_grad,
    *scratch,
):
    at = Place(n)
    seqs, rows, width = hidden_grad.shape
    line = Scatter(at, rows, *scratch[:7])
    weight_sum = GroupSum(at, width, *scratch[7:12], weight_grad)
    out_sum = GroupSum(at, out_part.shape[0], *scratch[12:17], out_grad, turn=1)
    small = SmallSum(at, *scratch[17:21], True)
    small_bias = SmallSum(at, *scratch[21:25], False)
    out_sum.tiles[0] = out_part[...]
    small.rows[0] = jnp.zeros(small.rows.shape[1:], f32)
    for row, j, scale in ((0, 0, HD ** (-0.5)), (1, 2, 1.0)):
        total = 0.0
        for s in range(seqs):
            total += jnp.sum(grads[j, s].astype(f32), axis=0, keepdims=True)
        small_bias.rows[0, row : row + 1] = scale * total
    at.greet(groups=True, cube=True)

    def final(s, there, total):
        back, terms = norm_rows_back(tokens[s, there].astype(f32), total, gain[...])
        grad[s, there] = hidden_grad[s, there] + back
        small.rows[0, 0:1] += jnp.sum(terms, axis=0, keepdims=True)
        small.rows[0, 1:2] += jnp.sum(total, axis=0, keepdims=True)

    scales = (HD ** (-0.5), 1.0, 1.0)

    def weight_tile(j):
        for first in range(0, width, 512):
            total = 0.0
            for s in range(seqs):
                total += lax.dot_general(
                    gathered[s, :, pl.ds(first, 512)],
                    grads[j, s],
                    TN,
                    preferred_element_type=f32,
                )
            weight_sum.tiles[j, pl.ds(first, 512)] = (scales[j] * total).astype(bf16)

    def work(s, o):
        here = rows_of(o, 2 * rows)
        for j in range(width // 512):
            cols = pl.ds(j * 512, 512)
            total = 0.0
            for i in range(3):
                total += scales[i] * lax.dot_general(
                    grads[i, s, here], weight[i, cols], NT, preferred_element_type=f32
                )
            line.part[s, o, :, cols] = total.astype(bf16)
        line.share(s, o)

    each = seqs * at.chips

    def weight_event(first, s, o):
        e = first + s * at.chips + o
        for j in range(3):
            pl.when(e == j)(functools.partial(weight_tile, j))
        weight_sum.event(e)

    def out_event(s, o):
        out_sum.event(s * at.chips + o)

    def code_of(kind, e):
        return (kind + e // each, e % each // at.chips, e % at.chips)

    def ops_of(c):
        chips = at.chips
        return (
            work_ops(c, chips, seqs, 0, lambda s, o: [], "part", 1.5, rank=0, far=True)
            + scatter_ops(c, chips, seqs, 1, "out", "part", last=4.0)
            + group_ops(
                c, at.group_bits, 3, PIECE, lambda e: code_of(2, e), 0, 0, 2.7, name="qkv"
            )
            + group_ops(
                c, at.group_bits, 1, PIECE, lambda e: code_of(5, e), 0, 1, 0.7, name="out_sum"
            )
        )

    actions = {0: work, 1: functools.partial(line.pass_on, final), 5: out_event}
    for i in range(3):
        actions[2 + i] = functools.partial(weight_event, i * each)
    Plan(at, seqs, ops_of).run(actions, small_bias.event)
    for e in range(small.phases + 1):
        small.event(e)
    sums_all[...] = small.rows[small.phases]
    bias_grad[...] = small_bias.rows[small_bias.phases]
    line.finish()
    weight_sum.finish()
    out_sum.finish()
    small.finish()
    small_bias.finish()


def heads_scatter(n, grads, weight, gathered, out_part, tokens, gain, hidden_grad):
    seqs, slots, part = grads.shape[1:]
    width = weight.shape[1]
    rows = slots // n
    dp = lax.axis_size("dp")
    vmem = pl.BlockSpec(memory_space=VMEM)
    hbm = pl.BlockSpec(memory_space=pl.ANY)
    return pl.pallas_call(
        functools.partial(heads_scatter_kernel, n),
        out_shape=(
            jax.ShapeDtypeStruct((seqs, rows, width), f32),
            jax.ShapeDtypeStruct((2, width), f32),
            jax.ShapeDtypeStruct((3, width, part), bf16),
            jax.ShapeDtypeStruct((1, part, width), bf16),
            jax.ShapeDtypeStruct((2, part), f32),
        ),
        in_specs=whole(7),
        out_specs=(vmem, vmem, hbm, hbm, vmem),
        scratch_shapes=Scatter.scratch(n, seqs, rows, width)
        + GroupSum.scratch(dp, 3, width, part)
        + GroupSum.scratch(dp, 1, part, width)
        + SmallSum.scratch(dp, n, 2, width, True)
        + SmallSum.scratch(dp, n, 2, part, False),
        compiler_params=pltpu.CompilerParams(
            collective_id=2, has_side_effects=True, vmem_limit_bytes=62 * 2**20
        ),
        name="heads_scatter",
    )(grads, weight, gathered, out_part, tokens, gain, hidden_grad)


def normal_cdf(values):
    x = jnp.clip(values * 0.7071067811865476, -3.832506856900711, 3.832506856900711)
    x2 = x * x
    top = 0.00022905065861350646
    for c in (0.0034082910107109506, 0.050955695062380861, 0.18520832239976145, 1.128379143519084):
        top = top * x2 + c
    low = -1.1791602954361697e-7
    for c in (
        0.000023547966471313185,
        0.0010179625278914885,
        0.014070470171167667,
        0.11098505178285362,
        0.49746925110067538,
        1.0,
    ):
        low = low * x2 + c
    return 0.5 + 0.5 * (x * top / low)


def mlp_kernel(
    n,
    normed,
    grad_all,
    up_weight,
    up_bias,
    down_weight,
    hidden,
    gain,
    mlp_part,
    hidden_grad,
    grad_low,
    sums,
    up_grad,
    up_bias_grad,
    down_grad,
    up_box,
    down_box,
    buf,
    send,
    recv,
    *scratch,
):
    at = Place(n)
    seqs, rows, width = normed.shape
    units_wide = up_weight.shape[1]
    line = Scatter(at, rows, *scratch[:7])
    act, pre, out_stage, out_sem, up_stage, down_stage, tile_sem, half_send, half_recv = scratch[7:]
    ring = Gather(at, rows, buf, send, recv)
    at.greet(groups=True)
    for s in range(seqs):
        buf[s, rows_of(at.me, rows)] = normed[s]
    up_bias_grad[...] = jnp.zeros_like(up_bias_grad)
    sums[...] = jnp.zeros_like(sums)
    ft = min(512, units_wide)

    def out_copy(s, o):
        return pltpu.make_async_copy(
            out_stage, mlp_part.at[s, rows_of(o, 2 * rows)], out_sem.at[0]
        )

    def work(s, o):
        ring.arrived(s, o, 1 - at.core)
        here = rows_of(o, 2 * rows)
        for j in range(units_wide // ft):
            cols = pl.ds(j * ft, ft)
            value = jnp.dot(buf[s, here], up_weight[:, cols], preferred_element_type=f32)
            value = value + up_bias[:, cols]
            spread = normal_cdf(value)
            act[s, here, cols] = (value * spread).astype(bf16)
            slope = spread + value * (0.3989422804014327 * jnp.exp(-0.5 * value * value))
            grad = lax.dot_general(
                grad_all[s, here], down_weight[cols], NT, preferred_element_type=f32
            )
            grad = (grad * slope).astype(bf16)
            pre[s, here, cols] = grad
            up_bias_grad[:, cols] += jnp.sum(grad.astype(f32), axis=0, keepdims=True)
        for j in range(width // 512):
            cols = pl.ds(j * 512, 512)
            line.part[s, o, :, cols] = lax.dot_general(
                pre[s, here], up_weight[cols], NT, preferred_element_type=f32
            ).astype(bf16)
        line.share(s, o)
        pl.when((s > 0) | (o != at.chip))(lambda: out_copy(s, o).wait())
        for j in range(width // 512):
            cols = pl.ds(j * 512, 512)
            out_stage[:, cols] = jnp.dot(
                act[s, here], down_weight[:, cols], preferred_element_type=f32
            ).astype(bf16)
        out_copy(s, o).start()

    def final(s, there, total):
        back, terms = norm_rows_back(hidden[s, there], total, gain[...])
        first = pl.multiple_of(at.me * rows + there.start, 16)
        grad_out = grad_all[s, pl.ds(first, there.size)].astype(f32)
        grad = grad_out + back
        hidden_grad[s, there] = grad
        grad_low[s, there] = grad.astype(bf16)
        add_row(sums, 0, terms)
        add_row(sums, 1, total)
        add_row(sums, 2, grad)
        add_row(sums, 3, grad_out)

    kinds = ((down_stage, down_grad, down_box, 0), (up_stage, up_grad, up_box, 1))

    def tile_copy(kind, t):
        stage, grad, box, turn = kinds[kind]
        return pltpu.make_async_copy(stage, grad.at[t], tile_sem.at[kind])

    def tile_half(kind, t):
        stage, grad, box, turn = kinds[kind]
        half = box.shape[1]
        which = (t + turn) % at.group_bits
        peer, mine = at.group_peer(which)
        return pltpu.make_async_remote_copy(
            src_ref=grad.at[t, rows_of(1 - mine, half)],
            dst_ref=box.at[t],
            send_sem=half_send.at[kind, t],
            recv_sem=half_recv.at[kind, t],
            device_id={"dp": peer},
            device_id_type=MESH,
        )

    def tile_sent(kind, t):
        tile_copy(kind, t).wait()
        tile_half(kind, t).start()

    order = [(i % 2, i // 2) for i in range(8)]

    def weight_tile(i):
        for j, (kind, t) in enumerate(order):
            @pl.when(i == j)
            def _():
                stage = kinds[kind][0]
                cols = pl.ds(t * stage.shape[0], stage.shape[0])
                total = 0.0
                for s in range(seqs):
                    if kind == 0:
                        left, right = act[s, :, cols], grad_all[s]
                    else:
                        left, right = buf[s, :, cols], pre[s]
                    total += lax.dot_general(left, right, TN, preferred_element_type=f32)
                if j >= 1:
                    tile_sent(*order[j - 1])
                stage[...] = total.astype(bf16)
                tile_copy(kind, t).start()

    def tile_work(s, o):
        weight_tile(s * at.chips + o)

    def ops_of(c):
        chips = at.chips
        units = [(s, o) for s in range(seqs) for o in range(chips)]
        ops = (
            gather_ops(c, chips, seqs, 0, "in")
            + scatter_ops(c, chips, seqs, 1, "back", "part", last=4.0)
            + work_ops(
                c, chips, seqs, 2, lambda s, o: [("in", c, s, o, "both")], "part", 5.7
            )
        )
        for i in range(len(ops)):
            rank, code, needs, time, sends, gives = ops[i]
            if code[0] == 2 and code[1:] != (0, c):
                ops[i] = (rank, code, needs + [("first", c)], time, sends, gives)
            if code == (2, 0, c):
                ops[i] = (rank, code, needs, time, sends, gives + [(0.0, ("first", c))])
        for e in range(len(order)):
            needs = [("part", c, s, o) for s, o in units]
            needs += [("tile", c, e - 1)] if e else []
            sends = [("axis%d" % (e % 2), c, ("half", c, e), PIECE)]
            code = (3, e // chips, e % chips)
            ops.append(((4, e, 0), code, needs, 2.7, sends, [(0.0, ("tile", c, e))]))
        return ops

    Plan(at, seqs, ops_of).run(
        {0: ring.relay, 1: functools.partial(line.pass_on, final), 2: work, 3: tile_work}
    )
    tile_sent(*order[7])
    ring.finish()
    line.finish()
    for kind, t in order:
        tile_half(kind, t).wait()
    out_copy(0, 0).wait()


def mlp_block(n, normed, grad_all, up_weight, up_bias, down_weight, hidden, gain):
    seqs, rows, width = normed.shape
    slots = n * rows
    units = up_weight.shape[1]
    hbm = pl.BlockSpec(memory_space=pl.ANY)
    vmem = pl.BlockSpec(memory_space=VMEM)
    down_size, up_size = units // 4, width // 4
    return pl.pallas_call(
        functools.partial(mlp_kernel, n),
        out_shape=(
            jax.ShapeDtypeStruct((seqs, slots, width), bf16),
            jax.ShapeDtypeStruct((seqs, rows, width), f32),
            jax.ShapeDtypeStruct((seqs, rows, width), bf16),
            jax.ShapeDtypeStruct((4, width), f32),
            jax.ShapeDtypeStruct((4, up_size, units), bf16),
            jax.ShapeDtypeStruct((1, units), f32),
            jax.ShapeDtypeStruct((4, down_size, width), bf16),
            jax.ShapeDtypeStruct((4, up_size // 2, units), bf16),
            jax.ShapeDtypeStruct((4, down_size // 2, width), bf16),
        ),
        in_specs=whole(7),
        out_specs=(hbm, vmem, vmem, vmem, hbm, vmem, hbm, hbm, hbm),
        scratch_shapes=[VMEM((seqs, slots, width), bf16)]
        + Gather.scratch(n, seqs)
        + Scatter.scratch(n, seqs, rows, width)
        + [
            VMEM((seqs, slots, units), bf16),
            VMEM((seqs, slots, units), bf16),
            VMEM((2 * rows, width), bf16),
            DMA((1,)),
            VMEM((up_size, units), bf16),
            VMEM((down_size, width), bf16),
            DMA((2,)),
            DMA((2, 4)),
            DMA((2, 4)),
        ],
        compiler_params=pltpu.CompilerParams(
            collective_id=3, has_side_effects=True, vmem_limit_bytes=62 * 2**20
        ),
        name="mlp_block",
    )(normed, grad_all, up_weight, up_bias, down_weight, hidden, gain)


def attn_grad_kernel(
    n,
    grad,
    mlp_part,
    hidden,
    bias,
    weight,
    mixed,
    sums,
    up_bias_part,
    up_part,
    down_part,
    up_box,
    down_box,
    lengths,
    heads,
    output,
    grads,
    weight_grad,
    sums_all,
    up_bias_grad,
    up_grad,
    down_grad,
    buf,
    send,
    recv,
    *scratch,
):
    at = Place(n)
    seqs, rows, width = grad.shape
    line = Scatter(at, rows, *scratch[:7])
    load_sem, tile_sem, box_sem = scratch[7:10]
    ring = Gather(at, rows, buf, send, recv)
    up_sum = GroupSum(at, up_part.shape[1], *scratch[10:15], up_grad, turn=1, skip=1)
    down_sum = GroupSum(at, down_part.shape[1], *scratch[15:20], down_grad, skip=1)
    small = SmallSum(at, *scratch[20:24], True)
    small_bias = SmallSum(at, *scratch[24:28], False)
    grad_heads, grad_key, grad_value = scratch[28:]
    pairs = ((up_sum, up_part, up_box), (down_sum, down_part, down_box))

    def tile_load(i, t):
        group, part, box = pairs[i]
        half = box.shape[1]
        return (
            pltpu.make_async_copy(
                part.at[t, group.span(group.base(t, 1), half)], group.tiles.at[t], tile_sem.at[i, t]
            ),
            pltpu.make_async_copy(box.at[t], group.box(t, 0), box_sem.at[i, t]),
        )

    def tile_loaded(i, t):
        for copy in tile_load(i, t):
            copy.wait()

    for t in range(4):
        for i in range(2):
            for copy in tile_load(i, t):
                copy.start()
    small.rows[0] = sums[...]
    small_bias.rows[0] = up_bias_part[...]

    def load(s, o):
        return pltpu.make_async_copy(
            mlp_part.at[s, rows_of(o, 2 * rows)], line.part.at[s, o], load_sem.at[s, o]
        )

    def load_one(i, carry):
        load(i // at.chips, lax.rem(i, at.chips)).start()
        return carry

    each = seqs * at.chips
    lax.fori_loop(0, each, load_one, 0)
    for s in range(seqs):
        buf[s, rows_of(at.me, rows)] = grad[s]
    at.greet(groups=True, cube=True)

    def final(s, there, total):
        output[s, there] = (hidden[s, there] + total + bias[...]).astype(bf16)

    def share(s, o):
        load(s, o).wait()
        line.share(s, o)

    def work(s, o):
        ring.arrived(s, o, 1 - at.core)
        here = rows_of(o, 2 * rows)
        grad_heads[s, here] = lax.dot_general(
            buf[s, here], weight[...], NT, preferred_element_type=f32
        ).astype(bf16)

    def back(s, o):
        block = min(512, n * rows)
        attend_back(heads, grad_heads, lengths, grads, grad_key, grad_value, block, s)

    def event(i, s, o):
        e = s * at.chips + o
        for j in range(2):
            group = pairs[j][0]
            group.event(e + i * each, functools.partial(tile_loaded, j))

    def ops_of(c):
        chips = at.chips
        code_of = lambda e: (4 + e // each, e % each // chips, e % chips)
        backs = []
        for s in range(seqs):
            needs = [("done", c, s, o) for o in range(chips)]
            backs.append(((4, s, 0), (6, s, 0), needs, 8.0, [], []))
        return backs + (
            gather_ops(c, chips, seqs, 0, "in")
            + scatter_ops(c, chips, seqs, 1, "out", "part", last=4.0)
            + work_ops(c, chips, seqs, 2, lambda s, o: [("in", c, s, o, "both")], "done", 1.0)
            + work_ops(c, chips, seqs, 3, lambda s, o: [], "part", 0.3, rank=0, far=True)
            + group_ops(c, at.group_bits, 4, PIECE, code_of, 1, 0, 0.7)
        )

    actions = {0: ring.relay, 1: functools.partial(line.pass_on, final), 2: work, 3: share}
    for i in range(2):
        actions[4 + i] = functools.partial(event, i)
    actions[6] = back

    def beside(k):
        pl.when(lax.rem(k, 3) == 0)(lambda: small.event(k // 3))
        small_bias.event(k)

    Plan(at, seqs, ops_of).run(actions, beside)
    sums_all[...] = small.rows[small.phases]
    up_bias_grad[...] = small_bias.rows[small_bias.phases]
    for j in range(width // 512):
        cols = pl.ds(j * 512, 512)
        total = 0.0
        for s in range(seqs):
            total += lax.dot_general(mixed[s], buf[s, :, cols], TN, preferred_element_type=f32)
        weight_grad[:, cols] = total.astype(bf16)
    ring.finish()
    line.finish()
    small.finish()
    small_bias.finish()
    up_sum.finish()
    down_sum.finish()


def attn_grad(
    n,
    grad,
    mlp_part,
    hidden,
    bias,
    weight,
    mixed,
    sums,
    up_bias_part,
    up_part,
    down_part,
    up_box,
    down_box,
    lengths,
    heads,
):
    seqs, rows, width = grad.shape
    slots = n * rows
    part = weight.shape[0]
    units = up_part.shape[2]
    dp = lax.axis_size("dp")
    vmem = pl.BlockSpec(memory_space=VMEM)
    hbm = pl.BlockSpec(memory_space=pl.ANY)
    return pl.pallas_call(
        functools.partial(attn_grad_kernel, n),
        out_shape=(
            jax.ShapeDtypeStruct((seqs, rows, width), bf16),
            jax.ShapeDtypeStruct(heads.shape, bf16),
            jax.ShapeDtypeStruct((part, width), bf16),
            jax.ShapeDtypeStruct(sums.shape, f32),
            jax.ShapeDtypeStruct((1, units), f32),
            jax.ShapeDtypeStruct(up_part.shape, bf16),
            jax.ShapeDtypeStruct(down_part.shape, bf16),
        ),
        in_specs=[vmem, hbm]
        + [vmem] * 6
        + [hbm] * 4
        + [pl.BlockSpec(memory_space=pltpu.SMEM), vmem],
        out_specs=(vmem,) * 5 + (hbm, hbm),
        scratch_shapes=[VMEM((seqs, slots, width), bf16)]
        + Gather.scratch(n, seqs)
        + Scatter.scratch(n, seqs, rows, width)
        + [DMA((seqs, n // 2)), DMA((2, 4)), DMA((2, 4))]
        + GroupSum.scratch(dp, 4, width // 4, units, 1)
        + GroupSum.scratch(dp, 4, units // 4, width, 1)
        + SmallSum.scratch(dp, n, sums.shape[0], width, True)
        + SmallSum.scratch(dp, n, 1, units, False)
        + [VMEM((seqs, slots, part), bf16), VMEM((slots, HD), f32), VMEM((slots, HD), f32)],
        compiler_params=pltpu.CompilerParams(
            collective_id=4, has_side_effects=True, vmem_limit_bytes=62 * 2**20
        ),
        name="attn_grad",
    )(
        grad,
        mlp_part,
        hidden,
        bias,
        weight,
        mixed,
        sums,
        up_bias_part,
        up_part,
        down_part,
        up_box,
        down_box,
        lengths,
        heads,
    )


def body(
    tokens,
    cotangent,
    lengths,
    ln1_gain,
    ln1_shift,
    qkv_weight,
    qkv_bias,
    out_weight,
    out_bias,
    ln2_gain,
    ln2_shift,
    up_weight,
    up_bias,
    down_weight,
    down_bias,
):
    n = lax.axis_size("tensor")
    gathered_one, heads, mixed_heads, hidden_state, normed_two, grad_mlp = attention_block(
        n,
        tokens,
        cotangent,
        lengths,
        ln1_gain[None],
        ln1_shift[None],
        qkv_weight,
        qkv_bias,
        out_weight,
        out_bias[None],
        ln2_gain[None],
        ln2_shift[None],
    )
    (
        mlp_part,
        hidden_grad,
        grad_attn,
        sums,
        up_part,
        up_bias_part,
        down_part,
        up_box,
        down_box,
    ) = mlp_block(
        n, normed_two, grad_mlp, up_weight, up_bias[None], down_weight, hidden_state, ln2_gain[None]
    )
    output, grads, out_part, sums, up_bias_grad, up_weight_grad, down_weight_grad = attn_grad(
        n,
        grad_attn,
        mlp_part,
        hidden_state,
        down_bias[None],
        out_weight,
        mixed_heads,
        sums,
        up_bias_part,
        up_part,
        down_part,
        up_box,
        down_box,
        lengths,
        heads,
    )
    ln2_gain_grad, ln2_shift_grad, out_bias_grad, down_bias_grad = [sums[i] for i in range(4)]
    input_grad, sums_one, qkv_weight_grad, out_weight_grad, qkv_bias_grad = heads_scatter(
        n, grads, qkv_weight, gathered_one, out_part, tokens, ln1_gain[None], hidden_grad
    )
    up_weight_grad = up_weight_grad.astype(jnp.float32).reshape(up_weight.shape)
    down_weight_grad = down_weight_grad.astype(jnp.float32).reshape(down_weight.shape)
    return (
        output,
        input_grad,
        sums_one[0],
        sums_one[1],
        qkv_weight_grad.astype(jnp.float32),
        qkv_bias_grad,
        out_weight_grad[0].astype(jnp.float32),
        out_bias_grad,
        ln2_gain_grad,
        ln2_shift_grad,
        up_weight_grad,
        up_bias_grad[0],
        down_weight_grad,
        down_bias_grad,
    )


def solution(mesh):
    in_specs = (
        P("dp", "tensor", None),
        P("dp", "tensor", None),
        P("dp"),
        P(),
        P(),
        P(None, None, "tensor"),
        P(None, "tensor"),
        P("tensor", None),
        P(),
        P(),
        P(),
        P(None, "tensor"),
        P("tensor"),
        P("tensor", None),
        P(),
    )
    out_specs = (
        P("dp", "tensor", None),
        P("dp", "tensor", None),
        P(),
        P(),
        P(None, None, "tensor"),
        P(None, "tensor"),
        P("tensor", None),
        P(),
        P(),
        P(),
        P(None, "tensor"),
        P("tensor"),
        P("tensor", None),
        P(),
    )
    return jax.shard_map(body, mesh=mesh, in_specs=in_specs, out_specs=out_specs, check_vma=False)
```

```python
import functools
import heapq

import jax
import jax.numpy as jnp
from jax import lax
from jax.experimental import pallas as pl
from jax.experimental.pallas import tpu as pltpu
from jax.sharding import PartitionSpec as P

HD = 128


norm_epsilon = 1e-05

MESH = pl.DeviceIdType.MESH
UP, DOWN, SIDE = 0, 1, 2
VMEM = pltpu.VMEM
DMA = pltpu.SemaphoreType.DMA
f32 = jnp.float32
bf16 = jnp.bfloat16
NT = (((1,), (1,)), ((), ()))
TN = (((0,), (0,)), ((), ()))


def order_of(chips, ops_of, backlog=8.0, hop=1.5):
    todo = [sorted(ops_of(c)) for c in range(chips)]
    order = [[] for _ in range(chips)]
    free, busy, have, queue = {}, [False] * chips, set(), []

    def push(time, what):
        heapq.heappush(queue, (time, len(pushed), what))
        pushed.append(0)

    pushed = []
    for c in range(chips):
        push(0.0, (c, None, ()))
    now = 0.0
    while queue:
        now, _, (c, signal, after) = heapq.heappop(queue)
        if signal is not None:
            have.add(signal)
        for part in after:
            if part[0] == "free":
                busy[c] = False
            elif part[0] == "send":
                _, link, to, sig, span = part
                start = max(now, free.get((c, link), 0.0))
                free[c, link] = start + span
                push(start + span + hop, (to, sig, ()))
            else:
                push(now + part[1], (c, part[2], ()))
        if busy[c]:
            continue
        for op in todo[c]:
            rank, code, needs, time, sends, gives = op
            if any(need not in have for need in needs):
                continue
            late = max([free.get((c, send[0]), 0.0) - now for send in sends], default=0.0)
            if late > backlog:
                push(now + late - backlog, (c, None, ()))
                continue
            todo[c].remove(op)
            order[c].append(code)
            busy[c] = True
            ends = [("free",)] + [("send",) + send for send in sends]
            push(now + time, (c, None, ends + [("give",) + give for give in gives]))
            break
    assert not any(todo)
    return order, now


PIECE = 12.0


def gather_ops(c, chips, seqs, kind, name, rank=0, time=0.5, gate=False, own=None):
    ops = []
    for s in range(seqs):
        for o in range(chips):
            up, down = [], []
            if o <= c < chips - 1:
                up.append((c + 1, c + 1, (name, c + 1, s, o), PIECE))
            if o >= c > 0:
                down.append((c - 1, c - 1, (name, c - 1, s, o), PIECE))
            both = [(3.0, (name, c, s, o, "both"))]
            if own is not None and o == c and s > 0:
                ops.append(((rank, s, -1), (own[0], s, o), [], time, [], both))
                for sends, which, others in ((up, own[1], range(c)), (down, own[2], range(c + 1, chips))):
                    needs = [(name, c, t, other) for t in (s - 1, s) for other in others]
                    if sends:
                        ops.append(((rank, s, chips), (which, s, o), needs, time, sends, []))
                continue
            needs = [] if o == c else [(name, c, s, o)]
            if gate and o == c and s > 0:
                for other in range(chips):
                    if other < c < chips - 1 or other > c > 0:
                        needs.append((name, c, s - 1, other))
            ops.append(((rank, s, abs(o - c)), (kind, s, o), needs, time, up + down, both))
    return ops


def scatter_ops(c, chips, seqs, kind, name, part, rank=1, time=1.3, last=2.0):
    ops = []
    for s in range(seqs):
        for o in range(chips):
            needs = [(part, c, s, o)]
            if o >= c > 0:
                needs.append((name, c, s, o, "below"))
            if o <= c < chips - 1:
                needs.append((name, c, s, o, "above"))
            sends = []
            if o > c:
                sends = [(c + 1, c + 1, (name, c + 1, s, o, "below"), PIECE)]
            if o < c:
                sends = [(c - 1, c - 1, (name, c - 1, s, o, "above"), PIECE)]
            order = (rank, s, -abs(o - c)) if o != c else (8, s, 0)
            ops.append((order, (kind, s, o), needs, last if o == c else time, sends, []))
    return ops


def work_ops(c, chips, seqs, kind, needs_of, gives, time, rank=2, far=False):
    return [
        (
            (rank, s, -abs(o - c) if far else abs(o - c)),
            (kind, s, o),
            needs_of(s, o),
            time,
            [],
            [(3.0, (gives, c, s, o))],
        )
        for s in range(seqs)
        for o in range(chips)
    ]


def group_ops(c, bits, count, span, code_of, skip, turns, first_time, rank=3, name="group"):
    ops = []
    for t in range(count):
        for stage in range(skip, 2 * bits + 1):
            needs, sends = [], []
            for turn in turns:
                if stage > skip:
                    needs.append((name, c, turn, t, stage))
                if stage < 2 * bits:
                    i = stage if stage < bits else 2 * bits - 1 - stage
                    axis = "axis%d" % ((t + turn + i) % bits)
                    sends.append((axis, c, (name, c, turn, t, stage + 1), span / 2**i))
            time = first_time if stage == 0 else 0.8 * len(turns)
            code = code_of((stage - skip) * count + t)
            ops.append(((rank, stage, t), code, needs, time, sends, []))
    return ops


class Plan:
    def __init__(self, at, seqs, ops_of):
        chips = at.chips
        order, self.length = order_of(chips, ops_of)
        self.per, self.each, self.chips, self.seqs = 1024, 3, chips, seqs
        self.count = max(len(codes) for codes in order)
        idle = self.per // (seqs * chips) - 1
        rows = []
        for codes in order:
            assert all(kind < idle for kind, s, o in codes)
            flat = [(kind * seqs + s) * chips + o for kind, s, o in codes]
            flat += [idle * seqs * chips] * (self.count - len(flat) + self.each)
            rows.append(
                [
                    sum(flat[i + j] * self.per**j for j in range(self.each))
                    for i in range(0, self.count, self.each)
                ]
            )
        self.words = []
        for w in range(len(rows[0])):
            word = jnp.int32(rows[0][w])
            for c in range(1, chips):
                word = jnp.where(at.chip == c, jnp.int32(rows[c][w]), word)
            self.words.append(word)

    def step(self, k):
        which, slot = k // self.each, lax.rem(k, self.each)
        word = jnp.int32(0)
        for w, value in enumerate(self.words):
            word = jnp.where(which == w, value, word)
        code = word
        for j in range(1, self.each):
            code = jnp.where(slot == j, word // self.per**j, code)
        code = lax.rem(code, self.per)
        each = self.seqs * self.chips
        return code // each, lax.rem(code, each) // self.chips, lax.rem(code, self.chips)

    def run(self, actions, beside=None):
        def step(k, carry):
            kind, s, o = self.step(k)
            for which, action in actions.items():
                pl.when(kind == which)(functools.partial(action, s, o))
            if beside is not None:
                beside(k)
            return carry

        lax.fori_loop(0, self.count, step, 0)


class Place:
    def __init__(self, n):
        self.n, self.chips = n, n // 2
        self.me = lax.axis_index("tensor")
        self.chip, self.core = self.me // 2, lax.rem(self.me, 2)
        self.side = self.me + 1 - 2 * self.core
        self.below = self.chip > 0
        self.above = self.chip < self.chips - 1
        self.group = lax.axis_index("dp")
        self.group_bits = lax.axis_size("dp").bit_length() - 1
        self.bits = n.bit_length() - 1

    def group_peer(self, q):
        mine = lax.rem(self.group // 2**q, 2)
        return self.group + (1 - 2 * mine) * 2**q, mine

    def peer(self, q):
        mine = lax.rem(self.me // 2**q, 2)
        return self.me + (1 - 2 * mine) * 2**q

    def greet(self, groups=False, cube=False, everyone=False):
        barrier = pltpu.get_barrier_semaphore()

        def tell(target):
            pl.semaphore_signal(
                barrier, inc=1, device_id={"tensor": target}, device_id_type=MESH
            )

        tell(self.side)
        pl.when(self.below)(lambda: tell(self.me - 2))
        pl.when(self.above)(lambda: tell(self.me + 2))
        peers = 1 + self.below.astype(jnp.int32) + self.above.astype(jnp.int32)
        if groups:
            for q in range(self.group_bits):
                pl.semaphore_signal(
                    barrier, inc=1, device_id={"dp": self.group_peer(q)[0]}, device_id_type=MESH
                )
            peers = peers + self.group_bits
        if everyone:
            for other in range(1, self.n):
                tell(lax.rem(self.me + other, self.n))
            for other in range(1, 2**self.group_bits):
                peer = lax.rem(self.group + other, 2**self.group_bits)
                pl.semaphore_signal(barrier, inc=1, device_id={"dp": peer}, device_id_type=MESH)
            peers = peers + (self.n - 1 + 2**self.group_bits - 1)
        if cube:
            for q in range(self.bits):
                tell(self.peer(q))
            peers = peers + self.bits
        pl.semaphore_wait(barrier, peers)


def rows_of(index, rows):
    return pl.ds(pl.multiple_of(index * rows, rows), rows)


class Gather:
    def __init__(self, at, rows, buf, send, recv):
        self.at, self.rows, self.buf, self.send, self.recv = at, rows, buf, send, recv
        self.seqs = buf.shape[0]

    @staticmethod
    def scratch(n, seqs):
        return [DMA((3, seqs, n // 2)), DMA((seqs, n))]

    def piece(self, s, o, k):
        return self.buf.at[s, rows_of(2 * o + k, self.rows)]

    def copy(self, s, o, kind):
        at = self.at
        target = (at.me + 2, at.me - 2, at.side)[kind]
        piece = self.piece(s, o, at.core)
        return pltpu.make_async_remote_copy(
            src_ref=piece,
            dst_ref=piece,
            send_sem=self.send.at[kind, s, o],
            recv_sem=self.recv.at[s, 2 * o + at.core],
            device_id={"tensor": target},
            device_id_type=MESH,
        )

    def arrived(self, s, o, k):
        at = self.at
        piece = self.piece(s, o, k)
        pltpu.make_async_remote_copy(
            src_ref=piece,
            dst_ref=piece,
            send_sem=self.send.at[SIDE, s, o],
            recv_sem=self.recv.at[s, 2 * o + k],
            device_id={"tensor": at.side},
            device_id_type=MESH,
        ).wait_recv()

    def relay(self, s, o):
        at = self.at
        pl.when(o != at.chip)(lambda: self.arrived(s, o, at.core))
        pl.when((o <= at.chip) & at.above)(lambda: self.copy(s, o, UP).start())
        pl.when((o >= at.chip) & at.below)(lambda: self.copy(s, o, DOWN).start())
        self.copy(s, o, SIDE).start()

    def own(self, kind, s, o):
        self.copy(s, o, kind).start()

    def owns(self, kinds):
        return {
            which: functools.partial(self.own, kind)
            for which, kind in zip(kinds, (SIDE, UP, DOWN))
        }

    def finish(self):
        at = self.at

        def one(i, carry):
            s, o = i // at.chips, lax.rem(i, at.chips)
            pl.when((o <= at.chip) & at.above)(lambda: self.copy(s, o, UP).wait_send())
            pl.when((o >= at.chip) & at.below)(lambda: self.copy(s, o, DOWN).wait_send())
            self.copy(s, o, SIDE).wait_send()
            return carry

        lax.fori_loop(0, self.seqs * at.chips, one, 0)


class Scatter:
    def __init__(self, at, rows, part, side, link, side_send, side_recv, send, recv):
        self.at, self.rows = at, rows
        self.part, self.side, self.link = part, side, link
        self.side_send, self.side_recv, self.send, self.recv = side_send, side_recv, send, recv
        self.seqs = part.shape[0]

    @staticmethod
    def scratch(n, seqs, rows, width):
        chips = n // 2
        return [
            VMEM((seqs, chips, 2 * rows, width), bf16),
            VMEM((seqs, chips, rows, width), bf16),
            VMEM((seqs, chips + 1, rows, width), bf16),
            DMA((seqs, chips)),
            DMA((seqs, chips)),
            DMA((seqs, chips)),
            DMA((seqs, chips + 1)),
        ]

    def side_copy(self, s, o):
        at = self.at
        return pltpu.make_async_remote_copy(
            src_ref=self.part.at[s, o, rows_of(1 - at.core, self.rows)],
            dst_ref=self.side.at[s, o],
            send_sem=self.side_send.at[s, o],
            recv_sem=self.side_recv.at[s, o],
            device_id={"tensor": at.side},
            device_id_type=MESH,
        )

    def link_copy(self, s, o, slot, target):
        return pltpu.make_async_remote_copy(
            src_ref=self.part.at[s, o, rows_of(self.at.core, self.rows)],
            dst_ref=self.link.at[s, slot],
            send_sem=self.send.at[s, o],
            recv_sem=self.recv.at[s, slot],
            device_id={"tensor": target},
            device_id_type=MESH,
        )

    def share(self, s, o):
        self.side_copy(s, o).start()

    def blocks(self, body):
        step = 16
        lax.fori_loop(0, self.rows // step, lambda i, c: (body(pl.multiple_of(i * step, step), step), c)[1], 0)

    def add_up(self, s, o, slots):
        base = self.at.core * self.rows

        def body(first, step):
            here = pl.ds(pl.multiple_of(base + first, step), step)
            there = pl.ds(first, step)
            total = self.part[s, o, here].astype(f32) + self.side[s, o, there].astype(f32)
            for slot in slots:
                total += self.link[s, slot, there].astype(f32)
            self.part[s, o, here] = total.astype(bf16)

        self.blocks(body)

    def pass_on(self, final, s, o):
        at = self.at
        self.side_copy(s, o).wait_recv()

        @pl.when(o > at.chip)
        def _():
            @pl.when(at.below)
            def _():
                self.link_copy(s, o, o, at.me).wait_recv()
                self.add_up(s, o, [o])

            pl.when(jnp.logical_not(at.below))(lambda: self.add_up(s, o, []))
            self.link_copy(s, o, o, at.me + 2).start()

        @pl.when(o < at.chip)
        def _():
            @pl.when(at.above)
            def _():
                self.link_copy(s, o, o, at.me).wait_recv()
                self.add_up(s, o, [o])

            pl.when(jnp.logical_not(at.above))(lambda: self.add_up(s, o, []))
            slot = jnp.where(o == at.chip - 1, at.chips, o)
            self.link_copy(s, o, slot, at.me - 2).start()

        @pl.when(o == at.chip)
        def _():
            pl.when(at.below)(lambda: self.link_copy(s, o, o, at.me).wait_recv())
            pl.when(at.above)(lambda: self.link_copy(s, o, at.chips, at.me).wait_recv())
            for slot, used in ((o, at.below), (at.chips, at.above)):
                @pl.when(jnp.logical_not(used))
                def _():
                    def clear(first, step):
                        self.link[s, slot, pl.ds(first, step)] = jnp.zeros(
                            (step, self.link.shape[-1]), bf16
                        )

                    self.blocks(clear)
            base = at.core * self.rows

            def body(first, step):
                here = pl.ds(pl.multiple_of(base + first, step), step)
                there = pl.ds(first, step)
                total = self.part[s, o, here].astype(f32) + self.side[s, o, there].astype(f32)
                total += self.link[s, o, there].astype(f32)
                total += self.link[s, at.chips, there].astype(f32)
                final(s, there, total)

            self.blocks(body)

    def finish(self):
        at = self.at

        def one(i, carry):
            s, o = i // at.chips, lax.rem(i, at.chips)
            self.side_copy(s, o).wait_send()
            pl.when(o != at.chip)(lambda: self.link_copy(s, o, o, at.side).wait_send())
            return carry

        lax.fori_loop(0, self.seqs * at.chips, one, 0)


class GroupSum:
    def __init__(self, at, rows, tiles, inbox, send, recv, keep_sem, out, turn=0, skip=0):
        self.at, self.tiles, self.inbox, self.send, self.recv = at, tiles, inbox, send, recv
        self.keep_sem, self.out, self.skip, self.turn, self.rows = keep_sem, out, skip, turn, rows
        self.bits = at.group_bits
        self.count = send.shape[0]

    @staticmethod
    def scratch(dp, count, rows, width, skip=0):
        phases = 2 * (dp.bit_length() - 1)
        return [
            VMEM((count, rows >> skip, width), bf16),
            VMEM((count, rows - rows // dp, width), bf16),
            DMA((count, phases)),
            DMA((count, phases)),
            DMA((count,)),
        ]

    def peer(self, t, i):
        which = lax.rem(t + i + self.turn, self.bits)
        peer, mine = 0, 0
        for q in range(self.bits):
            other, bit = self.at.group_peer(q)
            peer = peer + jnp.where(which == q, other, 0)
            mine = mine + jnp.where(which == q, bit, 0)
        return peer, mine

    def base(self, t, i):
        first = 0
        for p in range(i):
            first = first + self.peer(t, p)[1] * (self.rows >> (p + 1))
        return first

    def span(self, first, size):
        return pl.ds(pl.multiple_of(first, 16), size)

    def tile(self, t, first, size):
        return self.tiles.at[t, self.span(first - self.base(t, self.skip), size)]

    def box(self, t, i):
        return self.inbox.at[t, pl.ds(self.rows - (self.rows >> i), self.rows >> (i + 1))]

    def remote(self, source, target, t, phase, peer):
        return pltpu.make_async_remote_copy(
            src_ref=source,
            dst_ref=target,
            send_sem=self.send.at[t, phase],
            recv_sem=self.recv.at[t, phase],
            device_id={"dp": peer},
            device_id_type=MESH,
        )

    def halve(self, t, i):
        peer, mine = self.peer(t, i)
        half = self.rows >> (i + 1)
        source = self.tile(t, self.base(t, i) + (1 - mine) * half, half)
        return self.remote(source, self.box(t, i), t, i, peer)

    def add(self, t, i):
        half = self.rows >> (i + 1)
        keep = self.base(t, i + 1) - self.base(t, self.skip)
        box = self.rows - (self.rows >> i)

        def body(j, carry):
            here = self.span(keep + j * 16, 16)
            there = self.span(box + j * 16, 16)
            total = self.tiles[t, here].astype(f32) + self.inbox[t, there].astype(f32)
            self.tiles[t, here] = total.astype(bf16)
            return carry

        lax.fori_loop(0, half // 16, body, 0)

    def keep(self, t):
        first, size = self.base(t, self.bits), self.rows >> self.bits
        return pltpu.make_async_copy(
            self.tile(t, first, size), self.out.at[t, self.span(first, size)], self.keep_sem.at[t]
        )

    def double(self, t, i, back=False):
        peer, mine = self.peer(t, i)
        half = self.rows >> (i + 1)
        first = self.base(t, i) + ((1 - mine) if back else mine) * half
        piece = self.out.at[t, self.span(first, half)]
        source = piece
        if i == self.bits - 1 and not back:
            source = self.tile(t, first, half)
        return self.remote(source, piece, t, 2 * self.bits - 1 - i, peer)

    def events(self):
        return self.count * (2 * self.bits + 1 - self.skip)

    def event(self, e, loaded=None):
        k, t = e // self.count + self.skip, lax.rem(e, self.count)
        bits = self.bits

        def at_stage(stage):
            if stage == self.skip and loaded is not None:
                loaded(t)
            if stage == 0:
                self.halve(t, 0).start()
            elif stage <= bits:
                if stage > self.skip:
                    self.halve(t, stage - 1).wait_recv()
                self.add(t, stage - 1)
                if stage < bits:
                    self.halve(t, stage).start()
                else:
                    self.keep(t).start()
                    self.double(t, bits - 1).start()
            else:
                i = 2 * bits - stage
                self.double(t, i, back=True).wait_recv()
                if i == bits - 1:
                    self.keep(t).wait()
                if i > 0:
                    self.double(t, i - 1).start()

        for stage in range(self.skip, 2 * bits + 1):
            pl.when((k == stage) & (e >= 0))(functools.partial(at_stage, stage))

    def finish(self):
        def one(t, carry):
            for i in range(self.bits):
                if i >= self.skip:
                    self.halve(t, i).wait_send()
                self.double(t, i).wait_send()
            return carry

        lax.fori_loop(0, self.count, one, 0)


class SmallSum:
    def __init__(self, at, rows, inbox, send, recv, everywhere):
        self.at, self.rows, self.inbox, self.send, self.recv = at, rows, inbox, send, recv
        self.phases = at.group_bits + (at.bits if everywhere else 0)

    @staticmethod
    def scratch(dp, n, count, width, everywhere):
        phases = (dp.bit_length() - 1) + (n.bit_length() - 1 if everywhere else 0)
        return [
            VMEM((phases + 1, count, width), f32),
            VMEM((phases, count, width), f32),
            DMA((phases,)),
            DMA((phases,)),
        ]

    def copy(self, i):
        at = self.at
        if i < at.group_bits:
            target = {"dp": at.group_peer(i)[0]}
        else:
            target = {"tensor": at.peer(i - at.group_bits)}
        return pltpu.make_async_remote_copy(
            src_ref=self.rows.at[i],
            dst_ref=self.inbox.at[i],
            send_sem=self.send.at[i],
            recv_sem=self.recv.at[i],
            device_id=target,
            device_id_type=MESH,
        )

    def event(self, e):
        def run(i):
            if i > 0:
                self.copy(i - 1).wait_recv()
                self.rows[i] = self.rows[i - 1] + self.inbox[i - 1]
            if i < self.phases:
                self.copy(i).start()

        for i in range(self.phases + 1):
            if isinstance(e, int):
                if e == i:
                    run(i)
            else:
                pl.when(e == i)(functools.partial(run, i))

    def finish(self):
        for i in range(self.phases):
            self.copy(i).wait_send()


class DirectSum:
    def __init__(self, at, rows, group_box, line_box, send, recv):
        self.at, self.rows, self.send, self.recv = at, rows, send, recv
        self.boxes = (group_box, line_box)

    @staticmethod
    def scratch(dp, n, count, width):
        most = max(dp, n)
        return [
            VMEM((count, width), f32),
            VMEM((dp, count, width), f32),
            VMEM((n, count, width), f32),
            DMA((2, most)),
            DMA((2, most)),
        ]

    def copy(self, step, other, back=False):
        at, box = self.at, self.boxes[step]
        size, axis = box.shape[0], ("dp", "tensor")[step]
        mine = (at.group, at.me)[step]
        peer = lax.rem(mine + other, size)
        slot = peer if back else mine
        return pltpu.make_async_remote_copy(
            src_ref=box.at[mine],
            dst_ref=box.at[slot],
            send_sem=self.send.at[step, other],
            recv_sem=self.recv.at[step, slot],
            device_id={axis: peer},
            device_id_type=MESH,
        )

    def run(self):
        for step, box in enumerate(self.boxes):
            box[(self.at.group, self.at.me)[step]] = self.rows[...]
            for other in range(1, box.shape[0]):
                self.copy(step, other).start()
            for other in range(1, box.shape[0]):
                self.copy(step, other, back=True).wait_recv()
            total = box[0]
            for i in range(1, box.shape[0]):
                total = total + box[i]
            self.rows[...] = total
        for step, box in enumerate(self.boxes):
            for other in range(1, box.shape[0]):
                self.copy(step, other).wait_send()


def norm_rows(values, gain, shift):
    centre = values - jnp.mean(values, axis=-1, keepdims=True)
    spread = jnp.mean(centre * centre, axis=-1, keepdims=True)
    return centre * lax.rsqrt(spread + norm_epsilon) * gain + shift


def norm_rows_back(values, grad, gain):
    centre = values - jnp.mean(values, axis=-1, keepdims=True)
    scale = lax.rsqrt(jnp.mean(centre * centre, axis=-1, keepdims=True) + norm_epsilon)
    unit = centre * scale
    w = grad * gain
    back = w - jnp.mean(w, axis=-1, keepdims=True)
    back = scale * (back - unit * jnp.mean(w * unit, axis=-1, keepdims=True))
    return back, grad * unit


def add_row(ref, row, values):
    ref[row : row + 1] += jnp.sum(values, axis=0, keepdims=True)


def head_probs(query, keys, first, length):
    rows, cols = query.shape[0], keys.shape[0]
    scores = lax.dot_general(query, keys, NT, preferred_element_type=f32)
    row_ids = first + lax.broadcasted_iota(jnp.int32, (rows, cols), 0)
    col_ids = lax.broadcasted_iota(jnp.int32, (rows, cols), 1)
    scores = jnp.where((col_ids <= row_ids) & (col_ids < length), scores, -1e30)
    probs = jnp.exp(scores - jnp.max(scores, axis=-1, keepdims=True))
    return probs * (1.0 / jnp.sum(probs, axis=-1, keepdims=True))


def attend(heads, lengths, mixed, block, s):
    slots, part = mixed.shape[1:]

    def one(h, carry):
        cols = pl.ds(pl.multiple_of(h * HD, HD), HD)
        for first in range(0, slots, block):
            rows, seen = pl.ds(first, block), pl.ds(0, first + block)
            probs = head_probs(heads[0, s, rows, cols], heads[1, s, seen, cols], first, lengths[s])
            mixed[s, rows, cols] = jnp.dot(
                probs.astype(bf16), heads[2, s, seen, cols], preferred_element_type=f32
            ).astype(bf16)
        return carry

    lax.fori_loop(0, part // HD, one, 0)


def attend_back(heads, grad_heads, lengths, grads, grad_key, grad_value, block, s):
    slots, part = grad_heads.shape[1:]

    def one(h, carry):
        cols = pl.ds(pl.multiple_of(h * HD, HD), HD)
        grad_key[...] = jnp.zeros_like(grad_key)
        grad_value[...] = jnp.zeros_like(grad_value)
        for first in range(0, slots, block):
            rows, seen = pl.ds(first, block), pl.ds(0, first + block)
            query, grad = heads[0, s, rows, cols], grad_heads[s, rows, cols]
            keys = heads[1, s, seen, cols]
            probs = head_probs(query, keys, first, lengths[s])
            grad_value[seen] += lax.dot_general(
                probs.astype(bf16), grad, TN, preferred_element_type=f32
            )
            back = lax.dot_general(
                grad, heads[2, s, seen, cols], NT, preferred_element_type=f32
            )
            centre = jnp.sum(probs * back, axis=-1, keepdims=True)
            scores = (probs * (back - centre)).astype(bf16)
            grads[0, s, rows, cols] = jnp.dot(
                scores, keys, preferred_element_type=f32
            ).astype(bf16)
            grad_key[seen] += lax.dot_general(scores, query, TN, preferred_element_type=f32)
        grads[1, s, :, cols] = grad_key[...].astype(bf16)
        grads[2, s, :, cols] = grad_value[...].astype(bf16)
        return carry

    lax.fori_loop(0, part // HD, one, 0)


def attention_block_kernel(
    n,
    tokens,
    cotangent,
    lengths,
    gain,
    shift,
    weight,
    bias,
    out_weight,
    out_bias,
    gain_two,
    shift_two,
    gathered,
    heads,
    mixed,
    hidden,
    normed,
    grad_all,
    buf,
    send,
    recv,
    keep_sem,
    grad_send,
    grad_recv,
    masked,
    mask_sem,
    *scratch,
):
    at = Place(n)
    seqs, rows, width = tokens.shape
    ring = Gather(at, rows, buf, send, recv)
    grad_ring = Gather(at, rows, grad_all, grad_send, grad_recv)
    line = Scatter(at, rows, *scratch)

    def mask_copy(s):
        return pltpu.make_async_copy(
            masked.at[s], grad_all.at[s, rows_of(at.me, rows)], mask_sem.at[s]
        )

    for s in range(seqs):
        def block(i, carry):
            first = pl.multiple_of(i * 16, 16)
            here = pl.ds(first, 16)
            values = norm_rows(tokens[s, here].astype(f32), gain[...], shift[...])
            buf[s, pl.ds(pl.multiple_of(at.me * rows + first, 16), 16)] = values.astype(bf16)
            slot = at.me * rows + first + lax.broadcasted_iota(jnp.int32, (16, width), 0)
            grad = jnp.where(slot < lengths[s], cotangent[s, here].astype(f32), 0.0)
            masked[s, here] = grad.astype(bf16)
            return carry

        lax.fori_loop(0, rows // 16, block, 0)
        mask_copy(s).start()
    at.greet()
    for s in range(seqs):
        mask_copy(s).wait()

    def keep(s, o):
        here = rows_of(o, 2 * rows)
        return pltpu.make_async_copy(buf.at[s, here], gathered.at[s, here], keep_sem.at[s, o])

    def project(s, o):
        ring.arrived(s, o, 1 - at.core)
        keep(s, o).start()
        here = rows_of(o, 2 * rows)
        for j in range(3):
            total = jnp.dot(buf[s, here], weight[j], preferred_element_type=f32)
            if j == 0:
                total = (total + bias[0:1]) * HD ** (-0.5)
            if j == 2:
                total = total + bias[1:2]
            heads[j, s, here] = total.astype(bf16)

    def final(s, there, total):
        values = tokens[s, there].astype(f32) + total + out_bias[...]
        hidden[s, there] = values
        normed[s, there] = norm_rows(values, gain_two[...], shift_two[...]).astype(bf16)

    def mix(s, o):
        attend(heads, lengths, mixed, min(512, n * rows), s)

    def project_out(s, o):
        here = rows_of(o, 2 * rows)
        for j in range(width // 512):
            cols = pl.ds(j * 512, 512)
            total = jnp.dot(mixed[s, here], out_weight[:, cols], preferred_element_type=f32)
            line.part[s, o, :, cols] = total.astype(bf16)
        line.share(s, o)

    def ops_of(c):
        chips = at.chips
        mixing = []
        for s in range(seqs):
            needs = [("heads", c, s, o) for o in range(chips)]
            mixing.append(((2, s, 0), (2, s, 0), needs, 6.0, [], [(0.0, ("mixed", c, s))]))
        return (
            gather_ops(c, chips, seqs, 0, "in", gate=True)
            + work_ops(
                c, chips, seqs, 1, lambda s, o: [("in", c, s, o, "both")], "heads", 1.0
            )
            + mixing
            + work_ops(
                c, chips, seqs, 3, lambda s, o: [("mixed", c, s)], "part", 1.0, far=True
            )
            + scatter_ops(c, chips, seqs, 4, "out", "part", last=4.0)
            + gather_ops(c, chips, seqs, 5, "grad", rank=6)
        )

    Plan(at, seqs, ops_of).run(
        {
            0: ring.relay,
            1: project,
            2: mix,
            3: project_out,
            4: functools.partial(line.pass_on, final),
            5: grad_ring.relay,
        }
    )
    ring.finish()
    line.finish()
    grad_ring.finish()

    def close(i, carry):
        s, o = i // at.chips, lax.rem(i, at.chips)
        grad_ring.arrived(s, o, 1 - at.core)
        keep(s, o).wait()
        return carry

    lax.fori_loop(0, seqs * at.chips, close, 0)


def whole(count):
    return [pl.BlockSpec(memory_space=VMEM)] * count


def attention_block(
    n,
    tokens,
    cotangent,
    lengths,
    gain,
    shift,
    weight,
    bias,
    out_weight,
    out_bias,
    gain_two,
    shift_two,
):
    seqs, rows, width = tokens.shape
    part = weight.shape[2]
    vmem = pl.BlockSpec(memory_space=VMEM)
    hbm = pl.BlockSpec(memory_space=pl.ANY)
    smem = pl.BlockSpec(memory_space=pltpu.SMEM)
    return pl.pallas_call(
        functools.partial(attention_block_kernel, n),
        out_shape=(
            jax.ShapeDtypeStruct((seqs, n * rows, width), bf16),
            jax.ShapeDtypeStruct((3, seqs, n * rows, part), bf16),
            jax.ShapeDtypeStruct((seqs, n * rows, part), bf16),
            jax.ShapeDtypeStruct((seqs, rows, width), f32),
            jax.ShapeDtypeStruct((seqs, rows, width), bf16),
            jax.ShapeDtypeStruct((seqs, n * rows, width), bf16),
        ),
        in_specs=[vmem, vmem, smem] + [vmem] * 8,
        out_specs=(hbm, vmem, vmem, vmem, vmem, hbm),
        scratch_shapes=[VMEM((seqs, n * rows, width), bf16)]
        + Gather.scratch(n, seqs)
        + [DMA((seqs, n // 2))]
        + Gather.scratch(n, seqs)
        + [VMEM((seqs, rows, width), bf16), DMA((seqs,))]
        + Scatter.scratch(n, seqs, rows, width),
        compiler_params=pltpu.CompilerParams(
            collective_id=0, has_side_effects=True, vmem_limit_bytes=60 * 2**20
        ),
        name="attention_block",
    )(
        tokens,
        cotangent,
        lengths,
        gain,
        shift,
        weight,
        bias,
        out_weight,
        out_bias,
        gain_two,
        shift_two,
    )


def heads_scatter_kernel(
    n,
    grads,
    weight,
    gathered_hbm,
    out_part,
    tokens_hbm,
    gain,
    hidden_hbm,
    grad,
    sums_all,
    weight_grad,
    out_grad,
    bias_grad,
    *scratch,
):
    at = Place(n)
    seqs, rows, width = hidden_hbm.shape
    line = Scatter(at, rows, *scratch[:7])
    weight_sum = GroupSum(at, width, *scratch[7:12], weight_grad)
    out_sum = GroupSum(at, out_part.shape[0], *scratch[12:17], out_grad, turn=1)
    small = DirectSum(at, *scratch[17:22])
    small_bias = SmallSum(at, *scratch[22:26], False)
    gathered, tokens, hidden_grad, in_sem = scratch[26:]
    sources = ((gathered_hbm, gathered), (tokens_hbm, tokens), (hidden_hbm, hidden_grad))
    loads = [
        pltpu.make_async_copy(source, target, in_sem.at[i])
        for i, (source, target) in enumerate(sources)
    ]
    for copy in loads:
        copy.start()
    out_sum.tiles[0] = out_part[...]
    small.rows[...] = jnp.zeros_like(small.rows)
    for row, j, scale in ((0, 0, HD ** (-0.5)), (1, 2, 1.0)):
        total = 0.0
        for s in range(seqs):
            total += jnp.sum(grads[j, s].astype(f32), axis=0, keepdims=True)
        small_bias.rows[0, row : row + 1] = scale * total
    at.greet(groups=True, everyone=True)

    def final(s, there, total):
        back, terms = norm_rows_back(tokens[s, there].astype(f32), total, gain[...])
        grad[s, there] = hidden_grad[s, there] + back
        add_row(small.rows, 0, terms)
        add_row(small.rows, 1, total)

    scales = (HD ** (-0.5), 1.0, 1.0)

    def weight_tile(j):
        for first in range(0, width, 512):
            total = 0.0
            for s in range(seqs):
                total += lax.dot_general(
                    gathered[s, :, pl.ds(first, 512)],
                    grads[j, s],
                    TN,
                    preferred_element_type=f32,
                )
            weight_sum.tiles[j, pl.ds(first, 512)] = (scales[j] * total).astype(bf16)

    def work(s, o):
        here = rows_of(o, 2 * rows)
        for j in range(width // 512):
            cols = pl.ds(j * 512, 512)
            total = 0.0
            for i in range(3):
                total += scales[i] * lax.dot_general(
                    grads[i, s, here], weight[i, cols], NT, preferred_element_type=f32
                )
            line.part[s, o, :, cols] = total.astype(bf16)
        line.share(s, o)

    each = seqs * at.chips

    def weight_event(first, s, o):
        e = first + s * at.chips + o

        @pl.when(e == 0)
        def _():
            for copy in loads:
                copy.wait()

        for j in range(3):
            pl.when(e == j)(functools.partial(weight_tile, j))
        weight_sum.event(e)

    def out_event(s, o):
        out_sum.event(s * at.chips + o)

    def code_of(kind, e):
        return (kind + e // each, e % each // at.chips, e % at.chips)

    def ops_of(c):
        chips = at.chips
        finals = scatter_ops(c, chips, seqs, 1, "out", "part", last=4.0)
        loaded = ("qkv", c, 0, 0, 1)
        for i, (rank, code, needs, time, sends, gives) in enumerate(finals):
            if code[2] == c:
                finals[i] = (rank, code, needs + [loaded], time, sends, gives)
        return (
            work_ops(c, chips, seqs, 0, lambda s, o: [], "part", 1.5, rank=0, far=True)
            + finals
            + group_ops(
                c, at.group_bits, 3, PIECE, lambda e: code_of(2, e), 0, (0,), 2.7, name="qkv"
            )
            + group_ops(
                c, at.group_bits, 1, PIECE, lambda e: code_of(5, e), 0, (1,), 0.7, name="out_sum"
            )
        )

    actions = {0: work, 1: functools.partial(line.pass_on, final), 5: out_event}
    for i in range(3):
        actions[2 + i] = functools.partial(weight_event, i * each)
    Plan(at, seqs, ops_of).run(actions, small_bias.event)
    small.run()
    sums_all[...] = small.rows[...]
    bias_grad[...] = small_bias.rows[small_bias.phases]
    line.finish()
    weight_sum.finish()
    out_sum.finish()
    small_bias.finish()


def heads_scatter(n, grads, weight, gathered, out_part, tokens, gain, hidden_grad):
    seqs, slots, part = grads.shape[1:]
    width = weight.shape[1]
    rows = slots // n
    dp = lax.axis_size("dp")
    vmem = pl.BlockSpec(memory_space=VMEM)
    hbm = pl.BlockSpec(memory_space=pl.ANY)
    return pl.pallas_call(
        functools.partial(heads_scatter_kernel, n),
        out_shape=(
            jax.ShapeDtypeStruct((seqs, rows, width), f32),
            jax.ShapeDtypeStruct((2, width), f32),
            jax.ShapeDtypeStruct((3, width, part), bf16),
            jax.ShapeDtypeStruct((1, part, width), bf16),
            jax.ShapeDtypeStruct((2, part), f32),
        ),
        in_specs=[vmem, vmem, hbm, vmem, hbm, vmem, hbm],
        out_specs=(vmem, vmem, hbm, hbm, vmem),
        scratch_shapes=Scatter.scratch(n, seqs, rows, width)
        + GroupSum.scratch(dp, 3, width, part)
        + GroupSum.scratch(dp, 1, part, width)
        + DirectSum.scratch(dp, n, 2, width)
        + SmallSum.scratch(dp, n, 2, part, False)
        + [
            VMEM(gathered.shape, bf16),
            VMEM(tokens.shape, bf16),
            VMEM(hidden_grad.shape, f32),
            DMA((3,)),
        ],
        compiler_params=pltpu.CompilerParams(
            collective_id=2, has_side_effects=True, vmem_limit_bytes=62 * 2**20
        ),
        name="heads_scatter",
    )(grads, weight, gathered, out_part, tokens, gain, hidden_grad)


def normal_cdf(values):
    x = jnp.clip(values * 0.7071067811865476, -3.832506856900711, 3.832506856900711)
    x2 = x * x
    top = 0.00022905065861350646
    for c in (0.0034082910107109506, 0.050955695062380861, 0.18520832239976145, 1.128379143519084):
        top = top * x2 + c
    low = -1.1791602954361697e-7
    for c in (
        0.000023547966471313185,
        0.0010179625278914885,
        0.014070470171167667,
        0.11098505178285362,
        0.49746925110067538,
        1.0,
    ):
        low = low * x2 + c
    return 0.5 + 0.5 * (x * top / low)


def mlp_kernel(
    n,
    normed,
    grad_hbm,
    up_hbm,
    up_bias,
    down_hbm,
    hidden_hbm,
    gain,
    mlp_part,
    hidden_grad,
    grad_low,
    sums,
    up_grad,
    up_bias_grad,
    down_grad,
    down_box,
    buf,
    send,
    recv,
    grad_all,
    up_weight,
    down_weight,
    hidden,
    in_sem,
    *scratch,
):
    at = Place(n)
    seqs, rows, width = normed.shape
    units_wide = up_weight.shape[1]
    line = Scatter(at, rows, *scratch[:7])
    act, pre, out_stage, out_sem, up_stage, down_stage, tile_sem, half_send, half_recv = scratch[7:]
    ring = Gather(at, rows, buf, send, recv)
    loads = [
        pltpu.make_async_copy(source, target, in_sem.at[i])
        for i, (source, target) in enumerate(
            (
                (up_hbm, up_weight),
                (grad_hbm, grad_all),
                (down_hbm, down_weight),
                (hidden_hbm, hidden),
            )
        )
    ]
    for copy in loads:
        copy.start()
    at.greet(groups=True)
    for s in range(seqs):
        buf[s, rows_of(at.me, rows)] = normed[s]
    up_bias_grad[...] = jnp.zeros_like(up_bias_grad)
    sums[...] = jnp.zeros_like(sums)
    ft = min(512, units_wide)

    def out_copy(s, o):
        return pltpu.make_async_copy(
            out_stage, mlp_part.at[s, rows_of(o, 2 * rows)], out_sem.at[0]
        )

    def work(s, o):
        ring.arrived(s, o, 1 - at.core)

        @pl.when((s == 0) & (o == at.chip))
        def _():
            for copy in loads:
                copy.wait()

        here = rows_of(o, 2 * rows)
        for j in range(units_wide // ft):
            cols = pl.ds(j * ft, ft)
            value = jnp.dot(buf[s, here], up_weight[:, cols], preferred_element_type=f32)
            value = value + up_bias[:, cols]
            spread = normal_cdf(value)
            act[s, here, cols] = (value * spread).astype(bf16)
            slope = spread + value * (0.3989422804014327 * jnp.exp(-0.5 * value * value))
            grad = lax.dot_general(
                grad_all[s, here], down_weight[cols], NT, preferred_element_type=f32
            )
            grad = (grad * slope).astype(bf16)
            pre[s, here, cols] = grad
            up_bias_grad[:, cols] += jnp.sum(grad.astype(f32), axis=0, keepdims=True)
        for j in range(width // 512):
            cols = pl.ds(j * 512, 512)
            line.part[s, o, :, cols] = lax.dot_general(
                pre[s, here], up_weight[cols], NT, preferred_element_type=f32
            ).astype(bf16)
        line.share(s, o)
        pl.when((s > 0) | (o != at.chip))(lambda: out_copy(s, o).wait())
        for j in range(width // 512):
            cols = pl.ds(j * 512, 512)
            out_stage[:, cols] = jnp.dot(
                act[s, here], down_weight[:, cols], preferred_element_type=f32
            ).astype(bf16)
        out_copy(s, o).start()

    def final(s, there, total):
        back, terms = norm_rows_back(hidden[s, there], total, gain[...])
        first = pl.multiple_of(at.me * rows + there.start, 16)
        grad_out = grad_all[s, pl.ds(first, there.size)].astype(f32)
        grad = grad_out + back
        hidden_grad[s, there] = grad
        grad_low[s, there] = grad.astype(bf16)
        add_row(sums, 0, terms)
        add_row(sums, 1, total)
        add_row(sums, 2, grad)
        add_row(sums, 3, grad_out)

    kinds = ((down_stage, down_grad), (up_stage, up_grad))

    def tile_copy(kind, t):
        stage, grad = kinds[kind]
        return pltpu.make_async_copy(stage, grad.at[t], tile_sem.at[kind])

    def down_half(t):
        half = down_box.shape[1]
        peer, mine = at.group_peer(t % at.group_bits)
        return pltpu.make_async_remote_copy(
            src_ref=down_grad.at[t, rows_of(1 - mine, half)],
            dst_ref=down_box.at[t],
            send_sem=half_send.at[t],
            recv_sem=half_recv.at[t],
            device_id={"dp": peer},
            device_id_type=MESH,
        )

    def tile_sent(kind, t):
        tile_copy(kind, t).wait()
        if kind == 0:
            down_half(t).start()

    order = [(i // 4, i % 4) for i in range(8)]

    def weight_tile(i):
        for j, (kind, t) in enumerate(order):
            @pl.when(i == j)
            def _():
                stage = kinds[kind][0]
                cols = pl.ds(t * stage.shape[0], stage.shape[0])
                total = 0.0
                for s in range(seqs):
                    if kind == 0:
                        left, right = act[s, :, cols], grad_all[s]
                    else:
                        left, right = buf[s, :, cols], pre[s]
                    total += lax.dot_general(left, right, TN, preferred_element_type=f32)
                if j >= 1:
                    tile_sent(*order[j - 1])
                stage[...] = total.astype(bf16)
                tile_copy(kind, t).start()

    def tile_work(s, o):
        weight_tile(s * at.chips + o)

    own = (4, 5, 6)

    def ops_of(c):
        chips = at.chips
        units = [(s, o) for s in range(seqs) for o in range(chips)]
        ops = (
            gather_ops(c, chips, seqs, 0, "in", own=own)
            + scatter_ops(c, chips, seqs, 1, "back", "part", last=4.0)
            + work_ops(
                c, chips, seqs, 2, lambda s, o: [("in", c, s, o, "both")], "part", 5.7
            )
        )
        for i in range(len(ops)):
            rank, code, needs, time, sends, gives = ops[i]
            if code[0] == 2 and code[1:] != (0, c):
                ops[i] = (rank, code, needs + [("first", c)], time, sends, gives)
            if code == (2, 0, c):
                ops[i] = (rank, code, needs, time, sends, gives + [(0.0, ("first", c))])
        for e in range(len(order)):
            needs = [("part", c, s, o) for s, o in units]
            needs += [("tile", c, e - 1)] if e else []
            sends = [("axis%d" % (e % 2), c, ("half", c, e), PIECE)] if e < 4 else []
            code = (3, e // chips, e % chips)
            ops.append(((4, e, 0), code, needs, 2.7, sends, [(0.0, ("tile", c, e))]))
        return ops

    actions = {0: ring.relay, 1: functools.partial(line.pass_on, final), 2: work, 3: tile_work}
    actions.update(ring.owns(own))
    Plan(at, seqs, ops_of).run(actions)
    tile_sent(*order[7])
    ring.finish()
    line.finish()
    for t in range(4):
        down_half(t).wait()
    out_copy(0, 0).wait()


def mlp_block(n, normed, grad_all, up_weight, up_bias, down_weight, hidden, gain):
    seqs, rows, width = normed.shape
    slots = n * rows
    units = up_weight.shape[1]
    hbm = pl.BlockSpec(memory_space=pl.ANY)
    vmem = pl.BlockSpec(memory_space=VMEM)
    down_size, up_size = units // 4, width // 4
    return pl.pallas_call(
        functools.partial(mlp_kernel, n),
        out_shape=(
            jax.ShapeDtypeStruct((seqs, slots, width), bf16),
            jax.ShapeDtypeStruct((seqs, rows, width), f32),
            jax.ShapeDtypeStruct((seqs, rows, width), bf16),
            jax.ShapeDtypeStruct((4, width), f32),
            jax.ShapeDtypeStruct((4, up_size, units), bf16),
            jax.ShapeDtypeStruct((1, units), f32),
            jax.ShapeDtypeStruct((4, down_size, width), bf16),
            jax.ShapeDtypeStruct((4, down_size // 2, width), bf16),
        ),
        in_specs=[vmem, hbm, hbm, vmem, hbm, hbm, vmem],
        out_specs=(hbm, vmem, vmem, vmem, hbm, vmem, hbm, hbm),
        scratch_shapes=[VMEM((seqs, slots, width), bf16)]
        + Gather.scratch(n, seqs)
        + [
            VMEM((seqs, slots, width), bf16),
            VMEM(up_weight.shape, bf16),
            VMEM(down_weight.shape, bf16),
            VMEM(hidden.shape, f32),
            DMA((4,)),
        ]
        + Scatter.scratch(n, seqs, rows, width)
        + [
            VMEM((seqs, slots, units), bf16),
            VMEM((seqs, slots, units), bf16),
            VMEM((2 * rows, width), bf16),
            DMA((1,)),
            VMEM((up_size, units), bf16),
            VMEM((down_size, width), bf16),
            DMA((2,)),
            DMA((4,)),
            DMA((4,)),
        ],
        compiler_params=pltpu.CompilerParams(
            collective_id=3, has_side_effects=True, vmem_limit_bytes=62 * 2**20
        ),
        name="mlp_block",
    )(normed, grad_all, up_weight, up_bias, down_weight, hidden, gain)


def attn_grad_kernel(
    n,
    grad,
    mlp_part,
    hidden,
    bias,
    weight,
    mixed,
    sums,
    up_bias_part,
    up_part,
    down_part,
    down_box,
    lengths,
    heads,
    output,
    grads,
    weight_grad,
    sums_all,
    up_bias_grad,
    up_grad,
    down_grad,
    buf,
    send,
    recv,
    *scratch,
):
    at = Place(n)
    seqs, rows, width = grad.shape
    line = Scatter(at, rows, *scratch[:7])
    load_sem, tile_sem, box_sem = scratch[7:10]
    ring = Gather(at, rows, buf, send, recv)
    up_sum = GroupSum(at, up_part.shape[1], *scratch[10:15], up_grad, turn=1)
    down_sum = GroupSum(at, down_part.shape[1], *scratch[15:20], down_grad, skip=1)
    small = SmallSum(at, *scratch[20:24], True)
    small_bias = SmallSum(at, *scratch[24:28], False)
    grad_heads, grad_key, grad_value = scratch[28:]
    def up_load(t):
        return pltpu.make_async_copy(up_part.at[t], up_sum.tiles.at[t], tile_sem.at[0, t])

    def down_load(t):
        half = down_box.shape[1]
        kept = down_part.at[t, down_sum.span(down_sum.base(t, 1), half)]
        return (
            pltpu.make_async_copy(kept, down_sum.tiles.at[t], tile_sem.at[1, t]),
            pltpu.make_async_copy(down_box.at[t], down_sum.box(t, 0), box_sem.at[t]),
        )

    def up_loaded(t):
        up_load(t).wait()

    def down_loaded(t):
        for copy in down_load(t):
            copy.wait()

    for t in range(4):
        up_load(t).start()
        for copy in down_load(t):
            copy.start()
    small.rows[0] = sums[...]
    small_bias.rows[0] = up_bias_part[...]

    def load(s, o):
        return pltpu.make_async_copy(
            mlp_part.at[s, rows_of(o, 2 * rows)], line.part.at[s, o], load_sem.at[s, o]
        )

    def load_one(i, carry):
        load(i // at.chips, lax.rem(i, at.chips)).start()
        return carry

    each = seqs * at.chips
    lax.fori_loop(0, each, load_one, 0)
    for s in range(seqs):
        buf[s, rows_of(at.me, rows)] = grad[s]
    at.greet(groups=True, cube=True)

    def final(s, there, total):
        output[s, there] = (hidden[s, there] + total + bias[...]).astype(bf16)

    def share(s, o):
        load(s, o).wait()
        line.share(s, o)

    def work(s, o):
        ring.arrived(s, o, 1 - at.core)
        here = rows_of(o, 2 * rows)
        grad_heads[s, here] = lax.dot_general(
            buf[s, here], weight[...], NT, preferred_element_type=f32
        ).astype(bf16)

    def back(s, o):
        block = min(512, n * rows)
        attend_back(heads, grad_heads, lengths, grads, grad_key, grad_value, block, s)

    def up_event(first, s, o):
        up_sum.event(first + s * at.chips + o, up_loaded)

    def down_event(first, s, o):
        down_sum.event(first + s * at.chips + o, down_loaded)

    def ops_of(c):
        chips = at.chips
        code_of = lambda kind, e: (kind + e // each, e % each // chips, e % chips)
        backs = []
        for s in range(seqs):
            needs = [("done", c, s, o) for o in range(chips)]
            backs.append(((4, s, 0), (4, s, 0), needs, 8.0, [], []))
        return backs + (
            gather_ops(c, chips, seqs, 0, "in")
            + scatter_ops(c, chips, seqs, 1, "out", "part", last=4.0)
            + work_ops(c, chips, seqs, 2, lambda s, o: [("in", c, s, o, "both")], "done", 1.0)
            + work_ops(c, chips, seqs, 3, lambda s, o: [], "part", 0.3, rank=0, far=True)
            + group_ops(
                c, at.group_bits, 4, PIECE, lambda e: code_of(8, e), 0, (1,), 0.7, name="up"
            )
            + group_ops(
                c, at.group_bits, 4, PIECE, lambda e: code_of(16, e), 1, (0,), 0.7, name="down"
            )
        )

    actions = {0: ring.relay, 1: functools.partial(line.pass_on, final), 2: work, 3: share}
    actions[4] = back
    for i in range(-(-up_sum.events() // each)):
        actions[8 + i] = functools.partial(up_event, i * each)
    for i in range(-(-down_sum.events() // each)):
        actions[16 + i] = functools.partial(down_event, i * each)

    def beside(k):
        pl.when(lax.rem(k, 8) == 0)(lambda: small.event(k // 8))
        small_bias.event(k)

    Plan(at, seqs, ops_of).run(actions, beside)
    sums_all[...] = small.rows[small.phases]
    up_bias_grad[...] = small_bias.rows[small_bias.phases]
    for j in range(width // 512):
        cols = pl.ds(j * 512, 512)
        total = 0.0
        for s in range(seqs):
            total += lax.dot_general(mixed[s], buf[s, :, cols], TN, preferred_element_type=f32)
        weight_grad[:, cols] = total.astype(bf16)
    ring.finish()
    line.finish()
    small.finish()
    small_bias.finish()
    up_sum.finish()
    down_sum.finish()


def attn_grad(
    n,
    grad,
    mlp_part,
    hidden,
    bias,
    weight,
    mixed,
    sums,
    up_bias_part,
    up_part,
    down_part,
    down_box,
    lengths,
    heads,
):
    seqs, rows, width = grad.shape
    slots = n * rows
    part = weight.shape[0]
    units = up_part.shape[2]
    dp = lax.axis_size("dp")
    vmem = pl.BlockSpec(memory_space=VMEM)
    hbm = pl.BlockSpec(memory_space=pl.ANY)
    return pl.pallas_call(
        functools.partial(attn_grad_kernel, n),
        out_shape=(
            jax.ShapeDtypeStruct((seqs, rows, width), bf16),
            jax.ShapeDtypeStruct(heads.shape, bf16),
            jax.ShapeDtypeStruct((part, width), bf16),
            jax.ShapeDtypeStruct(sums.shape, f32),
            jax.ShapeDtypeStruct((1, units), f32),
            jax.ShapeDtypeStruct(up_part.shape, bf16),
            jax.ShapeDtypeStruct(down_part.shape, bf16),
        ),
        in_specs=[vmem, hbm]
        + [vmem] * 6
        + [hbm] * 3
        + [pl.BlockSpec(memory_space=pltpu.SMEM), vmem],
        out_specs=(vmem,) * 5 + (hbm, hbm),
        scratch_shapes=[VMEM((seqs, slots, width), bf16)]
        + Gather.scratch(n, seqs)
        + Scatter.scratch(n, seqs, rows, width)
        + [DMA((seqs, n // 2)), DMA((2, 4)), DMA((4,))]
        + GroupSum.scratch(dp, 4, width // 4, units)
        + GroupSum.scratch(dp, 4, units // 4, width, 1)
        + SmallSum.scratch(dp, n, sums.shape[0], width, True)
        + SmallSum.scratch(dp, n, 1, units, False)
        + [VMEM((seqs, slots, part), bf16), VMEM((slots, HD), f32), VMEM((slots, HD), f32)],
        compiler_params=pltpu.CompilerParams(
            collective_id=4, has_side_effects=True, vmem_limit_bytes=62 * 2**20
        ),
        name="attn_grad",
    )(
        grad,
        mlp_part,
        hidden,
        bias,
        weight,
        mixed,
        sums,
        up_bias_part,
        up_part,
        down_part,
        down_box,
        lengths,
        heads,
    )


def body(
    tokens,
    cotangent,
    lengths,
    ln1_gain,
    ln1_shift,
    qkv_weight,
    qkv_bias,
    out_weight,
    out_bias,
    ln2_gain,
    ln2_shift,
    up_weight,
    up_bias,
    down_weight,
    down_bias,
):
    n = lax.axis_size("tensor")
    gathered_one, heads, mixed_heads, hidden_state, normed_two, grad_mlp = attention_block(
        n,
        tokens,
        cotangent,
        lengths,
        ln1_gain[None],
        ln1_shift[None],
        qkv_weight,
        qkv_bias,
        out_weight,
        out_bias[None],
        ln2_gain[None],
        ln2_shift[None],
    )
    (
        mlp_part,
        hidden_grad,
        grad_attn,
        sums,
        up_part,
        up_bias_part,
        down_part,
        down_box,
    ) = mlp_block(
        n, normed_two, grad_mlp, up_weight, up_bias[None], down_weight, hidden_state, ln2_gain[None]
    )
    output, grads, out_part, sums, up_bias_grad, up_weight_grad, down_weight_grad = attn_grad(
        n,
        grad_attn,
        mlp_part,
        hidden_state,
        down_bias[None],
        out_weight,
        mixed_heads,
        sums,
        up_bias_part,
        up_part,
        down_part,
        down_box,
        lengths,
        heads,
    )
    ln2_gain_grad, ln2_shift_grad, out_bias_grad, down_bias_grad = [sums[i] for i in range(4)]
    input_grad, sums_one, qkv_weight_grad, out_weight_grad, qkv_bias_grad = heads_scatter(
        n, grads, qkv_weight, gathered_one, out_part, tokens, ln1_gain[None], hidden_grad
    )
    up_weight_grad = up_weight_grad.astype(jnp.float32).reshape(up_weight.shape)
    down_weight_grad = down_weight_grad.astype(jnp.float32).reshape(down_weight.shape)
    return (
        output,
        input_grad,
        sums_one[0],
        sums_one[1],
        qkv_weight_grad.astype(jnp.float32),
        qkv_bias_grad,
        out_weight_grad[0].astype(jnp.float32),
        out_bias_grad,
        ln2_gain_grad,
        ln2_shift_grad,
        up_weight_grad,
        up_bias_grad[0],
        down_weight_grad,
        down_bias_grad,
    )


def solution(mesh):
    in_specs = (
        P("dp", "tensor", None),
        P("dp", "tensor", None),
        P("dp"),
        P(),
        P(),
        P(None, None, "tensor"),
        P(None, "tensor"),
        P("tensor", None),
        P(),
        P(),
        P(),
        P(None, "tensor"),
        P("tensor"),
        P("tensor", None),
        P(),
    )
    out_specs = (
        P("dp", "tensor", None),
        P("dp", "tensor", None),
        P(),
        P(),
        P(None, None, "tensor"),
        P(None, "tensor"),
        P("tensor", None),
        P(),
        P(),
        P(),
        P(None, "tensor"),
        P("tensor"),
        P("tensor", None),
        P(),
    )
    return jax.shard_map(body, mesh=mesh, in_specs=in_specs, out_specs=out_specs, check_vma=False)
```

```python
import functools
import heapq

import jax
import jax.numpy as jnp
from jax import lax
from jax.experimental import pallas as pl
from jax.experimental.pallas import tpu as pltpu
from jax.sharding import PartitionSpec as P

HD = 128


norm_epsilon = 1e-05

MESH = pl.DeviceIdType.MESH
UP, DOWN, SIDE = 0, 1, 2
VMEM = pltpu.VMEM
DMA = pltpu.SemaphoreType.DMA
f32 = jnp.float32
bf16 = jnp.bfloat16
NT = (((1,), (1,)), ((), ()))
TN = (((0,), (0,)), ((), ()))


def order_of(chips, ops_of, backlog=8.0, hop=2.0):
    todo = [sorted(ops_of(c)) for c in range(chips)]
    order = [[] for _ in range(chips)]
    free, busy, have, queue = {}, [False] * chips, set(), []

    def push(time, what):
        heapq.heappush(queue, (time, len(pushed), what))
        pushed.append(0)

    pushed = []
    for c in range(chips):
        push(0.0, (c, None, ()))
    now = 0.0
    while queue:
        now, _, (c, signal, after) = heapq.heappop(queue)
        if signal is not None:
            have.add(signal)
        for part in after:
            if part[0] == "free":
                busy[c] = False
            elif part[0] == "send":
                _, link, to, sig, span = part
                start = max(now, free.get((c, link), 0.0))
                free[c, link] = start + span
                push(start + span + hop, (to, sig, ()))
            else:
                push(now + part[1], (c, part[2], ()))
        if busy[c]:
            continue
        for op in todo[c]:
            rank, code, needs, time, sends, gives = op
            if any(need not in have for need in needs):
                continue
            late = max([free.get((c, send[0]), 0.0) - now for send in sends], default=0.0)
            if late > backlog:
                push(now + late - backlog, (c, None, ()))
                continue
            todo[c].remove(op)
            order[c].append(code)
            busy[c] = True
            ends = [("free",)] + [("send",) + send for send in sends]
            push(now + time, (c, None, ends + [("give",) + give for give in gives]))
            break
    assert not any(todo)
    return order, now


PIECE = 12.0


def gather_ops(c, chips, seqs, kind, name, rank=0, time=0.5, gate=False, own=None):
    ops = []
    for s in range(seqs):
        for o in range(chips):
            up, down = [], []
            if o <= c < chips - 1:
                up.append((c + 1, c + 1, (name, c + 1, s, o), PIECE))
            if o >= c > 0:
                down.append((c - 1, c - 1, (name, c - 1, s, o), PIECE))
            both = [(3.0, (name, c, s, o, "both"))]
            if own is not None and o == c and s > 0:
                ops.append(((rank, s, -1), (own[0], s, o), [], time, [], both))
                for sends, which, others in ((up, own[1], range(c)), (down, own[2], range(c + 1, chips))):
                    needs = [(name, c, t, other) for t in (s - 1, s) for other in others]
                    if sends:
                        ops.append(((rank, s, chips), (which, s, o), needs, time, sends, []))
                continue
            needs = [] if o == c else [(name, c, s, o)]
            if gate and o == c and s > 0:
                for other in range(chips):
                    if other < c < chips - 1 or other > c > 0:
                        needs.append((name, c, s - 1, other))
            ops.append(((rank, s, abs(o - c)), (kind, s, o), needs, time, up + down, both))
    return ops


def scatter_ops(c, chips, seqs, kind, name, part, rank=1, time=1.3, last=2.0):
    ops = []
    for s in range(seqs):
        for o in range(chips):
            needs = [(part, c, s, o)]
            if o >= c > 0:
                needs.append((name, c, s, o, "below"))
            if o <= c < chips - 1:
                needs.append((name, c, s, o, "above"))
            sends = []
            if o > c:
                sends = [(c + 1, c + 1, (name, c + 1, s, o, "below"), PIECE)]
            if o < c:
                sends = [(c - 1, c - 1, (name, c - 1, s, o, "above"), PIECE)]
            order = (rank, s, -abs(o - c)) if o != c else (8, s, 0)
            ends = [(0.0, (name, c, s, "sum"))] if o == c else []
            ops.append((order, (kind, s, o), needs, last if o == c else time, sends, ends))
    return ops


def work_ops(c, chips, seqs, kind, needs_of, gives, time, rank=2, far=False):
    return [
        (
            (rank, s, -abs(o - c) if far else abs(o - c)),
            (kind, s, o),
            needs_of(s, o),
            time,
            [],
            [(3.0, (gives, c, s, o))],
        )
        for s in range(seqs)
        for o in range(chips)
    ]


def group_ops(c, bits, count, span, code_of, skip, turns, first_time, rank=3, name="group"):
    ops = []
    for t in range(count):
        for stage in range(skip, 2 * bits + 1):
            needs, sends = [], []
            for turn in turns:
                if stage > skip:
                    needs.append((name, c, turn, t, stage))
                if stage < 2 * bits:
                    i = stage if stage < bits else 2 * bits - 1 - stage
                    axis = "axis%d" % ((t + turn + i) % bits)
                    sends.append((axis, c, (name, c, turn, t, stage + 1), span / 2**i))
            time = first_time if stage == 0 else 0.8 * len(turns)
            code = code_of((stage - skip) * count + t)
            ops.append(((rank, stage, t), code, needs, time, sends, []))
    return ops


class Plan:
    def __init__(self, at, seqs, ops_of):
        chips = at.chips
        order, self.length = order_of(chips, ops_of)
        self.per, self.each, self.chips, self.seqs = 1024, 3, chips, seqs
        self.count = max(len(codes) for codes in order)
        idle = self.per // (seqs * chips) - 1
        rows = []
        for codes in order:
            assert all(kind < idle for kind, s, o in codes)
            flat = [(kind * seqs + s) * chips + o for kind, s, o in codes]
            flat += [idle * seqs * chips] * (self.count - len(flat) + self.each)
            rows.append(
                [
                    sum(flat[i + j] * self.per**j for j in range(self.each))
                    for i in range(0, self.count, self.each)
                ]
            )
        self.words = []
        for w in range(len(rows[0])):
            word = jnp.int32(rows[0][w])
            for c in range(1, chips):
                word = jnp.where(at.chip == c, jnp.int32(rows[c][w]), word)
            self.words.append(word)

    def step(self, k):
        which, slot = k // self.each, lax.rem(k, self.each)
        word = jnp.int32(0)
        for w, value in enumerate(self.words):
            word = jnp.where(which == w, value, word)
        code = word
        for j in range(1, self.each):
            code = jnp.where(slot == j, word // self.per**j, code)
        code = lax.rem(code, self.per)
        each = self.seqs * self.chips
        return code // each, lax.rem(code, each) // self.chips, lax.rem(code, self.chips)

    def run(self, actions, beside=None):
        def step(k, carry):
            kind, s, o = self.step(k)
            for which, action in actions.items():
                pl.when(kind == which)(functools.partial(action, s, o))
            if beside is not None:
                beside(k)
            return carry

        lax.fori_loop(0, self.count, step, 0)


class Place:
    def __init__(self, n):
        self.n, self.chips = n, n // 2
        self.me = lax.axis_index("tensor")
        self.chip, self.core = self.me // 2, lax.rem(self.me, 2)
        self.side = self.me + 1 - 2 * self.core
        self.below = self.chip > 0
        self.above = self.chip < self.chips - 1
        self.group = lax.axis_index("dp")
        self.group_bits = lax.axis_size("dp").bit_length() - 1
        self.bits = n.bit_length() - 1

    def group_peer(self, q):
        mine = lax.rem(self.group // 2**q, 2)
        return self.group + (1 - 2 * mine) * 2**q, mine

    def peer(self, q):
        mine = lax.rem(self.me // 2**q, 2)
        return self.me + (1 - 2 * mine) * 2**q

    def greet(self, groups=False, cube=False, everyone=False):
        barrier = pltpu.get_barrier_semaphore()

        def tell(target):
            pl.semaphore_signal(
                barrier, inc=1, device_id={"tensor": target}, device_id_type=MESH
            )

        tell(self.side)
        pl.when(self.below)(lambda: tell(self.me - 2))
        pl.when(self.above)(lambda: tell(self.me + 2))
        peers = 1 + self.below.astype(jnp.int32) + self.above.astype(jnp.int32)
        if groups:
            for q in range(self.group_bits):
                pl.semaphore_signal(
                    barrier, inc=1, device_id={"dp": self.group_peer(q)[0]}, device_id_type=MESH
                )
            peers = peers + self.group_bits
        if everyone:
            for other in range(1, self.n):
                tell(lax.rem(self.me + other, self.n))
            for other in range(1, 2**self.group_bits):
                peer = lax.rem(self.group + other, 2**self.group_bits)
                pl.semaphore_signal(barrier, inc=1, device_id={"dp": peer}, device_id_type=MESH)
            peers = peers + (self.n - 1 + 2**self.group_bits - 1)
        if cube:
            for q in range(self.bits):
                tell(self.peer(q))
            peers = peers + self.bits
        pl.semaphore_wait(barrier, peers)


def rows_of(index, rows):
    return pl.ds(pl.multiple_of(index * rows, rows), rows)


class Gather:
    def __init__(self, at, rows, buf, send, recv):
        self.at, self.rows, self.buf, self.send, self.recv = at, rows, buf, send, recv
        self.seqs = buf.shape[0]

    @staticmethod
    def scratch(n, seqs):
        return [DMA((3, seqs, n // 2)), DMA((seqs, n))]

    def piece(self, s, o, k):
        return self.buf.at[s, rows_of(2 * o + k, self.rows)]

    def copy(self, s, o, kind):
        at = self.at
        target = (at.me + 2, at.me - 2, at.side)[kind]
        piece = self.piece(s, o, at.core)
        return pltpu.make_async_remote_copy(
            src_ref=piece,
            dst_ref=piece,
            send_sem=self.send.at[kind, s, o],
            recv_sem=self.recv.at[s, 2 * o + at.core],
            device_id={"tensor": target},
            device_id_type=MESH,
        )

    def arrived(self, s, o, k):
        at = self.at
        piece = self.piece(s, o, k)
        pltpu.make_async_remote_copy(
            src_ref=piece,
            dst_ref=piece,
            send_sem=self.send.at[SIDE, s, o],
            recv_sem=self.recv.at[s, 2 * o + k],
            device_id={"tensor": at.side},
            device_id_type=MESH,
        ).wait_recv()

    def relay(self, s, o):
        at = self.at
        pl.when(o != at.chip)(lambda: self.arrived(s, o, at.core))
        pl.when((o <= at.chip) & at.above)(lambda: self.copy(s, o, UP).start())
        pl.when((o >= at.chip) & at.below)(lambda: self.copy(s, o, DOWN).start())
        self.copy(s, o, SIDE).start()

    def own(self, kind, s, o):
        self.copy(s, o, kind).start()

    def owns(self, kinds):
        return {
            which: functools.partial(self.own, kind)
            for which, kind in zip(kinds, (SIDE, UP, DOWN))
        }

    def finish(self):
        at = self.at

        def one(i, carry):
            s, o = i // at.chips, lax.rem(i, at.chips)
            pl.when((o <= at.chip) & at.above)(lambda: self.copy(s, o, UP).wait_send())
            pl.when((o >= at.chip) & at.below)(lambda: self.copy(s, o, DOWN).wait_send())
            self.copy(s, o, SIDE).wait_send()
            return carry

        lax.fori_loop(0, self.seqs * at.chips, one, 0)


class Scatter:
    def __init__(self, at, rows, part, side, link, side_send, side_recv, send, recv):
        self.at, self.rows = at, rows
        self.part, self.side, self.link = part, side, link
        self.side_send, self.side_recv, self.send, self.recv = side_send, side_recv, send, recv
        self.seqs = part.shape[0]

    @staticmethod
    def scratch(n, seqs, rows, width):
        chips = n // 2
        return [
            VMEM((seqs, chips, 2 * rows, width), bf16),
            VMEM((seqs, chips, rows, width), bf16),
            VMEM((seqs, chips + 1, rows, width), bf16),
            DMA((seqs, chips)),
            DMA((seqs, chips)),
            DMA((seqs, chips)),
            DMA((seqs, chips + 1)),
        ]

    def side_copy(self, s, o):
        at = self.at
        return pltpu.make_async_remote_copy(
            src_ref=self.part.at[s, o, rows_of(1 - at.core, self.rows)],
            dst_ref=self.side.at[s, o],
            send_sem=self.side_send.at[s, o],
            recv_sem=self.side_recv.at[s, o],
            device_id={"tensor": at.side},
            device_id_type=MESH,
        )

    def link_copy(self, s, o, slot, target):
        return pltpu.make_async_remote_copy(
            src_ref=self.part.at[s, o, rows_of(self.at.core, self.rows)],
            dst_ref=self.link.at[s, slot],
            send_sem=self.send.at[s, o],
            recv_sem=self.recv.at[s, slot],
            device_id={"tensor": target},
            device_id_type=MESH,
        )

    def share(self, s, o):
        self.side_copy(s, o).start()

    def blocks(self, body):
        step = 16
        lax.fori_loop(0, self.rows // step, lambda i, c: (body(pl.multiple_of(i * step, step), step), c)[1], 0)

    def add_up(self, s, o, slots):
        base = self.at.core * self.rows

        def body(first, step):
            here = pl.ds(pl.multiple_of(base + first, step), step)
            there = pl.ds(first, step)
            total = self.part[s, o, here].astype(f32) + self.side[s, o, there].astype(f32)
            for slot in slots:
                total += self.link[s, slot, there].astype(f32)
            self.part[s, o, here] = total.astype(bf16)

        self.blocks(body)

    def pass_on(self, final, s, o):
        at = self.at
        self.side_copy(s, o).wait_recv()

        @pl.when(o > at.chip)
        def _():
            @pl.when(at.below)
            def _():
                self.link_copy(s, o, o, at.me).wait_recv()
                self.add_up(s, o, [o])

            pl.when(jnp.logical_not(at.below))(lambda: self.add_up(s, o, []))
            self.link_copy(s, o, o, at.me + 2).start()

        @pl.when(o < at.chip)
        def _():
            @pl.when(at.above)
            def _():
                self.link_copy(s, o, o, at.me).wait_recv()
                self.add_up(s, o, [o])

            pl.when(jnp.logical_not(at.above))(lambda: self.add_up(s, o, []))
            slot = jnp.where(o == at.chip - 1, at.chips, o)
            self.link_copy(s, o, slot, at.me - 2).start()

        @pl.when(o == at.chip)
        def _():
            pl.when(at.below)(lambda: self.link_copy(s, o, o, at.me).wait_recv())
            pl.when(at.above)(lambda: self.link_copy(s, o, at.chips, at.me).wait_recv())
            for slot, used in ((o, at.below), (at.chips, at.above)):
                @pl.when(jnp.logical_not(used))
                def _():
                    def clear(first, step):
                        self.link[s, slot, pl.ds(first, step)] = jnp.zeros(
                            (step, self.link.shape[-1]), bf16
                        )

                    self.blocks(clear)
            base = at.core * self.rows

            def body(first, step):
                here = pl.ds(pl.multiple_of(base + first, step), step)
                there = pl.ds(first, step)
                total = self.part[s, o, here].astype(f32) + self.side[s, o, there].astype(f32)
                total += self.link[s, o, there].astype(f32)
                total += self.link[s, at.chips, there].astype(f32)
                final(s, there, total)

            self.blocks(body)

    def finish(self):
        at = self.at

        def one(i, carry):
            s, o = i // at.chips, lax.rem(i, at.chips)
            self.side_copy(s, o).wait_send()
            pl.when(o != at.chip)(lambda: self.link_copy(s, o, o, at.side).wait_send())
            return carry

        lax.fori_loop(0, self.seqs * at.chips, one, 0)


class GroupSum:
    def __init__(self, at, rows, tiles, inbox, send, recv, keep_sem, out, turn=0, skip=0):
        self.at, self.tiles, self.inbox, self.send, self.recv = at, tiles, inbox, send, recv
        self.keep_sem, self.out, self.skip, self.turn, self.rows = keep_sem, out, skip, turn, rows
        self.bits = at.group_bits
        self.count = send.shape[0]

    @staticmethod
    def scratch(dp, count, rows, width, skip=0):
        phases = 2 * (dp.bit_length() - 1)
        return [
            VMEM((count, rows >> skip, width), bf16),
            VMEM((count, rows - rows // dp, width), bf16),
            DMA((count, phases)),
            DMA((count, phases)),
            DMA((count,)),
        ]

    def peer(self, t, i):
        which = lax.rem(t + i + self.turn, self.bits)
        peer, mine = 0, 0
        for q in range(self.bits):
            other, bit = self.at.group_peer(q)
            peer = peer + jnp.where(which == q, other, 0)
            mine = mine + jnp.where(which == q, bit, 0)
        return peer, mine

    def base(self, t, i):
        first = 0
        for p in range(i):
            first = first + self.peer(t, p)[1] * (self.rows >> (p + 1))
        return first

    def span(self, first, size):
        return pl.ds(pl.multiple_of(first, 16), size)

    def tile(self, t, first, size):
        return self.tiles.at[t, self.span(first - self.base(t, self.skip), size)]

    def box(self, t, i):
        return self.inbox.at[t, pl.ds(self.rows - (self.rows >> i), self.rows >> (i + 1))]

    def remote(self, source, target, t, phase, peer):
        return pltpu.make_async_remote_copy(
            src_ref=source,
            dst_ref=target,
            send_sem=self.send.at[t, phase],
            recv_sem=self.recv.at[t, phase],
            device_id={"dp": peer},
            device_id_type=MESH,
        )

    def halve(self, t, i):
        peer, mine = self.peer(t, i)
        half = self.rows >> (i + 1)
        source = self.tile(t, self.base(t, i) + (1 - mine) * half, half)
        return self.remote(source, self.box(t, i), t, i, peer)

    def add(self, t, i):
        half = self.rows >> (i + 1)
        keep = self.base(t, i + 1) - self.base(t, self.skip)
        box = self.rows - (self.rows >> i)

        def body(j, carry):
            here = self.span(keep + j * 16, 16)
            there = self.span(box + j * 16, 16)
            total = self.tiles[t, here].astype(f32) + self.inbox[t, there].astype(f32)
            self.tiles[t, here] = total.astype(bf16)
            return carry

        lax.fori_loop(0, half // 16, body, 0)

    def keep(self, t):
        first, size = self.base(t, self.bits), self.rows >> self.bits
        return pltpu.make_async_copy(
            self.tile(t, first, size), self.out.at[t, self.span(first, size)], self.keep_sem.at[t]
        )

    def double(self, t, i, back=False):
        peer, mine = self.peer(t, i)
        half = self.rows >> (i + 1)
        first = self.base(t, i) + ((1 - mine) if back else mine) * half
        piece = self.out.at[t, self.span(first, half)]
        source = piece
        if i == self.bits - 1 and not back:
            source = self.tile(t, first, half)
        return self.remote(source, piece, t, 2 * self.bits - 1 - i, peer)

    def events(self):
        return self.count * (2 * self.bits + 1 - self.skip)

    def event(self, e, loaded=None):
        k, t = e // self.count + self.skip, lax.rem(e, self.count)
        bits = self.bits

        def at_stage(stage):
            if stage == self.skip and loaded is not None:
                loaded(t)
            if stage == 0:
                self.halve(t, 0).start()
            elif stage <= bits:
                if stage > self.skip:
                    self.halve(t, stage - 1).wait_recv()
                self.add(t, stage - 1)
                if stage < bits:
                    self.halve(t, stage).start()
                else:
                    self.keep(t).start()
                    self.double(t, bits - 1).start()
            else:
                i = 2 * bits - stage
                self.double(t, i, back=True).wait_recv()
                if i == bits - 1:
                    self.keep(t).wait()
                if i > 0:
                    self.double(t, i - 1).start()

        for stage in range(self.skip, 2 * bits + 1):
            pl.when((k == stage) & (e >= 0))(functools.partial(at_stage, stage))

    def finish(self):
        def one(t, carry):
            for i in range(self.bits):
                if i >= self.skip:
                    self.halve(t, i).wait_send()
                self.double(t, i).wait_send()
            return carry

        lax.fori_loop(0, self.count, one, 0)


class SmallSum:
    def __init__(self, at, rows, inbox, send, recv, everywhere):
        self.at, self.rows, self.inbox, self.send, self.recv = at, rows, inbox, send, recv
        self.phases = at.group_bits + (at.bits if everywhere else 0)

    @staticmethod
    def scratch(dp, n, count, width, everywhere):
        phases = (dp.bit_length() - 1) + (n.bit_length() - 1 if everywhere else 0)
        return [
            VMEM((phases + 1, count, width), f32),
            VMEM((phases, count, width), f32),
            DMA((phases,)),
            DMA((phases,)),
        ]

    def copy(self, i):
        at = self.at
        if i < at.group_bits:
            target = {"dp": at.group_peer(i)[0]}
        else:
            target = {"tensor": at.peer(i - at.group_bits)}
        return pltpu.make_async_remote_copy(
            src_ref=self.rows.at[i],
            dst_ref=self.inbox.at[i],
            send_sem=self.send.at[i],
            recv_sem=self.recv.at[i],
            device_id=target,
            device_id_type=MESH,
        )

    def event(self, e):
        def run(i):
            if i > 0:
                self.copy(i - 1).wait_recv()
                self.rows[i] = self.rows[i - 1] + self.inbox[i - 1]
            if i < self.phases:
                self.copy(i).start()

        for i in range(self.phases + 1):
            if isinstance(e, int):
                if e == i:
                    run(i)
            else:
                pl.when(e == i)(functools.partial(run, i))

    def finish(self):
        for i in range(self.phases):
            self.copy(i).wait_send()


class DirectSum:
    def __init__(self, at, rows, group_box, line_box, send, recv):
        self.at, self.rows, self.send, self.recv = at, rows, send, recv
        self.boxes = (group_box, line_box)

    @staticmethod
    def scratch(dp, n, count, width):
        most = max(dp, n)
        return [
            VMEM((count, width), f32),
            VMEM((dp, count, width), f32),
            VMEM((n, count, width), f32),
            DMA((2, most)),
            DMA((2, most)),
        ]

    def copy(self, step, other, back=False):
        at, box = self.at, self.boxes[step]
        size, axis = box.shape[0], ("dp", "tensor")[step]
        mine = (at.group, at.me)[step]
        peer = lax.rem(mine + other, size)
        slot = peer if back else mine
        return pltpu.make_async_remote_copy(
            src_ref=box.at[mine],
            dst_ref=box.at[slot],
            send_sem=self.send.at[step, other],
            recv_sem=self.recv.at[step, slot],
            device_id={axis: peer},
            device_id_type=MESH,
        )

    def event(self, e):
        if e > 0:
            box = self.boxes[e - 1]
            for other in range(1, box.shape[0]):
                self.copy(e - 1, other, back=True).wait_recv()
            total = box[0]
            for i in range(1, box.shape[0]):
                total = total + box[i]
            self.rows[...] = total
        if e < 2:
            box = self.boxes[e]
            box[(self.at.group, self.at.me)[e]] = self.rows[...]
            for other in range(1, box.shape[0]):
                self.copy(e, other).start()

    def finish(self):
        for step, box in enumerate(self.boxes):
            for other in range(1, box.shape[0]):
                self.copy(step, other).wait_send()


def norm_rows(values, gain, shift):
    centre = values - jnp.mean(values, axis=-1, keepdims=True)
    spread = jnp.mean(centre * centre, axis=-1, keepdims=True)
    return centre * lax.rsqrt(spread + norm_epsilon) * gain + shift


def norm_rows_back(values, grad, gain):
    centre = values - jnp.mean(values, axis=-1, keepdims=True)
    scale = lax.rsqrt(jnp.mean(centre * centre, axis=-1, keepdims=True) + norm_epsilon)
    unit = centre * scale
    w = grad * gain
    back = w - jnp.mean(w, axis=-1, keepdims=True)
    back = scale * (back - unit * jnp.mean(w * unit, axis=-1, keepdims=True))
    return back, grad * unit


def add_row(ref, row, values):
    ref[row : row + 1] += jnp.sum(values, axis=0, keepdims=True)


def head_probs(query, keys, first, length):
    rows, cols = query.shape[0], keys.shape[0]
    scores = lax.dot_general(query, keys, NT, preferred_element_type=f32)
    row_ids = first + lax.broadcasted_iota(jnp.int32, (rows, cols), 0)
    col_ids = lax.broadcasted_iota(jnp.int32, (rows, cols), 1)
    scores = jnp.where((col_ids <= row_ids) & (col_ids < length), scores, -1e30)
    probs = jnp.exp(scores - jnp.max(scores, axis=-1, keepdims=True))
    return probs * (1.0 / jnp.sum(probs, axis=-1, keepdims=True))


def attend(heads, lengths, mixed, block, s):
    slots, part = mixed.shape[1:]

    def one(h, carry):
        cols = pl.ds(pl.multiple_of(h * HD, HD), HD)
        for first in range(0, slots, block):
            rows, seen = pl.ds(first, block), pl.ds(0, first + block)
            probs = head_probs(heads[0, s, rows, cols], heads[1, s, seen, cols], first, lengths[s])
            mixed[s, rows, cols] = jnp.dot(
                probs.astype(bf16), heads[2, s, seen, cols], preferred_element_type=f32
            ).astype(bf16)
        return carry

    lax.fori_loop(0, part // HD, one, 0)


def attend_back(heads, grad_heads, lengths, grads, grad_key, grad_value, block, s):
    slots, part = grad_heads.shape[1:]

    def one(h, carry):
        cols = pl.ds(pl.multiple_of(h * HD, HD), HD)
        grad_key[...] = jnp.zeros_like(grad_key)
        grad_value[...] = jnp.zeros_like(grad_value)
        for first in range(0, slots, block):
            rows, seen = pl.ds(first, block), pl.ds(0, first + block)
            query, grad = heads[0, s, rows, cols], grad_heads[s, rows, cols]
            keys = heads[1, s, seen, cols]
            probs = head_probs(query, keys, first, lengths[s])
            grad_value[seen] += lax.dot_general(
                probs.astype(bf16), grad, TN, preferred_element_type=f32
            )
            back = lax.dot_general(
                grad, heads[2, s, seen, cols], NT, preferred_element_type=f32
            )
            centre = jnp.sum(probs * back, axis=-1, keepdims=True)
            scores = (probs * (back - centre)).astype(bf16)
            grads[0, s, rows, cols] = jnp.dot(
                scores, keys, preferred_element_type=f32
            ).astype(bf16)
            grad_key[seen] += lax.dot_general(scores, query, TN, preferred_element_type=f32)
        grads[1, s, :, cols] = grad_key[...].astype(bf16)
        grads[2, s, :, cols] = grad_value[...].astype(bf16)
        return carry

    lax.fori_loop(0, part // HD, one, 0)


def attention_block_kernel(
    n,
    tokens,
    cotangent,
    lengths,
    gain,
    shift,
    weight,
    bias,
    out_weight,
    out_bias,
    gain_two,
    shift_two,
    gathered,
    heads,
    mixed,
    hidden,
    normed,
    grad_all,
    buf,
    send,
    recv,
    keep_sem,
    grad_send,
    grad_recv,
    masked,
    mask_sem,
    *scratch,
):
    at = Place(n)
    seqs, rows, width = tokens.shape
    ring = Gather(at, rows, buf, send, recv)
    grad_ring = Gather(at, rows, grad_all, grad_send, grad_recv)
    line = Scatter(at, rows, *scratch)

    def mask_copy(s):
        return pltpu.make_async_copy(
            masked.at[s], grad_all.at[s, rows_of(at.me, rows)], mask_sem.at[s]
        )

    for s in range(seqs):
        def block(i, carry):
            first = pl.multiple_of(i * 16, 16)
            here = pl.ds(first, 16)
            values = norm_rows(tokens[s, here].astype(f32), gain[...], shift[...])
            buf[s, pl.ds(pl.multiple_of(at.me * rows + first, 16), 16)] = values.astype(bf16)
            slot = at.me * rows + first + lax.broadcasted_iota(jnp.int32, (16, width), 0)
            grad = jnp.where(slot < lengths[s], cotangent[s, here].astype(f32), 0.0)
            masked[s, here] = grad.astype(bf16)
            return carry

        lax.fori_loop(0, rows // 16, block, 0)
        mask_copy(s).start()
    at.greet()
    for s in range(seqs):
        mask_copy(s).wait()

    def keep(s, o):
        here = rows_of(o, 2 * rows)
        return pltpu.make_async_copy(buf.at[s, here], gathered.at[s, here], keep_sem.at[s, o])

    def project(s, o):
        ring.arrived(s, o, 1 - at.core)
        keep(s, o).start()
        here = rows_of(o, 2 * rows)
        for j in range(3):
            total = jnp.dot(buf[s, here], weight[j], preferred_element_type=f32)
            if j == 0:
                total = (total + bias[0:1]) * HD ** (-0.5)
            if j == 2:
                total = total + bias[1:2]
            heads[j, s, here] = total.astype(bf16)

    def final(s, there, total):
        values = tokens[s, there].astype(f32) + total + out_bias[...]
        hidden[s, there] = values
        normed[s, there] = norm_rows(values, gain_two[...], shift_two[...]).astype(bf16)

    def mix(s, o):
        attend(heads, lengths, mixed, min(512, n * rows), s)

    def project_out(s, o):
        here = rows_of(o, 2 * rows)
        for j in range(width // 512):
            cols = pl.ds(j * 512, 512)
            total = jnp.dot(mixed[s, here], out_weight[:, cols], preferred_element_type=f32)
            line.part[s, o, :, cols] = total.astype(bf16)
        line.share(s, o)

    def ops_of(c):
        chips = at.chips
        mixing = []
        for s in range(seqs):
            needs = [("heads", c, s, o) for o in range(chips)]
            mixing.append(((2, s, 0), (2, s, 0), needs, 6.0, [], [(0.0, ("mixed", c, s))]))
        return (
            gather_ops(c, chips, seqs, 0, "in", gate=True)
            + work_ops(
                c, chips, seqs, 1, lambda s, o: [("in", c, s, o, "both")], "heads", 1.0
            )
            + mixing
            + work_ops(
                c, chips, seqs, 3, lambda s, o: [("mixed", c, s)], "part", 1.0, far=True
            )
            + scatter_ops(c, chips, seqs, 4, "out", "part", last=4.0)
            + gather_ops(c, chips, seqs, 5, "grad", rank=6)
        )

    Plan(at, seqs, ops_of).run(
        {
            0: ring.relay,
            1: project,
            2: mix,
            3: project_out,
            4: functools.partial(line.pass_on, final),
            5: grad_ring.relay,
        }
    )
    ring.finish()
    line.finish()
    grad_ring.finish()

    def close(i, carry):
        s, o = i // at.chips, lax.rem(i, at.chips)
        grad_ring.arrived(s, o, 1 - at.core)
        keep(s, o).wait()
        return carry

    lax.fori_loop(0, seqs * at.chips, close, 0)


def whole(count):
    return [pl.BlockSpec(memory_space=VMEM)] * count


def attention_block(
    n,
    tokens,
    cotangent,
    lengths,
    gain,
    shift,
    weight,
    bias,
    out_weight,
    out_bias,
    gain_two,
    shift_two,
):
    seqs, rows, width = tokens.shape
    part = weight.shape[2]
    vmem = pl.BlockSpec(memory_space=VMEM)
    hbm = pl.BlockSpec(memory_space=pl.ANY)
    smem = pl.BlockSpec(memory_space=pltpu.SMEM)
    return pl.pallas_call(
        functools.partial(attention_block_kernel, n),
        out_shape=(
            jax.ShapeDtypeStruct((seqs, n * rows, width), bf16),
            jax.ShapeDtypeStruct((3, seqs, n * rows, part), bf16),
            jax.ShapeDtypeStruct((seqs, n * rows, part), bf16),
            jax.ShapeDtypeStruct((seqs, rows, width), f32),
            jax.ShapeDtypeStruct((seqs, rows, width), bf16),
            jax.ShapeDtypeStruct((seqs, n * rows, width), bf16),
        ),
        in_specs=[vmem, vmem, smem] + [vmem] * 8,
        out_specs=(hbm, vmem, vmem, vmem, vmem, hbm),
        scratch_shapes=[VMEM((seqs, n * rows, width), bf16)]
        + Gather.scratch(n, seqs)
        + [DMA((seqs, n // 2))]
        + Gather.scratch(n, seqs)
        + [VMEM((seqs, rows, width), bf16), DMA((seqs,))]
        + Scatter.scratch(n, seqs, rows, width),
        compiler_params=pltpu.CompilerParams(
            collective_id=0, has_side_effects=True, vmem_limit_bytes=60 * 2**20
        ),
        name="attention_block",
    )(
        tokens,
        cotangent,
        lengths,
        gain,
        shift,
        weight,
        bias,
        out_weight,
        out_bias,
        gain_two,
        shift_two,
    )


def heads_scatter_kernel(
    n,
    grads,
    weight,
    gathered_hbm,
    out_part,
    tokens_hbm,
    gain,
    hidden_hbm,
    grad,
    sums_all,
    weight_grad,
    out_grad,
    bias_grad,
    *scratch,
):
    at = Place(n)
    seqs, rows, width = hidden_hbm.shape
    line = Scatter(at, rows, *scratch[:7])
    weight_sum = GroupSum(at, width, *scratch[7:12], weight_grad)
    out_sum = GroupSum(at, out_part.shape[0], *scratch[12:17], out_grad, turn=1)
    small = DirectSum(at, *scratch[17:22])
    small_bias = SmallSum(at, *scratch[22:26], False)
    gathered, tokens, hidden_grad, in_sem = scratch[26:]
    sources = ((gathered_hbm, gathered), (tokens_hbm, tokens), (hidden_hbm, hidden_grad))
    loads = [
        pltpu.make_async_copy(source, target, in_sem.at[i])
        for i, (source, target) in enumerate(sources)
    ]
    for copy in loads:
        copy.start()
    out_sum.tiles[0] = out_part[...]
    small.rows[...] = jnp.zeros_like(small.rows)
    at.greet(groups=True, everyone=True)

    def bias_sums():
        for row, j, scale in ((0, 0, HD ** (-0.5)), (1, 2, 1.0)):
            total = 0.0
            for s in range(seqs):
                total += jnp.sum(grads[j, s].astype(f32), axis=0, keepdims=True)
            small_bias.rows[0, row : row + 1] = scale * total

    def beside(k):
        pl.when(k == 10)(bias_sums)
        for e in range(small_bias.phases + 1):
            pl.when(k == 11 + 6 * e)(functools.partial(small_bias.event, e))


    def final(s, there, total):
        back, terms = norm_rows_back(tokens[s, there].astype(f32), total, gain[...])
        grad[s, there] = hidden_grad[s, there] + back
        add_row(small.rows, 0, terms)
        add_row(small.rows, 1, total)

    scales = (HD ** (-0.5), 1.0, 1.0)

    def weight_tile(j):
        for first in range(0, width, 512):
            total = 0.0
            for s in range(seqs):
                total += lax.dot_general(
                    gathered[s, :, pl.ds(first, 512)],
                    grads[j, s],
                    TN,
                    preferred_element_type=f32,
                )
            weight_sum.tiles[j, pl.ds(first, 512)] = (scales[j] * total).astype(bf16)

    def work(s, o):
        here = rows_of(o, 2 * rows)
        for j in range(width // 512):
            cols = pl.ds(j * 512, 512)
            total = 0.0
            for i in range(3):
                total += scales[i] * lax.dot_general(
                    grads[i, s, here], weight[i, cols], NT, preferred_element_type=f32
                )
            line.part[s, o, :, cols] = total.astype(bf16)
        line.share(s, o)

    each = seqs * at.chips

    def weight_event(first, s, o):
        e = first + s * at.chips + o

        @pl.when(e == 0)
        def _():
            for copy in loads:
                copy.wait()

        for j in range(3):
            pl.when(e == j)(functools.partial(weight_tile, j))
        weight_sum.event(e)

    def out_event(s, o):
        out_sum.event(s * at.chips + o)

    def code_of(kind, e):
        return (kind + e // each, e % each // at.chips, e % at.chips)

    def ops_of(c):
        chips = at.chips
        finals = scatter_ops(c, chips, seqs, 1, "out", "part", last=4.0)
        loaded = ("qkv", c, 0, 0, 1)
        for i, (rank, code, needs, time, sends, gives) in enumerate(finals):
            if code[2] == c:
                finals[i] = (rank, code, needs + [loaded], time, sends, gives)
        smalls = []
        needs = [("out", c, s, "sum") for s in range(seqs)]
        for e in range(3):
            smalls.append(((0, e), (30 + e, 0, 0), needs, 0.5, [], [(4.0, ("small", c, e))]))
            needs = [("small", c, e)]
        return smalls + (
            work_ops(c, chips, seqs, 0, lambda s, o: [], "part", 1.5, far=True)
            + finals
            + group_ops(
                c, at.group_bits, 3, PIECE, lambda e: code_of(2, e), 0, (0,), 2.7, name="qkv"
            )
            + group_ops(
                c, at.group_bits, 1, PIECE, lambda e: code_of(5, e), 0, (1,), 0.7, name="out_sum"
            )
        )

    actions = {0: work, 1: functools.partial(line.pass_on, final), 5: out_event}
    for i in range(3):
        actions[2 + i] = functools.partial(weight_event, i * each)
        actions[30 + i] = lambda s, o, e=i: small.event(e)
    Plan(at, seqs, ops_of).run(actions, beside)
    small.finish()
    sums_all[...] = small.rows[...]
    bias_grad[...] = small_bias.rows[small_bias.phases]
    line.finish()
    weight_sum.finish()
    out_sum.finish()
    small_bias.finish()


def heads_scatter(n, grads, weight, gathered, out_part, tokens, gain, hidden_grad):
    seqs, slots, part = grads.shape[1:]
    width = weight.shape[1]
    rows = slots // n
    dp = lax.axis_size("dp")
    vmem = pl.BlockSpec(memory_space=VMEM)
    hbm = pl.BlockSpec(memory_space=pl.ANY)
    return pl.pallas_call(
        functools.partial(heads_scatter_kernel, n),
        out_shape=(
            jax.ShapeDtypeStruct((seqs, rows, width), f32),
            jax.ShapeDtypeStruct((2, width), f32),
            jax.ShapeDtypeStruct((3, width, part), bf16),
            jax.ShapeDtypeStruct((1, part, width), bf16),
            jax.ShapeDtypeStruct((2, part), f32),
        ),
        in_specs=[vmem, vmem, hbm, vmem, hbm, vmem, hbm],
        out_specs=(vmem, vmem, hbm, hbm, vmem),
        scratch_shapes=Scatter.scratch(n, seqs, rows, width)
        + GroupSum.scratch(dp, 3, width, part)
        + GroupSum.scratch(dp, 1, part, width)
        + DirectSum.scratch(dp, n, 2, width)
        + SmallSum.scratch(dp, n, 2, part, False)
        + [
            VMEM(gathered.shape, bf16),
            VMEM(tokens.shape, bf16),
            VMEM(hidden_grad.shape, f32),
            DMA((3,)),
        ],
        compiler_params=pltpu.CompilerParams(
            collective_id=2, has_side_effects=True, vmem_limit_bytes=62 * 2**20
        ),
        name="heads_scatter",
    )(grads, weight, gathered, out_part, tokens, gain, hidden_grad)


def normal_cdf(values):
    x = jnp.clip(values * 0.7071067811865476, -3.832506856900711, 3.832506856900711)
    x2 = x * x
    top = 0.00022905065861350646
    for c in (0.0034082910107109506, 0.050955695062380861, 0.18520832239976145, 1.128379143519084):
        top = top * x2 + c
    low = -1.1791602954361697e-7
    for c in (
        0.000023547966471313185,
        0.0010179625278914885,
        0.014070470171167667,
        0.11098505178285362,
        0.49746925110067538,
        1.0,
    ):
        low = low * x2 + c
    return 0.5 + 0.5 * (x * top / low)


def mlp_kernel(
    n,
    normed,
    grad_hbm,
    up_hbm,
    up_bias,
    down_hbm,
    hidden_hbm,
    gain,
    mlp_part,
    hidden_grad,
    grad_low,
    sums,
    up_grad,
    up_bias_grad,
    down_grad,
    down_box,
    buf,
    send,
    recv,
    grad_all,
    up_weight,
    down_weight,
    hidden,
    in_sem,
    *scratch,
):
    at = Place(n)
    seqs, rows, width = normed.shape
    units_wide = up_weight.shape[1]
    line = Scatter(at, rows, *scratch[:7])
    act, pre, out_stage, out_sem, up_stage, down_stage, tile_sem, half_send, half_recv = scratch[7:]
    ring = Gather(at, rows, buf, send, recv)
    loads = [
        pltpu.make_async_copy(source, target, in_sem.at[i])
        for i, (source, target) in enumerate(
            (
                (up_hbm, up_weight),
                (grad_hbm, grad_all),
                (down_hbm, down_weight),
                (hidden_hbm, hidden),
            )
        )
    ]
    for copy in loads:
        copy.start()
    at.greet(groups=True)
    for s in range(seqs):
        buf[s, rows_of(at.me, rows)] = normed[s]
    up_bias_grad[...] = jnp.zeros_like(up_bias_grad)
    sums[...] = jnp.zeros_like(sums)
    ft = min(512, units_wide)

    def out_copy(s, o):
        return pltpu.make_async_copy(
            out_stage, mlp_part.at[s, rows_of(o, 2 * rows)], out_sem.at[0]
        )

    def work(s, o):
        ring.arrived(s, o, 1 - at.core)

        @pl.when((s == 0) & (o == at.chip))
        def _():
            for copy in loads:
                copy.wait()

        here = rows_of(o, 2 * rows)
        for j in range(units_wide // ft):
            cols = pl.ds(j * ft, ft)
            value = jnp.dot(buf[s, here], up_weight[:, cols], preferred_element_type=f32)
            value = value + up_bias[:, cols]
            spread = normal_cdf(value)
            act[s, here, cols] = (value * spread).astype(bf16)
            slope = spread + value * (0.3989422804014327 * jnp.exp(-0.5 * value * value))
            grad = lax.dot_general(
                grad_all[s, here], down_weight[cols], NT, preferred_element_type=f32
            )
            grad = (grad * slope).astype(bf16)
            pre[s, here, cols] = grad
            up_bias_grad[:, cols] += jnp.sum(grad.astype(f32), axis=0, keepdims=True)
        for j in range(width // 512):
            cols = pl.ds(j * 512, 512)
            line.part[s, o, :, cols] = lax.dot_general(
                pre[s, here], up_weight[cols], NT, preferred_element_type=f32
            ).astype(bf16)
        line.share(s, o)
        pl.when((s > 0) | (o != at.chip))(lambda: out_copy(s, o).wait())
        for j in range(width // 512):
            cols = pl.ds(j * 512, 512)
            out_stage[:, cols] = jnp.dot(
                act[s, here], down_weight[:, cols], preferred_element_type=f32
            ).astype(bf16)
        out_copy(s, o).start()

    def final(s, there, total):
        back, terms = norm_rows_back(hidden[s, there], total, gain[...])
        first = pl.multiple_of(at.me * rows + there.start, 16)
        grad_out = grad_all[s, pl.ds(first, there.size)].astype(f32)
        grad = grad_out + back
        hidden_grad[s, there] = grad
        grad_low[s, there] = grad.astype(bf16)
        add_row(sums, 0, terms)
        add_row(sums, 1, total)
        add_row(sums, 2, grad)
        add_row(sums, 3, grad_out)

    kinds = ((down_stage, down_grad), (up_stage, up_grad))

    def tile_copy(kind, t):
        stage, grad = kinds[kind]
        return pltpu.make_async_copy(stage, grad.at[t], tile_sem.at[kind])

    def down_half(t):
        half = down_box.shape[1]
        peer, mine = at.group_peer(t % at.group_bits)
        return pltpu.make_async_remote_copy(
            src_ref=down_grad.at[t, rows_of(1 - mine, half)],
            dst_ref=down_box.at[t],
            send_sem=half_send.at[t],
            recv_sem=half_recv.at[t],
            device_id={"dp": peer},
            device_id_type=MESH,
        )

    def tile_sent(kind, t):
        tile_copy(kind, t).wait()
        if kind == 0:
            down_half(t).start()

    order = [(i // 4, i % 4) for i in range(8)]

    def weight_tile(i):
        for j, (kind, t) in enumerate(order):
            @pl.when(i == j)
            def _():
                stage = kinds[kind][0]
                cols = pl.ds(t * stage.shape[0], stage.shape[0])
                total = 0.0
                for s in range(seqs):
                    if kind == 0:
                        left, right = act[s, :, cols], grad_all[s]
                    else:
                        left, right = buf[s, :, cols], pre[s]
                    total += lax.dot_general(left, right, TN, preferred_element_type=f32)
                if j >= 1:
                    tile_sent(*order[j - 1])
                stage[...] = total.astype(bf16)
                tile_copy(kind, t).start()

    def tile_work(s, o):
        weight_tile(s * at.chips + o)

    own = (4, 5, 6)

    def ops_of(c):
        chips = at.chips
        units = [(s, o) for s in range(seqs) for o in range(chips)]
        ops = (
            gather_ops(c, chips, seqs, 0, "in", own=own)
            + scatter_ops(c, chips, seqs, 1, "back", "part", last=4.0)
            + work_ops(
                c, chips, seqs, 2, lambda s, o: [("in", c, s, o, "both")], "part", 5.7
            )
        )
        for i in range(len(ops)):
            rank, code, needs, time, sends, gives = ops[i]
            if code[0] == 2 and code[1:] != (0, c):
                ops[i] = (rank, code, needs + [("first", c)], time, sends, gives)
            if code == (2, 0, c):
                ops[i] = (rank, code, needs, time, sends, gives + [(0.0, ("first", c))])
        for e in range(len(order)):
            needs = [("part", c, s, o) for s, o in units]
            needs += [("tile", c, e - 1)] if e else []
            sends = [("axis%d" % (e % 2), c, ("half", c, e), PIECE)] if e < 4 else []
            code = (3, e // chips, e % chips)
            ops.append(((4, e, 0), code, needs, 2.7, sends, [(0.0, ("tile", c, e))]))
        return ops

    actions = {0: ring.relay, 1: functools.partial(line.pass_on, final), 2: work, 3: tile_work}
    actions.update(ring.owns(own))
    Plan(at, seqs, ops_of).run(actions)
    tile_sent(*order[7])
    ring.finish()
    line.finish()
    for t in range(4):
        down_half(t).wait()
    out_copy(0, 0).wait()


def mlp_block(n, normed, grad_all, up_weight, up_bias, down_weight, hidden, gain):
    seqs, rows, width = normed.shape
    slots = n * rows
    units = up_weight.shape[1]
    hbm = pl.BlockSpec(memory_space=pl.ANY)
    vmem = pl.BlockSpec(memory_space=VMEM)
    down_size, up_size = units // 4, width // 4
    return pl.pallas_call(
        functools.partial(mlp_kernel, n),
        out_shape=(
            jax.ShapeDtypeStruct((seqs, slots, width), bf16),
            jax.ShapeDtypeStruct((seqs, rows, width), f32),
            jax.ShapeDtypeStruct((seqs, rows, width), bf16),
            jax.ShapeDtypeStruct((4, width), f32),
            jax.ShapeDtypeStruct((4, up_size, units), bf16),
            jax.ShapeDtypeStruct((1, units), f32),
            jax.ShapeDtypeStruct((4, down_size, width), bf16),
            jax.ShapeDtypeStruct((4, down_size // 2, width), bf16),
        ),
        in_specs=[vmem, hbm, hbm, vmem, hbm, hbm, vmem],
        out_specs=(hbm, vmem, vmem, vmem, hbm, vmem, hbm, hbm),
        scratch_shapes=[VMEM((seqs, slots, width), bf16)]
        + Gather.scratch(n, seqs)
        + [
            VMEM((seqs, slots, width), bf16),
            VMEM(up_weight.shape, bf16),
            VMEM(down_weight.shape, bf16),
            VMEM(hidden.shape, f32),
            DMA((4,)),
        ]
        + Scatter.scratch(n, seqs, rows, width)
        + [
            VMEM((seqs, slots, units), bf16),
            VMEM((seqs, slots, units), bf16),
            VMEM((2 * rows, width), bf16),
            DMA((1,)),
            VMEM((up_size, units), bf16),
            VMEM((down_size, width), bf16),
            DMA((2,)),
            DMA((4,)),
            DMA((4,)),
        ],
        compiler_params=pltpu.CompilerParams(
            collective_id=3, has_side_effects=True, vmem_limit_bytes=62 * 2**20
        ),
        name="mlp_block",
    )(normed, grad_all, up_weight, up_bias, down_weight, hidden, gain)


def attn_grad_kernel(
    n,
    grad,
    mlp_part,
    hidden,
    bias,
    weight,
    mixed,
    sums,
    up_bias_part,
    up_part,
    down_part,
    down_box,
    lengths,
    heads,
    output,
    grads,
    weight_grad,
    sums_all,
    up_bias_grad,
    up_grad,
    down_grad,
    buf,
    send,
    recv,
    *scratch,
):
    at = Place(n)
    seqs, rows, width = grad.shape
    line = Scatter(at, rows, *scratch[:7])
    load_sem, tile_sem, box_sem = scratch[7:10]
    ring = Gather(at, rows, buf, send, recv)
    up_sum = GroupSum(at, up_part.shape[1], *scratch[10:15], up_grad, turn=1)
    down_sum = GroupSum(at, down_part.shape[1], *scratch[15:20], down_grad, skip=1)
    small = SmallSum(at, *scratch[20:24], True)
    small_bias = SmallSum(at, *scratch[24:28], False)
    grad_heads, grad_key, grad_value = scratch[28:]
    def up_load(t):
        return pltpu.make_async_copy(up_part.at[t], up_sum.tiles.at[t], tile_sem.at[0, t])

    def down_load(t):
        half = down_box.shape[1]
        kept = down_part.at[t, down_sum.span(down_sum.base(t, 1), half)]
        return (
            pltpu.make_async_copy(kept, down_sum.tiles.at[t], tile_sem.at[1, t]),
            pltpu.make_async_copy(down_box.at[t], down_sum.box(t, 0), box_sem.at[t]),
        )

    def up_loaded(t):
        up_load(t).wait()

    def down_loaded(t):
        for copy in down_load(t):
            copy.wait()

    for t in range(4):
        up_load(t).start()
        for copy in down_load(t):
            copy.start()
    small.rows[0] = sums[...]
    small_bias.rows[0] = up_bias_part[...]

    def load(s, o):
        return pltpu.make_async_copy(
            mlp_part.at[s, rows_of(o, 2 * rows)], line.part.at[s, o], load_sem.at[s, o]
        )

    def load_one(i, carry):
        load(i // at.chips, lax.rem(i, at.chips)).start()
        return carry

    each = seqs * at.chips
    lax.fori_loop(0, each, load_one, 0)
    for s in range(seqs):
        buf[s, rows_of(at.me, rows)] = grad[s]
    at.greet(groups=True, cube=True)

    def final(s, there, total):
        output[s, there] = (hidden[s, there] + total + bias[...]).astype(bf16)

    def share(s, o):
        load(s, o).wait()
        line.share(s, o)

    def work(s, o):
        ring.arrived(s, o, 1 - at.core)
        here = rows_of(o, 2 * rows)
        grad_heads[s, here] = lax.dot_general(
            buf[s, here], weight[...], NT, preferred_element_type=f32
        ).astype(bf16)

    def back(s, o):
        block = min(512, n * rows)
        attend_back(heads, grad_heads, lengths, grads, grad_key, grad_value, block, s)

    def weight_work(s, o):
        for j in range(width // 512):
            cols = pl.ds(j * 512, 512)
            total = 0.0
            for q in range(seqs):
                total += lax.dot_general(mixed[q], buf[q, :, cols], TN, preferred_element_type=f32)
            weight_grad[:, cols] = total.astype(bf16)

    def up_event(first, s, o):
        up_sum.event(first + s * at.chips + o, up_loaded)

    def down_event(first, s, o):
        down_sum.event(first + s * at.chips + o, down_loaded)

    def ops_of(c):
        chips = at.chips
        code_of = lambda kind, e: (kind + e // each, e % each // chips, e % chips)
        backs = []
        for s in range(seqs):
            needs = [("done", c, s, o) for o in range(chips)]
            backs.append(((4, s, 0), (4, s, 0), needs, 8.0, [], []))
        needs = [("done", c, s, o) for s in range(seqs) for o in range(chips)]
        backs.append(((5, 0, 0), (5, 0, 0), needs, 3.0, [], []))
        return backs + (
            gather_ops(c, chips, seqs, 0, "in")
            + scatter_ops(c, chips, seqs, 1, "out", "part", last=4.0)
            + work_ops(c, chips, seqs, 2, lambda s, o: [("in", c, s, o, "both")], "done", 1.0)
            + work_ops(c, chips, seqs, 3, lambda s, o: [], "part", 0.3, rank=0, far=True)
            + group_ops(
                c, at.group_bits, 4, PIECE, lambda e: code_of(8, e), 0, (1,), 0.7, -1, "up"
            )
            + group_ops(
                c, at.group_bits, 4, PIECE, lambda e: code_of(16, e), 1, (0,), 0.7, -1, "down"
            )
        )

    actions = {0: ring.relay, 1: functools.partial(line.pass_on, final), 2: work, 3: share}
    actions[4], actions[5] = back, weight_work
    for i in range(-(-up_sum.events() // each)):
        actions[8 + i] = functools.partial(up_event, i * each)
    for i in range(-(-down_sum.events() // each)):
        actions[16 + i] = functools.partial(down_event, i * each)

    def beside(k):
        pl.when(lax.rem(k, 8) == 0)(lambda: small.event(k // 8))
        small_bias.event(k)

    Plan(at, seqs, ops_of).run(actions, beside)
    sums_all[...] = small.rows[small.phases]
    up_bias_grad[...] = small_bias.rows[small_bias.phases]
    ring.finish()
    line.finish()
    small.finish()
    small_bias.finish()
    up_sum.finish()
    down_sum.finish()


def attn_grad(
    n,
    grad,
    mlp_part,
    hidden,
    bias,
    weight,
    mixed,
    sums,
    up_bias_part,
    up_part,
    down_part,
    down_box,
    lengths,
    heads,
):
    seqs, rows, width = grad.shape
    slots = n * rows
    part = weight.shape[0]
    units = up_part.shape[2]
    dp = lax.axis_size("dp")
    vmem = pl.BlockSpec(memory_space=VMEM)
    hbm = pl.BlockSpec(memory_space=pl.ANY)
    return pl.pallas_call(
        functools.partial(attn_grad_kernel, n),
        out_shape=(
            jax.ShapeDtypeStruct((seqs, rows, width), bf16),
            jax.ShapeDtypeStruct(heads.shape, bf16),
            jax.ShapeDtypeStruct((part, width), bf16),
            jax.ShapeDtypeStruct(sums.shape, f32),
            jax.ShapeDtypeStruct((1, units), f32),
            jax.ShapeDtypeStruct(up_part.shape, bf16),
            jax.ShapeDtypeStruct(down_part.shape, bf16),
        ),
        in_specs=[vmem, hbm]
        + [vmem] * 6
        + [hbm] * 3
        + [pl.BlockSpec(memory_space=pltpu.SMEM), vmem],
        out_specs=(vmem,) * 5 + (hbm, hbm),
        scratch_shapes=[VMEM((seqs, slots, width), bf16)]
        + Gather.scratch(n, seqs)
        + Scatter.scratch(n, seqs, rows, width)
        + [DMA((seqs, n // 2)), DMA((2, 4)), DMA((4,))]
        + GroupSum.scratch(dp, 4, width // 4, units)
        + GroupSum.scratch(dp, 4, units // 4, width, 1)
        + SmallSum.scratch(dp, n, sums.shape[0], width, True)
        + SmallSum.scratch(dp, n, 1, units, False)
        + [VMEM((seqs, slots, part), bf16), VMEM((slots, HD), f32), VMEM((slots, HD), f32)],
        compiler_params=pltpu.CompilerParams(
            collective_id=4, has_side_effects=True, vmem_limit_bytes=62 * 2**20
        ),
        name="attn_grad",
    )(
        grad,
        mlp_part,
        hidden,
        bias,
        weight,
        mixed,
        sums,
        up_bias_part,
        up_part,
        down_part,
        down_box,
        lengths,
        heads,
    )


def body(
    tokens,
    cotangent,
    lengths,
    ln1_gain,
    ln1_shift,
    qkv_weight,
    qkv_bias,
    out_weight,
    out_bias,
    ln2_gain,
    ln2_shift,
    up_weight,
    up_bias,
    down_weight,
    down_bias,
):
    n = lax.axis_size("tensor")
    gathered_one, heads, mixed_heads, hidden_state, normed_two, grad_mlp = attention_block(
        n,
        tokens,
        cotangent,
        lengths,
        ln1_gain[None],
        ln1_shift[None],
        qkv_weight,
        qkv_bias,
        out_weight,
        out_bias[None],
        ln2_gain[None],
        ln2_shift[None],
    )
    (
        mlp_part,
        hidden_grad,
        grad_attn,
        sums,
        up_part,
        up_bias_part,
        down_part,
        down_box,
    ) = mlp_block(
        n, normed_two, grad_mlp, up_weight, up_bias[None], down_weight, hidden_state, ln2_gain[None]
    )
    output, grads, out_part, sums, up_bias_grad, up_weight_grad, down_weight_grad = attn_grad(
        n,
        grad_attn,
        mlp_part,
        hidden_state,
        down_bias[None],
        out_weight,
        mixed_heads,
        sums,
        up_bias_part,
        up_part,
        down_part,
        down_box,
        lengths,
        heads,
    )
    ln2_gain_grad, ln2_shift_grad, out_bias_grad, down_bias_grad = [sums[i] for i in range(4)]
    input_grad, sums_one, qkv_weight_grad, out_weight_grad, qkv_bias_grad = heads_scatter(
        n, grads, qkv_weight, gathered_one, out_part, tokens, ln1_gain[None], hidden_grad
    )
    up_weight_grad = up_weight_grad.astype(jnp.float32).reshape(up_weight.shape)
    down_weight_grad = down_weight_grad.astype(jnp.float32).reshape(down_weight.shape)
    return (
        output,
        input_grad,
        sums_one[0],
        sums_one[1],
        qkv_weight_grad.astype(jnp.float32),
        qkv_bias_grad,
        out_weight_grad[0].astype(jnp.float32),
        out_bias_grad,
        ln2_gain_grad,
        ln2_shift_grad,
        up_weight_grad,
        up_bias_grad[0],
        down_weight_grad,
        down_bias_grad,
    )


def solution(mesh):
    in_specs = (
        P("dp", "tensor", None),
        P("dp", "tensor", None),
        P("dp"),
        P(),
        P(),
        P(None, None, "tensor"),
        P(None, "tensor"),
        P("tensor", None),
        P(),
        P(),
        P(),
        P(None, "tensor"),
        P("tensor"),
        P("tensor", None),
        P(),
    )
    out_specs = (
        P("dp", "tensor", None),
        P("dp", "tensor", None),
        P(),
        P(),
        P(None, None, "tensor"),
        P(None, "tensor"),
        P("tensor", None),
        P(),
        P(),
        P(),
        P(None, "tensor"),
        P("tensor"),
        P("tensor", None),
        P(),
    )
    return jax.shard_map(body, mesh=mesh, in_specs=in_specs, out_specs=out_specs, check_vma=False)
```

```python
import functools
import heapq
import itertools

import jax
import jax.numpy as jnp
from jax import lax
from jax.experimental import pallas as pl
from jax.experimental.pallas import tpu as pltpu
from jax.sharding import PartitionSpec as P

HD = 128


norm_epsilon = 1e-05

MESH = pl.DeviceIdType.MESH
UP, DOWN, SIDE = 0, 1, 2
VMEM = pltpu.VMEM
DMA = pltpu.SemaphoreType.DMA
f32 = jnp.float32
bf16 = jnp.bfloat16
NT = (((1,), (1,)), ((), ()))
TN = (((0,), (0,)), ((), ()))


def order_of(chips, ops_of, backlog=8.0, hop=2.0):
    todo = [sorted(ops_of(c)) for c in range(chips)]
    order = [[] for _ in range(chips)]
    free, busy, have, queue = {}, [False] * chips, set(), []

    def push(time, what):
        heapq.heappush(queue, (time, len(pushed), what))
        pushed.append(0)

    pushed = []
    for c in range(chips):
        push(0.0, (c, None, ()))
    now = 0.0
    while queue:
        now, _, (c, signal, after) = heapq.heappop(queue)
        if signal is not None:
            have.add(signal)
        for part in after:
            if part[0] == "free":
                busy[c] = False
            elif part[0] == "send":
                _, link, to, sig, span = part
                start = max(now, free.get((c, link), 0.0))
                free[c, link] = start + span
                push(start + span + hop, (to, sig, ()))
            else:
                push(now + part[1], (c, part[2], ()))
        if busy[c]:
            continue
        for op in todo[c]:
            rank, code, needs, time, sends, gives = op
            if any(need not in have for need in needs):
                continue
            late = max([free.get((c, send[0]), 0.0) - now for send in sends], default=0.0)
            if late > backlog:
                push(now + late - backlog, (c, None, ()))
                continue
            todo[c].remove(op)
            order[c].append(code)
            busy[c] = True
            ends = [("free",)] + [("send",) + send for send in sends]
            push(now + time, (c, None, ends + [("give",) + give for give in gives]))
            break
    assert not any(todo)
    return order, now


PIECE = 12.0


PART = 40


def gather_ops(c, chips, seqs, kind, name, rank=0, time=0.5, gate=False, own=None, parts=1):
    ops = []
    for s, o, j in itertools.product(range(seqs), range(chips), range(parts)):
        up, down = [], []
        if o <= c < chips - 1:
            up.append((c + 1, c + 1, (name, c + 1, s, o, j), PIECE / parts))
        if o >= c > 0:
            down.append((c - 1, c - 1, (name, c - 1, s, o, j), PIECE / parts))
        both = [(3.0, (name, c, s, o, "both", j))]
        add = j * PART
        if own is not None and o == c and s > 0:
            ops.append(((rank, s, -1, j), (own[0] + add, s, o), [], time, [], both))
            for sends, which, others in ((up, own[1], range(c)), (down, own[2], range(c + 1, chips))):
                needs = [(name, c, t, q, parts - 1) for t in (s - 1, s) for q in others]
                if sends:
                    code = (which + add, s, o)
                    ops.append(((rank, s, chips, j), code, needs, time, sends, []))
            continue
        needs = [] if o == c else [(name, c, s, o, j)]
        if gate and o == c and s > 0:
            for q in range(chips):
                if q < c < chips - 1 or q > c > 0:
                    needs.append((name, c, s - 1, q, parts - 1))
        ops.append(((rank, s, abs(o - c), j), (kind + add, s, o), needs, time, up + down, both))
    return ops


def gathered_here(name, c, s, o, parts=1):
    return [(name, c, s, o, "both", j) for j in range(parts)]


def scatter_ops(c, chips, seqs, kind, name, part, rank=1, time=1.3, last=2.0, parts=1):
    ops = []
    for s, o, j in itertools.product(range(seqs), range(chips), range(parts)):
        needs = [(part, c, s, o)]
        if o >= c > 0:
            needs.append((name, c, s, o, "below", j))
        if o <= c < chips - 1:
            needs.append((name, c, s, o, "above", j))
        sends = []
        if o > c:
            sends = [(c + 1, c + 1, (name, c + 1, s, o, "below", j), PIECE / parts)]
        if o < c:
            sends = [(c - 1, c - 1, (name, c - 1, s, o, "above", j), PIECE / parts)]
        order = (rank, s, -abs(o - c), j) if o != c else (8, s, j)
        ends = [(0.0, (name, c, s, "sum", j))] if o == c else []
        span = (last if o == c else time) / parts + 0.2 * (parts - 1)
        ops.append((order, (kind + j * PART, s, o), needs, span, sends, ends))
    return ops


def work_ops(c, chips, seqs, kind, needs_of, gives, time, rank=2, far=False):
    return [
        (
            (rank, s, -abs(o - c) if far else abs(o - c)),
            (kind, s, o),
            needs_of(s, o),
            time,
            [],
            [(3.0, (gives, c, s, o))],
        )
        for s in range(seqs)
        for o in range(chips)
    ]


def group_ops(c, bits, count, span, code_of, skip, turns, first_time, rank=3, name="group"):
    ops = []
    for t in range(count):
        for stage in range(skip, 2 * bits + 1):
            needs, sends = [], []
            for turn in turns:
                if stage > skip:
                    needs.append((name, c, turn, t, stage))
                if stage < 2 * bits:
                    i = stage if stage < bits else 2 * bits - 1 - stage
                    axis = "axis%d" % ((t + turn + i) % bits)
                    sends.append((axis, c, (name, c, turn, t, stage + 1), span / 2**i))
            time = first_time if stage == 0 else 0.8 * len(turns)
            code = code_of((stage - skip) * count + t)
            ops.append(((rank, stage, t), code, needs, time, sends, []))
    return ops


class Plan:
    def __init__(self, at, seqs, ops_of):
        chips = at.chips
        order, self.length = order_of(chips, ops_of)
        self.per, self.each, self.chips, self.seqs = 1024, 3, chips, seqs
        self.count = max(len(codes) for codes in order)
        idle = self.per // (seqs * chips) - 1
        rows = []
        for codes in order:
            assert all(kind < idle for kind, s, o in codes)
            flat = [(kind * seqs + s) * chips + o for kind, s, o in codes]
            flat += [idle * seqs * chips] * (self.count - len(flat) + self.each)
            rows.append(
                [
                    sum(flat[i + j] * self.per**j for j in range(self.each))
                    for i in range(0, self.count, self.each)
                ]
            )
        self.words = []
        for w in range(len(rows[0])):
            word = jnp.int32(rows[0][w])
            for c in range(1, chips):
                word = jnp.where(at.chip == c, jnp.int32(rows[c][w]), word)
            self.words.append(word)

    def step(self, k):
        which, slot = k // self.each, lax.rem(k, self.each)
        word = jnp.int32(0)
        for w, value in enumerate(self.words):
            word = jnp.where(which == w, value, word)
        code = word
        for j in range(1, self.each):
            code = jnp.where(slot == j, word // self.per**j, code)
        code = lax.rem(code, self.per)
        each = self.seqs * self.chips
        return code // each, lax.rem(code, each) // self.chips, lax.rem(code, self.chips)

    def run(self, actions, beside=None):
        def step(k, carry):
            kind, s, o = self.step(k)
            for which, action in actions.items():
                pl.when(kind == which)(functools.partial(action, s, o))
            if beside is not None:
                beside(k)
            return carry

        lax.fori_loop(0, self.count, step, 0)


class Place:
    def __init__(self, n):
        self.n, self.chips = n, n // 2
        self.me = lax.axis_index("tensor")
        self.chip, self.core = self.me // 2, lax.rem(self.me, 2)
        self.side = self.me + 1 - 2 * self.core
        self.below = self.chip > 0
        self.above = self.chip < self.chips - 1
        self.group = lax.axis_index("dp")
        self.group_bits = lax.axis_size("dp").bit_length() - 1
        self.bits = n.bit_length() - 1

    def group_peer(self, q):
        mine = lax.rem(self.group // 2**q, 2)
        return self.group + (1 - 2 * mine) * 2**q, mine

    def peer(self, q):
        mine = lax.rem(self.me // 2**q, 2)
        return self.me + (1 - 2 * mine) * 2**q

    def greet(self, groups=False, cube=False, everyone=False):
        barrier = pltpu.get_barrier_semaphore()

        def tell(target):
            pl.semaphore_signal(
                barrier, inc=1, device_id={"tensor": target}, device_id_type=MESH
            )

        tell(self.side)
        pl.when(self.below)(lambda: tell(self.me - 2))
        pl.when(self.above)(lambda: tell(self.me + 2))
        peers = 1 + self.below.astype(jnp.int32) + self.above.astype(jnp.int32)
        if groups:
            for q in range(self.group_bits):
                pl.semaphore_signal(
                    barrier, inc=1, device_id={"dp": self.group_peer(q)[0]}, device_id_type=MESH
                )
            peers = peers + self.group_bits
        if everyone:
            for other in range(1, self.n):
                tell(lax.rem(self.me + other, self.n))
            for other in range(1, 2**self.group_bits):
                peer = lax.rem(self.group + other, 2**self.group_bits)
                pl.semaphore_signal(barrier, inc=1, device_id={"dp": peer}, device_id_type=MESH)
            peers = peers + (self.n - 1 + 2**self.group_bits - 1)
        if cube:
            for q in range(self.bits):
                tell(self.peer(q))
            peers = peers + self.bits
        pl.semaphore_wait(barrier, peers)


def rows_of(index, rows):
    return pl.ds(pl.multiple_of(index * rows, rows), rows)


class Gather:
    def __init__(self, at, rows, buf, send, recv):
        self.at, self.rows, self.buf, self.send, self.recv = at, rows, buf, send, recv
        self.seqs, self.parts = buf.shape[0], recv.shape[2]

    @staticmethod
    def scratch(n, seqs, parts=1):
        return [DMA((3, seqs, n // 2, parts)), DMA((seqs, n, parts))]

    def copy(self, s, o, kind, j, owner=None):
        at = self.at
        target = (at.me + 2, at.me - 2, at.side)[kind]
        owner = 2 * o + at.core if owner is None else owner
        piece = self.buf.at[s, rows_of(owner * self.parts + j, self.rows // self.parts)]
        return pltpu.make_async_remote_copy(
            src_ref=piece,
            dst_ref=piece,
            send_sem=self.send.at[kind, s, o, j],
            recv_sem=self.recv.at[s, owner, j],
            device_id={"tensor": target},
            device_id_type=MESH,
        )

    def arrived(self, s, o):
        for j in range(self.parts):
            self.copy(s, o, SIDE, j, 2 * o + 1 - self.at.core).wait_recv()

    def relay(self, j, s, o):
        at = self.at
        pl.when(o != at.chip)(lambda: self.copy(s, o, SIDE, j).wait_recv())
        pl.when((o <= at.chip) & at.above)(lambda: self.copy(s, o, UP, j).start())
        pl.when((o >= at.chip) & at.below)(lambda: self.copy(s, o, DOWN, j).start())
        self.copy(s, o, SIDE, j).start()

    def own(self, kind, j, s, o):
        self.copy(s, o, kind, j).start()

    def actions(self, kind, own=()):
        found = {}
        for j in range(self.parts):
            found[kind + j * PART] = functools.partial(self.relay, j)
            for which, way in zip(own, (SIDE, UP, DOWN)):
                found[which + j * PART] = functools.partial(self.own, way, j)
        return found

    def finish(self):
        at = self.at

        def one(i, carry):
            s, o = i // at.chips, lax.rem(i, at.chips)
            for j in range(self.parts):
                pl.when((o <= at.chip) & at.above)(lambda: self.copy(s, o, UP, j).wait_send())
                pl.when((o >= at.chip) & at.below)(lambda: self.copy(s, o, DOWN, j).wait_send())
                self.copy(s, o, SIDE, j).wait_send()
            return carry

        lax.fori_loop(0, self.seqs * at.chips, one, 0)


class Scatter:
    def __init__(self, at, rows, part, side, link, side_send, side_recv, send, recv):
        self.at, self.rows = at, rows
        self.part, self.side, self.link = part, side, link
        self.side_send, self.side_recv, self.send, self.recv = side_send, side_recv, send, recv
        self.seqs, self.parts = part.shape[0], recv.shape[2]
        self.size = rows // self.parts

    @staticmethod
    def scratch(n, seqs, rows, width, parts=1):
        chips = n // 2
        return [
            VMEM((seqs, chips, 2 * rows, width), bf16),
            VMEM((seqs, chips, rows, width), bf16),
            VMEM((seqs, chips + 1, rows, width), bf16),
            DMA((seqs, chips, parts)),
            DMA((seqs, chips, parts)),
            DMA((seqs, chips, parts)),
            DMA((seqs, chips + 1, parts)),
        ]

    def side_copy(self, s, o, j):
        at = self.at
        return pltpu.make_async_remote_copy(
            src_ref=self.part.at[s, o, rows_of((1 - at.core) * self.parts + j, self.size)],
            dst_ref=self.side.at[s, o, pl.ds(j * self.size, self.size)],
            send_sem=self.side_send.at[s, o, j],
            recv_sem=self.side_recv.at[s, o, j],
            device_id={"tensor": at.side},
            device_id_type=MESH,
        )

    def link_copy(self, s, o, slot, target, j):
        return pltpu.make_async_remote_copy(
            src_ref=self.part.at[s, o, rows_of(self.at.core * self.parts + j, self.size)],
            dst_ref=self.link.at[s, slot, pl.ds(j * self.size, self.size)],
            send_sem=self.send.at[s, o, j],
            recv_sem=self.recv.at[s, slot, j],
            device_id={"tensor": target},
            device_id_type=MESH,
        )

    def share(self, s, o):
        for j in range(self.parts):
            self.side_copy(s, o, j).start()

    def blocks(self, j, body):
        step = 16

        def one(i, carry):
            body(pl.multiple_of(j * self.size + i * step, step), step)
            return carry

        lax.fori_loop(0, self.size // step, one, 0)

    def total(self, s, o, first, step, slots):
        here = pl.ds(pl.multiple_of(self.at.core * self.rows + first, step), step)
        there = pl.ds(first, step)
        total = self.part[s, o, here].astype(f32) + self.side[s, o, there].astype(f32)
        for slot in slots:
            total += self.link[s, slot, there].astype(f32)
        return here, total

    def add_up(self, s, o, slots, j):
        def body(first, step):
            here, total = self.total(s, o, first, step, slots)
            self.part[s, o, here] = total.astype(bf16)

        self.blocks(j, body)

    def pass_on(self, final, j, s, o):
        at = self.at
        self.side_copy(s, o, j).wait_recv()

        def onward(before, slot, target):
            @pl.when(before)
            def _():
                self.link_copy(s, o, o, at.me, j).wait_recv()
                self.add_up(s, o, [o], j)

            pl.when(jnp.logical_not(before))(lambda: self.add_up(s, o, [], j))
            self.link_copy(s, o, slot, target, j).start()

        pl.when(o > at.chip)(lambda: onward(at.below, o, at.me + 2))
        last = jnp.where(o == at.chip - 1, at.chips, o)
        pl.when(o < at.chip)(lambda: onward(at.above, last, at.me - 2))

        @pl.when(o == at.chip)
        def _():
            for slot, used in ((o, at.below), (at.chips, at.above)):
                pl.when(used)(lambda: self.link_copy(s, o, slot, at.me, j).wait_recv())

                @pl.when(jnp.logical_not(used))
                def _():
                    def clear(first, step):
                        self.link[s, slot, pl.ds(first, step)] = jnp.zeros(
                            (step, self.link.shape[-1]), bf16
                        )

                    self.blocks(j, clear)

            def body(first, step):
                total = self.total(s, o, first, step, [o, at.chips])[1]
                final(s, pl.ds(first, step), total)

            self.blocks(j, body)

    def actions(self, kind, final):
        return {
            kind + j * PART: functools.partial(self.pass_on, final, j) for j in range(self.parts)
        }

    def finish(self):
        at = self.at

        def one(i, carry):
            s, o = i // at.chips, lax.rem(i, at.chips)
            for j in range(self.parts):
                self.side_copy(s, o, j).wait_send()
                pl.when(o != at.chip)(lambda: self.link_copy(s, o, o, at.side, j).wait_send())
            return carry

        lax.fori_loop(0, self.seqs * at.chips, one, 0)


class GroupSum:
    def __init__(self, at, rows, tiles, inbox, send, recv, keep_sem, out, turn=0, skip=0):
        self.at, self.tiles, self.inbox, self.send, self.recv = at, tiles, inbox, send, recv
        self.keep_sem, self.out, self.skip, self.turn, self.rows = keep_sem, out, skip, turn, rows
        self.bits = at.group_bits
        self.count = send.shape[0]

    @staticmethod
    def scratch(dp, count, rows, width, skip=0):
        phases = 2 * (dp.bit_length() - 1)
        return [
            VMEM((count, rows >> skip, width), bf16),
            VMEM((count, rows - rows // dp, width), bf16),
            DMA((count, phases)),
            DMA((count, phases)),
            DMA((count,)),
        ]

    def peer(self, t, i):
        which = lax.rem(t + i + self.turn, self.bits)
        peer, mine = 0, 0
        for q in range(self.bits):
            other, bit = self.at.group_peer(q)
            peer = peer + jnp.where(which == q, other, 0)
            mine = mine + jnp.where(which == q, bit, 0)
        return peer, mine

    def base(self, t, i):
        first = 0
        for p in range(i):
            first = first + self.peer(t, p)[1] * (self.rows >> (p + 1))
        return first

    def span(self, first, size):
        return pl.ds(pl.multiple_of(first, 16), size)

    def tile(self, t, first, size):
        return self.tiles.at[t, self.span(first - self.base(t, self.skip), size)]

    def box(self, t, i):
        return self.inbox.at[t, pl.ds(self.rows - (self.rows >> i), self.rows >> (i + 1))]

    def remote(self, source, target, t, phase, peer):
        return pltpu.make_async_remote_copy(
            src_ref=source,
            dst_ref=target,
            send_sem=self.send.at[t, phase],
            recv_sem=self.recv.at[t, phase],
            device_id={"dp": peer},
            device_id_type=MESH,
        )

    def halve(self, t, i):
        peer, mine = self.peer(t, i)
        half = self.rows >> (i + 1)
        source = self.tile(t, self.base(t, i) + (1 - mine) * half, half)
        return self.remote(source, self.box(t, i), t, i, peer)

    def add(self, t, i):
        half = self.rows >> (i + 1)
        keep = self.base(t, i + 1) - self.base(t, self.skip)
        box = self.rows - (self.rows >> i)

        def body(j, carry):
            here = self.span(keep + j * 16, 16)
            there = self.span(box + j * 16, 16)
            total = self.tiles[t, here].astype(f32) + self.inbox[t, there].astype(f32)
            self.tiles[t, here] = total.astype(bf16)
            return carry

        lax.fori_loop(0, half // 16, body, 0)

    def keep(self, t):
        first, size = self.base(t, self.bits), self.rows >> self.bits
        return pltpu.make_async_copy(
            self.tile(t, first, size), self.out.at[t, self.span(first, size)], self.keep_sem.at[t]
        )

    def double(self, t, i, back=False):
        peer, mine = self.peer(t, i)
        half = self.rows >> (i + 1)
        first = self.base(t, i) + ((1 - mine) if back else mine) * half
        piece = self.out.at[t, self.span(first, half)]
        source = piece
        if i == self.bits - 1 and not back:
            source = self.tile(t, first, half)
        return self.remote(source, piece, t, 2 * self.bits - 1 - i, peer)

    def events(self):
        return self.count * (2 * self.bits + 1 - self.skip)

    def event(self, e, loaded=None):
        k, t = e // self.count + self.skip, lax.rem(e, self.count)
        bits = self.bits

        def at_stage(stage):
            if stage == self.skip and loaded is not None:
                loaded(t)
            if stage == 0:
                self.halve(t, 0).start()
            elif stage <= bits:
                if stage > self.skip:
                    self.halve(t, stage - 1).wait_recv()
                self.add(t, stage - 1)
                if stage < bits:
                    self.halve(t, stage).start()
                else:
                    self.keep(t).start()
                    self.double(t, bits - 1).start()
            else:
                i = 2 * bits - stage
                self.double(t, i, back=True).wait_recv()
                if i == bits - 1:
                    self.keep(t).wait()
                if i > 0:
                    self.double(t, i - 1).start()

        for stage in range(self.skip, 2 * bits + 1):
            pl.when((k == stage) & (e >= 0))(functools.partial(at_stage, stage))

    def finish(self):
        def one(t, carry):
            for i in range(self.bits):
                if i >= self.skip:
                    self.halve(t, i).wait_send()
                self.double(t, i).wait_send()
            return carry

        lax.fori_loop(0, self.count, one, 0)


class SmallSum:
    def __init__(self, at, rows, inbox, send, recv, everywhere):
        self.at, self.rows, self.inbox, self.send, self.recv = at, rows, inbox, send, recv
        self.phases = at.group_bits + (at.bits if everywhere else 0)

    @staticmethod
    def scratch(dp, n, count, width, everywhere):
        phases = (dp.bit_length() - 1) + (n.bit_length() - 1 if everywhere else 0)
        return [
            VMEM((phases + 1, count, width), f32),
            VMEM((phases, count, width), f32),
            DMA((phases,)),
            DMA((phases,)),
        ]

    def copy(self, i):
        at = self.at
        if i < at.group_bits:
            target = {"dp": at.group_peer(i)[0]}
        else:
            target = {"tensor": at.peer(i - at.group_bits)}
        return pltpu.make_async_remote_copy(
            src_ref=self.rows.at[i],
            dst_ref=self.inbox.at[i],
            send_sem=self.send.at[i],
            recv_sem=self.recv.at[i],
            device_id=target,
            device_id_type=MESH,
        )

    def event(self, e):
        def run(i):
            if i > 0:
                self.copy(i - 1).wait_recv()
                self.rows[i] = self.rows[i - 1] + self.inbox[i - 1]
            if i < self.phases:
                self.copy(i).start()

        for i in range(self.phases + 1):
            if isinstance(e, int):
                if e == i:
                    run(i)
            else:
                pl.when(e == i)(functools.partial(run, i))

    def finish(self):
        for i in range(self.phases):
            self.copy(i).wait_send()


class DirectSum:
    def __init__(self, at, rows, group_box, line_box, send, recv):
        self.at, self.rows, self.send, self.recv = at, rows, send, recv
        self.boxes = (group_box, line_box)

    @staticmethod
    def scratch(dp, n, count, width):
        most = max(dp, n)
        return [
            VMEM((count, width), f32),
            VMEM((dp, count, width), f32),
            VMEM((n, count, width), f32),
            DMA((2, most)),
            DMA((2, most)),
        ]

    def copy(self, step, other, back=False):
        at, box = self.at, self.boxes[step]
        size, axis = box.shape[0], ("dp", "tensor")[step]
        mine = (at.group, at.me)[step]
        peer = lax.rem(mine + other, size)
        slot = peer if back else mine
        return pltpu.make_async_remote_copy(
            src_ref=box.at[mine],
            dst_ref=box.at[slot],
            send_sem=self.send.at[step, other],
            recv_sem=self.recv.at[step, slot],
            device_id={axis: peer},
            device_id_type=MESH,
        )

    def event(self, e):
        if e > 0:
            box = self.boxes[e - 1]
            for other in range(1, box.shape[0]):
                self.copy(e - 1, other, back=True).wait_recv()
            total = box[0]
            for i in range(1, box.shape[0]):
                total = total + box[i]
            self.rows[...] = total
        if e < 2:
            box = self.boxes[e]
            box[(self.at.group, self.at.me)[e]] = self.rows[...]
            for other in range(1, box.shape[0]):
                self.copy(e, other).start()

    def finish(self):
        for step, box in enumerate(self.boxes):
            for other in range(1, box.shape[0]):
                self.copy(step, other).wait_send()


def norm_rows(values, gain, shift):
    centre = values - jnp.mean(values, axis=-1, keepdims=True)
    spread = jnp.mean(centre * centre, axis=-1, keepdims=True)
    return centre * lax.rsqrt(spread + norm_epsilon) * gain + shift


def norm_rows_back(values, grad, gain):
    centre = values - jnp.mean(values, axis=-1, keepdims=True)
    scale = lax.rsqrt(jnp.mean(centre * centre, axis=-1, keepdims=True) + norm_epsilon)
    unit = centre * scale
    w = grad * gain
    back = w - jnp.mean(w, axis=-1, keepdims=True)
    back = scale * (back - unit * jnp.mean(w * unit, axis=-1, keepdims=True))
    return back, grad * unit


def add_row(ref, row, values):
    ref[row : row + 1] += jnp.sum(values, axis=0, keepdims=True)


def head_probs(query, keys, first, length):
    rows, cols = query.shape[0], keys.shape[0]
    scores = lax.dot_general(query, keys, NT, preferred_element_type=f32)
    row_ids = first + lax.broadcasted_iota(jnp.int32, (rows, cols), 0)
    col_ids = lax.broadcasted_iota(jnp.int32, (rows, cols), 1)
    scores = jnp.where((col_ids <= row_ids) & (col_ids < length), scores, -1e30)
    probs = jnp.exp(scores - jnp.max(scores, axis=-1, keepdims=True))
    return probs * (1.0 / jnp.sum(probs, axis=-1, keepdims=True))


def attend(heads, lengths, mixed, block, s):
    slots, part = mixed.shape[1:]

    def one(h, carry):
        cols = pl.ds(pl.multiple_of(h * HD, HD), HD)
        for first in range(0, slots, block):
            rows, seen = pl.ds(first, block), pl.ds(0, first + block)
            probs = head_probs(heads[0, s, rows, cols], heads[1, s, seen, cols], first, lengths[s])
            mixed[s, rows, cols] = jnp.dot(
                probs.astype(bf16), heads[2, s, seen, cols], preferred_element_type=f32
            ).astype(bf16)
        return carry

    lax.fori_loop(0, part // HD, one, 0)


def attend_back(heads, grad_heads, lengths, grads, grad_key, grad_value, block, s):
    slots, part = grad_heads.shape[1:]

    def one(h, carry):
        cols = pl.ds(pl.multiple_of(h * HD, HD), HD)
        grad_key[...] = jnp.zeros_like(grad_key)
        grad_value[...] = jnp.zeros_like(grad_value)
        for first in range(0, slots, block):
            rows, seen = pl.ds(first, block), pl.ds(0, first + block)
            query, grad = heads[0, s, rows, cols], grad_heads[s, rows, cols]
            keys = heads[1, s, seen, cols]
            probs = head_probs(query, keys, first, lengths[s])
            grad_value[seen] += lax.dot_general(
                probs.astype(bf16), grad, TN, preferred_element_type=f32
            )
            back = lax.dot_general(
                grad, heads[2, s, seen, cols], NT, preferred_element_type=f32
            )
            centre = jnp.sum(probs * back, axis=-1, keepdims=True)
            scores = (probs * (back - centre)).astype(bf16)
            grads[0, s, rows, cols] = jnp.dot(
                scores, keys, preferred_element_type=f32
            ).astype(bf16)
            grad_key[seen] += lax.dot_general(scores, query, TN, preferred_element_type=f32)
        grads[1, s, :, cols] = grad_key[...].astype(bf16)
        grads[2, s, :, cols] = grad_value[...].astype(bf16)
        return carry

    lax.fori_loop(0, part // HD, one, 0)


def attention_block_kernel(
    n,
    tokens,
    cotangent,
    lengths,
    gain,
    shift,
    weight,
    bias,
    out_weight,
    out_bias,
    gain_two,
    shift_two,
    gathered,
    heads,
    mixed,
    hidden,
    normed,
    grad_all,
    buf,
    send,
    recv,
    keep_sem,
    grad_send,
    grad_recv,
    masked,
    mask_sem,
    *scratch,
):
    at = Place(n)
    seqs, rows, width = tokens.shape
    ring = Gather(at, rows, buf, send, recv)
    grad_ring = Gather(at, rows, grad_all, grad_send, grad_recv)
    line = Scatter(at, rows, *scratch)

    def mask_copy(s):
        return pltpu.make_async_copy(
            masked.at[s], grad_all.at[s, rows_of(at.me, rows)], mask_sem.at[s]
        )

    for s in range(seqs):
        def block(i, carry):
            first = pl.multiple_of(i * 16, 16)
            here = pl.ds(first, 16)
            values = norm_rows(tokens[s, here].astype(f32), gain[...], shift[...])
            buf[s, pl.ds(pl.multiple_of(at.me * rows + first, 16), 16)] = values.astype(bf16)
            slot = at.me * rows + first + lax.broadcasted_iota(jnp.int32, (16, width), 0)
            grad = jnp.where(slot < lengths[s], cotangent[s, here].astype(f32), 0.0)
            masked[s, here] = grad.astype(bf16)
            return carry

        lax.fori_loop(0, rows // 16, block, 0)
        mask_copy(s).start()
    at.greet()
    for s in range(seqs):
        mask_copy(s).wait()

    def keep(s, o):
        here = rows_of(o, 2 * rows)
        return pltpu.make_async_copy(buf.at[s, here], gathered.at[s, here], keep_sem.at[s, o])

    def project(s, o):
        ring.arrived(s, o)
        keep(s, o).start()
        here = rows_of(o, 2 * rows)
        for j in range(3):
            total = jnp.dot(buf[s, here], weight[j], preferred_element_type=f32)
            if j == 0:
                total = (total + bias[0:1]) * HD ** (-0.5)
            if j == 2:
                total = total + bias[1:2]
            heads[j, s, here] = total.astype(bf16)

    def final(s, there, total):
        values = tokens[s, there].astype(f32) + total + out_bias[...]
        hidden[s, there] = values
        normed[s, there] = norm_rows(values, gain_two[...], shift_two[...]).astype(bf16)

    def mix(s, o):
        attend(heads, lengths, mixed, min(512, n * rows), s)

    def project_out(s, o):
        here = rows_of(o, 2 * rows)
        for j in range(width // 512):
            cols = pl.ds(j * 512, 512)
            total = jnp.dot(mixed[s, here], out_weight[:, cols], preferred_element_type=f32)
            line.part[s, o, :, cols] = total.astype(bf16)
        line.share(s, o)

    def ops_of(c):
        chips = at.chips
        mixing = []
        for s in range(seqs):
            needs = [("heads", c, s, o) for o in range(chips)]
            mixing.append(((2, s, 0), (2, s, 0), needs, 6.0, [], [(0.0, ("mixed", c, s))]))
        return (
            gather_ops(c, chips, seqs, 0, "in", gate=True)
            + work_ops(
                c, chips, seqs, 1, lambda s, o: gathered_here("in", c, s, o), "heads", 1.0
            )
            + mixing
            + work_ops(
                c, chips, seqs, 3, lambda s, o: [("mixed", c, s)], "part", 1.0, far=True
            )
            + scatter_ops(c, chips, seqs, 4, "out", "part", last=4.0)
            + gather_ops(c, chips, seqs, 5, "grad", rank=6)
        )

    Plan(at, seqs, ops_of).run(
        {
            1: project,
            2: mix,
            3: project_out,
            **ring.actions(0),
            **line.actions(4, final),
            **grad_ring.actions(5),
        }
    )
    ring.finish()
    line.finish()
    grad_ring.finish()

    def close(i, carry):
        s, o = i // at.chips, lax.rem(i, at.chips)
        grad_ring.arrived(s, o)
        keep(s, o).wait()
        return carry

    lax.fori_loop(0, seqs * at.chips, close, 0)


def whole(count):
    return [pl.BlockSpec(memory_space=VMEM)] * count


def attention_block(
    n,
    tokens,
    cotangent,
    lengths,
    gain,
    shift,
    weight,
    bias,
    out_weight,
    out_bias,
    gain_two,
    shift_two,
):
    seqs, rows, width = tokens.shape
    part = weight.shape[2]
    vmem = pl.BlockSpec(memory_space=VMEM)
    hbm = pl.BlockSpec(memory_space=pl.ANY)
    smem = pl.BlockSpec(memory_space=pltpu.SMEM)
    return pl.pallas_call(
        functools.partial(attention_block_kernel, n),
        out_shape=(
            jax.ShapeDtypeStruct((seqs, n * rows, width), bf16),
            jax.ShapeDtypeStruct((3, seqs, n * rows, part), bf16),
            jax.ShapeDtypeStruct((seqs, n * rows, part), bf16),
            jax.ShapeDtypeStruct((seqs, rows, width), f32),
            jax.ShapeDtypeStruct((seqs, rows, width), bf16),
            jax.ShapeDtypeStruct((seqs, n * rows, width), bf16),
        ),
        in_specs=[vmem, vmem, smem] + [vmem] * 8,
        out_specs=(hbm, vmem, vmem, vmem, vmem, hbm),
        scratch_shapes=[VMEM((seqs, n * rows, width), bf16)]
        + Gather.scratch(n, seqs)
        + [DMA((seqs, n // 2))]
        + Gather.scratch(n, seqs)
        + [VMEM((seqs, rows, width), bf16), DMA((seqs,))]
        + Scatter.scratch(n, seqs, rows, width),
        compiler_params=pltpu.CompilerParams(
            collective_id=0, has_side_effects=True, vmem_limit_bytes=60 * 2**20
        ),
        name="attention_block",
    )(
        tokens,
        cotangent,
        lengths,
        gain,
        shift,
        weight,
        bias,
        out_weight,
        out_bias,
        gain_two,
        shift_two,
    )


def heads_scatter_kernel(
    n,
    grads,
    weight,
    gathered_hbm,
    out_part,
    tokens_hbm,
    gain,
    hidden_hbm,
    grad,
    sums_all,
    weight_grad,
    out_grad,
    bias_grad,
    *scratch,
):
    at = Place(n)
    seqs, rows, width = hidden_hbm.shape
    line = Scatter(at, rows, *scratch[:7])
    weight_sum = GroupSum(at, width, *scratch[7:12], weight_grad)
    out_sum = GroupSum(at, out_part.shape[0], *scratch[12:17], out_grad, turn=1)
    small = DirectSum(at, *scratch[17:22])
    small_bias = SmallSum(at, *scratch[22:26], False)
    gathered, tokens, hidden_grad, in_sem = scratch[26:]
    sources = ((gathered_hbm, gathered), (tokens_hbm, tokens), (hidden_hbm, hidden_grad))
    loads = [
        pltpu.make_async_copy(source, target, in_sem.at[i])
        for i, (source, target) in enumerate(sources)
    ]
    for copy in loads:
        copy.start()
    out_sum.tiles[0] = out_part[...]
    small.rows[...] = jnp.zeros_like(small.rows)
    at.greet(groups=True, everyone=True)

    def bias_sums():
        for row, j, scale in ((0, 0, HD ** (-0.5)), (1, 2, 1.0)):
            total = 0.0
            for s in range(seqs):
                total += jnp.sum(grads[j, s].astype(f32), axis=0, keepdims=True)
            small_bias.rows[0, row : row + 1] = scale * total

    def beside(k):
        pl.when(k == 10)(bias_sums)
        for e in range(small_bias.phases + 1):
            pl.when(k == 11 + 6 * e)(functools.partial(small_bias.event, e))


    def final(s, there, total):
        back, terms = norm_rows_back(tokens[s, there].astype(f32), total, gain[...])
        grad[s, there] = hidden_grad[s, there] + back
        add_row(small.rows, 0, terms)
        add_row(small.rows, 1, total)

    scales = (HD ** (-0.5), 1.0, 1.0)

    def weight_tile(j):
        for first in range(0, width, 512):
            total = 0.0
            for s in range(seqs):
                total += lax.dot_general(
                    gathered[s, :, pl.ds(first, 512)],
                    grads[j, s],
                    TN,
                    preferred_element_type=f32,
                )
            weight_sum.tiles[j, pl.ds(first, 512)] = (scales[j] * total).astype(bf16)

    def work(s, o):
        here = rows_of(o, 2 * rows)
        for j in range(width // 512):
            cols = pl.ds(j * 512, 512)
            total = 0.0
            for i in range(3):
                total += scales[i] * lax.dot_general(
                    grads[i, s, here], weight[i, cols], NT, preferred_element_type=f32
                )
            line.part[s, o, :, cols] = total.astype(bf16)
        line.share(s, o)

    each = seqs * at.chips

    def weight_event(first, s, o):
        e = first + s * at.chips + o

        @pl.when(e == 0)
        def _():
            for copy in loads:
                copy.wait()

        for j in range(3):
            pl.when(e == j)(functools.partial(weight_tile, j))
        weight_sum.event(e)

    def out_event(s, o):
        out_sum.event(s * at.chips + o)

    def code_of(kind, e):
        return (kind + e // each, e % each // at.chips, e % at.chips)

    def ops_of(c):
        chips = at.chips
        finals = scatter_ops(c, chips, seqs, 1, "out", "part", last=4.0, parts=line.parts)
        loaded = ("qkv", c, 0, 0, 1)
        for i, (rank, code, needs, time, sends, gives) in enumerate(finals):
            if code[2] == c:
                finals[i] = (rank, code, needs + [loaded], time, sends, gives)
        smalls = []
        needs = [("out", c, s, "sum", j) for s in range(seqs) for j in range(line.parts)]
        for e in range(3):
            smalls.append(((0, e), (30 + e, 0, 0), needs, 0.5, [], [(4.0, ("small", c, e))]))
            needs = [("small", c, e)]
        return smalls + (
            work_ops(c, chips, seqs, 0, lambda s, o: [], "part", 1.5, far=True)
            + finals
            + group_ops(
                c, at.group_bits, 3, PIECE, lambda e: code_of(2, e), 0, (0,), 2.7, name="qkv"
            )
            + group_ops(
                c, at.group_bits, 1, PIECE, lambda e: code_of(5, e), 0, (1,), 0.7, name="out_sum"
            )
        )

    actions = {0: work, 5: out_event, **line.actions(1, final)}
    for i in range(3):
        actions[2 + i] = functools.partial(weight_event, i * each)
        actions[30 + i] = lambda s, o, e=i: small.event(e)
    Plan(at, seqs, ops_of).run(actions, beside)
    small.finish()
    sums_all[...] = small.rows[...]
    bias_grad[...] = small_bias.rows[small_bias.phases]
    line.finish()
    weight_sum.finish()
    out_sum.finish()
    small_bias.finish()


def heads_scatter(n, grads, weight, gathered, out_part, tokens, gain, hidden_grad):
    seqs, slots, part = grads.shape[1:]
    width = weight.shape[1]
    rows = slots // n
    dp = lax.axis_size("dp")
    vmem = pl.BlockSpec(memory_space=VMEM)
    hbm = pl.BlockSpec(memory_space=pl.ANY)
    return pl.pallas_call(
        functools.partial(heads_scatter_kernel, n),
        out_shape=(
            jax.ShapeDtypeStruct((seqs, rows, width), f32),
            jax.ShapeDtypeStruct((2, width), f32),
            jax.ShapeDtypeStruct((3, width, part), bf16),
            jax.ShapeDtypeStruct((1, part, width), bf16),
            jax.ShapeDtypeStruct((2, part), f32),
        ),
        in_specs=[vmem, vmem, hbm, vmem, hbm, vmem, hbm],
        out_specs=(vmem, vmem, hbm, hbm, vmem),
        scratch_shapes=Scatter.scratch(n, seqs, rows, width, 2)
        + GroupSum.scratch(dp, 3, width, part)
        + GroupSum.scratch(dp, 1, part, width)
        + DirectSum.scratch(dp, n, 2, width)
        + SmallSum.scratch(dp, n, 2, part, False)
        + [
            VMEM(gathered.shape, bf16),
            VMEM(tokens.shape, bf16),
            VMEM(hidden_grad.shape, f32),
            DMA((3,)),
        ],
        compiler_params=pltpu.CompilerParams(
            collective_id=2, has_side_effects=True, vmem_limit_bytes=62 * 2**20
        ),
        name="heads_scatter",
    )(grads, weight, gathered, out_part, tokens, gain, hidden_grad)


def normal_cdf(values):
    x = jnp.clip(values * 0.7071067811865476, -3.832506856900711, 3.832506856900711)
    x2 = x * x
    top = 0.00022905065861350646
    for c in (0.0034082910107109506, 0.050955695062380861, 0.18520832239976145, 1.128379143519084):
        top = top * x2 + c
    low = -1.1791602954361697e-7
    for c in (
        0.000023547966471313185,
        0.0010179625278914885,
        0.014070470171167667,
        0.11098505178285362,
        0.49746925110067538,
        1.0,
    ):
        low = low * x2 + c
    return 0.5 + 0.5 * (x * top / low)


def mlp_kernel(
    n,
    normed,
    grad_hbm,
    up_hbm,
    up_bias,
    down_hbm,
    hidden_hbm,
    gain,
    mlp_part,
    hidden_grad,
    grad_low,
    sums,
    up_grad,
    up_bias_grad,
    down_grad,
    down_box,
    buf,
    send,
    recv,
    grad_all,
    up_weight,
    down_weight,
    hidden,
    in_sem,
    *scratch,
):
    at = Place(n)
    seqs, rows, width = normed.shape
    units_wide = up_weight.shape[1]
    line = Scatter(at, rows, *scratch[:7])
    act, pre, out_stage, out_sem, up_stage, down_stage, tile_sem, half_send, half_recv = scratch[7:]
    ring = Gather(at, rows, buf, send, recv)
    loads = [
        pltpu.make_async_copy(source, target, in_sem.at[i])
        for i, (source, target) in enumerate(
            (
                (up_hbm, up_weight),
                (grad_hbm, grad_all),
                (down_hbm, down_weight),
                (hidden_hbm, hidden),
            )
        )
    ]
    for copy in loads:
        copy.start()
    at.greet(groups=True)
    for s in range(seqs):
        buf[s, rows_of(at.me, rows)] = normed[s]
    up_bias_grad[...] = jnp.zeros_like(up_bias_grad)
    sums[...] = jnp.zeros_like(sums)
    ft = min(512, units_wide)

    def out_copy(s, o):
        return pltpu.make_async_copy(
            out_stage, mlp_part.at[s, rows_of(o, 2 * rows)], out_sem.at[0]
        )

    def work(s, o):
        ring.arrived(s, o)

        @pl.when((s == 0) & (o == at.chip))
        def _():
            for copy in loads:
                copy.wait()

        here = rows_of(o, 2 * rows)
        for j in range(units_wide // ft):
            cols = pl.ds(j * ft, ft)
            value = jnp.dot(buf[s, here], up_weight[:, cols], preferred_element_type=f32)
            value = value + up_bias[:, cols]
            spread = normal_cdf(value)
            act[s, here, cols] = (value * spread).astype(bf16)
            slope = spread + value * (0.3989422804014327 * jnp.exp(-0.5 * value * value))
            grad = lax.dot_general(
                grad_all[s, here], down_weight[cols], NT, preferred_element_type=f32
            )
            grad = (grad * slope).astype(bf16)
            pre[s, here, cols] = grad
            up_bias_grad[:, cols] += jnp.sum(grad.astype(f32), axis=0, keepdims=True)
        for j in range(width // 512):
            cols = pl.ds(j * 512, 512)
            line.part[s, o, :, cols] = lax.dot_general(
                pre[s, here], up_weight[cols], NT, preferred_element_type=f32
            ).astype(bf16)
        line.share(s, o)
        pl.when((s > 0) | (o != at.chip))(lambda: out_copy(s, o).wait())
        for j in range(width // 512):
            cols = pl.ds(j * 512, 512)
            out_stage[:, cols] = jnp.dot(
                act[s, here], down_weight[:, cols], preferred_element_type=f32
            ).astype(bf16)
        out_copy(s, o).start()

    def final(s, there, total):
        back, terms = norm_rows_back(hidden[s, there], total, gain[...])
        first = pl.multiple_of(at.me * rows + there.start, 16)
        grad_out = grad_all[s, pl.ds(first, there.size)].astype(f32)
        grad = grad_out + back
        hidden_grad[s, there] = grad
        grad_low[s, there] = grad.astype(bf16)
        add_row(sums, 0, terms)
        add_row(sums, 1, total)
        add_row(sums, 2, grad)
        add_row(sums, 3, grad_out)

    kinds = ((down_stage, down_grad), (up_stage, up_grad))

    def tile_copy(kind, t):
        stage, grad = kinds[kind]
        return pltpu.make_async_copy(stage, grad.at[t], tile_sem.at[kind])

    def down_half(t):
        half = down_box.shape[1]
        peer, mine = at.group_peer(t % at.group_bits)
        return pltpu.make_async_remote_copy(
            src_ref=down_grad.at[t, rows_of(1 - mine, half)],
            dst_ref=down_box.at[t],
            send_sem=half_send.at[t],
            recv_sem=half_recv.at[t],
            device_id={"dp": peer},
            device_id_type=MESH,
        )

    def tile_sent(kind, t):
        tile_copy(kind, t).wait()
        if kind == 0:
            down_half(t).start()

    order = [(i // 4, i % 4) for i in range(8)]

    def weight_tile(i):
        for j, (kind, t) in enumerate(order):
            @pl.when(i == j)
            def _():
                stage = kinds[kind][0]
                cols = pl.ds(t * stage.shape[0], stage.shape[0])
                total = 0.0
                for s in range(seqs):
                    if kind == 0:
                        left, right = act[s, :, cols], grad_all[s]
                    else:
                        left, right = buf[s, :, cols], pre[s]
                    total += lax.dot_general(left, right, TN, preferred_element_type=f32)
                if j >= 1:
                    tile_sent(*order[j - 1])
                stage[...] = total.astype(bf16)
                tile_copy(kind, t).start()

    def tile_work(s, o):
        weight_tile(s * at.chips + o)

    own = (4, 5, 6)

    def ops_of(c):
        chips = at.chips
        units = [(s, o) for s in range(seqs) for o in range(chips)]
        ops = (
            gather_ops(c, chips, seqs, 0, "in", own=own, parts=ring.parts)
            + scatter_ops(c, chips, seqs, 1, "back", "part", last=4.0)
            + work_ops(
                c, chips, seqs, 2, lambda s, o: gathered_here("in", c, s, o, ring.parts), "part", 5.7
            )
        )
        for i in range(len(ops)):
            rank, code, needs, time, sends, gives = ops[i]
            if code[0] == 2 and code[1:] != (0, c):
                ops[i] = (rank, code, needs + [("first", c)], time, sends, gives)
            if code == (2, 0, c):
                ops[i] = (rank, code, needs, time, sends, gives + [(0.0, ("first", c))])
        for e in range(len(order)):
            needs = [("part", c, s, o) for s, o in units]
            needs += [("tile", c, e - 1)] if e else []
            sends = [("axis%d" % (e % 2), c, ("half", c, e), PIECE)] if e < 4 else []
            code = (3, e // chips, e % chips)
            ops.append(((4, e, 0), code, needs, 2.7, sends, [(0.0, ("tile", c, e))]))
        return ops

    actions = {2: work, 3: tile_work, **ring.actions(0, own), **line.actions(1, final)}
    Plan(at, seqs, ops_of).run(actions)
    tile_sent(*order[7])
    ring.finish()
    line.finish()
    for t in range(4):
        down_half(t).wait()
    out_copy(0, 0).wait()


def mlp_block(n, normed, grad_all, up_weight, up_bias, down_weight, hidden, gain):
    seqs, rows, width = normed.shape
    slots = n * rows
    units = up_weight.shape[1]
    hbm = pl.BlockSpec(memory_space=pl.ANY)
    vmem = pl.BlockSpec(memory_space=VMEM)
    down_size, up_size = units // 4, width // 4
    return pl.pallas_call(
        functools.partial(mlp_kernel, n),
        out_shape=(
            jax.ShapeDtypeStruct((seqs, slots, width), bf16),
            jax.ShapeDtypeStruct((seqs, rows, width), f32),
            jax.ShapeDtypeStruct((seqs, rows, width), bf16),
            jax.ShapeDtypeStruct((4, width), f32),
            jax.ShapeDtypeStruct((4, up_size, units), bf16),
            jax.ShapeDtypeStruct((1, units), f32),
            jax.ShapeDtypeStruct((4, down_size, width), bf16),
            jax.ShapeDtypeStruct((4, down_size // 2, width), bf16),
        ),
        in_specs=[vmem, hbm, hbm, vmem, hbm, hbm, vmem],
        out_specs=(hbm, vmem, vmem, vmem, hbm, vmem, hbm, hbm),
        scratch_shapes=[VMEM((seqs, slots, width), bf16)]
        + Gather.scratch(n, seqs, 2)
        + [
            VMEM((seqs, slots, width), bf16),
            VMEM(up_weight.shape, bf16),
            VMEM(down_weight.shape, bf16),
            VMEM(hidden.shape, f32),
            DMA((4,)),
        ]
        + Scatter.scratch(n, seqs, rows, width)
        + [
            VMEM((seqs, slots, units), bf16),
            VMEM((seqs, slots, units), bf16),
            VMEM((2 * rows, width), bf16),
            DMA((1,)),
            VMEM((up_size, units), bf16),
            VMEM((down_size, width), bf16),
            DMA((2,)),
            DMA((4,)),
            DMA((4,)),
        ],
        compiler_params=pltpu.CompilerParams(
            collective_id=3, has_side_effects=True, vmem_limit_bytes=62 * 2**20
        ),
        name="mlp_block",
    )(normed, grad_all, up_weight, up_bias, down_weight, hidden, gain)


def attn_grad_kernel(
    n,
    grad,
    mlp_part,
    hidden,
    bias,
    weight,
    mixed,
    sums,
    up_bias_part,
    up_part,
    down_part,
    down_box,
    lengths,
    heads,
    output,
    grads,
    weight_grad,
    sums_all,
    up_bias_grad,
    up_grad,
    down_grad,
    buf,
    send,
    recv,
    *scratch,
):
    at = Place(n)
    seqs, rows, width = grad.shape
    line = Scatter(at, rows, *scratch[:7])
    load_sem, tile_sem, box_sem = scratch[7:10]
    ring = Gather(at, rows, buf, send, recv)
    up_sum = GroupSum(at, up_part.shape[1], *scratch[10:15], up_grad, turn=1)
    down_sum = GroupSum(at, down_part.shape[1], *scratch[15:20], down_grad, skip=1)
    small = SmallSum(at, *scratch[20:24], True)
    small_bias = SmallSum(at, *scratch[24:28], False)
    grad_heads, grad_key, grad_value = scratch[28:]
    def up_load(t):
        return pltpu.make_async_copy(up_part.at[t], up_sum.tiles.at[t], tile_sem.at[0, t])

    def down_load(t):
        half = down_box.shape[1]
        kept = down_part.at[t, down_sum.span(down_sum.base(t, 1), half)]
        return (
            pltpu.make_async_copy(kept, down_sum.tiles.at[t], tile_sem.at[1, t]),
            pltpu.make_async_copy(down_box.at[t], down_sum.box(t, 0), box_sem.at[t]),
        )

    def up_loaded(t):
        up_load(t).wait()

    def down_loaded(t):
        for copy in down_load(t):
            copy.wait()

    for t in range(4):
        up_load(t).start()
        for copy in down_load(t):
            copy.start()
    small.rows[0] = sums[...]
    small_bias.rows[0] = up_bias_part[...]

    def load(s, o):
        return pltpu.make_async_copy(
            mlp_part.at[s, rows_of(o, 2 * rows)], line.part.at[s, o], load_sem.at[s, o]
        )

    def load_one(i, carry):
        load(i // at.chips, lax.rem(i, at.chips)).start()
        return carry

    each = seqs * at.chips
    lax.fori_loop(0, each, load_one, 0)
    for s in range(seqs):
        buf[s, rows_of(at.me, rows)] = grad[s]
    at.greet(groups=True, cube=True)

    def final(s, there, total):
        output[s, there] = (hidden[s, there] + total + bias[...]).astype(bf16)

    def share(s, o):
        load(s, o).wait()
        line.share(s, o)

    def work(s, o):
        ring.arrived(s, o)
        here = rows_of(o, 2 * rows)
        grad_heads[s, here] = lax.dot_general(
            buf[s, here], weight[...], NT, preferred_element_type=f32
        ).astype(bf16)

    def back(s, o):
        block = min(512, n * rows)
        attend_back(heads, grad_heads, lengths, grads, grad_key, grad_value, block, s)

    def weight_work(s, o):
        for j in range(width // 512):
            cols = pl.ds(j * 512, 512)
            total = 0.0
            for q in range(seqs):
                total += lax.dot_general(mixed[q], buf[q, :, cols], TN, preferred_element_type=f32)
            weight_grad[:, cols] = total.astype(bf16)

    def up_event(first, s, o):
        up_sum.event(first + s * at.chips + o, up_loaded)

    def down_event(first, s, o):
        down_sum.event(first + s * at.chips + o, down_loaded)

    def ops_of(c):
        chips = at.chips
        code_of = lambda kind, e: (kind + e // each, e % each // chips, e % chips)
        backs = []
        for s in range(seqs):
            needs = [("done", c, s, o) for o in range(chips)]
            backs.append(((4, s, 0), (4, s, 0), needs, 8.0, [], []))
        needs = [("done", c, s, o) for s in range(seqs) for o in range(chips)]
        backs.append(((5, 0, 0), (5, 0, 0), needs, 3.0, [], []))
        return backs + (
            gather_ops(c, chips, seqs, 0, "in")
            + scatter_ops(c, chips, seqs, 1, "out", "part", last=4.0)
            + work_ops(c, chips, seqs, 2, lambda s, o: gathered_here("in", c, s, o), "done", 1.0)
            + work_ops(c, chips, seqs, 3, lambda s, o: [], "part", 0.3, rank=0, far=True)
            + group_ops(
                c, at.group_bits, 4, PIECE, lambda e: code_of(8, e), 0, (1,), 0.7, -1, "up"
            )
            + group_ops(
                c, at.group_bits, 4, PIECE, lambda e: code_of(16, e), 1, (0,), 0.7, -1, "down"
            )
        )

    actions = {2: work, 3: share, **ring.actions(0), **line.actions(1, final)}
    actions[4], actions[5] = back, weight_work
    for i in range(-(-up_sum.events() // each)):
        actions[8 + i] = functools.partial(up_event, i * each)
    for i in range(-(-down_sum.events() // each)):
        actions[16 + i] = functools.partial(down_event, i * each)

    def beside(k):
        pl.when(lax.rem(k, 8) == 0)(lambda: small.event(k // 8))
        small_bias.event(k)

    Plan(at, seqs, ops_of).run(actions, beside)
    sums_all[...] = small.rows[small.phases]
    up_bias_grad[...] = small_bias.rows[small_bias.phases]
    ring.finish()
    line.finish()
    small.finish()
    small_bias.finish()
    up_sum.finish()
    down_sum.finish()


def attn_grad(
    n,
    grad,
    mlp_part,
    hidden,
    bias,
    weight,
    mixed,
    sums,
    up_bias_part,
    up_part,
    down_part,
    down_box,
    lengths,
    heads,
):
    seqs, rows, width = grad.shape
    slots = n * rows
    part = weight.shape[0]
    units = up_part.shape[2]
    dp = lax.axis_size("dp")
    vmem = pl.BlockSpec(memory_space=VMEM)
    hbm = pl.BlockSpec(memory_space=pl.ANY)
    return pl.pallas_call(
        functools.partial(attn_grad_kernel, n),
        out_shape=(
            jax.ShapeDtypeStruct((seqs, rows, width), bf16),
            jax.ShapeDtypeStruct(heads.shape, bf16),
            jax.ShapeDtypeStruct((part, width), bf16),
            jax.ShapeDtypeStruct(sums.shape, f32),
            jax.ShapeDtypeStruct((1, units), f32),
            jax.ShapeDtypeStruct(up_part.shape, bf16),
            jax.ShapeDtypeStruct(down_part.shape, bf16),
        ),
        in_specs=[vmem, hbm]
        + [vmem] * 6
        + [hbm] * 3
        + [pl.BlockSpec(memory_space=pltpu.SMEM), vmem],
        out_specs=(vmem,) * 5 + (hbm, hbm),
        scratch_shapes=[VMEM((seqs, slots, width), bf16)]
        + Gather.scratch(n, seqs)
        + Scatter.scratch(n, seqs, rows, width)
        + [DMA((seqs, n // 2)), DMA((2, 4)), DMA((4,))]
        + GroupSum.scratch(dp, 4, width // 4, units)
        + GroupSum.scratch(dp, 4, units // 4, width, 1)
        + SmallSum.scratch(dp, n, sums.shape[0], width, True)
        + SmallSum.scratch(dp, n, 1, units, False)
        + [VMEM((seqs, slots, part), bf16), VMEM((slots, HD), f32), VMEM((slots, HD), f32)],
        compiler_params=pltpu.CompilerParams(
            collective_id=4, has_side_effects=True, vmem_limit_bytes=62 * 2**20
        ),
        name="attn_grad",
    )(
        grad,
        mlp_part,
        hidden,
        bias,
        weight,
        mixed,
        sums,
        up_bias_part,
        up_part,
        down_part,
        down_box,
        lengths,
        heads,
    )


def finish_kernel(*refs):
    sums_two, sums_one = refs[8:10]
    targets = refs[10:]
    for source, target in zip(refs[:8], targets):
        target[...] = source[...].astype(target.dtype)
    rows = [sums_one[i : i + 1] for i in range(2)] + [sums_two[i : i + 1] for i in range(4)]
    for row, target in zip(rows, targets[8:]):
        target[...] = row


def finish(blocks, wholes, sums_two, sums_one, steps=4):
    width = sums_one.shape[1]
    specs = [pl.BlockSpec((a.shape[0] // steps, a.shape[1]), lambda i: (i, 0)) for a, t in blocks]
    specs += [pl.BlockSpec(a.shape, lambda i: (0, 0)) for a in wholes]
    row = pl.BlockSpec((1, width), lambda i: (0, 0))
    shapes = [jax.ShapeDtypeStruct(a.shape, t) for a, t in blocks]
    shapes += [jax.ShapeDtypeStruct(a.shape, f32) for a in wholes]
    return pl.pallas_call(
        finish_kernel,
        grid=(steps,),
        out_shape=shapes + [jax.ShapeDtypeStruct((1, width), f32)] * 6,
        in_specs=specs + [pl.BlockSpec(a.shape, lambda i: (0, 0)) for a in (sums_two, sums_one)],
        out_specs=specs + [row] * 6,
        compiler_params=pltpu.CompilerParams(vmem_limit_bytes=62 * 2**20),
        name="finish",
    )(*[a for a, t in blocks], *wholes, sums_two, sums_one)


def body(
    tokens,
    cotangent,
    lengths,
    ln1_gain,
    ln1_shift,
    qkv_weight,
    qkv_bias,
    out_weight,
    out_bias,
    ln2_gain,
    ln2_shift,
    up_weight,
    up_bias,
    down_weight,
    down_bias,
):
    n = lax.axis_size("tensor")
    gathered_one, heads, mixed_heads, hidden_state, normed_two, grad_mlp = attention_block(
        n,
        tokens,
        cotangent,
        lengths,
        ln1_gain[None],
        ln1_shift[None],
        qkv_weight,
        qkv_bias,
        out_weight,
        out_bias[None],
        ln2_gain[None],
        ln2_shift[None],
    )
    (
        mlp_part,
        hidden_grad,
        grad_attn,
        sums,
        up_part,
        up_bias_part,
        down_part,
        down_box,
    ) = mlp_block(
        n, normed_two, grad_mlp, up_weight, up_bias[None], down_weight, hidden_state, ln2_gain[None]
    )
    output, grads, out_part, sums, up_bias_grad, up_weight_grad, down_weight_grad = attn_grad(
        n,
        grad_attn,
        mlp_part,
        hidden_state,
        down_bias[None],
        out_weight,
        mixed_heads,
        sums,
        up_bias_part,
        up_part,
        down_part,
        down_box,
        lengths,
        heads,
    )
    input_grad, sums_one, qkv_weight_grad, out_weight_grad, qkv_bias_grad = heads_scatter(
        n, grads, qkv_weight, gathered_one, out_part, tokens, ln1_gain[None], hidden_grad
    )
    width = tokens.shape[2]
    (
        qkv_weight_grad,
        out_weight_grad,
        up_weight_grad,
        down_weight_grad,
        output,
        input_grad,
        qkv_bias_grad,
        up_bias_grad,
        *rows,
    ) = finish(
        (
            (qkv_weight_grad.reshape(-1, qkv_weight.shape[2]), f32),
            (out_weight_grad.reshape(out_weight.shape), f32),
            (up_weight_grad.reshape(up_weight.shape), f32),
            (down_weight_grad.reshape(down_weight.shape), f32),
            (output.reshape(-1, width), bf16),
            (input_grad.reshape(-1, width), f32),
        ),
        (qkv_bias_grad, up_bias_grad),
        sums,
        sums_one,
    )
    ln1_gain_grad, ln1_shift_grad, ln2_gain_grad, ln2_shift_grad, out_bias_grad, down_bias_grad = [
        row[0] for row in rows
    ]
    return (
        output.reshape(tokens.shape),
        input_grad.reshape(tokens.shape),
        ln1_gain_grad,
        ln1_shift_grad,
        qkv_weight_grad.reshape(qkv_weight.shape),
        qkv_bias_grad,
        out_weight_grad,
        out_bias_grad,
        ln2_gain_grad,
        ln2_shift_grad,
        up_weight_grad,
        up_bias_grad[0],
        down_weight_grad,
        down_bias_grad,
    )


def solution(mesh):
    in_specs = (
        P("dp", "tensor", None),
        P("dp", "tensor", None),
        P("dp"),
        P(),
        P(),
        P(None, None, "tensor"),
        P(None, "tensor"),
        P("tensor", None),
        P(),
        P(),
        P(),
        P(None, "tensor"),
        P("tensor"),
        P("tensor", None),
        P(),
    )
    out_specs = (
        P("dp", "tensor", None),
        P("dp", "tensor", None),
        P(),
        P(),
        P(None, None, "tensor"),
        P(None, "tensor"),
        P("tensor", None),
        P(),
        P(),
        P(),
        P(None, "tensor"),
        P("tensor"),
        P("tensor", None),
        P(),
    )
    return jax.shard_map(body, mesh=mesh, in_specs=in_specs, out_specs=out_specs, check_vma=False)
```

```python
import functools
import heapq
import itertools

import jax
import jax.numpy as jnp
from jax import lax
from jax.experimental import pallas as pl
from jax.experimental.pallas import tpu as pltpu
from jax.sharding import PartitionSpec as P

HD = 128


norm_epsilon = 1e-05

MESH = pl.DeviceIdType.MESH
UP, DOWN, SIDE = 0, 1, 2
VMEM = pltpu.VMEM
DMA = pltpu.SemaphoreType.DMA
f32 = jnp.float32
bf16 = jnp.bfloat16
NT = (((1,), (1,)), ((), ()))
TN = (((0,), (0,)), ((), ()))


def order_of(chips, ops_of, backlog=8.0, hop=2.0):
    todo = [sorted(ops_of(c)) for c in range(chips)]
    order = [[] for _ in range(chips)]
    free, busy, have, queue = {}, [False] * chips, set(), []

    def push(time, what):
        heapq.heappush(queue, (time, len(pushed), what))
        pushed.append(0)

    pushed = []
    for c in range(chips):
        push(0.0, (c, None, ()))
    now = 0.0
    while queue:
        now, _, (c, signal, after) = heapq.heappop(queue)
        if signal is not None:
            have.add(signal)
        for part in after:
            if part[0] == "free":
                busy[c] = False
            elif part[0] == "send":
                _, link, to, sig, span = part
                start = max(now, free.get((c, link), 0.0))
                free[c, link] = start + span
                push(start + span + hop, (to, sig, ()))
            else:
                push(now + part[1], (c, part[2], ()))
        if busy[c]:
            continue
        for op in todo[c]:
            rank, code, needs, time, sends, gives = op
            if any(need not in have for need in needs):
                continue
            late = max([free.get((c, send[0]), 0.0) - now for send in sends], default=0.0)
            if late > backlog:
                push(now + late - backlog, (c, None, ()))
                continue
            todo[c].remove(op)
            order[c].append(code)
            busy[c] = True
            ends = [("free",)] + [("send",) + send for send in sends]
            push(now + time, (c, None, ends + [("give",) + give for give in gives]))
            break
    assert not any(todo)
    return order, now


PIECE = 12.0


PART = 12


def gather_ops(c, chips, seqs, kind, name, rank=0, time=0.5, gate=False, own=None, parts=1):
    ops = []
    for s, o, j in itertools.product(range(seqs), range(chips), range(parts)):
        up, down = [], []
        if o <= c < chips - 1:
            up.append((c + 1, c + 1, (name, c + 1, s, o, j), PIECE / parts))
        if o >= c > 0:
            down.append((c - 1, c - 1, (name, c - 1, s, o, j), PIECE / parts))
        both = [(3.0, (name, c, s, o, "both", j))]
        add = j * PART
        if own is not None and o == c and s > 0:
            ops.append(((rank, s, -1, j), (own[0] + add, s, o), [], time, [], both))
            for sends, which, others in ((up, own[1], range(c)), (down, own[2], range(c + 1, chips))):
                needs = [(name, c, t, q, parts - 1) for t in (s - 1, s) for q in others]
                if sends:
                    code = (which + add, s, o)
                    ops.append(((rank, s, chips, j), code, needs, time, sends, []))
            continue
        needs = [] if o == c else [(name, c, s, o, j)]
        if gate and o == c and s > 0:
            for q in range(chips):
                if q < c < chips - 1 or q > c > 0:
                    needs.append((name, c, s - 1, q, parts - 1))
        ops.append(((rank, s, abs(o - c), j), (kind + add, s, o), needs, time, up + down, both))
    return ops


def gathered_here(name, c, s, o, parts=1):
    return [(name, c, s, o, "both", j) for j in range(parts)]


def scatter_ops(c, chips, seqs, kind, name, part, rank=1, time=1.3, last=2.0, parts=1):
    ops = []
    for s, o, j in itertools.product(range(seqs), range(chips), range(parts)):
        needs = [(part, c, s, o)]
        if o >= c > 0:
            needs.append((name, c, s, o, "below", j))
        if o <= c < chips - 1:
            needs.append((name, c, s, o, "above", j))
        sends = []
        if o > c:
            sends = [(c + 1, c + 1, (name, c + 1, s, o, "below", j), PIECE / parts)]
        if o < c:
            sends = [(c - 1, c - 1, (name, c - 1, s, o, "above", j), PIECE / parts)]
        order = (rank, s, -abs(o - c), j) if o != c else (8, s, j)
        ends = [(0.0, (name, c, s, "sum", j))] if o == c else []
        span = (last if o == c else time) / parts + 0.2 * (parts - 1)
        ops.append((order, (kind + j * PART, s, o), needs, span, sends, ends))
    return ops


def work_ops(c, chips, seqs, kind, needs_of, gives, time, rank=2, far=False):
    return [
        (
            (rank, s, -abs(o - c) if far else abs(o - c)),
            (kind, s, o),
            needs_of(s, o),
            time,
            [],
            [(3.0, (gives, c, s, o))],
        )
        for s in range(seqs)
        for o in range(chips)
    ]


def group_ops(c, bits, count, span, code_of, skip, turns, first_time, rank=3, name="group"):
    ops = []
    for t in range(count):
        for stage in range(skip, 2 * bits + 1):
            needs, sends = [], []
            for turn in turns:
                if stage > skip:
                    needs.append((name, c, turn, t, stage))
                if stage < 2 * bits:
                    i = stage if stage < bits else 2 * bits - 1 - stage
                    axis = "axis%d" % ((t + turn + i) % bits)
                    sends.append((axis, c, (name, c, turn, t, stage + 1), span / 2**i))
            time = first_time if stage == 0 else 0.8 * len(turns)
            code = code_of((stage - skip) * count + t)
            ops.append(((rank, stage, t), code, needs, time, sends, []))
    return ops


class Plan:
    def __init__(self, at, seqs, ops_of):
        chips = at.chips
        order, self.length = order_of(chips, ops_of)
        self.per, self.each, self.chips, self.seqs = 1024, 3, chips, seqs
        self.count = max(len(codes) for codes in order)
        idle = self.per // (seqs * chips) - 1
        rows = []
        for codes in order:
            assert all(kind < idle for kind, s, o in codes)
            flat = [(kind * seqs + s) * chips + o for kind, s, o in codes]
            flat += [idle * seqs * chips] * (self.count - len(flat) + self.each)
            rows.append(
                [
                    sum(flat[i + j] * self.per**j for j in range(self.each))
                    for i in range(0, self.count, self.each)
                ]
            )
        self.words = []
        for w in range(len(rows[0])):
            word = jnp.int32(rows[0][w])
            for c in range(1, chips):
                word = jnp.where(at.chip == c, jnp.int32(rows[c][w]), word)
            self.words.append(word)

    def step(self, k):
        which, slot = k // self.each, lax.rem(k, self.each)
        word = jnp.int32(0)
        for w, value in enumerate(self.words):
            word = jnp.where(which == w, value, word)
        code = word
        for j in range(1, self.each):
            code = jnp.where(slot == j, word // self.per**j, code)
        code = lax.rem(code, self.per)
        each = self.seqs * self.chips
        return code // each, lax.rem(code, each) // self.chips, lax.rem(code, self.chips)

    def run(self, actions, beside=None):
        def step(k, carry):
            kind, s, o = self.step(k)
            for which, action in actions.items():
                pl.when(kind == which)(functools.partial(action, s, o))
            if beside is not None:
                beside(k)
            return carry

        lax.fori_loop(0, self.count, step, 0)


class Place:
    def __init__(self, n):
        self.n, self.chips = n, n // 2
        self.me = lax.axis_index("tensor")
        self.chip, self.core = self.me // 2, lax.rem(self.me, 2)
        self.side = self.me + 1 - 2 * self.core
        self.below = self.chip > 0
        self.above = self.chip < self.chips - 1
        self.group = lax.axis_index("dp")
        self.group_bits = lax.axis_size("dp").bit_length() - 1
        self.bits = n.bit_length() - 1

    def group_peer(self, q):
        mine = lax.rem(self.group // 2**q, 2)
        return self.group + (1 - 2 * mine) * 2**q, mine

    def peer(self, q):
        mine = lax.rem(self.me // 2**q, 2)
        return self.me + (1 - 2 * mine) * 2**q

    def greet(self, groups=False, cube=False, everyone=False):
        barrier = pltpu.get_barrier_semaphore()

        def tell(target):
            pl.semaphore_signal(
                barrier, inc=1, device_id={"tensor": target}, device_id_type=MESH
            )

        tell(self.side)
        pl.when(self.below)(lambda: tell(self.me - 2))
        pl.when(self.above)(lambda: tell(self.me + 2))
        peers = 1 + self.below.astype(jnp.int32) + self.above.astype(jnp.int32)
        if groups:
            for q in range(self.group_bits):
                pl.semaphore_signal(
                    barrier, inc=1, device_id={"dp": self.group_peer(q)[0]}, device_id_type=MESH
                )
            peers = peers + self.group_bits
        if everyone:
            for other in range(1, self.n):
                tell(lax.rem(self.me + other, self.n))
            for other in range(1, 2**self.group_bits):
                peer = lax.rem(self.group + other, 2**self.group_bits)
                pl.semaphore_signal(barrier, inc=1, device_id={"dp": peer}, device_id_type=MESH)
            peers = peers + (self.n - 1 + 2**self.group_bits - 1)
        if cube:
            for q in range(self.bits):
                tell(self.peer(q))
            peers = peers + self.bits
        pl.semaphore_wait(barrier, peers)


def rows_of(index, rows):
    return pl.ds(pl.multiple_of(index * rows, rows), rows)


class Gather:
    def __init__(self, at, rows, buf, send, recv):
        self.at, self.rows, self.buf, self.send, self.recv = at, rows, buf, send, recv
        self.seqs, self.parts = buf.shape[0], recv.shape[2]

    @staticmethod
    def scratch(n, seqs, parts=1):
        return [DMA((3, seqs, n // 2, parts)), DMA((seqs, n, parts))]

    def copy(self, s, o, kind, j, owner=None):
        at = self.at
        target = (at.me + 2, at.me - 2, at.side)[kind]
        owner = 2 * o + at.core if owner is None else owner
        piece = self.buf.at[s, rows_of(owner * self.parts + j, self.rows // self.parts)]
        return pltpu.make_async_remote_copy(
            src_ref=piece,
            dst_ref=piece,
            send_sem=self.send.at[kind, s, o, j],
            recv_sem=self.recv.at[s, owner, j],
            device_id={"tensor": target},
            device_id_type=MESH,
        )

    def arrived(self, s, o):
        for j in range(self.parts):
            self.copy(s, o, SIDE, j, 2 * o + 1 - self.at.core).wait_recv()

    def relay(self, j, s, o):
        at = self.at
        pl.when(o != at.chip)(lambda: self.copy(s, o, SIDE, j).wait_recv())
        pl.when((o <= at.chip) & at.above)(lambda: self.copy(s, o, UP, j).start())
        pl.when((o >= at.chip) & at.below)(lambda: self.copy(s, o, DOWN, j).start())
        self.copy(s, o, SIDE, j).start()

    def own(self, kind, j, s, o):
        self.copy(s, o, kind, j).start()

    def actions(self, kind, own=()):
        found = {}
        for j in range(self.parts):
            found[kind + j * PART] = functools.partial(self.relay, j)
            for which, way in zip(own, (SIDE, UP, DOWN)):
                found[which + j * PART] = functools.partial(self.own, way, j)
        return found

    def finish(self):
        at = self.at

        def one(i, carry):
            s, o = i // at.chips, lax.rem(i, at.chips)
            for j in range(self.parts):
                pl.when((o <= at.chip) & at.above)(lambda: self.copy(s, o, UP, j).wait_send())
                pl.when((o >= at.chip) & at.below)(lambda: self.copy(s, o, DOWN, j).wait_send())
                self.copy(s, o, SIDE, j).wait_send()
            return carry

        lax.fori_loop(0, self.seqs * at.chips, one, 0)


class Scatter:
    def __init__(self, at, rows, part, side, link, side_send, side_recv, send, recv):
        self.at, self.rows = at, rows
        self.part, self.side, self.link = part, side, link
        self.side_send, self.side_recv, self.send, self.recv = side_send, side_recv, send, recv
        self.seqs, self.parts = part.shape[0], recv.shape[2]
        self.size = rows // self.parts

    @staticmethod
    def scratch(n, seqs, rows, width, parts=1):
        chips = n // 2
        return [
            VMEM((seqs, chips, 2 * rows, width), bf16),
            VMEM((seqs, chips, rows, width), bf16),
            VMEM((seqs, chips + 1, rows, width), bf16),
            DMA((seqs, chips, parts)),
            DMA((seqs, chips, parts)),
            DMA((seqs, chips, parts)),
            DMA((seqs, chips + 1, parts)),
        ]

    def side_copy(self, s, o, j):
        at = self.at
        return pltpu.make_async_remote_copy(
            src_ref=self.part.at[s, o, rows_of((1 - at.core) * self.parts + j, self.size)],
            dst_ref=self.side.at[s, o, pl.ds(j * self.size, self.size)],
            send_sem=self.side_send.at[s, o, j],
            recv_sem=self.side_recv.at[s, o, j],
            device_id={"tensor": at.side},
            device_id_type=MESH,
        )

    def link_copy(self, s, o, slot, target, j):
        return pltpu.make_async_remote_copy(
            src_ref=self.part.at[s, o, rows_of(self.at.core * self.parts + j, self.size)],
            dst_ref=self.link.at[s, slot, pl.ds(j * self.size, self.size)],
            send_sem=self.send.at[s, o, j],
            recv_sem=self.recv.at[s, slot, j],
            device_id={"tensor": target},
            device_id_type=MESH,
        )

    def share(self, s, o):
        for j in range(self.parts):
            self.side_copy(s, o, j).start()

    def blocks(self, j, body):
        step = 16

        def one(i, carry):
            body(pl.multiple_of(j * self.size + i * step, step), step)
            return carry

        lax.fori_loop(0, self.size // step, one, 0)

    def total(self, s, o, first, step, slots):
        here = pl.ds(pl.multiple_of(self.at.core * self.rows + first, step), step)
        there = pl.ds(first, step)
        total = self.part[s, o, here].astype(f32) + self.side[s, o, there].astype(f32)
        for slot in slots:
            total += self.link[s, slot, there].astype(f32)
        return here, total

    def add_up(self, s, o, slots, j):
        def body(first, step):
            here, total = self.total(s, o, first, step, slots)
            self.part[s, o, here] = total.astype(bf16)

        self.blocks(j, body)

    def pass_on(self, final, j, s, o):
        at = self.at
        self.side_copy(s, o, j).wait_recv()

        def onward(before, slot, target):
            @pl.when(before)
            def _():
                self.link_copy(s, o, o, at.me, j).wait_recv()
                self.add_up(s, o, [o], j)

            pl.when(jnp.logical_not(before))(lambda: self.add_up(s, o, [], j))
            self.link_copy(s, o, slot, target, j).start()

        pl.when(o > at.chip)(lambda: onward(at.below, o, at.me + 2))
        last = jnp.where(o == at.chip - 1, at.chips, o)
        pl.when(o < at.chip)(lambda: onward(at.above, last, at.me - 2))

        @pl.when(o == at.chip)
        def _():
            for slot, used in ((o, at.below), (at.chips, at.above)):
                pl.when(used)(lambda: self.link_copy(s, o, slot, at.me, j).wait_recv())

                @pl.when(jnp.logical_not(used))
                def _():
                    def clear(first, step):
                        self.link[s, slot, pl.ds(first, step)] = jnp.zeros(
                            (step, self.link.shape[-1]), bf16
                        )

                    self.blocks(j, clear)

            def body(first, step):
                total = self.total(s, o, first, step, [o, at.chips])[1]
                final(s, pl.ds(first, step), total)

            self.blocks(j, body)

    def actions(self, kind, final):
        return {
            kind + j * PART: functools.partial(self.pass_on, final, j) for j in range(self.parts)
        }

    def finish(self):
        at = self.at

        def one(i, carry):
            s, o = i // at.chips, lax.rem(i, at.chips)
            for j in range(self.parts):
                self.side_copy(s, o, j).wait_send()
                pl.when(o != at.chip)(lambda: self.link_copy(s, o, o, at.side, j).wait_send())
            return carry

        lax.fori_loop(0, self.seqs * at.chips, one, 0)


class GroupSum:
    def __init__(self, at, rows, tiles, inbox, send, recv, keep_sem, out, turn=0, skip=0):
        self.at, self.tiles, self.inbox, self.send, self.recv = at, tiles, inbox, send, recv
        self.keep_sem, self.out, self.skip, self.turn, self.rows = keep_sem, out, skip, turn, rows
        self.bits = at.group_bits
        self.count = send.shape[0]

    @staticmethod
    def scratch(dp, count, rows, width, skip=0):
        phases = 2 * (dp.bit_length() - 1)
        return [
            VMEM((count, rows >> skip, width), bf16),
            VMEM((count, rows - rows // dp, width), bf16),
            DMA((count, phases)),
            DMA((count, phases)),
            DMA((count,)),
        ]

    def peer(self, t, i):
        which = lax.rem(t + i + self.turn, self.bits)
        peer, mine = 0, 0
        for q in range(self.bits):
            other, bit = self.at.group_peer(q)
            peer = peer + jnp.where(which == q, other, 0)
            mine = mine + jnp.where(which == q, bit, 0)
        return peer, mine

    def base(self, t, i):
        first = 0
        for p in range(i):
            first = first + self.peer(t, p)[1] * (self.rows >> (p + 1))
        return first

    def span(self, first, size):
        return pl.ds(pl.multiple_of(first, 16), size)

    def tile(self, t, first, size):
        return self.tiles.at[t, self.span(first - self.base(t, self.skip), size)]

    def box(self, t, i):
        return self.inbox.at[t, pl.ds(self.rows - (self.rows >> i), self.rows >> (i + 1))]

    def remote(self, source, target, t, phase, peer):
        return pltpu.make_async_remote_copy(
            src_ref=source,
            dst_ref=target,
            send_sem=self.send.at[t, phase],
            recv_sem=self.recv.at[t, phase],
            device_id={"dp": peer},
            device_id_type=MESH,
        )

    def halve(self, t, i):
        peer, mine = self.peer(t, i)
        half = self.rows >> (i + 1)
        source = self.tile(t, self.base(t, i) + (1 - mine) * half, half)
        return self.remote(source, self.box(t, i), t, i, peer)

    def add(self, t, i):
        half = self.rows >> (i + 1)
        keep = self.base(t, i + 1) - self.base(t, self.skip)
        box = self.rows - (self.rows >> i)

        def body(j, carry):
            here = self.span(keep + j * 16, 16)
            there = self.span(box + j * 16, 16)
            total = self.tiles[t, here].astype(f32) + self.inbox[t, there].astype(f32)
            self.tiles[t, here] = total.astype(bf16)
            return carry

        lax.fori_loop(0, half // 16, body, 0)

    def keep(self, t):
        first, size = self.base(t, self.bits), self.rows >> self.bits
        return pltpu.make_async_copy(
            self.tile(t, first, size), self.out.at[t, self.span(first, size)], self.keep_sem.at[t]
        )

    def double(self, t, i, back=False):
        peer, mine = self.peer(t, i)
        half = self.rows >> (i + 1)
        first = self.base(t, i) + ((1 - mine) if back else mine) * half
        piece = self.out.at[t, self.span(first, half)]
        source = piece
        if i == self.bits - 1 and not back:
            source = self.tile(t, first, half)
        return self.remote(source, piece, t, 2 * self.bits - 1 - i, peer)

    def events(self):
        return self.count * (2 * self.bits + 1 - self.skip)

    def event(self, e, loaded=None):
        k, t = e // self.count + self.skip, lax.rem(e, self.count)
        bits = self.bits

        def at_stage(stage):
            if stage == self.skip and loaded is not None:
                loaded(t)
            if stage == 0:
                self.halve(t, 0).start()
            elif stage <= bits:
                if stage > self.skip:
                    self.halve(t, stage - 1).wait_recv()
                self.add(t, stage - 1)
                if stage < bits:
                    self.halve(t, stage).start()
                else:
                    self.keep(t).start()
                    self.double(t, bits - 1).start()
            else:
                i = 2 * bits - stage
                self.double(t, i, back=True).wait_recv()
                if i == bits - 1:
                    self.keep(t).wait()
                if i > 0:
                    self.double(t, i - 1).start()

        for stage in range(self.skip, 2 * bits + 1):
            pl.when((k == stage) & (e >= 0))(functools.partial(at_stage, stage))

    def finish(self):
        def one(t, carry):
            for i in range(self.bits):
                if i >= self.skip:
                    self.halve(t, i).wait_send()
                self.double(t, i).wait_send()
            return carry

        lax.fori_loop(0, self.count, one, 0)


class SmallSum:
    def __init__(self, at, rows, inbox, send, recv, everywhere):
        self.at, self.rows, self.inbox, self.send, self.recv = at, rows, inbox, send, recv
        self.phases = at.group_bits + (at.bits if everywhere else 0)

    @staticmethod
    def scratch(dp, n, count, width, everywhere):
        phases = (dp.bit_length() - 1) + (n.bit_length() - 1 if everywhere else 0)
        return [
            VMEM((phases + 1, count, width), f32),
            VMEM((phases, count, width), f32),
            DMA((phases,)),
            DMA((phases,)),
        ]

    def copy(self, i):
        at = self.at
        if i < at.group_bits:
            target = {"dp": at.group_peer(i)[0]}
        else:
            target = {"tensor": at.peer(i - at.group_bits)}
        return pltpu.make_async_remote_copy(
            src_ref=self.rows.at[i],
            dst_ref=self.inbox.at[i],
            send_sem=self.send.at[i],
            recv_sem=self.recv.at[i],
            device_id=target,
            device_id_type=MESH,
        )

    def event(self, e):
        def run(i):
            if i > 0:
                self.copy(i - 1).wait_recv()
                self.rows[i] = self.rows[i - 1] + self.inbox[i - 1]
            if i < self.phases:
                self.copy(i).start()

        for i in range(self.phases + 1):
            if isinstance(e, int):
                if e == i:
                    run(i)
            else:
                pl.when(e == i)(functools.partial(run, i))

    def finish(self):
        for i in range(self.phases):
            self.copy(i).wait_send()


class DirectSum:
    def __init__(self, at, rows, group_box, line_box, send, recv):
        self.at, self.rows, self.send, self.recv = at, rows, send, recv
        self.boxes = (group_box, line_box)

    @staticmethod
    def scratch(dp, n, count, width):
        most = max(dp, n)
        return [
            VMEM((count, width), f32),
            VMEM((dp, count, width), f32),
            VMEM((n, count, width), f32),
            DMA((2, most)),
            DMA((2, most)),
        ]

    def copy(self, step, other, back=False):
        at, box = self.at, self.boxes[step]
        size, axis = box.shape[0], ("dp", "tensor")[step]
        mine = (at.group, at.me)[step]
        peer = lax.rem(mine + other, size)
        slot = peer if back else mine
        return pltpu.make_async_remote_copy(
            src_ref=box.at[mine],
            dst_ref=box.at[slot],
            send_sem=self.send.at[step, other],
            recv_sem=self.recv.at[step, slot],
            device_id={axis: peer},
            device_id_type=MESH,
        )

    def event(self, e):
        if e > 0:
            box = self.boxes[e - 1]
            for other in range(1, box.shape[0]):
                self.copy(e - 1, other, back=True).wait_recv()
            total = box[0]
            for i in range(1, box.shape[0]):
                total = total + box[i]
            self.rows[...] = total
        if e < 2:
            box = self.boxes[e]
            box[(self.at.group, self.at.me)[e]] = self.rows[...]
            for other in range(1, box.shape[0]):
                self.copy(e, other).start()

    def finish(self):
        for step, box in enumerate(self.boxes):
            for other in range(1, box.shape[0]):
                self.copy(step, other).wait_send()


def norm_rows(values, gain, shift):
    centre = values - jnp.mean(values, axis=-1, keepdims=True)
    spread = jnp.mean(centre * centre, axis=-1, keepdims=True)
    return centre * lax.rsqrt(spread + norm_epsilon) * gain + shift


def norm_rows_back(values, grad, gain):
    centre = values - jnp.mean(values, axis=-1, keepdims=True)
    scale = lax.rsqrt(jnp.mean(centre * centre, axis=-1, keepdims=True) + norm_epsilon)
    unit = centre * scale
    w = grad * gain
    back = w - jnp.mean(w, axis=-1, keepdims=True)
    back = scale * (back - unit * jnp.mean(w * unit, axis=-1, keepdims=True))
    return back, grad * unit


def add_row(ref, row, values):
    ref[row : row + 1] += jnp.sum(values, axis=0, keepdims=True)


def head_probs(query, keys, first, length):
    rows, cols = query.shape[0], keys.shape[0]
    scores = lax.dot_general(query, keys, NT, preferred_element_type=f32)
    row_ids = first + lax.broadcasted_iota(jnp.int32, (rows, cols), 0)
    col_ids = lax.broadcasted_iota(jnp.int32, (rows, cols), 1)
    scores = jnp.where((col_ids <= row_ids) & (col_ids < length), scores, -1e30)
    probs = jnp.exp(scores - jnp.max(scores, axis=-1, keepdims=True))
    return probs * (1.0 / jnp.sum(probs, axis=-1, keepdims=True))


def attend(heads, lengths, mixed, block, s):
    slots, part = mixed.shape[1:]

    def one(h, carry):
        cols = pl.ds(pl.multiple_of(h * HD, HD), HD)
        for first in range(0, slots, block):
            rows, seen = pl.ds(first, block), pl.ds(0, first + block)
            probs = head_probs(heads[0, s, rows, cols], heads[1, s, seen, cols], first, lengths[s])
            mixed[s, rows, cols] = jnp.dot(
                probs.astype(bf16), heads[2, s, seen, cols], preferred_element_type=f32
            ).astype(bf16)
        return carry

    lax.fori_loop(0, part // HD, one, 0)


def attend_back(heads, grad_heads, lengths, grads, grad_key, grad_value, block, s):
    slots, part = grad_heads.shape[1:]

    def one(h, carry):
        cols = pl.ds(pl.multiple_of(h * HD, HD), HD)
        grad_key[...] = jnp.zeros_like(grad_key)
        grad_value[...] = jnp.zeros_like(grad_value)
        for first in range(0, slots, block):
            rows, seen = pl.ds(first, block), pl.ds(0, first + block)
            query, grad = heads[0, s, rows, cols], grad_heads[s, rows, cols]
            keys = heads[1, s, seen, cols]
            probs = head_probs(query, keys, first, lengths[s])
            grad_value[seen] += lax.dot_general(
                probs.astype(bf16), grad, TN, preferred_element_type=f32
            )
            back = lax.dot_general(
                grad, heads[2, s, seen, cols], NT, preferred_element_type=f32
            )
            centre = jnp.sum(probs * back, axis=-1, keepdims=True)
            scores = (probs * (back - centre)).astype(bf16)
            grads[0, s, rows, cols] = jnp.dot(
                scores, keys, preferred_element_type=f32
            ).astype(bf16)
            grad_key[seen] += lax.dot_general(scores, query, TN, preferred_element_type=f32)
        grads[1, s, :, cols] = grad_key[...].astype(bf16)
        grads[2, s, :, cols] = grad_value[...].astype(bf16)
        return carry

    lax.fori_loop(0, part // HD, one, 0)


def attention_block_kernel(
    n,
    tokens,
    cotangent,
    lengths,
    gain,
    shift,
    weight,
    bias,
    out_weight,
    out_bias,
    gain_two,
    shift_two,
    gathered,
    heads_hbm,
    mixed_hbm,
    hidden,
    normed,
    grad_all,
    heads,
    mixed,
    result_sem,
    buf,
    send,
    recv,
    keep_sem,
    grad_send,
    grad_recv,
    masked,
    mask_sem,
    *scratch,
):
    at = Place(n)
    seqs, rows, width = tokens.shape
    ring = Gather(at, rows, buf, send, recv)
    grad_ring = Gather(at, rows, grad_all, grad_send, grad_recv)
    line = Scatter(at, rows, *scratch)

    def mask_copy(s):
        return pltpu.make_async_copy(
            masked.at[s], grad_all.at[s, rows_of(at.me, rows)], mask_sem.at[s]
        )

    for s in range(seqs):
        def block(i, carry):
            first = pl.multiple_of(i * 16, 16)
            here = pl.ds(first, 16)
            values = norm_rows(tokens[s, here].astype(f32), gain[...], shift[...])
            buf[s, pl.ds(pl.multiple_of(at.me * rows + first, 16), 16)] = values.astype(bf16)
            slot = at.me * rows + first + lax.broadcasted_iota(jnp.int32, (16, width), 0)
            grad = jnp.where(slot < lengths[s], cotangent[s, here].astype(f32), 0.0)
            masked[s, here] = grad.astype(bf16)
            return carry

        lax.fori_loop(0, rows // 16, block, 0)
        mask_copy(s).start()
    at.greet()
    for s in range(seqs):
        mask_copy(s).wait()

    def keep(s, o):
        here = rows_of(o, 2 * rows)
        return pltpu.make_async_copy(buf.at[s, here], gathered.at[s, here], keep_sem.at[s, o])

    def project(s, o):
        ring.arrived(s, o)
        keep(s, o).start()
        here = rows_of(o, 2 * rows)
        for j in range(3):
            total = jnp.dot(buf[s, here], weight[j], preferred_element_type=f32)
            if j == 0:
                total = (total + bias[0:1]) * HD ** (-0.5)
            if j == 2:
                total = total + bias[1:2]
            heads[j, s, here] = total.astype(bf16)

    def final(s, there, total):
        values = tokens[s, there].astype(f32) + total + out_bias[...]
        hidden[s, there] = values
        normed[s, there] = norm_rows(values, gain_two[...], shift_two[...]).astype(bf16)

    def results(s):
        pairs = [(heads.at[j, s], heads_hbm.at[j, s]) for j in range(3)]
        pairs.append((mixed.at[s], mixed_hbm.at[s]))
        return [
            pltpu.make_async_copy(source, target, result_sem.at[s, j])
            for j, (source, target) in enumerate(pairs)
        ]

    def mix(s, o):
        attend(heads, lengths, mixed, min(512, n * rows), s)
        for copy in results(s):
            copy.start()

    def project_out(s, o):
        here = rows_of(o, 2 * rows)
        for j in range(width // 512):
            cols = pl.ds(j * 512, 512)
            total = jnp.dot(mixed[s, here], out_weight[:, cols], preferred_element_type=f32)
            line.part[s, o, :, cols] = total.astype(bf16)
        line.share(s, o)

    def ops_of(c):
        chips = at.chips
        mixing = []
        for s in range(seqs):
            needs = [("heads", c, s, o) for o in range(chips)]
            mixing.append(((2, s, 0), (2, s, 0), needs, 6.0, [], [(0.0, ("mixed", c, s))]))
        return (
            gather_ops(c, chips, seqs, 0, "in", gate=True)
            + work_ops(
                c, chips, seqs, 1, lambda s, o: gathered_here("in", c, s, o), "heads", 1.0
            )
            + mixing
            + work_ops(
                c, chips, seqs, 3, lambda s, o: [("mixed", c, s)], "part", 1.0, far=True
            )
            + scatter_ops(c, chips, seqs, 4, "out", "part", last=4.0)
            + gather_ops(c, chips, seqs, 5, "grad", rank=6)
        )

    Plan(at, seqs, ops_of).run(
        {
            1: project,
            2: mix,
            3: project_out,
            **ring.actions(0),
            **line.actions(4, final),
            **grad_ring.actions(5),
        }
    )
    ring.finish()
    line.finish()
    grad_ring.finish()

    for s in range(seqs):
        for copy in results(s):
            copy.wait()

    def close(i, carry):
        s, o = i // at.chips, lax.rem(i, at.chips)
        grad_ring.arrived(s, o)
        keep(s, o).wait()
        return carry

    lax.fori_loop(0, seqs * at.chips, close, 0)


def whole(count):
    return [pl.BlockSpec(memory_space=VMEM)] * count


def attention_block(
    n,
    tokens,
    cotangent,
    lengths,
    gain,
    shift,
    weight,
    bias,
    out_weight,
    out_bias,
    gain_two,
    shift_two,
):
    seqs, rows, width = tokens.shape
    part = weight.shape[2]
    vmem = pl.BlockSpec(memory_space=VMEM)
    hbm = pl.BlockSpec(memory_space=pl.ANY)
    smem = pl.BlockSpec(memory_space=pltpu.SMEM)
    return pl.pallas_call(
        functools.partial(attention_block_kernel, n),
        out_shape=(
            jax.ShapeDtypeStruct((seqs, n * rows, width), bf16),
            jax.ShapeDtypeStruct((3, seqs, n * rows, part), bf16),
            jax.ShapeDtypeStruct((seqs, n * rows, part), bf16),
            jax.ShapeDtypeStruct((seqs, rows, width), f32),
            jax.ShapeDtypeStruct((seqs, rows, width), bf16),
            jax.ShapeDtypeStruct((seqs, n * rows, width), bf16),
        ),
        in_specs=[vmem, vmem, smem] + [vmem] * 8,
        out_specs=(hbm, hbm, hbm, vmem, vmem, hbm),
        scratch_shapes=[
            VMEM((3, seqs, n * rows, part), bf16),
            VMEM((seqs, n * rows, part), bf16),
            DMA((seqs, 4)),
            VMEM((seqs, n * rows, width), bf16),
        ]
        + Gather.scratch(n, seqs)
        + [DMA((seqs, n // 2))]
        + Gather.scratch(n, seqs)
        + [VMEM((seqs, rows, width), bf16), DMA((seqs,))]
        + Scatter.scratch(n, seqs, rows, width),
        compiler_params=pltpu.CompilerParams(
            collective_id=0, has_side_effects=True, vmem_limit_bytes=60 * 2**20
        ),
        name="attention_block",
    )(
        tokens,
        cotangent,
        lengths,
        gain,
        shift,
        weight,
        bias,
        out_weight,
        out_bias,
        gain_two,
        shift_two,
    )


def heads_scatter_kernel(
    n,
    grads,
    weight,
    gathered_hbm,
    out_part,
    tokens_hbm,
    gain,
    hidden_hbm,
    up_part,
    grad,
    sums_all,
    weight_grad,
    out_grad,
    bias_grad,
    up_grad,
    *scratch,
):
    at = Place(n)
    seqs, rows, width = hidden_hbm.shape
    line = Scatter(at, rows, *scratch[:7])
    weight_sum = GroupSum(at, width, *scratch[7:12], weight_grad)
    out_sum = GroupSum(at, out_part.shape[0], *scratch[12:17], out_grad, turn=1)
    small = DirectSum(at, *scratch[17:22])
    small_bias = SmallSum(at, *scratch[22:26], False)
    gathered, tokens, hidden_grad, in_sem = scratch[26:30]
    up_sum = GroupSum(at, up_part.shape[1], *scratch[30:35], up_grad, turn=1)
    up_load = pltpu.make_async_copy(up_part.at[3], up_sum.tiles.at[0], in_sem.at[3])
    up_load.start()
    sources = ((gathered_hbm, gathered), (tokens_hbm, tokens), (hidden_hbm, hidden_grad))
    loads = [
        pltpu.make_async_copy(source, target, in_sem.at[i])
        for i, (source, target) in enumerate(sources)
    ]
    for copy in loads:
        copy.start()
    out_sum.tiles[0] = out_part[...]
    small.rows[...] = jnp.zeros_like(small.rows)
    at.greet(groups=True, everyone=True)

    def bias_sums():
        for row, j, scale in ((0, 0, HD ** (-0.5)), (1, 2, 1.0)):
            total = 0.0
            for s in range(seqs):
                total += jnp.sum(grads[j, s].astype(f32), axis=0, keepdims=True)
            small_bias.rows[0, row : row + 1] = scale * total

    def beside(k):
        pl.when(k == 10)(bias_sums)
        for e in range(small_bias.phases + 1):
            pl.when(k == 11 + 6 * e)(functools.partial(small_bias.event, e))


    def final(s, there, total):
        back, terms = norm_rows_back(tokens[s, there].astype(f32), total, gain[...])
        grad[s, there] = hidden_grad[s, there] + back
        add_row(small.rows, 0, terms)
        add_row(small.rows, 1, total)

    scales = (HD ** (-0.5), 1.0, 1.0)

    def weight_tile(j):
        for first in range(0, width, 512):
            total = 0.0
            for s in range(seqs):
                total += lax.dot_general(
                    gathered[s, :, pl.ds(first, 512)],
                    grads[j, s],
                    TN,
                    preferred_element_type=f32,
                )
            weight_sum.tiles[j, pl.ds(first, 512)] = (scales[j] * total).astype(bf16)

    def work(s, o):
        here = rows_of(o, 2 * rows)
        for j in range(width // 512):
            cols = pl.ds(j * 512, 512)
            total = 0.0
            for i in range(3):
                total += scales[i] * lax.dot_general(
                    grads[i, s, here], weight[i, cols], NT, preferred_element_type=f32
                )
            line.part[s, o, :, cols] = total.astype(bf16)
        line.share(s, o)

    each = seqs * at.chips

    def weight_event(first, s, o):
        e = first + s * at.chips + o

        @pl.when(e == 0)
        def _():
            for copy in loads:
                copy.wait()

        for j in range(3):
            pl.when(e == j)(functools.partial(weight_tile, j))
        weight_sum.event(e)

    def out_event(s, o):
        out_sum.event(s * at.chips + o)

    def up_event(first, s, o):
        up_sum.event(first + s * at.chips + o, lambda t: up_load.wait())

    def code_of(kind, e):
        return (kind + e // each, e % each // at.chips, e % at.chips)

    def ops_of(c):
        chips = at.chips
        finals = scatter_ops(c, chips, seqs, 1, "out", "part", last=4.0, parts=line.parts)
        loaded = ("qkv", c, 0, 0, 1)
        for i, (rank, code, needs, time, sends, gives) in enumerate(finals):
            if code[2] == c:
                finals[i] = (rank, code, needs + [loaded], time, sends, gives)
        smalls = []
        needs = [("out", c, s, "sum", j) for s in range(seqs) for j in range(line.parts)]
        for e in range(3):
            smalls.append(((0, e), (30 + e, 0, 0), needs, 0.5, [], [(4.0, ("small", c, e))]))
            needs = [("small", c, e)]
        return smalls + (
            work_ops(c, chips, seqs, 0, lambda s, o: [], "part", 1.5, far=True)
            + finals
            + group_ops(
                c, at.group_bits, 3, PIECE, lambda e: code_of(2, e), 0, (0,), 2.7, -1, "qkv"
            )
            + group_ops(
                c, at.group_bits, 1, PIECE, lambda e: code_of(5, e), 0, (1,), 0.7, -1, "out_sum"
            )
            + group_ops(
                c, at.group_bits, 1, PIECE, lambda e: code_of(20, e), 0, (1,), 0.7, -2, "up"
            )
        )

    actions = {0: work, 5: out_event, **line.actions(1, final)}
    for i in range(-(-up_sum.events() // each)):
        actions[20 + i] = functools.partial(up_event, i * each)
    for i in range(3):
        actions[2 + i] = functools.partial(weight_event, i * each)
        actions[30 + i] = lambda s, o, e=i: small.event(e)
    Plan(at, seqs, ops_of).run(actions, beside)
    small.finish()
    sums_all[...] = small.rows[...]
    bias_grad[...] = small_bias.rows[small_bias.phases]
    line.finish()
    weight_sum.finish()
    out_sum.finish()
    up_sum.finish()
    small_bias.finish()


def heads_scatter(n, grads, weight, gathered, out_part, tokens, gain, hidden_grad, up_part):
    seqs, slots, part = grads.shape[1:]
    width = weight.shape[1]
    rows = slots // n
    dp = lax.axis_size("dp")
    vmem = pl.BlockSpec(memory_space=VMEM)
    hbm = pl.BlockSpec(memory_space=pl.ANY)
    return pl.pallas_call(
        functools.partial(heads_scatter_kernel, n),
        out_shape=(
            jax.ShapeDtypeStruct((seqs, rows, width), f32),
            jax.ShapeDtypeStruct((2, width), f32),
            jax.ShapeDtypeStruct((3, width, part), bf16),
            jax.ShapeDtypeStruct((1, part, width), bf16),
            jax.ShapeDtypeStruct((2, part), f32),
            jax.ShapeDtypeStruct((1,) + up_part.shape[1:], bf16),
        ),
        in_specs=[vmem, vmem, hbm, vmem, hbm, vmem, hbm, hbm],
        out_specs=(vmem, vmem, hbm, hbm, vmem, hbm),
        scratch_shapes=Scatter.scratch(n, seqs, rows, width, 2)
        + GroupSum.scratch(dp, 3, width, part)
        + GroupSum.scratch(dp, 1, part, width)
        + DirectSum.scratch(dp, n, 2, width)
        + SmallSum.scratch(dp, n, 2, part, False)
        + [
            VMEM(gathered.shape, bf16),
            VMEM(tokens.shape, bf16),
            VMEM(hidden_grad.shape, f32),
            DMA((4,)),
        ]
        + GroupSum.scratch(dp, 1, *up_part.shape[1:]),
        compiler_params=pltpu.CompilerParams(
            collective_id=2, has_side_effects=True, vmem_limit_bytes=62 * 2**20
        ),
        name="heads_scatter",
    )(grads, weight, gathered, out_part, tokens, gain, hidden_grad, up_part)


def normal_cdf(values):
    x = jnp.clip(values * 0.7071067811865476, -3.832506856900711, 3.832506856900711)
    x2 = x * x
    top = 0.00022905065861350646
    for c in (0.0034082910107109506, 0.050955695062380861, 0.18520832239976145, 1.128379143519084):
        top = top * x2 + c
    low = -1.1791602954361697e-7
    for c in (
        0.000023547966471313185,
        0.0010179625278914885,
        0.014070470171167667,
        0.11098505178285362,
        0.49746925110067538,
        1.0,
    ):
        low = low * x2 + c
    return 0.5 + 0.5 * (x * top / low)


def mlp_kernel(
    n,
    normed,
    grad_hbm,
    up_hbm,
    up_bias,
    down_hbm,
    hidden_hbm,
    gain,
    mlp_part,
    hidden_grad,
    grad_low,
    sums,
    up_grad,
    up_bias_grad,
    down_grad,
    down_box,
    buf,
    send,
    recv,
    grad_all,
    up_weight,
    down_weight,
    hidden,
    in_sem,
    *scratch,
):
    at = Place(n)
    seqs, rows, width = normed.shape
    units_wide = up_weight.shape[1]
    line = Scatter(at, rows, *scratch[:7])
    act, pre, out_stage, out_sem, up_stage, down_stage, tile_sem, half_send, half_recv = scratch[7:]
    ring = Gather(at, rows, buf, send, recv)
    loads = [
        pltpu.make_async_copy(source, target, in_sem.at[i])
        for i, (source, target) in enumerate(
            (
                (up_hbm, up_weight),
                (grad_hbm, grad_all),
                (down_hbm, down_weight),
                (hidden_hbm, hidden),
            )
        )
    ]
    for copy in loads:
        copy.start()
    at.greet(groups=True)
    for s in range(seqs):
        buf[s, rows_of(at.me, rows)] = normed[s]
    up_bias_grad[...] = jnp.zeros_like(up_bias_grad)
    sums[...] = jnp.zeros_like(sums)
    ft = min(512, units_wide)

    def out_copy(s, o):
        return pltpu.make_async_copy(
            out_stage, mlp_part.at[s, rows_of(o, 2 * rows)], out_sem.at[0]
        )

    def work(s, o):
        ring.arrived(s, o)

        @pl.when((s == 0) & (o == at.chip))
        def _():
            for copy in loads:
                copy.wait()

        here = rows_of(o, 2 * rows)
        for j in range(units_wide // ft):
            cols = pl.ds(j * ft, ft)
            value = jnp.dot(buf[s, here], up_weight[:, cols], preferred_element_type=f32)
            value = value + up_bias[:, cols]
            spread = normal_cdf(value)
            act[s, here, cols] = (value * spread).astype(bf16)
            slope = spread + value * (0.3989422804014327 * jnp.exp(-0.5 * value * value))
            grad = lax.dot_general(
                grad_all[s, here], down_weight[cols], NT, preferred_element_type=f32
            )
            grad = (grad * slope).astype(bf16)
            pre[s, here, cols] = grad
            up_bias_grad[:, cols] += jnp.sum(grad.astype(f32), axis=0, keepdims=True)
        for j in range(width // 512):
            cols = pl.ds(j * 512, 512)
            line.part[s, o, :, cols] = lax.dot_general(
                pre[s, here], up_weight[cols], NT, preferred_element_type=f32
            ).astype(bf16)
        line.share(s, o)

    def work_down(s, o):
        here = rows_of(o, 2 * rows)
        pl.when((s > 0) | (o != at.chip))(lambda: out_copy(s, o).wait())
        for j in range(width // 512):
            cols = pl.ds(j * 512, 512)
            out_stage[:, cols] = jnp.dot(
                act[s, here], down_weight[:, cols], preferred_element_type=f32
            ).astype(bf16)
        out_copy(s, o).start()

    def final(s, there, total):
        back, terms = norm_rows_back(hidden[s, there], total, gain[...])
        first = pl.multiple_of(at.me * rows + there.start, 16)
        grad_out = grad_all[s, pl.ds(first, there.size)].astype(f32)
        grad = grad_out + back
        hidden_grad[s, there] = grad
        grad_low[s, there] = grad.astype(bf16)
        add_row(sums, 0, terms)
        add_row(sums, 1, total)
        add_row(sums, 2, grad)
        add_row(sums, 3, grad_out)

    kinds = ((down_stage, down_grad), (up_stage, up_grad))

    def tile_copy(kind, t):
        stage, grad = kinds[kind]
        return pltpu.make_async_copy(stage, grad.at[t], tile_sem.at[kind])

    def down_half(t):
        half = down_box.shape[1]
        peer, mine = at.group_peer(t % at.group_bits)
        return pltpu.make_async_remote_copy(
            src_ref=down_grad.at[t, rows_of(1 - mine, half)],
            dst_ref=down_box.at[t],
            send_sem=half_send.at[t],
            recv_sem=half_recv.at[t],
            device_id={"dp": peer},
            device_id_type=MESH,
        )

    def tile_sent(kind, t):
        tile_copy(kind, t).wait()
        if kind == 0:
            down_half(t).start()

    order = [(i // 4, i % 4) for i in range(8)]

    def weight_tile(i):
        for j, (kind, t) in enumerate(order):
            @pl.when(i == j)
            def _():
                stage = kinds[kind][0]
                cols = pl.ds(t * stage.shape[0], stage.shape[0])
                total = 0.0
                for s in range(seqs):
                    if kind == 0:
                        left, right = act[s, :, cols], grad_all[s]
                    else:
                        left, right = buf[s, :, cols], pre[s]
                    total += lax.dot_general(left, right, TN, preferred_element_type=f32)
                if j >= 1:
                    tile_sent(*order[j - 1])
                stage[...] = total.astype(bf16)
                tile_copy(kind, t).start()

    def tile_work(s, o):
        weight_tile(s * at.chips + o)

    own = (4, 5, 6)

    def ops_of(c):
        chips = at.chips
        units = [(s, o) for s in range(seqs) for o in range(chips)]
        ops = gather_ops(c, chips, seqs, 0, "in", own=own, parts=ring.parts)
        ops += scatter_ops(c, chips, seqs, 1, "back", "part", last=4.0)
        for s, o in units:
            needs = gathered_here("in", c, s, o, ring.parts)
            gives = [(3.0, ("part", c, s, o)), (0.0, ("done", c, s, o))]
            needs_down, gives_down = [("done", c, s, o)], []
            if (s, o) == (0, c):
                gives.append((0.0, ("first", c)))
                gives_down.append((0.0, ("first down", c)))
            else:
                needs.append(("first", c))
                needs_down.append(("first down", c))
            rank = (s, abs(o - c))
            ops.append(((2,) + rank, (2, s, o), needs, 4.3, [], gives))
            ops.append(((3,) + rank, (7, s, o), needs_down, 1.4, [], gives_down))
        for e in range(len(order)):
            needs = [("part", c, s, o) for s, o in units]
            needs += [("tile", c, e - 1)] if e else []
            sends = [("axis%d" % (e % 2), c, ("half", c, e), PIECE)] if e < 4 else []
            code = (3, e // chips, e % chips)
            ops.append(((4, e, 0), code, needs, 2.7, sends, [(0.0, ("tile", c, e))]))
        return ops

    actions = {2: work, 3: tile_work, 7: work_down}
    actions.update({**ring.actions(0, own), **line.actions(1, final)})
    Plan(at, seqs, ops_of).run(actions)
    tile_sent(*order[7])
    ring.finish()
    line.finish()
    for t in range(4):
        down_half(t).wait()
    out_copy(0, 0).wait()


def mlp_block(n, normed, grad_all, up_weight, up_bias, down_weight, hidden, gain):
    seqs, rows, width = normed.shape
    slots = n * rows
    units = up_weight.shape[1]
    hbm = pl.BlockSpec(memory_space=pl.ANY)
    vmem = pl.BlockSpec(memory_space=VMEM)
    down_size, up_size = units // 4, width // 4
    return pl.pallas_call(
        functools.partial(mlp_kernel, n),
        out_shape=(
            jax.ShapeDtypeStruct((seqs, slots, width), bf16),
            jax.ShapeDtypeStruct((seqs, rows, width), f32),
            jax.ShapeDtypeStruct((seqs, rows, width), bf16),
            jax.ShapeDtypeStruct((4, width), f32),
            jax.ShapeDtypeStruct((4, up_size, units), bf16),
            jax.ShapeDtypeStruct((1, units), f32),
            jax.ShapeDtypeStruct((4, down_size, width), bf16),
            jax.ShapeDtypeStruct((4, down_size // 2, width), bf16),
        ),
        in_specs=[vmem, hbm, hbm, vmem, hbm, hbm, vmem],
        out_specs=(hbm, vmem, vmem, vmem, hbm, vmem, hbm, hbm),
        scratch_shapes=[VMEM((seqs, slots, width), bf16)]
        + Gather.scratch(n, seqs, 4)
        + [
            VMEM((seqs, slots, width), bf16),
            VMEM(up_weight.shape, bf16),
            VMEM(down_weight.shape, bf16),
            VMEM(hidden.shape, f32),
            DMA((4,)),
        ]
        + Scatter.scratch(n, seqs, rows, width)
        + [
            VMEM((seqs, slots, units), bf16),
            VMEM((seqs, slots, units), bf16),
            VMEM((2 * rows, width), bf16),
            DMA((1,)),
            VMEM((up_size, units), bf16),
            VMEM((down_size, width), bf16),
            DMA((2,)),
            DMA((4,)),
            DMA((4,)),
        ],
        compiler_params=pltpu.CompilerParams(
            collective_id=3, has_side_effects=True, vmem_limit_bytes=62 * 2**20
        ),
        name="mlp_block",
    )(normed, grad_all, up_weight, up_bias, down_weight, hidden, gain)


def attn_grad_kernel(
    n,
    grad,
    mlp_part,
    hidden_hbm,
    bias,
    weight_hbm,
    mixed_hbm,
    sums,
    up_bias_part,
    up_part,
    down_part,
    down_box,
    lengths,
    heads_hbm,
    output,
    grads,
    weight_grad,
    sums_all,
    up_bias_grad,
    up_grad,
    down_grad,
    buf,
    send,
    recv,
    *scratch,
):
    at = Place(n)
    seqs, rows, width = grad.shape
    line = Scatter(at, rows, *scratch[:7])
    load_sem, tile_sem, box_sem = scratch[7:10]
    ring = Gather(at, rows, buf, send, recv)
    up_sum = GroupSum(at, up_part.shape[1], *scratch[10:15], up_grad, turn=1)
    down_sum = GroupSum(at, down_part.shape[1], *scratch[15:20], down_grad, skip=1)
    small = SmallSum(at, *scratch[20:24], True)
    small_bias = SmallSum(at, *scratch[24:28], False)
    grad_heads, grad_key, grad_value, hidden, weight, mixed, heads, in_sem = scratch[28:]
    sources = (weight_hbm, weight), (hidden_hbm, hidden), (mixed_hbm, mixed), (heads_hbm, heads)
    loads = [
        pltpu.make_async_copy(source, target, in_sem.at[i])
        for i, (source, target) in enumerate(sources)
    ]
    for copy in loads:
        copy.start()
    def up_load(t):
        return pltpu.make_async_copy(up_part.at[t], up_sum.tiles.at[t], tile_sem.at[0, t])

    def down_load(t):
        half = down_box.shape[1]
        kept = down_part.at[t, down_sum.span(down_sum.base(t, 1), half)]
        return (
            pltpu.make_async_copy(kept, down_sum.tiles.at[t], tile_sem.at[1, t]),
            pltpu.make_async_copy(down_box.at[t], down_sum.box(t, 0), box_sem.at[t]),
        )

    def up_loaded(t):
        up_load(t).wait()

    def down_loaded(t):
        for copy in down_load(t):
            copy.wait()

    for t in range(4):
        if t < up_sum.count:
            up_load(t).start()
        for copy in down_load(t):
            copy.start()
    small.rows[0] = sums[...]
    small_bias.rows[0] = up_bias_part[...]

    def load(s, o):
        return pltpu.make_async_copy(
            mlp_part.at[s, rows_of(o, 2 * rows)], line.part.at[s, o], load_sem.at[s, o]
        )

    def load_one(i, carry):
        load(i // at.chips, lax.rem(i, at.chips)).start()
        return carry

    each = seqs * at.chips
    lax.fori_loop(0, each, load_one, 0)
    for s in range(seqs):
        buf[s, rows_of(at.me, rows)] = grad[s]
    at.greet(groups=True, cube=True)

    def final(s, there, total):
        output[s, there] = (hidden[s, there] + total + bias[...]).astype(bf16)

    def share(s, o):
        load(s, o).wait()
        line.share(s, o)

    def work(s, o):
        ring.arrived(s, o)
        here = rows_of(o, 2 * rows)
        grad_heads[s, here] = lax.dot_general(
            buf[s, here], weight[...], NT, preferred_element_type=f32
        ).astype(bf16)

    def loaded(s, o):
        for copy in loads:
            copy.wait()

    def back(s, o):
        block = min(512, n * rows)
        attend_back(heads, grad_heads, lengths, grads, grad_key, grad_value, block, s)

    def weight_work(s, o):
        for j in range(width // 512):
            cols = pl.ds(j * 512, 512)
            total = 0.0
            for q in range(seqs):
                total += lax.dot_general(mixed[q], buf[q, :, cols], TN, preferred_element_type=f32)
            weight_grad[:, cols] = total.astype(bf16)

    def up_event(first, s, o):
        up_sum.event(first + s * at.chips + o, up_loaded)

    def down_event(first, s, o):
        down_sum.event(first + s * at.chips + o, down_loaded)

    def ops_of(c):
        chips = at.chips
        code_of = lambda kind, e: (kind + e // each, e % each // chips, e % chips)
        have = ("loaded", c)
        ops = [((0, 0, 0), (6, 0, 0), gathered_here("in", c, 0, c), 0.2, [], [(0.0, have)])]
        for s in range(seqs):
            needs = [("done", c, s, o) for o in range(chips)]
            ops.append(((4, s, 0), (4, s, 0), needs, 8.0, [], []))
        needs = [("done", c, s, o) for s in range(seqs) for o in range(chips)]
        ops.append(((5, 0, 0), (5, 0, 0), needs, 3.0, [], []))
        for rank, code, needs, time, sends, gives in scatter_ops(
            c, chips, seqs, 1, "out", "part", last=4.0, parts=line.parts
        ):
            needs = needs + [have] if code[2] == c else needs
            ops.append((rank, code, needs, time, sends, gives))
        return ops + (
            gather_ops(c, chips, seqs, 0, "in")
            + work_ops(
                c,
                chips,
                seqs,
                2,
                lambda s, o: gathered_here("in", c, s, o) + [have],
                "done",
                1.0,
            )
            + work_ops(c, chips, seqs, 3, lambda s, o: [], "part", 0.3, rank=0, far=True)
            + group_ops(
                c, at.group_bits, 3, PIECE, lambda e: code_of(8, e), 0, (1,), 0.7, -1, "up"
            )
            + group_ops(
                c, at.group_bits, 4, PIECE, lambda e: code_of(16, e), 1, (0,), 0.7, -1, "down"
            )
        )

    actions = {2: work, 3: share, **ring.actions(0), **line.actions(1, final)}
    actions[4], actions[5], actions[6] = back, weight_work, loaded
    for i in range(-(-up_sum.events() // each)):
        actions[8 + i] = functools.partial(up_event, i * each)
    for i in range(-(-down_sum.events() // each)):
        actions[16 + i] = functools.partial(down_event, i * each)

    def beside(k):
        pl.when(lax.rem(k, 8) == 0)(lambda: small.event(k // 8))
        small_bias.event(k)

    Plan(at, seqs, ops_of).run(actions, beside)
    sums_all[...] = small.rows[small.phases]
    up_bias_grad[...] = small_bias.rows[small_bias.phases]
    ring.finish()
    line.finish()
    small.finish()
    small_bias.finish()
    up_sum.finish()
    down_sum.finish()


def attn_grad(
    n,
    grad,
    mlp_part,
    hidden,
    bias,
    weight,
    mixed,
    sums,
    up_bias_part,
    up_part,
    down_part,
    down_box,
    lengths,
    heads,
):
    seqs, rows, width = grad.shape
    slots = n * rows
    part = weight.shape[0]
    units = up_part.shape[2]
    dp = lax.axis_size("dp")
    vmem = pl.BlockSpec(memory_space=VMEM)
    hbm = pl.BlockSpec(memory_space=pl.ANY)
    return pl.pallas_call(
        functools.partial(attn_grad_kernel, n),
        out_shape=(
            jax.ShapeDtypeStruct((seqs, rows, width), bf16),
            jax.ShapeDtypeStruct(heads.shape, bf16),
            jax.ShapeDtypeStruct((part, width), bf16),
            jax.ShapeDtypeStruct(sums.shape, f32),
            jax.ShapeDtypeStruct((1, units), f32),
            jax.ShapeDtypeStruct((3,) + up_part.shape[1:], bf16),
            jax.ShapeDtypeStruct(down_part.shape, bf16),
        ),
        in_specs=[vmem, hbm, hbm, vmem, hbm, hbm, vmem, vmem]
        + [hbm] * 3
        + [pl.BlockSpec(memory_space=pltpu.SMEM), hbm],
        out_specs=(vmem,) * 5 + (hbm, hbm),
        scratch_shapes=[VMEM((seqs, slots, width), bf16)]
        + Gather.scratch(n, seqs)
        + Scatter.scratch(n, seqs, rows, width, 2)
        + [DMA((seqs, n // 2)), DMA((2, 4)), DMA((4,))]
        + GroupSum.scratch(dp, 3, width // 4, units)
        + GroupSum.scratch(dp, 4, units // 4, width, 1)
        + SmallSum.scratch(dp, n, sums.shape[0], width, True)
        + SmallSum.scratch(dp, n, 1, units, False)
        + [VMEM((seqs, slots, part), bf16), VMEM((slots, HD), f32), VMEM((slots, HD), f32)]
        + [VMEM(hidden.shape, f32)]
        + [VMEM(a.shape, bf16) for a in (weight, mixed, heads)]
        + [DMA((4,))],
        compiler_params=pltpu.CompilerParams(
            collective_id=4, has_side_effects=True, vmem_limit_bytes=62 * 2**20
        ),
        name="attn_grad",
    )(
        grad,
        mlp_part,
        hidden,
        bias,
        weight,
        mixed,
        sums,
        up_bias_part,
        up_part,
        down_part,
        down_box,
        lengths,
        heads,
    )


def finish_kernel(*refs):
    up_last, sums_two, sums_one = refs[8:11]
    targets = refs[11:]
    step = pl.program_id(0)
    last = step == pl.num_programs(0) - 1
    for i, (source, target) in enumerate(zip(refs[:8], targets)):
        if i > 0:
            target[...] = source[...].astype(target.dtype)

    @pl.when(last)
    def _():
        targets[0][...] = up_last[...].astype(f32)

    @pl.when(jnp.logical_not(last))
    def _():
        targets[0][...] = refs[0][...].astype(f32)

    rows = [sums_one[i : i + 1] for i in range(2)] + [sums_two[i : i + 1] for i in range(4)]
    for row, target in zip(rows, targets[8:]):
        target[...] = row


def finish(blocks, wholes, up_last, sums_two, sums_one, steps=4):
    width = sums_one.shape[1]
    ins, outs, shapes = [], [], []
    for i, (a, kind, count) in enumerate(blocks):
        block = (count // steps, a.shape[1])
        held = a.shape[0] // block[0] - 1
        ins.append(pl.BlockSpec(block, lambda i, held=held: (jnp.minimum(i, held), 0)))
        outs.append(pl.BlockSpec(block, lambda i: (i, 0)))
        shapes.append(jax.ShapeDtypeStruct((count, a.shape[1]), kind))
    whole_specs = [pl.BlockSpec(a.shape, lambda i: (0, 0)) for a in wholes]
    shapes += [jax.ShapeDtypeStruct(a.shape, f32) for a in wholes]
    lasts = (up_last, sums_two, sums_one)
    return pl.pallas_call(
        finish_kernel,
        grid=(steps,),
        out_shape=shapes + [jax.ShapeDtypeStruct((1, width), f32)] * 6,
        in_specs=ins + whole_specs + [pl.BlockSpec(a.shape, lambda i: (0, 0)) for a in lasts],
        out_specs=outs + whole_specs + [pl.BlockSpec((1, width), lambda i: (0, 0))] * 6,
        compiler_params=pltpu.CompilerParams(vmem_limit_bytes=62 * 2**20),
        name="finish",
    )(*[block[0] for block in blocks], *wholes, *lasts)


def body(
    tokens,
    cotangent,
    lengths,
    ln1_gain,
    ln1_shift,
    qkv_weight,
    qkv_bias,
    out_weight,
    out_bias,
    ln2_gain,
    ln2_shift,
    up_weight,
    up_bias,
    down_weight,
    down_bias,
):
    n = lax.axis_size("tensor")
    gathered_one, heads, mixed_heads, hidden_state, normed_two, grad_mlp = attention_block(
        n,
        tokens,
        cotangent,
        lengths,
        ln1_gain[None],
        ln1_shift[None],
        qkv_weight,
        qkv_bias,
        out_weight,
        out_bias[None],
        ln2_gain[None],
        ln2_shift[None],
    )
    (
        mlp_part,
        hidden_grad,
        grad_attn,
        sums,
        up_part,
        up_bias_part,
        down_part,
        down_box,
    ) = mlp_block(
        n, normed_two, grad_mlp, up_weight, up_bias[None], down_weight, hidden_state, ln2_gain[None]
    )
    output, grads, out_part, sums, up_bias_grad, up_weight_grad, down_weight_grad = attn_grad(
        n,
        grad_attn,
        mlp_part,
        hidden_state,
        down_bias[None],
        out_weight,
        mixed_heads,
        sums,
        up_bias_part,
        up_part,
        down_part,
        down_box,
        lengths,
        heads,
    )
    input_grad, sums_one, qkv_weight_grad, out_weight_grad, qkv_bias_grad, up_last = heads_scatter(
        n, grads, qkv_weight, gathered_one, out_part, tokens, ln1_gain[None], hidden_grad, up_part
    )
    width, part, units = tokens.shape[2], qkv_weight.shape[2], up_weight.shape[1]
    seq_rows = tokens.shape[0] * tokens.shape[1]
    (
        up_weight_grad,
        down_weight_grad,
        qkv_weight_grad,
        out_weight_grad,
        output,
        input_grad,
        qkv_bias_grad,
        up_bias_grad,
        *rows,
    ) = finish(
        (
            (up_weight_grad.reshape(-1, units), f32, width),
            (down_weight_grad.reshape(-1, width), f32, units),
            (qkv_weight_grad.reshape(-1, part), f32, 3 * width),
            (out_weight_grad.reshape(-1, width), f32, part),
            (output.reshape(-1, width), bf16, seq_rows),
            (input_grad.reshape(-1, width), f32, seq_rows),
        ),
        (qkv_bias_grad, up_bias_grad),
        up_last[0],
        sums,
        sums_one,
    )
    ln1_gain_grad, ln1_shift_grad, ln2_gain_grad, ln2_shift_grad, out_bias_grad, down_bias_grad = [
        row[0] for row in rows
    ]
    return (
        output.reshape(tokens.shape),
        input_grad.reshape(tokens.shape),
        ln1_gain_grad,
        ln1_shift_grad,
        qkv_weight_grad.reshape(qkv_weight.shape),
        qkv_bias_grad,
        out_weight_grad,
        out_bias_grad,
        ln2_gain_grad,
        ln2_shift_grad,
        up_weight_grad,
        up_bias_grad[0],
        down_weight_grad,
        down_bias_grad,
    )


def solution(mesh):
    in_specs = (
        P("dp", "tensor", None),
        P("dp", "tensor", None),
        P("dp"),
        P(),
        P(),
        P(None, None, "tensor"),
        P(None, "tensor"),
        P("tensor", None),
        P(),
        P(),
        P(),
        P(None, "tensor"),
        P("tensor"),
        P("tensor", None),
        P(),
    )
    out_specs = (
        P("dp", "tensor", None),
        P("dp", "tensor", None),
        P(),
        P(),
        P(None, None, "tensor"),
        P(None, "tensor"),
        P("tensor", None),
        P(),
        P(),
        P(),
        P(None, "tensor"),
        P("tensor"),
        P("tensor", None),
        P(),
    )
    return jax.shard_map(body, mesh=mesh, in_specs=in_specs, out_specs=out_specs, check_vma=False)
```

```python
import functools
import heapq
import itertools

import jax
import jax.numpy as jnp
from jax import lax
from jax.experimental import pallas as pl
from jax.experimental.pallas import tpu as pltpu
from jax.sharding import PartitionSpec as P

HD = 128


norm_epsilon = 1e-05

MESH = pl.DeviceIdType.MESH
UP, DOWN, SIDE = 0, 1, 2
VMEM = pltpu.VMEM
DMA = pltpu.SemaphoreType.DMA
f32 = jnp.float32
bf16 = jnp.bfloat16
NT = (((1,), (1,)), ((), ()))
TN = (((0,), (0,)), ((), ()))


def order_of(chips, ops_of, backlog=8.0, hop=2.0):
    todo = [sorted(ops_of(c)) for c in range(chips)]
    order = [[] for _ in range(chips)]
    free, busy, have, queue = {}, [False] * chips, set(), []

    def push(time, what):
        heapq.heappush(queue, (time, len(pushed), what))
        pushed.append(0)

    pushed = []
    for c in range(chips):
        push(0.0, (c, None, ()))
    now = 0.0
    while queue:
        now, _, (c, signal, after) = heapq.heappop(queue)
        if signal is not None:
            have.add(signal)
        for part in after:
            if part[0] == "free":
                busy[c] = False
            elif part[0] == "send":
                _, link, to, sig, span = part
                start = max(now, free.get((c, link), 0.0))
                free[c, link] = start + span
                push(start + span + hop, (to, sig, ()))
            else:
                push(now + part[1], (c, part[2], ()))
        if busy[c]:
            continue
        for op in todo[c]:
            rank, code, needs, time, sends, gives = op
            if any(need not in have for need in needs):
                continue
            late = max([free.get((c, send[0]), 0.0) - now for send in sends], default=0.0)
            if late > backlog:
                push(now + late - backlog, (c, None, ()))
                continue
            todo[c].remove(op)
            order[c].append(code)
            busy[c] = True
            ends = [("free",)] + [("send",) + send for send in sends]
            push(now + time, (c, None, ends + [("give",) + give for give in gives]))
            break
    assert not any(todo)
    return order, now


PIECE = 12.0


PART = 12


def gather_ops(c, chips, seqs, kind, name, rank=0, time=0.5, gate=False, own=None, parts=1):
    ops = []
    for s, o, j in itertools.product(range(seqs), range(chips), range(parts)):
        up, down = [], []
        if o <= c < chips - 1:
            up.append((c + 1, c + 1, (name, c + 1, s, o, j), PIECE / parts))
        if o >= c > 0:
            down.append((c - 1, c - 1, (name, c - 1, s, o, j), PIECE / parts))
        both = [(3.0, (name, c, s, o, "both", j))]
        add = j * PART
        if own is not None and o == c and s > 0:
            ops.append(((rank, s, -1, j), (own[0] + add, s, o), [], time, [], both))
            for sends, which, others in ((up, own[1], range(c)), (down, own[2], range(c + 1, chips))):
                needs = [(name, c, t, q, parts - 1) for t in (s - 1, s) for q in others]
                if sends:
                    code = (which + add, s, o)
                    ops.append(((rank, s, chips, j), code, needs, time, sends, []))
            continue
        needs = [] if o == c else [(name, c, s, o, j)]
        if gate and o == c and s > 0:
            for q in range(chips):
                if q < c < chips - 1 or q > c > 0:
                    needs.append((name, c, s - 1, q, parts - 1))
        ops.append(((rank, s, abs(o - c), j), (kind + add, s, o), needs, time, up + down, both))
    return ops


def gathered_here(name, c, s, o, parts=1):
    return [(name, c, s, o, "both", j) for j in range(parts)]


def scatter_ops(c, chips, seqs, kind, name, part, rank=1, time=1.3, last=2.0, parts=1):
    ops = []
    for s, o, j in itertools.product(range(seqs), range(chips), range(parts)):
        needs = [(part, c, s, o)]
        if o >= c > 0:
            needs.append((name, c, s, o, "below", j))
        if o <= c < chips - 1:
            needs.append((name, c, s, o, "above", j))
        sends = []
        if o > c:
            sends = [(c + 1, c + 1, (name, c + 1, s, o, "below", j), PIECE / parts)]
        if o < c:
            sends = [(c - 1, c - 1, (name, c - 1, s, o, "above", j), PIECE / parts)]
        order = (rank, s, -abs(o - c), j) if o != c else (8, s, j)
        ends = [(0.0, (name, c, s, "sum", j))] if o == c else []
        span = (last if o == c else time) / parts + 0.2 * (parts - 1)
        ops.append((order, (kind + j * PART, s, o), needs, span, sends, ends))
    return ops


def work_ops(c, chips, seqs, kind, needs_of, gives, time, rank=2, far=False):
    return [
        (
            (rank, s, -abs(o - c) if far else abs(o - c)),
            (kind, s, o),
            needs_of(s, o),
            time,
            [],
            [(3.0, (gives, c, s, o))],
        )
        for s in range(seqs)
        for o in range(chips)
    ]


def group_ops(c, bits, count, span, code_of, skip, turns, first_time, rank=3, name="group"):
    ops = []
    for t in range(count):
        for stage in range(skip, 2 * bits + 1):
            needs, sends = [], []
            for turn in turns:
                if stage > skip:
                    needs.append((name, c, turn, t, stage))
                if stage < 2 * bits:
                    i = stage if stage < bits else 2 * bits - 1 - stage
                    axis = "axis%d" % ((t + turn + i) % bits)
                    sends.append((axis, c, (name, c, turn, t, stage + 1), span / 2**i))
            time = first_time if stage == 0 else 0.8 * len(turns)
            code = code_of((stage - skip) * count + t)
            ops.append(((rank, stage, t), code, needs, time, sends, []))
    return ops


class Plan:
    def __init__(self, at, seqs, ops_of):
        chips = at.chips
        order, self.length = order_of(chips, ops_of)
        self.per, self.each, self.chips, self.seqs = 1024, 3, chips, seqs
        self.count = max(len(codes) for codes in order)
        idle = self.per // (seqs * chips) - 1
        rows = []
        for codes in order:
            assert all(kind < idle for kind, s, o in codes)
            flat = [(kind * seqs + s) * chips + o for kind, s, o in codes]
            flat += [idle * seqs * chips] * (self.count - len(flat) + self.each)
            rows.append(
                [
                    sum(flat[i + j] * self.per**j for j in range(self.each))
                    for i in range(0, self.count, self.each)
                ]
            )
        self.words = []
        for w in range(len(rows[0])):
            word = jnp.int32(rows[0][w])
            for c in range(1, chips):
                word = jnp.where(at.chip == c, jnp.int32(rows[c][w]), word)
            self.words.append(word)

    def step(self, k):
        which, slot = k // self.each, lax.rem(k, self.each)
        word = jnp.int32(0)
        for w, value in enumerate(self.words):
            word = jnp.where(which == w, value, word)
        code = word
        for j in range(1, self.each):
            code = jnp.where(slot == j, word // self.per**j, code)
        code = lax.rem(code, self.per)
        each = self.seqs * self.chips
        return code // each, lax.rem(code, each) // self.chips, lax.rem(code, self.chips)

    def run(self, actions, beside=None):
        def step(k, carry):
            kind, s, o = self.step(k)
            for which, action in actions.items():
                pl.when(kind == which)(functools.partial(action, s, o))
            if beside is not None:
                beside(k)
            return carry

        lax.fori_loop(0, self.count, step, 0)


class Place:
    def __init__(self, n):
        self.n, self.chips = n, n // 2
        self.me = lax.axis_index("tensor")
        self.chip, self.core = self.me // 2, lax.rem(self.me, 2)
        self.side = self.me + 1 - 2 * self.core
        self.below = self.chip > 0
        self.above = self.chip < self.chips - 1
        self.group = lax.axis_index("dp")
        self.group_bits = lax.axis_size("dp").bit_length() - 1
        self.bits = n.bit_length() - 1

    def group_peer(self, q):
        mine = lax.rem(self.group // 2**q, 2)
        return self.group + (1 - 2 * mine) * 2**q, mine

    def peer(self, q):
        mine = lax.rem(self.me // 2**q, 2)
        return self.me + (1 - 2 * mine) * 2**q

    def greet(self, groups=False, cube=False, everyone=False):
        barrier = pltpu.get_barrier_semaphore()

        def tell(target):
            pl.semaphore_signal(
                barrier, inc=1, device_id={"tensor": target}, device_id_type=MESH
            )

        tell(self.side)
        pl.when(self.below)(lambda: tell(self.me - 2))
        pl.when(self.above)(lambda: tell(self.me + 2))
        peers = 1 + self.below.astype(jnp.int32) + self.above.astype(jnp.int32)
        if groups:
            for q in range(self.group_bits):
                pl.semaphore_signal(
                    barrier, inc=1, device_id={"dp": self.group_peer(q)[0]}, device_id_type=MESH
                )
            peers = peers + self.group_bits
        if everyone:
            for other in range(1, self.n):
                tell(lax.rem(self.me + other, self.n))
            for other in range(1, 2**self.group_bits):
                peer = lax.rem(self.group + other, 2**self.group_bits)
                pl.semaphore_signal(barrier, inc=1, device_id={"dp": peer}, device_id_type=MESH)
            peers = peers + (self.n - 1 + 2**self.group_bits - 1)
        if cube:
            for q in range(self.bits):
                tell(self.peer(q))
            peers = peers + self.bits
        pl.semaphore_wait(barrier, peers)


def rows_of(index, rows):
    return pl.ds(pl.multiple_of(index * rows, rows), rows)


class Gather:
    def __init__(self, at, rows, buf, send, recv):
        self.at, self.rows, self.buf, self.send, self.recv = at, rows, buf, send, recv
        self.seqs, self.parts = buf.shape[0], recv.shape[2]

    @staticmethod
    def scratch(n, seqs, parts=1):
        return [DMA((3, seqs, n // 2, parts)), DMA((seqs, n, parts))]

    def copy(self, s, o, kind, j, owner=None):
        at = self.at
        target = (at.me + 2, at.me - 2, at.side)[kind]
        owner = 2 * o + at.core if owner is None else owner
        piece = self.buf.at[s, rows_of(owner * self.parts + j, self.rows // self.parts)]
        return pltpu.make_async_remote_copy(
            src_ref=piece,
            dst_ref=piece,
            send_sem=self.send.at[kind, s, o, j],
            recv_sem=self.recv.at[s, owner, j],
            device_id={"tensor": target},
            device_id_type=MESH,
        )

    def arrived(self, s, o):
        for j in range(self.parts):
            self.copy(s, o, SIDE, j, 2 * o + 1 - self.at.core).wait_recv()

    def relay(self, j, s, o):
        at = self.at
        pl.when(o != at.chip)(lambda: self.copy(s, o, SIDE, j).wait_recv())
        pl.when((o <= at.chip) & at.above)(lambda: self.copy(s, o, UP, j).start())
        pl.when((o >= at.chip) & at.below)(lambda: self.copy(s, o, DOWN, j).start())
        self.copy(s, o, SIDE, j).start()

    def own(self, kind, j, s, o):
        self.copy(s, o, kind, j).start()

    def actions(self, kind, own=()):
        found = {}
        for j in range(self.parts):
            found[kind + j * PART] = functools.partial(self.relay, j)
            for which, way in zip(own, (SIDE, UP, DOWN)):
                found[which + j * PART] = functools.partial(self.own, way, j)
        return found

    def finish(self):
        at = self.at

        def one(i, carry):
            s, o = i // at.chips, lax.rem(i, at.chips)
            for j in range(self.parts):
                pl.when((o <= at.chip) & at.above)(lambda: self.copy(s, o, UP, j).wait_send())
                pl.when((o >= at.chip) & at.below)(lambda: self.copy(s, o, DOWN, j).wait_send())
                self.copy(s, o, SIDE, j).wait_send()
            return carry

        lax.fori_loop(0, self.seqs * at.chips, one, 0)


class Scatter:
    def __init__(self, at, rows, part, side, link, side_send, side_recv, send, recv):
        self.at, self.rows = at, rows
        self.part, self.side, self.link = part, side, link
        self.side_send, self.side_recv, self.send, self.recv = side_send, side_recv, send, recv
        self.seqs, self.parts = part.shape[0], recv.shape[2]
        self.size = rows // self.parts

    @staticmethod
    def scratch(n, seqs, rows, width, parts=1):
        chips = n // 2
        return [
            VMEM((seqs, chips, 2 * rows, width), bf16),
            VMEM((seqs, chips, rows, width), bf16),
            VMEM((seqs, chips + 1, rows, width), bf16),
            DMA((seqs, chips, parts)),
            DMA((seqs, chips, parts)),
            DMA((seqs, chips, parts)),
            DMA((seqs, chips + 1, parts)),
        ]

    def side_copy(self, s, o, j):
        at = self.at
        return pltpu.make_async_remote_copy(
            src_ref=self.part.at[s, o, rows_of((1 - at.core) * self.parts + j, self.size)],
            dst_ref=self.side.at[s, o, pl.ds(j * self.size, self.size)],
            send_sem=self.side_send.at[s, o, j],
            recv_sem=self.side_recv.at[s, o, j],
            device_id={"tensor": at.side},
            device_id_type=MESH,
        )

    def link_copy(self, s, o, slot, target, j):
        return pltpu.make_async_remote_copy(
            src_ref=self.part.at[s, o, rows_of(self.at.core * self.parts + j, self.size)],
            dst_ref=self.link.at[s, slot, pl.ds(j * self.size, self.size)],
            send_sem=self.send.at[s, o, j],
            recv_sem=self.recv.at[s, slot, j],
            device_id={"tensor": target},
            device_id_type=MESH,
        )

    def share(self, s, o):
        for j in range(self.parts):
            self.side_copy(s, o, j).start()

    def blocks(self, j, body):
        step = 16

        def one(i, carry):
            body(pl.multiple_of(j * self.size + i * step, step), step)
            return carry

        lax.fori_loop(0, self.size // step, one, 0)

    def total(self, s, o, first, step, slots):
        here = pl.ds(pl.multiple_of(self.at.core * self.rows + first, step), step)
        there = pl.ds(first, step)
        total = self.part[s, o, here].astype(f32) + self.side[s, o, there].astype(f32)
        for slot in slots:
            total += self.link[s, slot, there].astype(f32)
        return here, total

    def add_up(self, s, o, slots, j):
        def body(first, step):
            here, total = self.total(s, o, first, step, slots)
            self.part[s, o, here] = total.astype(bf16)

        self.blocks(j, body)

    def pass_on(self, final, j, s, o):
        at = self.at
        self.side_copy(s, o, j).wait_recv()

        def onward(before, slot, target):
            @pl.when(before)
            def _():
                self.link_copy(s, o, o, at.me, j).wait_recv()
                self.add_up(s, o, [o], j)

            pl.when(jnp.logical_not(before))(lambda: self.add_up(s, o, [], j))
            self.link_copy(s, o, slot, target, j).start()

        pl.when(o > at.chip)(lambda: onward(at.below, o, at.me + 2))
        last = jnp.where(o == at.chip - 1, at.chips, o)
        pl.when(o < at.chip)(lambda: onward(at.above, last, at.me - 2))

        @pl.when(o == at.chip)
        def _():
            for slot, used in ((o, at.below), (at.chips, at.above)):
                pl.when(used)(lambda: self.link_copy(s, o, slot, at.me, j).wait_recv())

                @pl.when(jnp.logical_not(used))
                def _():
                    def clear(first, step):
                        self.link[s, slot, pl.ds(first, step)] = jnp.zeros(
                            (step, self.link.shape[-1]), bf16
                        )

                    self.blocks(j, clear)

            def body(first, step):
                total = self.total(s, o, first, step, [o, at.chips])[1]
                final(s, pl.ds(first, step), total)

            self.blocks(j, body)

    def actions(self, kind, final):
        return {
            kind + j * PART: functools.partial(self.pass_on, final, j) for j in range(self.parts)
        }

    def finish(self):
        at = self.at

        def one(i, carry):
            s, o = i // at.chips, lax.rem(i, at.chips)
            for j in range(self.parts):
                self.side_copy(s, o, j).wait_send()
                pl.when(o != at.chip)(lambda: self.link_copy(s, o, o, at.side, j).wait_send())
            return carry

        lax.fori_loop(0, self.seqs * at.chips, one, 0)


class GroupSum:
    def __init__(self, at, rows, tiles, inbox, send, recv, keep_sem, out, turn=0, skip=0):
        self.at, self.tiles, self.inbox, self.send, self.recv = at, tiles, inbox, send, recv
        self.keep_sem, self.out, self.skip, self.turn, self.rows = keep_sem, out, skip, turn, rows
        self.bits = at.group_bits
        self.count = send.shape[0]

    @staticmethod
    def scratch(dp, count, rows, width, skip=0):
        phases = 2 * (dp.bit_length() - 1)
        return [
            VMEM((count, rows >> skip, width), bf16),
            VMEM((count, rows - rows // dp, width), bf16),
            DMA((count, phases)),
            DMA((count, phases)),
            DMA((count,)),
        ]

    def peer(self, t, i):
        which = lax.rem(t + i + self.turn, self.bits)
        peer, mine = 0, 0
        for q in range(self.bits):
            other, bit = self.at.group_peer(q)
            peer = peer + jnp.where(which == q, other, 0)
            mine = mine + jnp.where(which == q, bit, 0)
        return peer, mine

    def base(self, t, i):
        first = 0
        for p in range(i):
            first = first + self.peer(t, p)[1] * (self.rows >> (p + 1))
        return first

    def span(self, first, size):
        return pl.ds(pl.multiple_of(first, 16), size)

    def tile(self, t, first, size):
        return self.tiles.at[t, self.span(first - self.base(t, self.skip), size)]

    def box(self, t, i):
        return self.inbox.at[t, pl.ds(self.rows - (self.rows >> i), self.rows >> (i + 1))]

    def remote(self, source, target, t, phase, peer):
        return pltpu.make_async_remote_copy(
            src_ref=source,
            dst_ref=target,
            send_sem=self.send.at[t, phase],
            recv_sem=self.recv.at[t, phase],
            device_id={"dp": peer},
            device_id_type=MESH,
        )

    def halve(self, t, i):
        peer, mine = self.peer(t, i)
        half = self.rows >> (i + 1)
        source = self.tile(t, self.base(t, i) + (1 - mine) * half, half)
        return self.remote(source, self.box(t, i), t, i, peer)

    def add(self, t, i):
        half = self.rows >> (i + 1)
        keep = self.base(t, i + 1) - self.base(t, self.skip)
        box = self.rows - (self.rows >> i)

        def body(j, carry):
            here = self.span(keep + j * 16, 16)
            there = self.span(box + j * 16, 16)
            total = self.tiles[t, here].astype(f32) + self.inbox[t, there].astype(f32)
            self.tiles[t, here] = total.astype(bf16)
            return carry

        lax.fori_loop(0, half // 16, body, 0)

    def keep(self, t):
        first, size = self.base(t, self.bits), self.rows >> self.bits
        return pltpu.make_async_copy(
            self.tile(t, first, size), self.out.at[t, self.span(first, size)], self.keep_sem.at[t]
        )

    def double(self, t, i, back=False):
        peer, mine = self.peer(t, i)
        half = self.rows >> (i + 1)
        first = self.base(t, i) + ((1 - mine) if back else mine) * half
        piece = self.out.at[t, self.span(first, half)]
        source = piece
        if i == self.bits - 1 and not back:
            source = self.tile(t, first, half)
        return self.remote(source, piece, t, 2 * self.bits - 1 - i, peer)

    def events(self):
        return self.count * (2 * self.bits + 1 - self.skip)

    def event(self, e, loaded=None):
        k, t = e // self.count + self.skip, lax.rem(e, self.count)
        bits = self.bits

        def at_stage(stage):
            if stage == self.skip and loaded is not None:
                loaded(t)
            if stage == 0:
                self.halve(t, 0).start()
            elif stage <= bits:
                if stage > self.skip:
                    self.halve(t, stage - 1).wait_recv()
                self.add(t, stage - 1)
                if stage < bits:
                    self.halve(t, stage).start()
                else:
                    self.keep(t).start()
                    self.double(t, bits - 1).start()
            else:
                i = 2 * bits - stage
                self.double(t, i, back=True).wait_recv()
                if i == bits - 1:
                    self.keep(t).wait()
                if i > 0:
                    self.double(t, i - 1).start()

        for stage in range(self.skip, 2 * bits + 1):
            pl.when((k == stage) & (e >= 0))(functools.partial(at_stage, stage))

    def finish(self):
        def one(t, carry):
            for i in range(self.bits):
                if i >= self.skip:
                    self.halve(t, i).wait_send()
                self.double(t, i).wait_send()
            return carry

        lax.fori_loop(0, self.count, one, 0)


class SmallSum:
    def __init__(self, at, rows, inbox, send, recv, everywhere):
        self.at, self.rows, self.inbox, self.send, self.recv = at, rows, inbox, send, recv
        self.phases = at.group_bits + (at.bits if everywhere else 0)

    @staticmethod
    def scratch(dp, n, count, width, everywhere):
        phases = (dp.bit_length() - 1) + (n.bit_length() - 1 if everywhere else 0)
        return [
            VMEM((phases + 1, count, width), f32),
            VMEM((phases, count, width), f32),
            DMA((phases,)),
            DMA((phases,)),
        ]

    def copy(self, i):
        at = self.at
        if i < at.group_bits:
            target = {"dp": at.group_peer(i)[0]}
        else:
            target = {"tensor": at.peer(i - at.group_bits)}
        return pltpu.make_async_remote_copy(
            src_ref=self.rows.at[i],
            dst_ref=self.inbox.at[i],
            send_sem=self.send.at[i],
            recv_sem=self.recv.at[i],
            device_id=target,
            device_id_type=MESH,
        )

    def event(self, e):
        def run(i):
            if i > 0:
                self.copy(i - 1).wait_recv()
                self.rows[i] = self.rows[i - 1] + self.inbox[i - 1]
            if i < self.phases:
                self.copy(i).start()

        for i in range(self.phases + 1):
            if isinstance(e, int):
                if e == i:
                    run(i)
            else:
                pl.when(e == i)(functools.partial(run, i))

    def finish(self):
        for i in range(self.phases):
            self.copy(i).wait_send()


class DirectSum:
    def __init__(self, at, rows, group_box, line_box, send, recv):
        self.at, self.rows, self.send, self.recv = at, rows, send, recv
        self.boxes = (group_box, line_box)

    @staticmethod
    def scratch(dp, n, count, width):
        most = max(dp, n)
        return [
            VMEM((count, width), f32),
            VMEM((dp, count, width), f32),
            VMEM((n, count, width), f32),
            DMA((2, most)),
            DMA((2, most)),
        ]

    def copy(self, step, other, back=False):
        at, box = self.at, self.boxes[step]
        size, axis = box.shape[0], ("dp", "tensor")[step]
        mine = (at.group, at.me)[step]
        peer = lax.rem(mine + other, size)
        slot = peer if back else mine
        return pltpu.make_async_remote_copy(
            src_ref=box.at[mine],
            dst_ref=box.at[slot],
            send_sem=self.send.at[step, other],
            recv_sem=self.recv.at[step, slot],
            device_id={axis: peer},
            device_id_type=MESH,
        )

    def event(self, e):
        if e > 0:
            box = self.boxes[e - 1]
            for other in range(1, box.shape[0]):
                self.copy(e - 1, other, back=True).wait_recv()
            total = box[0]
            for i in range(1, box.shape[0]):
                total = total + box[i]
            self.rows[...] = total
        if e < 2:
            box = self.boxes[e]
            box[(self.at.group, self.at.me)[e]] = self.rows[...]
            for other in range(1, box.shape[0]):
                self.copy(e, other).start()

    def finish(self):
        for step, box in enumerate(self.boxes):
            for other in range(1, box.shape[0]):
                self.copy(step, other).wait_send()


def norm_rows(values, gain, shift):
    centre = values - jnp.mean(values, axis=-1, keepdims=True)
    spread = jnp.mean(centre * centre, axis=-1, keepdims=True)
    return centre * lax.rsqrt(spread + norm_epsilon) * gain + shift


def norm_rows_back(values, grad, gain):
    centre = values - jnp.mean(values, axis=-1, keepdims=True)
    scale = lax.rsqrt(jnp.mean(centre * centre, axis=-1, keepdims=True) + norm_epsilon)
    unit = centre * scale
    w = grad * gain
    back = w - jnp.mean(w, axis=-1, keepdims=True)
    back = scale * (back - unit * jnp.mean(w * unit, axis=-1, keepdims=True))
    return back, grad * unit


def add_row(ref, row, values):
    ref[row : row + 1] += jnp.sum(values, axis=0, keepdims=True)


def head_probs(query, keys, first, length):
    rows, cols = query.shape[0], keys.shape[0]
    scores = lax.dot_general(query, keys, NT, preferred_element_type=f32)
    row_ids = first + lax.broadcasted_iota(jnp.int32, (rows, cols), 0)
    col_ids = lax.broadcasted_iota(jnp.int32, (rows, cols), 1)
    scores = jnp.where((col_ids <= row_ids) & (col_ids < length), scores, -1e30)
    probs = jnp.exp(scores - jnp.max(scores, axis=-1, keepdims=True))
    return probs * (1.0 / jnp.sum(probs, axis=-1, keepdims=True))


def attend(heads, lengths, mixed, block, s):
    slots, part = mixed.shape[1:]

    def one(h, carry):
        cols = pl.ds(pl.multiple_of(h * HD, HD), HD)
        for first in range(0, slots, block):
            rows, seen = pl.ds(first, block), pl.ds(0, first + block)
            probs = head_probs(heads[0, s, rows, cols], heads[1, s, seen, cols], first, lengths[s])
            mixed[s, rows, cols] = jnp.dot(
                probs.astype(bf16), heads[2, s, seen, cols], preferred_element_type=f32
            ).astype(bf16)
        return carry

    lax.fori_loop(0, part // HD, one, 0)


def attend_back(heads, grad_heads, lengths, grads, grad_key, grad_value, block, s):
    slots, part = grad_heads.shape[1:]

    def one(h, carry):
        cols = pl.ds(pl.multiple_of(h * HD, HD), HD)
        grad_key[...] = jnp.zeros_like(grad_key)
        grad_value[...] = jnp.zeros_like(grad_value)
        for first in range(0, slots, block):
            rows, seen = pl.ds(first, block), pl.ds(0, first + block)
            query, grad = heads[0, s, rows, cols], grad_heads[s, rows, cols]
            keys = heads[1, s, seen, cols]
            probs = head_probs(query, keys, first, lengths[s])
            grad_value[seen] += lax.dot_general(
                probs.astype(bf16), grad, TN, preferred_element_type=f32
            )
            back = lax.dot_general(
                grad, heads[2, s, seen, cols], NT, preferred_element_type=f32
            )
            centre = jnp.sum(probs * back, axis=-1, keepdims=True)
            scores = (probs * (back - centre)).astype(bf16)
            grads[0, s, rows, cols] = jnp.dot(
                scores, keys, preferred_element_type=f32
            ).astype(bf16)
            grad_key[seen] += lax.dot_general(scores, query, TN, preferred_element_type=f32)
        grads[1, s, :, cols] = grad_key[...].astype(bf16)
        grads[2, s, :, cols] = grad_value[...].astype(bf16)
        return carry

    lax.fori_loop(0, part // HD, one, 0)


def attention_block_kernel(
    n,
    tokens,
    cotangent_hbm,
    lengths,
    gain,
    shift,
    weight_hbm,
    bias,
    out_weight_hbm,
    out_bias,
    gain_two,
    shift_two,
    gathered,
    heads_hbm,
    mixed_hbm,
    hidden,
    normed,
    grad_all,
    heads,
    mixed,
    result_sem,
    buf,
    send,
    recv,
    keep_sem,
    grad_send,
    grad_recv,
    masked,
    mask_sem,
    cotangent,
    weight,
    out_weight,
    in_sem,
    *scratch,
):
    at = Place(n)
    seqs, rows, width = tokens.shape
    ring = Gather(at, rows, buf, send, recv)
    grad_ring = Gather(at, rows, grad_all, grad_send, grad_recv)
    line = Scatter(at, rows, *scratch)

    sources = (weight_hbm, weight), (cotangent_hbm, cotangent), (out_weight_hbm, out_weight)
    loads = [
        pltpu.make_async_copy(source, target, in_sem.at[i])
        for i, (source, target) in enumerate(sources)
    ]
    for copy in loads:
        copy.start()

    def mask_copy(s):
        return pltpu.make_async_copy(
            masked.at[s], grad_all.at[s, rows_of(at.me, rows)], mask_sem.at[s]
        )

    def norm(s, o):
        def block(i, carry):
            first = pl.multiple_of(i * 16, 16)
            values = tokens[s, pl.ds(first, 16)].astype(f32)
            values = norm_rows(values, gain[...], shift[...])
            buf[s, pl.ds(pl.multiple_of(at.me * rows + first, 16), 16)] = values.astype(bf16)
            return carry

        lax.fori_loop(0, rows // 16, block, 0)

    def loaded(s, o):
        for copy in loads:
            copy.wait()

    def mask(s, o):
        def block(i, carry):
            first = pl.multiple_of(i * 16, 16)
            here = pl.ds(first, 16)
            slot = at.me * rows + first + lax.broadcasted_iota(jnp.int32, (16, width), 0)
            grad = jnp.where(slot < lengths[s], cotangent[s, here].astype(f32), 0.0)
            masked[s, here] = grad.astype(bf16)
            return carry

        lax.fori_loop(0, rows // 16, block, 0)
        mask_copy(s).start()
        mask_copy(s).wait()

    at.greet()

    def keep(s, o):
        here = rows_of(o, 2 * rows)
        return pltpu.make_async_copy(buf.at[s, here], gathered.at[s, here], keep_sem.at[s, o])

    def project(s, o):
        ring.arrived(s, o)
        keep(s, o).start()
        here = rows_of(o, 2 * rows)
        for j in range(3):
            total = jnp.dot(buf[s, here], weight[j], preferred_element_type=f32)
            if j == 0:
                total = (total + bias[0:1]) * HD ** (-0.5)
            if j == 2:
                total = total + bias[1:2]
            heads[j, s, here] = total.astype(bf16)

    def final(s, there, total):
        values = tokens[s, there].astype(f32) + total + out_bias[...]
        hidden[s, there] = values
        normed[s, there] = norm_rows(values, gain_two[...], shift_two[...]).astype(bf16)

    def results(s):
        pairs = [(heads.at[j, s], heads_hbm.at[j, s]) for j in range(3)]
        pairs.append((mixed.at[s], mixed_hbm.at[s]))
        return [
            pltpu.make_async_copy(source, target, result_sem.at[s, j])
            for j, (source, target) in enumerate(pairs)
        ]

    def mix(s, o):
        attend(heads, lengths, mixed, min(512, n * rows), s)
        for copy in results(s):
            copy.start()

    def project_out(s, o):
        here = rows_of(o, 2 * rows)
        for j in range(width // 512):
            cols = pl.ds(j * 512, 512)
            total = jnp.dot(mixed[s, here], out_weight[:, cols], preferred_element_type=f32)
            line.part[s, o, :, cols] = total.astype(bf16)
        line.share(s, o)

    def ops_of(c):
        chips = at.chips
        have = ("loaded", c)
        singles = [((-1, 9, 0), (8, 0, 0), [("norm", c, seqs - 1)], 0.2, [], [(0.0, have)])]
        gathers = []
        for s in range(seqs):
            needs = [("heads", c, s, o) for o in range(chips)]
            singles.append(((2, s, 0), (2, s, 0), needs, 6.0, [], [(0.0, ("mixed", c, s))]))
            singles.append(((-2 + s, 0, 0), (6, s, 0), [], 2.0, [], [(0.0, ("norm", c, s))]))
            singles.append(((3 + s, 0, 0), (7, s, 0), [have], 2.0, [], [(0.0, ("mask", c, s))]))
        for ops, first in (
            (gather_ops(c, chips, seqs, 0, "in", gate=True), "norm"),
            (gather_ops(c, chips, seqs, 5, "grad", rank=6), "mask"),
        ):
            for rank, code, needs, time, sends, gives in ops:
                needs = needs + [(first, c, code[1])] if code[2] == c else needs
                gathers.append((rank, code, needs, time, sends, gives))
        return (
            singles
            + gathers
            + work_ops(
                c, chips, seqs, 1, lambda s, o: gathered_here("in", c, s, o) + [have], "heads", 1.0
            )
            + work_ops(
                c, chips, seqs, 3, lambda s, o: [("mixed", c, s)], "part", 1.0, far=True
            )
            + scatter_ops(c, chips, seqs, 4, "out", "part", last=4.0)
        )

    Plan(at, seqs, ops_of).run(
        {
            1: project,
            2: mix,
            3: project_out,
            6: norm,
            7: mask,
            8: loaded,
            **ring.actions(0),
            **line.actions(4, final),
            **grad_ring.actions(5),
        }
    )
    ring.finish()
    line.finish()
    grad_ring.finish()

    for s in range(seqs):
        for copy in results(s):
            copy.wait()

    def close(i, carry):
        s, o = i // at.chips, lax.rem(i, at.chips)
        grad_ring.arrived(s, o)
        keep(s, o).wait()
        return carry

    lax.fori_loop(0, seqs * at.chips, close, 0)


def whole(count):
    return [pl.BlockSpec(memory_space=VMEM)] * count


def attention_block(
    n,
    tokens,
    cotangent,
    lengths,
    gain,
    shift,
    weight,
    bias,
    out_weight,
    out_bias,
    gain_two,
    shift_two,
):
    seqs, rows, width = tokens.shape
    part = weight.shape[2]
    vmem = pl.BlockSpec(memory_space=VMEM)
    hbm = pl.BlockSpec(memory_space=pl.ANY)
    smem = pl.BlockSpec(memory_space=pltpu.SMEM)
    return pl.pallas_call(
        functools.partial(attention_block_kernel, n),
        out_shape=(
            jax.ShapeDtypeStruct((seqs, n * rows, width), bf16),
            jax.ShapeDtypeStruct((3, seqs, n * rows, part), bf16),
            jax.ShapeDtypeStruct((seqs, n * rows, part), bf16),
            jax.ShapeDtypeStruct((seqs, rows, width), f32),
            jax.ShapeDtypeStruct((seqs, rows, width), bf16),
            jax.ShapeDtypeStruct((seqs, n * rows, width), bf16),
        ),
        in_specs=[vmem, hbm, smem, vmem, vmem, hbm, vmem, hbm, vmem, vmem, vmem],
        out_specs=(hbm, hbm, hbm, vmem, vmem, hbm),
        scratch_shapes=[
            VMEM((3, seqs, n * rows, part), bf16),
            VMEM((seqs, n * rows, part), bf16),
            DMA((seqs, 4)),
            VMEM((seqs, n * rows, width), bf16),
        ]
        + Gather.scratch(n, seqs)
        + [DMA((seqs, n // 2))]
        + Gather.scratch(n, seqs)
        + [VMEM((seqs, rows, width), bf16), DMA((seqs,))]
        + [VMEM(a.shape, bf16) for a in (cotangent, weight, out_weight)]
        + [DMA((3,))]
        + Scatter.scratch(n, seqs, rows, width),
        compiler_params=pltpu.CompilerParams(
            collective_id=0, has_side_effects=True, vmem_limit_bytes=60 * 2**20
        ),
        name="attention_block",
    )(
        tokens,
        cotangent,
        lengths,
        gain,
        shift,
        weight,
        bias,
        out_weight,
        out_bias,
        gain_two,
        shift_two,
    )


def heads_scatter_kernel(
    n,
    grads_hbm,
    weight_hbm,
    gathered_hbm,
    out_part,
    tokens_hbm,
    gain,
    hidden_hbm,
    up_part,
    grad,
    sums_all,
    weight_grad,
    out_grad,
    bias_grad,
    up_grad,
    *scratch,
):
    at = Place(n)
    seqs, rows, width = hidden_hbm.shape
    line = Scatter(at, rows, *scratch[:7])
    weight_sum = GroupSum(at, width, *scratch[7:12], weight_grad)
    out_sum = GroupSum(at, out_part.shape[0], *scratch[12:17], out_grad, turn=1)
    small = DirectSum(at, *scratch[17:22])
    small_bias = SmallSum(at, *scratch[22:26], False)
    gathered, tokens, hidden_grad, grads, weight, in_sem = scratch[26:32]
    early = [
        pltpu.make_async_copy(grads_hbm, grads, in_sem.at[4]),
        pltpu.make_async_copy(weight_hbm, weight, in_sem.at[5]),
        pltpu.make_async_copy(out_part, out_sum.tiles.at[0], in_sem.at[6]),
    ]
    for copy in early:
        copy.start()
    up_sum = GroupSum(at, up_part.shape[1], *scratch[32:37], up_grad, turn=1)
    up_load = pltpu.make_async_copy(up_part.at[3], up_sum.tiles.at[0], in_sem.at[3])
    up_load.start()
    sources = ((gathered_hbm, gathered), (tokens_hbm, tokens), (hidden_hbm, hidden_grad))
    loads = [
        pltpu.make_async_copy(source, target, in_sem.at[i])
        for i, (source, target) in enumerate(sources)
    ]
    for copy in loads:
        copy.start()
    small.rows[...] = jnp.zeros_like(small.rows)
    at.greet(groups=True, everyone=True)
    for copy in early:
        copy.wait()

    def bias_sums():
        for row, j, scale in ((0, 0, HD ** (-0.5)), (1, 2, 1.0)):
            total = 0.0
            for s in range(seqs):
                total += jnp.sum(grads[j, s].astype(f32), axis=0, keepdims=True)
            small_bias.rows[0, row : row + 1] = scale * total

    def beside(k):
        pl.when(k == 10)(bias_sums)
        for e in range(small_bias.phases + 1):
            pl.when(k == 11 + 6 * e)(functools.partial(small_bias.event, e))


    def final(s, there, total):
        back, terms = norm_rows_back(tokens[s, there].astype(f32), total, gain[...])
        grad[s, there] = hidden_grad[s, there] + back
        add_row(small.rows, 0, terms)
        add_row(small.rows, 1, total)

    scales = (HD ** (-0.5), 1.0, 1.0)

    def weight_tile(j):
        for first in range(0, width, 512):
            total = 0.0
            for s in range(seqs):
                total += lax.dot_general(
                    gathered[s, :, pl.ds(first, 512)],
                    grads[j, s],
                    TN,
                    preferred_element_type=f32,
                )
            weight_sum.tiles[j, pl.ds(first, 512)] = (scales[j] * total).astype(bf16)

    def work(s, o):
        here = rows_of(o, 2 * rows)
        for j in range(width // 512):
            cols = pl.ds(j * 512, 512)
            total = 0.0
            for i in range(3):
                total += scales[i] * lax.dot_general(
                    grads[i, s, here], weight[i, cols], NT, preferred_element_type=f32
                )
            line.part[s, o, :, cols] = total.astype(bf16)
        line.share(s, o)

    each = seqs * at.chips

    def weight_event(first, s, o):
        e = first + s * at.chips + o

        @pl.when(e == 0)
        def _():
            for copy in loads:
                copy.wait()

        for j in range(3):
            pl.when(e == j)(functools.partial(weight_tile, j))
        weight_sum.event(e)

    def out_event(s, o):
        out_sum.event(s * at.chips + o)

    def up_event(first, s, o):
        up_sum.event(first + s * at.chips + o, lambda t: up_load.wait())

    def code_of(kind, e):
        return (kind + e // each, e % each // at.chips, e % at.chips)

    def ops_of(c):
        chips = at.chips
        finals = scatter_ops(c, chips, seqs, 1, "out", "part", last=4.0, parts=line.parts)
        loaded = ("qkv", c, 0, 0, 1)
        for i, (rank, code, needs, time, sends, gives) in enumerate(finals):
            if code[2] == c:
                finals[i] = (rank, code, needs + [loaded], time, sends, gives)
        smalls = []
        needs = [("out", c, s, "sum", j) for s in range(seqs) for j in range(line.parts)]
        for e in range(3):
            smalls.append(((0, e), (30 + e, 0, 0), needs, 0.5, [], [(4.0, ("small", c, e))]))
            needs = [("small", c, e)]
        return smalls + (
            work_ops(c, chips, seqs, 0, lambda s, o: [], "part", 1.5, far=True)
            + finals
            + group_ops(
                c, at.group_bits, 3, PIECE, lambda e: code_of(2, e), 0, (0,), 2.7, -1, "qkv"
            )
            + group_ops(
                c, at.group_bits, 1, PIECE, lambda e: code_of(5, e), 0, (1,), 0.7, -1, "out_sum"
            )
            + group_ops(
                c, at.group_bits, 1, PIECE, lambda e: code_of(20, e), 0, (1,), 0.7, -2, "up"
            )
        )

    actions = {0: work, 5: out_event, **line.actions(1, final)}
    for i in range(-(-up_sum.events() // each)):
        actions[20 + i] = functools.partial(up_event, i * each)
    for i in range(3):
        actions[2 + i] = functools.partial(weight_event, i * each)
        actions[30 + i] = lambda s, o, e=i: small.event(e)
    Plan(at, seqs, ops_of).run(actions, beside)
    small.finish()
    sums_all[...] = small.rows[...]
    bias_grad[...] = small_bias.rows[small_bias.phases]
    line.finish()
    weight_sum.finish()
    out_sum.finish()
    up_sum.finish()
    small_bias.finish()


def heads_scatter(n, grads, weight, gathered, out_part, tokens, gain, hidden_grad, up_part):
    seqs, slots, part = grads.shape[1:]
    width = weight.shape[1]
    rows = slots // n
    dp = lax.axis_size("dp")
    vmem = pl.BlockSpec(memory_space=VMEM)
    hbm = pl.BlockSpec(memory_space=pl.ANY)
    return pl.pallas_call(
        functools.partial(heads_scatter_kernel, n),
        out_shape=(
            jax.ShapeDtypeStruct((seqs, rows, width), f32),
            jax.ShapeDtypeStruct((2, width), f32),
            jax.ShapeDtypeStruct((3, width, part), bf16),
            jax.ShapeDtypeStruct((1, part, width), bf16),
            jax.ShapeDtypeStruct((2, part), f32),
            jax.ShapeDtypeStruct((1,) + up_part.shape[1:], bf16),
        ),
        in_specs=[hbm, hbm, hbm, hbm, hbm, vmem, hbm, hbm],
        out_specs=(vmem, vmem, hbm, hbm, vmem, hbm),
        scratch_shapes=Scatter.scratch(n, seqs, rows, width, 2)
        + GroupSum.scratch(dp, 3, width, part)
        + GroupSum.scratch(dp, 1, part, width)
        + DirectSum.scratch(dp, n, 2, width)
        + SmallSum.scratch(dp, n, 2, part, False)
        + [
            VMEM(gathered.shape, bf16),
            VMEM(tokens.shape, bf16),
            VMEM(hidden_grad.shape, f32),
            VMEM(grads.shape, bf16),
            VMEM(weight.shape, bf16),
            DMA((7,)),
        ]
        + GroupSum.scratch(dp, 1, *up_part.shape[1:]),
        compiler_params=pltpu.CompilerParams(
            collective_id=2, has_side_effects=True, vmem_limit_bytes=62 * 2**20
        ),
        name="heads_scatter",
    )(grads, weight, gathered, out_part, tokens, gain, hidden_grad, up_part)


def normal_cdf(values):
    x = jnp.clip(values * 0.7071067811865476, -3.832506856900711, 3.832506856900711)
    x2 = x * x
    top = 0.00022905065861350646
    for c in (0.0034082910107109506, 0.050955695062380861, 0.18520832239976145, 1.128379143519084):
        top = top * x2 + c
    low = -1.1791602954361697e-7
    for c in (
        0.000023547966471313185,
        0.0010179625278914885,
        0.014070470171167667,
        0.11098505178285362,
        0.49746925110067538,
        1.0,
    ):
        low = low * x2 + c
    return 0.5 + 0.5 * (x * top / low)


def mlp_kernel(
    n,
    normed,
    grad_hbm,
    up_hbm,
    up_bias,
    down_hbm,
    hidden_hbm,
    gain,
    mlp_part,
    hidden_grad,
    grad_low,
    sums,
    up_grad,
    up_bias_grad,
    down_grad,
    down_box,
    buf,
    send,
    recv,
    grad_all,
    up_weight,
    down_weight,
    hidden,
    in_sem,
    *scratch,
):
    at = Place(n)
    seqs, rows, width = normed.shape
    units_wide = up_weight.shape[1]
    line = Scatter(at, rows, *scratch[:7])
    act, pre, out_stage, out_sem, up_stage, down_stage, tile_sem, half_send, half_recv = scratch[7:]
    ring = Gather(at, rows, buf, send, recv)
    loads = [
        pltpu.make_async_copy(source, target, in_sem.at[i])
        for i, (source, target) in enumerate(
            (
                (up_hbm, up_weight),
                (grad_hbm, grad_all),
                (down_hbm, down_weight),
                (hidden_hbm, hidden),
            )
        )
    ]
    for copy in loads:
        copy.start()
    at.greet(groups=True)
    for s in range(seqs):
        buf[s, rows_of(at.me, rows)] = normed[s]
    up_bias_grad[...] = jnp.zeros_like(up_bias_grad)
    sums[...] = jnp.zeros_like(sums)
    ft = min(512, units_wide)

    def out_copy(s, o):
        return pltpu.make_async_copy(
            out_stage, mlp_part.at[s, rows_of(o, 2 * rows)], out_sem.at[0]
        )

    def work(s, o):
        ring.arrived(s, o)

        @pl.when((s == 0) & (o == at.chip))
        def _():
            for copy in loads:
                copy.wait()

        here = rows_of(o, 2 * rows)
        for j in range(units_wide // ft):
            cols = pl.ds(j * ft, ft)
            value = jnp.dot(buf[s, here], up_weight[:, cols], preferred_element_type=f32)
            value = value + up_bias[:, cols]
            spread = normal_cdf(value)
            act[s, here, cols] = (value * spread).astype(bf16)
            slope = spread + value * (0.3989422804014327 * jnp.exp(-0.5 * value * value))
            grad = lax.dot_general(
                grad_all[s, here], down_weight[cols], NT, preferred_element_type=f32
            )
            grad = (grad * slope).astype(bf16)
            pre[s, here, cols] = grad
            up_bias_grad[:, cols] += jnp.sum(grad.astype(f32), axis=0, keepdims=True)
        for j in range(width // 512):
            cols = pl.ds(j * 512, 512)
            line.part[s, o, :, cols] = lax.dot_general(
                pre[s, here], up_weight[cols], NT, preferred_element_type=f32
            ).astype(bf16)
        line.share(s, o)

    def work_down(s, o):
        here = rows_of(o, 2 * rows)
        pl.when((s > 0) | (o != at.chip))(lambda: out_copy(s, o).wait())
        for j in range(width // 512):
            cols = pl.ds(j * 512, 512)
            out_stage[:, cols] = jnp.dot(
                act[s, here], down_weight[:, cols], preferred_element_type=f32
            ).astype(bf16)
        out_copy(s, o).start()

    def final(s, there, total):
        back, terms = norm_rows_back(hidden[s, there], total, gain[...])
        first = pl.multiple_of(at.me * rows + there.start, 16)
        grad_out = grad_all[s, pl.ds(first, there.size)].astype(f32)
        grad = grad_out + back
        hidden_grad[s, there] = grad
        grad_low[s, there] = grad.astype(bf16)
        add_row(sums, 0, terms)
        add_row(sums, 1, total)
        add_row(sums, 2, grad)
        add_row(sums, 3, grad_out)

    kinds = ((down_stage, down_grad), (up_stage, up_grad))

    def tile_copy(kind, t):
        stage, grad = kinds[kind]
        return pltpu.make_async_copy(stage, grad.at[t], tile_sem.at[kind])

    def down_half(t):
        half = down_box.shape[1]
        peer, mine = at.group_peer(t % at.group_bits)
        return pltpu.make_async_remote_copy(
            src_ref=down_grad.at[t, rows_of(1 - mine, half)],
            dst_ref=down_box.at[t],
            send_sem=half_send.at[t],
            recv_sem=half_recv.at[t],
            device_id={"dp": peer},
            device_id_type=MESH,
        )

    def tile_sent(kind, t):
        tile_copy(kind, t).wait()
        if kind == 0:
            down_half(t).start()

    order = [(i // 4, i % 4) for i in range(8)]

    def weight_tile(i):
        for j, (kind, t) in enumerate(order):
            @pl.when(i == j)
            def _():
                stage = kinds[kind][0]
                cols = pl.ds(t * stage.shape[0], stage.shape[0])
                total = 0.0
                for s in range(seqs):
                    if kind == 0:
                        left, right = act[s, :, cols], grad_all[s]
                    else:
                        left, right = buf[s, :, cols], pre[s]
                    total += lax.dot_general(left, right, TN, preferred_element_type=f32)
                if j >= 1:
                    tile_sent(*order[j - 1])
                stage[...] = total.astype(bf16)
                tile_copy(kind, t).start()

    def tile_work(s, o):
        weight_tile(s * at.chips + o)

    own = (4, 5, 6)

    def ops_of(c):
        chips = at.chips
        units = [(s, o) for s in range(seqs) for o in range(chips)]
        ops = gather_ops(c, chips, seqs, 0, "in", own=own, parts=ring.parts)
        ops += scatter_ops(c, chips, seqs, 1, "back", "part", last=4.0)
        for s, o in units:
            needs = gathered_here("in", c, s, o, ring.parts)
            gives = [(3.0, ("part", c, s, o)), (0.0, ("done", c, s, o))]
            needs_down, gives_down = [("done", c, s, o)], []
            if (s, o) == (0, c):
                gives.append((0.0, ("first", c)))
                gives_down.append((0.0, ("first down", c)))
            else:
                needs.append(("first", c))
                needs_down.append(("first down", c))
            rank = (s, abs(o - c))
            ops.append(((2,) + rank, (2, s, o), needs, 4.3, [], gives))
            ops.append(((3,) + rank, (7, s, o), needs_down, 1.4, [], gives_down))
        for e in range(len(order)):
            needs = [("part", c, s, o) for s, o in units]
            needs += [("tile", c, e - 1)] if e else []
            sends = [("axis%d" % (e % 2), c, ("half", c, e), PIECE)] if e < 4 else []
            code = (3, e // chips, e % chips)
            ops.append(((4, e, 0), code, needs, 2.7, sends, [(0.0, ("tile", c, e))]))
        return ops

    actions = {2: work, 3: tile_work, 7: work_down}
    actions.update({**ring.actions(0, own), **line.actions(1, final)})
    Plan(at, seqs, ops_of).run(actions)
    tile_sent(*order[7])
    ring.finish()
    line.finish()
    for t in range(4):
        down_half(t).wait()
    out_copy(0, 0).wait()


def mlp_block(n, normed, grad_all, up_weight, up_bias, down_weight, hidden, gain):
    seqs, rows, width = normed.shape
    slots = n * rows
    units = up_weight.shape[1]
    hbm = pl.BlockSpec(memory_space=pl.ANY)
    vmem = pl.BlockSpec(memory_space=VMEM)
    down_size, up_size = units // 4, width // 4
    return pl.pallas_call(
        functools.partial(mlp_kernel, n),
        out_shape=(
            jax.ShapeDtypeStruct((seqs, slots, width), bf16),
            jax.ShapeDtypeStruct((seqs, rows, width), f32),
            jax.ShapeDtypeStruct((seqs, rows, width), bf16),
            jax.ShapeDtypeStruct((4, width), f32),
            jax.ShapeDtypeStruct((4, up_size, units), bf16),
            jax.ShapeDtypeStruct((1, units), f32),
            jax.ShapeDtypeStruct((4, down_size, width), bf16),
            jax.ShapeDtypeStruct((4, down_size // 2, width), bf16),
        ),
        in_specs=[vmem, hbm, hbm, vmem, hbm, hbm, vmem],
        out_specs=(hbm, vmem, vmem, vmem, hbm, vmem, hbm, hbm),
        scratch_shapes=[VMEM((seqs, slots, width), bf16)]
        + Gather.scratch(n, seqs, 4)
        + [
            VMEM((seqs, slots, width), bf16),
            VMEM(up_weight.shape, bf16),
            VMEM(down_weight.shape, bf16),
            VMEM(hidden.shape, f32),
            DMA((4,)),
        ]
        + Scatter.scratch(n, seqs, rows, width)
        + [
            VMEM((seqs, slots, units), bf16),
            VMEM((seqs, slots, units), bf16),
            VMEM((2 * rows, width), bf16),
            DMA((1,)),
            VMEM((up_size, units), bf16),
            VMEM((down_size, width), bf16),
            DMA((2,)),
            DMA((4,)),
            DMA((4,)),
        ],
        compiler_params=pltpu.CompilerParams(
            collective_id=3, has_side_effects=True, vmem_limit_bytes=62 * 2**20
        ),
        name="mlp_block",
    )(normed, grad_all, up_weight, up_bias, down_weight, hidden, gain)


def attn_grad_kernel(
    n,
    grad,
    mlp_part,
    hidden_hbm,
    bias,
    weight_hbm,
    mixed_hbm,
    sums,
    up_bias_part,
    up_part,
    down_part,
    down_box,
    lengths,
    heads_hbm,
    output,
    grads,
    weight_grad,
    sums_all,
    up_bias_grad,
    up_grad,
    down_grad,
    buf,
    send,
    recv,
    *scratch,
):
    at = Place(n)
    seqs, rows, width = grad.shape
    line = Scatter(at, rows, *scratch[:7])
    load_sem, tile_sem, box_sem = scratch[7:10]
    ring = Gather(at, rows, buf, send, recv)
    up_sum = GroupSum(at, up_part.shape[1], *scratch[10:15], up_grad, turn=1)
    down_sum = GroupSum(at, down_part.shape[1], *scratch[15:20], down_grad, skip=1)
    small = SmallSum(at, *scratch[20:24], True)
    small_bias = SmallSum(at, *scratch[24:28], False)
    grad_heads, grad_key, grad_value, hidden, weight, mixed, heads, in_sem = scratch[28:]
    sources = (weight_hbm, weight), (hidden_hbm, hidden), (mixed_hbm, mixed), (heads_hbm, heads)
    loads = [
        pltpu.make_async_copy(source, target, in_sem.at[i])
        for i, (source, target) in enumerate(sources)
    ]
    for copy in loads:
        copy.start()
    def up_load(t):
        return pltpu.make_async_copy(up_part.at[t], up_sum.tiles.at[t], tile_sem.at[0, t])

    def down_load(t):
        half = down_box.shape[1]
        kept = down_part.at[t, down_sum.span(down_sum.base(t, 1), half)]
        return (
            pltpu.make_async_copy(kept, down_sum.tiles.at[t], tile_sem.at[1, t]),
            pltpu.make_async_copy(down_box.at[t], down_sum.box(t, 0), box_sem.at[t]),
        )

    def up_loaded(t):
        up_load(t).wait()

    def down_loaded(t):
        for copy in down_load(t):
            copy.wait()

    for t in range(4):
        if t < up_sum.count:
            up_load(t).start()
        for copy in down_load(t):
            copy.start()
    small.rows[0] = sums[...]
    small_bias.rows[0] = up_bias_part[...]

    def load(s, o):
        return pltpu.make_async_copy(
            mlp_part.at[s, rows_of(o, 2 * rows)], line.part.at[s, o], load_sem.at[s, o]
        )

    def load_one(i, carry):
        load(i // at.chips, lax.rem(i, at.chips)).start()
        return carry

    each = seqs * at.chips
    lax.fori_loop(0, each, load_one, 0)
    for s in range(seqs):
        buf[s, rows_of(at.me, rows)] = grad[s]
    at.greet(groups=True, cube=True)

    def final(s, there, total):
        output[s, there] = (hidden[s, there] + total + bias[...]).astype(bf16)

    def share(s, o):
        load(s, o).wait()
        line.share(s, o)

    def work(s, o):
        ring.arrived(s, o)
        here = rows_of(o, 2 * rows)
        grad_heads[s, here] = lax.dot_general(
            buf[s, here], weight[...], NT, preferred_element_type=f32
        ).astype(bf16)

    def loaded(s, o):
        for copy in loads:
            copy.wait()

    def back(s, o):
        block = min(512, n * rows)
        attend_back(heads, grad_heads, lengths, grads, grad_key, grad_value, block, s)

    def weight_work(s, o):
        for j in range(width // 512):
            cols = pl.ds(j * 512, 512)
            total = 0.0
            for q in range(seqs):
                total += lax.dot_general(mixed[q], buf[q, :, cols], TN, preferred_element_type=f32)
            weight_grad[:, cols] = total.astype(bf16)

    def up_event(first, s, o):
        up_sum.event(first + s * at.chips + o, up_loaded)

    def down_event(first, s, o):
        down_sum.event(first + s * at.chips + o, down_loaded)

    def ops_of(c):
        chips = at.chips
        code_of = lambda kind, e: (kind + e // each, e % each // chips, e % chips)
        have = ("loaded", c)
        ops = [((0, 0, 0), (6, 0, 0), gathered_here("in", c, 0, c), 0.2, [], [(0.0, have)])]
        for s in range(seqs):
            needs = [("done", c, s, o) for o in range(chips)]
            ops.append(((4, s, 0), (4, s, 0), needs, 8.0, [], []))
        needs = [("done", c, s, o) for s in range(seqs) for o in range(chips)]
        ops.append(((5, 0, 0), (5, 0, 0), needs, 3.0, [], []))
        for rank, code, needs, time, sends, gives in scatter_ops(
            c, chips, seqs, 1, "out", "part", last=4.0, parts=line.parts
        ):
            needs = needs + [have] if code[2] == c else needs
            ops.append((rank, code, needs, time, sends, gives))
        return ops + (
            gather_ops(c, chips, seqs, 0, "in")
            + work_ops(
                c,
                chips,
                seqs,
                2,
                lambda s, o: gathered_here("in", c, s, o) + [have],
                "done",
                1.0,
            )
            + work_ops(c, chips, seqs, 3, lambda s, o: [], "part", 0.3, rank=0, far=True)
            + group_ops(
                c, at.group_bits, 3, PIECE, lambda e: code_of(8, e), 0, (1,), 0.7, -1, "up"
            )
            + group_ops(
                c, at.group_bits, 4, PIECE, lambda e: code_of(16, e), 1, (0,), 0.7, -1, "down"
            )
        )

    actions = {2: work, 3: share, **ring.actions(0), **line.actions(1, final)}
    actions[4], actions[5], actions[6] = back, weight_work, loaded
    for i in range(-(-up_sum.events() // each)):
        actions[8 + i] = functools.partial(up_event, i * each)
    for i in range(-(-down_sum.events() // each)):
        actions[16 + i] = functools.partial(down_event, i * each)

    def beside(k):
        pl.when(lax.rem(k, 8) == 0)(lambda: small.event(k // 8))
        small_bias.event(k)

    Plan(at, seqs, ops_of).run(actions, beside)
    sums_all[...] = small.rows[small.phases]
    up_bias_grad[...] = small_bias.rows[small_bias.phases]
    ring.finish()
    line.finish()
    small.finish()
    small_bias.finish()
    up_sum.finish()
    down_sum.finish()


def attn_grad(
    n,
    grad,
    mlp_part,
    hidden,
    bias,
    weight,
    mixed,
    sums,
    up_bias_part,
    up_part,
    down_part,
    down_box,
    lengths,
    heads,
):
    seqs, rows, width = grad.shape
    slots = n * rows
    part = weight.shape[0]
    units = up_part.shape[2]
    dp = lax.axis_size("dp")
    vmem = pl.BlockSpec(memory_space=VMEM)
    hbm = pl.BlockSpec(memory_space=pl.ANY)
    return pl.pallas_call(
        functools.partial(attn_grad_kernel, n),
        out_shape=(
            jax.ShapeDtypeStruct((seqs, rows, width), bf16),
            jax.ShapeDtypeStruct(heads.shape, bf16),
            jax.ShapeDtypeStruct((part, width), bf16),
            jax.ShapeDtypeStruct(sums.shape, f32),
            jax.ShapeDtypeStruct((1, units), f32),
            jax.ShapeDtypeStruct((3,) + up_part.shape[1:], bf16),
            jax.ShapeDtypeStruct(down_part.shape, bf16),
        ),
        in_specs=[vmem, hbm, hbm, vmem, hbm, hbm, vmem, vmem]
        + [hbm] * 3
        + [pl.BlockSpec(memory_space=pltpu.SMEM), hbm],
        out_specs=(vmem,) * 5 + (hbm, hbm),
        scratch_shapes=[VMEM((seqs, slots, width), bf16)]
        + Gather.scratch(n, seqs)
        + Scatter.scratch(n, seqs, rows, width, 2)
        + [DMA((seqs, n // 2)), DMA((2, 4)), DMA((4,))]
        + GroupSum.scratch(dp, 3, width // 4, units)
        + GroupSum.scratch(dp, 4, units // 4, width, 1)
        + SmallSum.scratch(dp, n, sums.shape[0], width, True)
        + SmallSum.scratch(dp, n, 1, units, False)
        + [VMEM((seqs, slots, part), bf16), VMEM((slots, HD), f32), VMEM((slots, HD), f32)]
        + [VMEM(hidden.shape, f32)]
        + [VMEM(a.shape, bf16) for a in (weight, mixed, heads)]
        + [DMA((4,))],
        compiler_params=pltpu.CompilerParams(
            collective_id=4, has_side_effects=True, vmem_limit_bytes=62 * 2**20
        ),
        name="attn_grad",
    )(
        grad,
        mlp_part,
        hidden,
        bias,
        weight,
        mixed,
        sums,
        up_bias_part,
        up_part,
        down_part,
        down_box,
        lengths,
        heads,
    )


def finish_kernel(*refs):
    up_last, sums_two, sums_one = refs[8:11]
    targets = refs[11:]
    step = pl.program_id(0)
    last = step == pl.num_programs(0) - 1
    for i, (source, target) in enumerate(zip(refs[:8], targets)):
        if i > 0:
            target[...] = source[...].astype(target.dtype)

    @pl.when(last)
    def _():
        targets[0][...] = up_last[...].astype(f32)

    @pl.when(jnp.logical_not(last))
    def _():
        targets[0][...] = refs[0][...].astype(f32)

    rows = [sums_one[i : i + 1] for i in range(2)] + [sums_two[i : i + 1] for i in range(4)]
    for row, target in zip(rows, targets[8:]):
        target[...] = row


def finish(blocks, wholes, up_last, sums_two, sums_one, steps=4):
    width = sums_one.shape[1]
    ins, outs, shapes = [], [], []
    for i, (a, kind, count) in enumerate(blocks):
        block = (count // steps, a.shape[1])
        held = a.shape[0] // block[0] - 1
        ins.append(pl.BlockSpec(block, lambda i, held=held: (jnp.minimum(i, held), 0)))
        outs.append(pl.BlockSpec(block, lambda i: (i, 0)))
        shapes.append(jax.ShapeDtypeStruct((count, a.shape[1]), kind))
    whole_specs = [pl.BlockSpec(a.shape, lambda i: (0, 0)) for a in wholes]
    shapes += [jax.ShapeDtypeStruct(a.shape, f32) for a in wholes]
    lasts = (up_last, sums_two, sums_one)
    return pl.pallas_call(
        finish_kernel,
        grid=(steps,),
        out_shape=shapes + [jax.ShapeDtypeStruct((1, width), f32)] * 6,
        in_specs=ins + whole_specs + [pl.BlockSpec(a.shape, lambda i: (0, 0)) for a in lasts],
        out_specs=outs + whole_specs + [pl.BlockSpec((1, width), lambda i: (0, 0))] * 6,
        compiler_params=pltpu.CompilerParams(vmem_limit_bytes=62 * 2**20),
        name="finish",
    )(*[block[0] for block in blocks], *wholes, *lasts)


def body(
    tokens,
    cotangent,
    lengths,
    ln1_gain,
    ln1_shift,
    qkv_weight,
    qkv_bias,
    out_weight,
    out_bias,
    ln2_gain,
    ln2_shift,
    up_weight,
    up_bias,
    down_weight,
    down_bias,
):
    n = lax.axis_size("tensor")
    gathered_one, heads, mixed_heads, hidden_state, normed_two, grad_mlp = attention_block(
        n,
        tokens,
        cotangent,
        lengths,
        ln1_gain[None],
        ln1_shift[None],
        qkv_weight,
        qkv_bias,
        out_weight,
        out_bias[None],
        ln2_gain[None],
        ln2_shift[None],
    )
    (
        mlp_part,
        hidden_grad,
        grad_attn,
        sums,
        up_part,
        up_bias_part,
        down_part,
        down_box,
    ) = mlp_block(
        n, normed_two, grad_mlp, up_weight, up_bias[None], down_weight, hidden_state, ln2_gain[None]
    )
    output, grads, out_part, sums, up_bias_grad, up_weight_grad, down_weight_grad = attn_grad(
        n,
        grad_attn,
        mlp_part,
        hidden_state,
        down_bias[None],
        out_weight,
        mixed_heads,
        sums,
        up_bias_part,
        up_part,
        down_part,
        down_box,
        lengths,
        heads,
    )
    input_grad, sums_one, qkv_weight_grad, out_weight_grad, qkv_bias_grad, up_last = heads_scatter(
        n, grads, qkv_weight, gathered_one, out_part, tokens, ln1_gain[None], hidden_grad, up_part
    )
    width, part, units = tokens.shape[2], qkv_weight.shape[2], up_weight.shape[1]
    seq_rows = tokens.shape[0] * tokens.shape[1]
    (
        up_weight_grad,
        down_weight_grad,
        qkv_weight_grad,
        out_weight_grad,
        output,
        input_grad,
        qkv_bias_grad,
        up_bias_grad,
        *rows,
    ) = finish(
        (
            (up_weight_grad.reshape(-1, units), f32, width),
            (down_weight_grad.reshape(-1, width), f32, units),
            (qkv_weight_grad.reshape(-1, part), f32, 3 * width),
            (out_weight_grad.reshape(-1, width), f32, part),
            (output.reshape(-1, width), bf16, seq_rows),
            (input_grad.reshape(-1, width), f32, seq_rows),
        ),
        (qkv_bias_grad, up_bias_grad),
        up_last[0],
        sums,
        sums_one,
    )
    ln1_gain_grad, ln1_shift_grad, ln2_gain_grad, ln2_shift_grad, out_bias_grad, down_bias_grad = [
        row[0] for row in rows
    ]
    return (
        output.reshape(tokens.shape),
        input_grad.reshape(tokens.shape),
        ln1_gain_grad,
        ln1_shift_grad,
        qkv_weight_grad.reshape(qkv_weight.shape),
        qkv_bias_grad,
        out_weight_grad,
        out_bias_grad,
        ln2_gain_grad,
        ln2_shift_grad,
        up_weight_grad,
        up_bias_grad[0],
        down_weight_grad,
        down_bias_grad,
    )


def solution(mesh):
    in_specs = (
        P("dp", "tensor", None),
        P("dp", "tensor", None),
        P("dp"),
        P(),
        P(),
        P(None, None, "tensor"),
        P(None, "tensor"),
        P("tensor", None),
        P(),
        P(),
        P(),
        P(None, "tensor"),
        P("tensor"),
        P("tensor", None),
        P(),
    )
    out_specs = (
        P("dp", "tensor", None),
        P("dp", "tensor", None),
        P(),
        P(),
        P(None, None, "tensor"),
        P(None, "tensor"),
        P("tensor", None),
        P(),
        P(),
        P(),
        P(None, "tensor"),
        P("tensor"),
        P("tensor", None),
        P(),
    )
    return jax.shard_map(body, mesh=mesh, in_specs=in_specs, out_specs=out_specs, check_vma=False)
```
